32 devices in a mesh: ta: 2 (over x), gx: 4 (over z), gy: 4 (over y, core).
Axes of the slice: x: 2, y: 2, z: 4, core: 2. Of those that a mesh axis runs over, the one named last changes fastest.
Arguments:
- eigvecs: bfloat16 [2, 4, 8, 24, 3, 2, 128], P('ta', 'gx', 'gy'), may hold values from -6 to 6
- links: bfloat16 [2, 4, 8, 24, 3, 2, 3, 3], P('ta', 'gx', 'gy'), may hold values from -4 to 4
- op_dirs: int32 [8], replicated, may hold values from 0 to 6, as said below
- op_moms: int32 [8], replicated, may hold values from 0 to 2
- perams: bfloat16 [8, 2, 512, 512], P(('ta', 'gx')), may hold values from -0.25 to 0.25
- pair_times: int32 [8, 2], P(('ta', 'gx')), may hold values from 0 to 1
- slot_counts: int32 [8], P(('ta', 'gx')), may hold values from 1 to 1, as said below
Outputs:
- margins: float32 [2, 8, 2, 128, 128], P('ta', 'gy')
- correlators: float32 [8, 8, 2], P(('ta', 'gx'), 'gy')
The draws below stay inside these ranges and needn't reach their ends.
Inputs may be any that keep to these rules, and one draw needn't show every extreme that they name: Owner k holds slot k of the slot dimension; slot_counts[k] is 1 in every draw. `op_dirs`: codes 0, 1, 2 step forward along the first, second, third dimension, codes 3, 4, 5 step backward along them, code 6 is no displacement. Every code is used by some operator. `op_moms`: momentum in units of 2 pi / 24.
All inputs are finite; a program needn't handle non-finite values.
Results may differ from the reference program's by a relative error of at most 0.0061.
Values may be sent and summed in bfloat16 or wider, within the bound.
No kernel may reach another device: no remote copies, remote signals or barrier semaphores. Data moves between devices by JAX's collectives and lax.ppermute only.
A program may use at most 64 MiB of HBM per device.

```python
import math
import jax
import jax.numpy as jnp
from jax import lax

NEV = 128
NOP = 8
LZ = 24
SLOTS = 1
NT = 2
LX = 4
LY = 8
OWNERS = 8
PERAMS = 8
DIM = 512


def draw_slot_counts(key, part):
    first_key, second_key, third_key = jax.random.split(jax.random.fold_in(key, 17), 3)
    first_draw = jax.random.randint(first_key, (OWNERS,), 0, SLOTS)
    second_draw = jax.random.randint(second_key, (OWNERS,), 0, SLOTS)
    slot_fill = 1 + jnp.minimum(first_draw, second_draw)
    busiest = jax.random.randint(third_key, (), 0, OWNERS)
    return jnp.where(jnp.arange(OWNERS) == busiest, SLOTS, slot_fill).astype(jnp.int32)


def draw_op_dirs(key, part):
    first_key, second_key, third_key = jax.random.split(jax.random.fold_in(key, 29), 3)
    every_code = jax.random.permutation(first_key, jnp.arange(7, dtype=jnp.int32))
    extra_codes = jax.random.randint(second_key, (NOP - 7,), 0, 7).astype(jnp.int32)
    listed = jnp.concatenate([every_code, extra_codes])
    order_keys = jax.random.permutation(third_key, jnp.arange(NOP, dtype=jnp.int32))
    return listed[order_keys].astype(jnp.int32)


def plant(values, own_key, smallest, top_value):
    index_at = [jax.random.randint(jax.random.fold_in(own_key, axis), (), 0, length) for axis, length in enumerate(values.shape)]
    longest = values.shape.index(max(values.shape))
    beside = index_at[:longest] + [(index_at[longest] + 1) % values.shape[longest]] + index_at[longest + 1:]
    return values.at[tuple(index_at)].set(smallest).at[tuple(beside)].set(top_value)


def shard_levels(rng, extent, shards, low, top_value):
    def one(axis_at, blocks):
        steps = jax.random.uniform(jax.random.fold_in(jax.random.fold_in(rng, 6), axis_at), (blocks,), jnp.float32, low / len(shards), top_value / len(shards))
        return jnp.repeat(jnp.exp(steps), extent[axis_at] // blocks).reshape((-1,) + (1,) * (len(extent) - axis_at - 1))

    factor_of = one(*shards[0])
    for cut in shards[1:]:
        factor_of = factor_of * one(*cut)
    return factor_of


def bell_draw(rng, extent, deviation, bound, shards=(), kind=jnp.bfloat16):
    result = deviation * jax.random.normal(rng, extent, jnp.float32)
    if shards:
        result = result * shard_levels(rng, extent, shards, -0.22, 0.18)
    return jnp.clip(result, -bound, bound).astype(kind)


def setup_inputs(seed: int = 0) -> dict:
    arg_keys = jax.random.split(jax.random.key(seed), 8)
    return {
        "eigvecs": bell_draw(arg_keys[0], (NT, LX, LY, LZ, 3, 2, NEV), 1.0, 6.0, ((0, 2), (1, 4), (2, 4))),
        "links": bell_draw(arg_keys[1], (NT, LX, LY, LZ, 3, 2, 3, 3), 0.41, 4.0, ((0, 2), (1, 4), (2, 4))),
        "op_dirs": draw_op_dirs(jax.random.fold_in(arg_keys[7], 71), 0),
        "op_moms": plant(jax.random.randint(arg_keys[3], (NOP,), 0, 3), jax.random.fold_in(arg_keys[3], 1), 0, 2).astype(jnp.int32),
        "perams": bell_draw(arg_keys[4], (PERAMS, 2, DIM, DIM), DIM ** -0.5, 0.25, ((0, 8),)),
        "pair_times": plant(jax.random.randint(arg_keys[5], (PERAMS, 2), 0, NT), jax.random.fold_in(arg_keys[5], 1), 0, NT - 1).astype(jnp.int32),
        "slot_counts": draw_slot_counts(jax.random.fold_in(arg_keys[7], 71), 0),
    }


def color_apply(link_dir, vec_field):
    link_real = link_dir[..., 0, :, :].astype(jnp.float32)
    link_imag = link_dir[..., 1, :, :].astype(jnp.float32)
    field_real = vec_field[..., :, 0, :].astype(jnp.float32)
    field_imag = vec_field[..., :, 1, :].astype(jnp.float32)
    real_part = jnp.einsum('...ab,...bn->...an', link_real, field_real) - jnp.einsum('...ab,...bn->...an', link_imag, field_imag)
    imag_part = jnp.einsum('...ab,...bn->...an', link_real, field_imag) + jnp.einsum('...ab,...bn->...an', link_imag, field_real)
    return jnp.stack([real_part, imag_part], axis=-2)

def color_adjoint(link_dir, vec_field):
    link_real = link_dir[..., 0, :, :].astype(jnp.float32)
    link_imag = link_dir[..., 1, :, :].astype(jnp.float32)
    field_real = vec_field[..., :, 0, :].astype(jnp.float32)
    field_imag = vec_field[..., :, 1, :].astype(jnp.float32)
    real_part = jnp.einsum('...ba,...bn->...an', link_real, field_real) + jnp.einsum('...ba,...bn->...an', link_imag, field_imag)
    imag_part = jnp.einsum('...ba,...bn->...an', link_real, field_imag) - jnp.einsum('...ba,...bn->...an', link_imag, field_real)
    return jnp.stack([real_part, imag_part], axis=-2)

def phase_turn(values, momentum, z_coord):
    angle = 2.0 * math.pi * momentum.astype(jnp.float32) * z_coord / z_coord.shape[0]
    cosine = jnp.cos(angle)[:, None, None]
    sine = jnp.sin(angle)[:, None, None]
    values_real = values[..., 0, :]
    values_imag = values[..., 1, :]
    return jnp.stack([cosine * values_real - sine * values_imag, sine * values_real + cosine * values_imag], axis=-2)

def margin_block(vec_field, displaced):
    vectors = vec_field.shape[-1]
    left_matrix = vec_field.reshape(-1, vectors)
    rotated = jnp.stack([displaced[..., 1, :], -displaced[..., 0, :]], axis=-2)
    right_matrix = jnp.concatenate([displaced.reshape(-1, vectors), rotated.reshape(-1, vectors)], axis=1)
    product = jnp.dot(left_matrix.T, right_matrix, preferred_element_type=jnp.float32)
    return product.reshape(vectors, 2, vectors).transpose(1, 0, 2)

def contract(tau_matrix, sink_margin, source_margin):
    order = tau_matrix.shape[-1]
    vectors = sink_margin.shape[-1]
    spins = order // vectors
    count_ops = sink_margin.shape[0]
    tau_real = tau_matrix[0].astype(jnp.float32)
    tau_imag = tau_matrix[1].astype(jnp.float32)
    sink_real = sink_margin[:, 0].astype(jnp.float32)
    sink_imag = sink_margin[:, 1].astype(jnp.float32)
    source_real = source_margin[:, 0].astype(jnp.float32)
    source_imag = source_margin[:, 1].astype(jnp.float32)
    rows_real = tau_real.reshape(spins, vectors, order)
    rows_imag = tau_imag.reshape(spins, vectors, order)
    left_real = jnp.einsum('oab,sbc->osac', sink_real, rows_real) - jnp.einsum('oab,sbc->osac', sink_imag, rows_imag)
    left_imag = jnp.einsum('oab,sbc->osac', sink_real, rows_imag) + jnp.einsum('oab,sbc->osac', sink_imag, rows_real)
    cols_real = tau_real.reshape(order, spins, vectors)
    cols_imag = tau_imag.reshape(order, spins, vectors)
    right_real = jnp.einsum('isd,ocd->oisc', cols_real, source_real) + jnp.einsum('isd,ocd->oisc', cols_imag, source_imag)
    right_imag = jnp.einsum('isd,ocd->oisc', cols_imag, source_real) - jnp.einsum('isd,ocd->oisc', cols_real, source_imag)
    left_real = left_real.reshape(count_ops, order, order)
    left_imag = left_imag.reshape(count_ops, order, order)
    right_real = right_real.reshape(count_ops, order, order)
    right_imag = right_imag.reshape(count_ops, order, order)
    trace_real = lax.optimization_barrier(jnp.sum(left_real * right_real + left_imag * right_imag, axis=(1, 2)))
    trace_imag = lax.optimization_barrier(jnp.sum(left_imag * right_real - left_real * right_imag, axis=(1, 2)))
    return jnp.stack([trace_real, trace_imag], axis=-1) / vectors

def make_branches():
    branches = []
    for d in range(3):
        branches.append(partial_forward(d))
    for d in range(3):
        branches.append(partial_backward(d))
    branches.append(lambda vec_field, link_time: vec_field.astype(jnp.float32))
    return branches

def partial_forward(d):

    def forward(vec_field, link_time):
        return color_apply(link_time[..., d, :, :, :], jnp.roll(vec_field, -1, axis=d))
    return forward

def partial_backward(d):

    def backward(vec_field, link_time):
        carried = color_adjoint(link_time[..., d, :, :, :], vec_field).astype(jnp.bfloat16)
        return jnp.roll(carried, 1, axis=d).astype(jnp.float32)
    return backward

def reference(eigvecs, links, op_dirs, op_moms, perams, pair_times, slot_counts):
    branches = make_branches()
    norm_factor = 1.0 / math.sqrt(3.0 * LX * LY * LZ)
    z_coord = jnp.arange(LZ, dtype=jnp.float32)

    def one_time(inputs):
        vec_field, link_time = inputs
        op_rows = []
        for o in range(NOP):
            moved = lax.switch(op_dirs[o], branches, vec_field, link_time)
            displaced = phase_turn(moved, op_moms[o], z_coord).astype(jnp.bfloat16)
            op_rows.append(margin_block(vec_field, displaced))
        return jnp.stack(op_rows) * norm_factor
    margins = lax.map(one_time, (eigvecs, links))
    margins_b = margins.astype(jnp.bfloat16)

    def one_slot(inputs):
        tau_matrix, pair_row, slot_index = inputs
        sink_margin = lax.dynamic_index_in_dim(margins_b, pair_row[0], 0, keepdims=False)
        source_margin = lax.dynamic_index_in_dim(margins_b, pair_row[1], 0, keepdims=False)
        slot_value = contract(tau_matrix, sink_margin, source_margin)
        is_live = slot_index % SLOTS < slot_counts[slot_index // SLOTS]
        return jnp.where(is_live, slot_value, jnp.zeros_like(slot_value))
    correlators = lax.map(one_slot, (perams, pair_times, jnp.arange(PERAMS, dtype=jnp.int32)))
    return (margins, correlators)
```

```python
import functools
import math

import jax
import jax.numpy as jnp
import numpy as np
from jax import lax
from jax.experimental import pallas as pl
from jax.experimental.pallas import tpu as pltpu
from jax.sharding import PartitionSpec as P

VMEM_LIMIT = 24 * 1024 * 1024
MOMENTA = 3
LINK_COLS = 54
DIRECT_LIMIT = 8


def line_constants(cells_z):
    order = 6 * cells_z
    rows = np.arange(2 * order)
    turned = rows // order
    row = rows % order
    z_row, a_row, r_row = row // 6, (row % 6) // 2, row % 2
    spread = (z_row[:, None] == np.arange(cells_z)[None, :]).astype(np.float32)
    cols = np.arange(128)
    live = cols < 2 * LINK_COLS
    copy, dir_col = cols // LINK_COLS, (cols % LINK_COLS) // 18
    a_col, b_col, part_col = (cols % 18) // 6, (cols % 6) // 2, cols % 2
    source_part = np.where(turned == 0, r_row, 1 - r_row)
    sign = np.where((turned == 1) & (r_row == 0), -1.0, 1.0)
    pick = (a_row[:, None] == a_col[None, :]) & (source_part[:, None] == copy[None, :])
    pick = (pick & live[None, :]) * sign[:, None]
    out = np.arange(order)
    z_out, b_out, s_out = out // 6, (out % 6) // 2, out % 2
    needed = np.where(copy[:, None] == 0, s_out[None, :], 1 - s_out[None, :])
    value = np.where((copy[:, None] == 0) & (s_out[None, :] == 1), -1.0, 1.0)
    expand = []
    for d in range(3):
        hit = (dir_col[:, None] == d) & (b_col[:, None] == b_out[None, :]) & live[:, None]
        expand.append(np.where(hit & (part_col[:, None] == needed), value, 0.0))
    same = (z_row[:, None] == z_out[None, :]).astype(np.float32)
    plain = np.zeros((2 * order, order), np.float32)
    plain[np.arange(order), np.arange(order)] = 1.0
    partner = np.where(r_row == 0, row + 1, row - 1)
    plain[rows[order:], partner[order:]] = sign[order:]
    as_b = lambda x: jnp.asarray(np.asarray(x, np.float32), jnp.bfloat16)
    return (
        as_b(spread),
        as_b(pick),
        as_b(np.stack(expand)),
        as_b(same),
        as_b(plain),
        as_b(wave_constants(cells_z)),
    )


def wave_constants(cells_z):
    z_row = np.arange(6 * cells_z) // 6
    columns = []
    for ahead in range(2):
        for momentum in range(MOMENTA):
            angle = 2.0 * math.pi * momentum * ((z_row + ahead) % cells_z) / cells_z
            columns.append(np.cos(angle))
            columns.append(np.sin(angle))
    left = np.stack(columns, axis=1).astype(np.float32)
    terms = []
    for _ in range(3):
        term = left.astype(jnp.bfloat16).astype(np.float32)
        terms.append(term)
        left = left - term
    return np.concatenate(terms, axis=1)


def halo_fields(cells_x, cells_y):
    pairs = [(0, (cells_x - 1) * cells_y + y) for y in range(cells_y)]
    return pairs + [(1, x * cells_y + cells_y - 1) for x in range(cells_x)]


def local_fields(cells_x, cells_y):
    lines = cells_x * cells_y
    outside = halo_fields(cells_x, cells_y)
    every = [(code, line) for code in range(7) for line in range(lines)]
    return [pair for pair in every if pair not in outside]


def prepare_kernel(cells_x, cells_y, *refs):
    inputs, refs = refs[:10], refs[10:]
    matrix_ref, local_ref, left_ref, phase_ref = refs[:4]
    held, link_rows_ref, sems = refs[4:14], refs[14], refs[15]
    copies = [
        pltpu.make_async_copy(src, dst, sems.at[k])
        for k, (src, dst) in enumerate(zip(inputs, held))
    ]
    for copy in copies:
        copy.start()
    v_ref, link_ref, dirs_ref, moms_ref, spread_ref, pick_ref, expand_ref, near_ref = held[:8]
    plain_ref, waves_ref = held[8:]
    f32, bf16 = jnp.float32, jnp.bfloat16
    order, vectors = v_ref.shape[2], v_ref.shape[3]
    lines = cells_x * cells_y
    link_rows_ref[...] = jnp.zeros_like(link_rows_ref)
    for copy in copies:
        copy.wait()
    for line in range(lines):
        for k in range(LINK_COLS // 2):
            pair = link_ref[line, k].astype(f32)
            link_rows_ref[line, 2 * k : 2 * k + 2] = pair
            link_rows_ref[line, LINK_COLS + 2 * k : LINK_COLS + 2 * k + 2] = pair
    outside = halo_fields(cells_x, cells_y)
    inside = local_fields(cells_x, cells_y)
    for line in range(lines):
        x, y = line // cells_y, line % cells_y
        seen = lax.dot_general(
            spread_ref[...],
            link_rows_ref[line].astype(bf16),
            (((1,), (1,)), ((), ())),
            preferred_element_type=f32,
        )
        seen = (seen * pick_ref[...].astype(f32)).astype(bf16)
        for d in range(3):
            matrix = jnp.dot(seen, expand_ref[d], preferred_element_type=f32)
            matrix = (matrix * near_ref[...].astype(f32)).astype(bf16)
            carried = lax.dot_general(
                matrix[:order],
                v_ref[x, y],
                (((0,), (0,)), ((), ())),
                preferred_element_type=f32,
            ).astype(bf16)
            local_ref[inside.index((3 + d, line))] = jnp.dot(
                plain_ref[...], carried, preferred_element_type=f32
            )
            if (d, line) in outside:
                matrix_ref[outside.index((d, line))] = matrix
                continue
            if d == 2:
                ahead = jnp.concatenate([v_ref[x, y, 6:], v_ref[x, y, :6]], axis=0)
            else:
                ahead = v_ref[x + 1, y] if d == 0 else v_ref[x, y + 1]
            local_ref[inside.index((d, line))] = jnp.dot(
                matrix, ahead, preferred_element_type=f32
            )
        local_ref[inside.index((6, line))] = jnp.dot(
            plain_ref[...], v_ref[x, y], preferred_element_type=f32
        )
        here = v_ref[x, y].astype(f32).T
        columns = slice(line * order, (line + 1) * order)
        left_ref[0, :, columns] = here.astype(bf16)
        left_ref[1, :, columns] = jnp.concatenate([here[:, 6:], here[:, :6]], axis=1).astype(bf16)
    wave_cols = waves_ref.shape[1]
    per_term = wave_cols // 3
    wave_row = lax.broadcasted_iota(jnp.int32, (wave_cols, 2 * vectors), 0) % per_term
    wave_half = lax.broadcasted_iota(jnp.int32, (wave_cols, 2 * vectors), 1) // vectors
    wave_at = wave_row - wave_half
    for o in range(phase_ref.shape[0]):
        code = dirs_ref[o]
        column = 2 * (jnp.where(code == 5, MOMENTA, 0) + moms_ref[o])
        chosen = (wave_at == column).astype(f32).astype(bf16)
        phase_ref[o] = jnp.dot(waves_ref[...], chosen, preferred_element_type=f32)


def low_bit(j):
    return (j & -j).bit_length() - 1


def margin_kernel(cells_x, cells_y, groups, *refs):
    matrix_ref, local_ref, left_ref, phase_ref, halo_x_ref, halo_y_ref, dirs_hbm = refs[:7]
    levels = groups.bit_length() - 1
    out_refs = refs[7 : 8 + levels]
    field_ref, pair_ref, side_ref, dirs_ref, sem = refs[8 + levels :]
    f32, bf16 = jnp.float32, jnp.bfloat16
    copy = pltpu.make_async_copy(dirs_hbm, dirs_ref, sem)
    copy.start()
    lines = cells_x * cells_y
    order, vectors = halo_x_ref.shape[2], halo_x_ref.shape[3]
    for k, (d, line) in enumerate(halo_fields(cells_x, cells_y)):
        x, y = line // cells_y, line % cells_y
        ahead = halo_x_ref[0, y] if d == 0 else halo_y_ref[x, 0]
        field_ref[d, line] = jnp.dot(matrix_ref[k], ahead, preferred_element_type=f32)
    for k, (code, line) in enumerate(local_fields(cells_x, cells_y)):
        field_ref[code, line] = local_ref[k]
    side_ref[0] = left_ref[0]
    side_ref[3] = left_ref[1]
    for line in range(lines):
        x, y = line // cells_y, line % cells_y
        columns = slice(line * order, (line + 1) * order)
        if x + 1 < cells_x:
            ahead = slice((line + cells_y) * order, (line + cells_y + 1) * order)
            side_ref[1, :, columns] = left_ref[0, :, ahead]
        else:
            side_ref[1, :, columns] = halo_x_ref[0, y].astype(f32).T.astype(bf16)
        if y + 1 < cells_y:
            ahead = slice((line + 1) * order, (line + 2) * order)
            side_ref[2, :, columns] = left_ref[0, :, ahead]
        else:
            side_ref[2, :, columns] = halo_y_ref[x, 0].astype(f32).T.astype(bf16)
    copy.wait()
    count_ops = dirs_ref.shape[0]
    own_ops = count_ops // groups
    me = lax.axis_index("gy")
    for j in range(groups):
        for i in range(own_ops):
            o = (me ^ j) * own_ops + i
            code = dirs_ref[o]
            side = jnp.where((code >= 3) & (code < 6), code - 2, 0)
            slot = j * own_ops + i
            for line in range(lines):
                plain = field_ref[code, line, 0:order]
                turned = field_ref[code, line, order : 2 * order]
                cosine = phase_ref[o, :, 0:vectors]
                sine = phase_ref[o, :, vectors : 2 * vectors]
                rows = slice(line * order, (line + 1) * order)
                pair_ref[slot, rows, 0:vectors] = (cosine * plain + sine * turned).astype(bf16)
                pair_ref[slot, rows, vectors : 2 * vectors] = (
                    sine * plain - cosine * turned
                ).astype(bf16)
            product = jnp.dot(side_ref[side], pair_ref[slot], preferred_element_type=f32)
            level = levels if j == 0 else low_bit(j)
            out_ref = out_refs[level]
            place = 0 if j == 0 else j >> (level + 1)
            first = 2 * i * vectors
            out_ref[place, first : first + vectors] = product[:, :vectors].astype(out_ref.dtype)
            out_ref[place, first + vectors : first + 2 * vectors] = product[:, vectors:].astype(
                out_ref.dtype
            )


def fold_kernel(level, *refs):
    held_ref, received, out_ref = refs[0], refs[1:-1], refs[-1]
    f32 = jnp.float32
    for k in range(held_ref.shape[0]):
        j = (2 * k + 1) << level
        total = held_ref[k]
        for b, ref in enumerate(received):
            total = total + ref[j >> (b + 1)].astype(f32)
        out_ref[k] = total.astype(out_ref.dtype)


def share_kernel(levels, *refs):
    held_ref, received, outs = refs[0], refs[1 : 1 + levels], refs[1 + levels :]
    f32 = jnp.float32
    count = len(outs)
    rows = outs[0].shape[0]
    me = lax.axis_index("gx")
    for step, out_ref in enumerate(outs):
        chunk = lax.rem(me + step, count)
        span = pl.ds(pl.multiple_of(chunk * rows, rows), rows)
        total = held_ref[0, span]
        for ref in received:
            total = total + ref[0, span].astype(f32)
        out_ref[...] = total.astype(out_ref.dtype)


def sum_kernel(norm_factor, *refs):
    own_ref, received, out_ref = refs[0], refs[1:-1], refs[-1]
    total = own_ref[...]
    for ref in received:
        total = total + ref[...].astype(jnp.float32)
    out_ref[...] = (total * norm_factor).astype(out_ref.dtype)


def contract_kernel(times, shares, count_chunks, *refs):
    pair_hbm, live_hbm = refs[:2]
    chunks, refs = refs[2 : 2 + count_chunks], refs[2 + count_chunks :]
    tau_ref, margin_ref, corr_ref = refs[:3]
    every_ref, left_ref, right_ref, pair_ref, live_ref, sems = refs[3:]
    f32 = jnp.float32
    copies = [
        pltpu.make_async_copy(src, dst, sems.at[k])
        for k, (src, dst) in enumerate(
            ((pair_hbm, pair_ref), (live_hbm, live_ref))
        )
    ]
    for copy in copies:
        copy.start()
    vectors = every_ref.shape[2]
    count_ops = margin_ref.shape[1]
    order = tau_ref.shape[2]
    spins = order // vectors
    me_t, me_x = lax.axis_index("ta"), lax.axis_index("gx")
    if count_chunks == 1:
        every_ref[...] = chunks[0][...]
    else:
        rows = chunks[0].shape[0]
        for k in range(count_chunks):
            at_t = lax.rem(me_t + k // shares, times)
            at_x = lax.rem(me_x + k % shares, shares)
            span = pl.ds(pl.multiple_of(at_x * rows, rows), rows)
            every_ref[at_t, span] = chunks[k][...]
    for copy in copies:
        copy.wait()
    sink, source = pair_ref[0, 0], pair_ref[0, 1]
    live = live_ref[0] > 0
    for o in range(count_ops):
        first = 2 * o * vectors
        part = lambda t, k: every_ref[t, first + k * vectors : first + (k + 1) * vectors]
        margin_ref[0, o, 0] = part(me_t, 0).astype(f32)
        margin_ref[0, o, 1] = part(me_t, 1).astype(f32)
        a_r, a_i = part(sink, 0), part(sink, 1)
        b_r, b_i = part(source, 0).T, part(source, 1).T
        left_ref[o, 0:vectors, 0:vectors] = a_r
        left_ref[o, 0:vectors, vectors:] = -a_i
        left_ref[o, vectors:, 0:vectors] = a_i
        left_ref[o, vectors:, vectors:] = a_r
        right_ref[o, 0:vectors, 0:vectors] = b_r
        right_ref[o, 0:vectors, vectors:] = -b_i
        right_ref[o, vectors:, 0:vectors] = b_i
        right_ref[o, vectors:, vectors:] = b_r
        real = jnp.zeros((8, vectors), f32)
        imag = jnp.zeros((8, vectors), f32)
        fold = lambda t: jnp.sum(t.reshape(vectors // 8, 8, vectors), axis=0)
        for s in range(spins):
            rows = slice(s * vectors, (s + 1) * vectors)
            x = jnp.dot(
                left_ref[o],
                jnp.concatenate([tau_ref[0, rows], tau_ref[1, rows]], axis=0),
                preferred_element_type=f32,
            )
            for c in range(spins):
                cols = slice(c * vectors, (c + 1) * vectors)
                y = jnp.dot(
                    jnp.concatenate([tau_ref[0, rows, cols], tau_ref[1, rows, cols]], axis=1),
                    right_ref[o],
                    preferred_element_type=f32,
                )
                x_r, x_i = x[:vectors, cols], x[vectors:, cols]
                y_r, y_i = y[:, :vectors], y[:, vectors:]
                real = real + fold(x_r * y_r + x_i * y_i)
                imag = imag + fold(x_i * y_r - x_r * y_i)
        scale = 1.0 / vectors
        corr_ref[0, o, 0] = jnp.where(live, jnp.sum(real) * scale, 0.0)
        corr_ref[0, o, 1] = jnp.where(live, jnp.sum(imag) * scale, 0.0)


def vmem_spec():
    return pl.BlockSpec(memory_space=pltpu.VMEM)


def smem_spec():
    return pl.BlockSpec(memory_space=pltpu.SMEM)


def hbm_spec():
    return pl.BlockSpec(memory_space=pltpu.HBM)


def local_call(body, name, outs, in_specs, out_specs, scratch=(), cost=None):
    return pl.pallas_call(
        body,
        out_shape=outs,
        in_specs=in_specs,
        out_specs=out_specs,
        scratch_shapes=list(scratch),
        compiler_params=pltpu.CompilerParams(vmem_limit_bytes=VMEM_LIMIT),
        cost_estimate=cost,
        name=name,
    )


def from_ahead(block, axis):
    count = lax.axis_size(axis)
    return lax.ppermute(block, axis, [((i + 1) % count, i) for i in range(count)])


def per_device(eigvecs, links, op_dirs, op_moms, perams, pair_times, slot_counts):
    f32, bf16 = jnp.float32, jnp.bfloat16
    _, cells_x, cells_y, cells_z, colors, _, vectors = eigvecs.shape
    order = cells_z * colors * 2
    lines = cells_x * cells_y
    count_ops = op_dirs.shape[0]
    times, shares, groups = lax.axis_size("ta"), lax.axis_size("gx"), lax.axis_size("gy")
    levels = groups.bit_length() - 1
    own_ops = count_ops // groups
    own_rows = own_ops * 2 * vectors
    field = eigvecs.reshape(cells_x, cells_y, order, vectors)
    halo_x = from_ahead(field[0:1], "gx")
    halo_y = from_ahead(field, "gy")
    link_field = links[0].transpose(0, 1, 3, 5, 6, 4, 2).reshape(lines, 27, 2, cells_z)
    constants = line_constants(cells_z)
    outside, inside = halo_fields(cells_x, cells_y), local_fields(cells_x, cells_y)
    inputs = (field, link_field, op_dirs, op_moms) + constants
    held = [
        pltpu.SMEM(x.shape, x.dtype) if x.ndim == 1 else pltpu.VMEM(x.shape, x.dtype)
        for x in inputs
    ]
    matrices, local, left, phases = local_call(
        functools.partial(prepare_kernel, cells_x, cells_y),
        "prepare_lines",
        (
            jax.ShapeDtypeStruct((len(outside), 2 * order, order), bf16),
            jax.ShapeDtypeStruct((len(inside), 2 * order, vectors), f32),
            jax.ShapeDtypeStruct((2, vectors, lines * order), bf16),
            jax.ShapeDtypeStruct((count_ops, order, 2 * vectors), f32),
        ),
        [hbm_spec()] * len(inputs),
        (vmem_spec(),) * 4,
        held
        + [
            pltpu.VMEM((lines, 128, cells_z), f32),
            pltpu.SemaphoreType.DMA((len(inputs),)),
        ],
    )(*inputs)
    part_shapes = [
        jax.ShapeDtypeStruct((groups >> (b + 1), own_rows, vectors), f32)
        for b in range(levels)
    ] + [jax.ShapeDtypeStruct((1, own_rows, vectors), f32)]
    parts = local_call(
        functools.partial(margin_kernel, cells_x, cells_y, groups),
        "partial_margins",
        tuple(part_shapes),
        [vmem_spec()] * 6 + [hbm_spec()],
        (vmem_spec(),) * len(part_shapes),
        [
            pltpu.VMEM((7, lines, 2 * order, vectors), f32),
            pltpu.VMEM((count_ops, lines * order, 2 * vectors), bf16),
            pltpu.VMEM((4, vectors, lines * order), bf16),
            pltpu.SMEM((count_ops,), jnp.int32),
            pltpu.SemaphoreType.DMA,
        ],
    )(matrices, local, left, phases, halo_x, halo_y, op_dirs)
    received = []
    for b in range(levels):
        sent = parts[b]
        if b:
            sent = local_call(
                functools.partial(fold_kernel, b),
                "fold_groups",
                jax.ShapeDtypeStruct(sent.shape, f32),
                [vmem_spec()] * (1 + b),
                vmem_spec(),
            )(sent, *received)
        received.append(lax.ppermute(sent, "gy", [(i, i ^ (1 << b)) for i in range(groups)]))
    norm_factor = 1.0 / math.sqrt(3.0 * cells_x * shares * cells_y * groups * cells_z)
    direct = times * shares <= DIRECT_LIMIT and own_rows % shares == 0
    steps = shares if direct else 1
    rows = own_rows // steps
    chunk_shapes = [jax.ShapeDtypeStruct((rows, vectors), f32) for k in range(steps)]
    chunks = local_call(
        functools.partial(share_kernel, levels),
        "share_rows",
        tuple(chunk_shapes),
        [vmem_spec()] * (1 + levels),
        (vmem_spec(),) * steps,
    )(parts[levels], *received)
    if direct:
        arrived = [
            lax.ppermute(chunks[k], "gx", [(i, (i + k) % shares) for i in range(shares)])
            for k in range(1, shares)
        ]
        own = local_call(
            functools.partial(sum_kernel, norm_factor),
            "sum_shares",
            jax.ShapeDtypeStruct((rows, vectors), bf16),
            [vmem_spec()] * shares,
            vmem_spec(),
        )(chunks[0], *arrived)
        every = [own]
        for k in range(1, times * shares):
            step_t, step_x = k // shares, k % shares
            perm = []
            for t in range(times):
                for x in range(shares):
                    source = ((t + step_t) % times) * shares + (x + step_x) % shares
                    perm.append((source, t * shares + x))
            every.append(lax.ppermute(own, ("ta", "gx"), perm))
    else:
        own = (lax.psum(chunks[0], "gx") * norm_factor).astype(bf16)
        every = [lax.all_gather(own, "ta", axis=0, tiled=False)]
    margins, correlators = local_call(
        functools.partial(contract_kernel, times, shares, len(every)),
        "contraction",
        (
            jax.ShapeDtypeStruct((1, own_ops, 2, vectors, vectors), f32),
            jax.ShapeDtypeStruct((1, own_ops, 2), f32),
        ),
        [hbm_spec()] * 2 + [vmem_spec()] * (len(every) + 1),
        (vmem_spec(), smem_spec()),
        [
            pltpu.VMEM((times, own_rows, vectors), bf16),
            pltpu.VMEM((own_ops, 2 * vectors, 2 * vectors), bf16),
            pltpu.VMEM((own_ops, 2 * vectors, 2 * vectors), bf16),
            pltpu.SMEM((1, 2), jnp.int32),
            pltpu.SMEM((1,), jnp.int32),
            pltpu.SemaphoreType.DMA((2,)),
        ],
    )(pair_times, slot_counts, *every, perams[0])
    return (margins, correlators)


def solution(mesh):
    placed = (
        P("ta", "gx", "gy", None, None, None, None),
        P("ta", "gx", "gy", None, None, None, None, None),
        P(),
        P(),
        P(("ta", "gx"), None, None, None),
        P(("ta", "gx"), None),
        P(("ta", "gx")),
    )
    return jax.shard_map(
        per_device,
        mesh=mesh,
        in_specs=placed,
        out_specs=(P("ta", "gy", None, None, None), P(("ta", "gx"), "gy", None)),
        check_vma=False,
    )
```

```python
import functools
import math

import jax
import jax.numpy as jnp
import numpy as np
from jax import lax
from jax.experimental import pallas as pl
from jax.experimental.pallas import tpu as pltpu
from jax.sharding import PartitionSpec as P

VMEM_LIMIT = 24 * 1024 * 1024
MOMENTA = 3
LINK_COLS = 54
DIRECT_LIMIT = 8


def wave_constants(cells_z):
    z_row = np.arange(3 * cells_z) // 3
    columns = []
    for ahead in range(2):
        for momentum in range(MOMENTA):
            angle = 2.0 * math.pi * momentum * ((z_row + ahead) % cells_z) / cells_z
            columns.append(np.cos(angle))
            columns.append(np.sin(angle))
    left = np.stack(columns, axis=1).astype(np.float32)
    terms = []
    for _ in range(3):
        term = left.astype(jnp.bfloat16).astype(np.float32)
        terms.append(term)
        left = left - term
    return jnp.asarray(np.concatenate(terms, axis=1), jnp.bfloat16)


def iota(shape, axis):
    return lax.broadcasted_iota(jnp.int32, shape, axis)


def third(x):
    return (x * 21846) >> 16


def one_hot(condition):
    return condition.astype(jnp.float32).astype(jnp.bfloat16)


def planar_order(order):
    row, col = iota((order, order), 0), iota((order, order), 1)
    half = order // 2
    source = jnp.where(row < half, 2 * row, 2 * (row - half) + 1)
    return one_hot(col == source)


def side_by_side(planar):
    half = planar.shape[0] // 2
    return jnp.concatenate([planar[:half], planar[half:]], axis=1).astype(jnp.bfloat16)


def transport(matrix, pair, sign):
    half, vectors = matrix.shape[0] // 2, pair.shape[1] // 2
    parts = jnp.dot(matrix, pair, preferred_element_type=jnp.float32)
    real, imag = parts[:half], parts[half:]
    if sign > 0:
        return jnp.concatenate(
            [real[:, :vectors] - imag[:, vectors:], real[:, vectors:] + imag[:, :vectors]], axis=0
        )
    return jnp.concatenate(
        [real[:, :vectors] + imag[:, vectors:], real[:, vectors:] - imag[:, :vectors]], axis=0
    )


def halo_fields(cells_x, cells_y):
    pairs = [(0, (cells_x - 1) * cells_y + y) for y in range(cells_y)]
    return pairs + [(1, x * cells_y + cells_y - 1) for x in range(cells_x)]


def local_fields(cells_x, cells_y):
    lines = cells_x * cells_y
    outside = halo_fields(cells_x, cells_y)
    every = [(code, line) for code in range(7) for line in range(lines)]
    return [pair for pair in every if pair not in outside]


def prepare_kernel(cells_x, cells_y, *refs):
    inputs, refs = refs[:5], refs[5:]
    matrix_ref, local_ref, left_ref, phase_ref = refs[:4]
    held, link_rows_ref, sems = refs[4:9], refs[9], refs[10]
    copies = [
        pltpu.make_async_copy(src, dst, sems.at[k])
        for k, (src, dst) in enumerate(zip(inputs, held))
    ]
    for copy in copies:
        copy.start()
    v_ref, link_ref, dirs_ref, moms_ref, waves_ref = held
    f32, bf16 = jnp.float32, jnp.bfloat16
    order, vectors = v_ref.shape[2], v_ref.shape[3]
    half, cells_z = order // 2, order // 6
    lines = cells_x * cells_y
    spread = one_hot(third(iota((half, cells_z), 0)) == iota((half, cells_z), 1))
    row, col = iota((half, LINK_COLS), 0), iota((half, LINK_COLS), 1)
    row_color = row - 3 * third(row)
    pair_at = third(col >> 1)
    col_in, col_out = (col >> 1) - 3 * pair_at, pair_at - 3 * third(pair_at)
    pick = [(row_color == col_out).astype(f32), (row_color == col_in).astype(f32)]
    wide = (LINK_COLS, 6 * 128)
    row, col = iota(wide, 0), iota(wide, 1)
    block, place = col >> 7, col & 127
    color = place - 3 * third(place)
    pair_at = third(row >> 1)
    row_in, row_out = (row >> 1) - 3 * pair_at, pair_at - 3 * third(pair_at)
    fits = 2 * third(pair_at) + (row & 1) == block
    expand = [one_hot(fits & (row_in == color)), one_hot(fits & (row_out == color))]
    row, col = iota((half, 128), 0), iota((half, 128), 1)
    near = ((third(row) == third(col)) & (col < half)).astype(f32)
    planar = planar_order(order)
    for copy in copies:
        copy.wait()
    for line in range(lines):
        for k in range(LINK_COLS // 2):
            link_rows_ref[line, 2 * k : 2 * k + 2] = link_ref[line, k].astype(f32)
    outside = halo_fields(cells_x, cells_y)
    inside = local_fields(cells_x, cells_y)
    ordered = []
    for line in range(lines):
        here = jnp.dot(
            planar, v_ref[line // cells_y, line % cells_y], preferred_element_type=f32
        )
        ordered.append(here)
        local_ref[inside.index((6, line))] = here
    for line in range(lines):
        here = ordered[line]
        ahead_z = jnp.concatenate(
            [here[3:half], here[:3], here[half + 3 :], here[half : half + 3]], axis=0
        )
        columns = slice(line * order, (line + 1) * order)
        left_ref[0, :, columns] = here.T.astype(bf16)
        left_ref[1, :, columns] = ahead_z.T.astype(bf16)
        seen = lax.dot_general(
            spread,
            link_rows_ref[line].astype(bf16),
            (((1,), (1,)), ((), ())),
            preferred_element_type=f32,
        )
        pair = side_by_side(here)
        for way in range(2):
            blocks = jnp.dot(
                (seen * pick[way]).astype(bf16), expand[way], preferred_element_type=f32
            )
            for d in range(3):
                matrix = jnp.concatenate(
                    [
                        blocks[:, 256 * d : 256 * d + 128] * near,
                        blocks[:, 256 * d + 128 : 256 * d + 256] * near,
                    ],
                    axis=0,
                ).astype(bf16)
                if way == 1:
                    carried = transport(matrix[:, :half], pair, -1)
                    local_ref[inside.index((3 + d, line))] = carried.astype(bf16).astype(f32)
                elif (d, line) in outside:
                    matrix_ref[outside.index((d, line))] = matrix
                else:
                    ahead = ahead_z if d == 2 else ordered[line + (cells_y if d == 0 else 1)]
                    local_ref[inside.index((d, line))] = transport(
                        matrix[:, :half], side_by_side(ahead), 1
                    )
    wave_cols = waves_ref.shape[1]
    per_term = wave_cols // 3
    row, col = iota((wave_cols, 2 * vectors), 0), iota((wave_cols, 2 * vectors), 1)
    term = (row >= per_term).astype(jnp.int32) + (row >= 2 * per_term).astype(jnp.int32)
    wave_at = row - per_term * term - (col >= vectors).astype(jnp.int32)
    for o in range(phase_ref.shape[0]):
        column = 2 * (jnp.where(dirs_ref[o] == 5, MOMENTA, 0) + moms_ref[o])
        phase_ref[o] = jnp.dot(
            waves_ref[...], one_hot(wave_at == column), preferred_element_type=f32
        )


def low_bit(j):
    return (j & -j).bit_length() - 1


def margin_kernel(cells_x, cells_y, groups, *refs):
    matrix_ref, local_ref, left_ref, phase_ref, halo_x_ref, halo_y_ref, dirs_hbm = refs[:7]
    levels = groups.bit_length() - 1
    out_refs = refs[7 : 8 + levels]
    field_ref, side_ref, dirs_ref, sem = refs[8 + levels :]
    f32, bf16 = jnp.float32, jnp.bfloat16
    copy = pltpu.make_async_copy(dirs_hbm, dirs_ref, sem)
    copy.start()
    lines = cells_x * cells_y
    order, vectors = halo_x_ref.shape[2], halo_x_ref.shape[3]
    half = order // 2
    planar = planar_order(order)
    side_ref[0] = left_ref[0]
    side_ref[3] = left_ref[1]
    outside = halo_fields(cells_x, cells_y)
    for d in range(2):
        for line in range(lines):
            x, y = line // cells_y, line % cells_y
            columns = slice(line * order, (line + 1) * order)
            if (d, line) not in outside:
                ahead = line + (cells_y if d == 0 else 1)
                side_ref[1 + d, :, columns] = left_ref[0, :, ahead * order : (ahead + 1) * order]
                continue
            halo = halo_x_ref[0, y] if d == 0 else halo_y_ref[x, 0]
            ahead = jnp.dot(planar, halo, preferred_element_type=f32)
            side_ref[1 + d, :, columns] = ahead.T.astype(bf16)
            matrix = matrix_ref[outside.index((d, line))]
            field_ref[d, line] = transport(matrix[:, :half], side_by_side(ahead), 1)
    for k, (code, line) in enumerate(local_fields(cells_x, cells_y)):
        field_ref[code, line] = local_ref[k]
    copy.wait()
    count_ops = dirs_ref.shape[0]
    own_ops = count_ops // groups
    me = lax.axis_index("gy")
    for j in range(groups):
        for i in range(own_ops):
            o = (me ^ j) * own_ops + i
            code = dirs_ref[o]
            side = jnp.where((code >= 3) & (code < 6), code - 2, 0)
            cosine = phase_ref[o, :, 0:vectors]
            sine = phase_ref[o, :, vectors : 2 * vectors]
            pairs = []
            for line in range(lines):
                real, imag = field_ref[code, line, 0:half], field_ref[code, line, half:order]
                turned_r, turned_i = cosine * real - sine * imag, sine * real + cosine * imag
                pairs.append(jnp.concatenate([turned_r, turned_i], axis=1))
                pairs.append(jnp.concatenate([turned_i, -turned_r], axis=1))
            product = jnp.dot(
                side_ref[side],
                jnp.concatenate(pairs, axis=0).astype(bf16),
                preferred_element_type=f32,
            )
            level = levels if j == 0 else low_bit(j)
            out_ref = out_refs[level]
            place = 0 if j == 0 else j >> (level + 1)
            first = 2 * i * vectors
            out_ref[place, first : first + vectors] = product[:, :vectors]
            out_ref[place, first + vectors : first + 2 * vectors] = product[:, vectors:]


def fold_kernel(level, *refs):
    held_ref, received, out_ref = refs[0], refs[1:-1], refs[-1]
    f32 = jnp.float32
    for k in range(held_ref.shape[0]):
        j = (2 * k + 1) << level
        total = held_ref[k]
        for b, ref in enumerate(received):
            total = total + ref[j >> (b + 1)].astype(f32)
        out_ref[k] = total.astype(out_ref.dtype)


def share_kernel(levels, *refs):
    held_ref, received, outs = refs[0], refs[1 : 1 + levels], refs[1 + levels :]
    f32 = jnp.float32
    count = len(outs)
    rows = outs[0].shape[0]
    me = lax.axis_index("gx")
    for step, out_ref in enumerate(outs):
        chunk = lax.rem(me + step, count)
        span = pl.ds(pl.multiple_of(chunk * rows, rows), rows)
        total = held_ref[0, span]
        for ref in received:
            total = total + ref[0, span].astype(f32)
        out_ref[...] = total.astype(out_ref.dtype)


def sum_kernel(norm_factor, *refs):
    own_ref, received, out_ref = refs[0], refs[1:-1], refs[-1]
    total = own_ref[...]
    for ref in received:
        total = total + ref[...].astype(jnp.float32)
    out_ref[...] = (total * norm_factor).astype(out_ref.dtype)


def pack_kernel(*refs):
    chunks, out_ref = refs[:-1], refs[-1]
    rows = chunks[0].shape[0]
    me = lax.axis_index("gx")
    for k, ref in enumerate(chunks):
        place = lax.rem(me + k, len(chunks))
        out_ref[pl.ds(pl.multiple_of(place * rows, rows), rows)] = ref[...]


def contract_kernel(times, *refs):
    pair_hbm, live_ref = refs[:2]
    blocks, refs = refs[2 : 2 + times], refs[2 + times :]
    tau_ref, margin_ref, corr_ref = refs[:3]
    every_ref, left_ref, right_ref, pair_ref, sem = refs[3:]
    f32 = jnp.float32
    copy = pltpu.make_async_copy(pair_hbm, pair_ref, sem)
    copy.start()
    vectors = every_ref.shape[2]
    count_ops = margin_ref.shape[1]
    order = tau_ref.shape[2]
    spins = order // vectors
    me_t = lax.axis_index("ta")
    for k in range(times):
        every_ref[lax.rem(me_t + k, times)] = blocks[k][...]
    copy.wait()
    sink, source = pair_ref[0, 0], pair_ref[0, 1]
    live = live_ref[0] > 0
    for o in range(count_ops):
        first = 2 * o * vectors
        part = lambda t, k: every_ref[t, first + k * vectors : first + (k + 1) * vectors]
        margin_ref[0, o, 0] = part(me_t, 0).astype(f32)
        margin_ref[0, o, 1] = part(me_t, 1).astype(f32)
        a_r, a_i = part(sink, 0), part(sink, 1)
        b_r, b_i = part(source, 0).T, part(source, 1).T
        left_ref[o, 0:vectors, 0:vectors] = a_r
        left_ref[o, 0:vectors, vectors:] = -a_i
        left_ref[o, vectors:, 0:vectors] = a_i
        left_ref[o, vectors:, vectors:] = a_r
        right_ref[o, 0:vectors, 0:vectors] = b_r
        right_ref[o, 0:vectors, vectors:] = -b_i
        right_ref[o, vectors:, 0:vectors] = b_i
        right_ref[o, vectors:, vectors:] = b_r
        real = jnp.zeros((8, vectors), f32)
        imag = jnp.zeros((8, vectors), f32)
        fold = lambda t: jnp.sum(t.reshape(vectors // 8, 8, vectors), axis=0)
        for s in range(spins):
            rows = slice(s * vectors, (s + 1) * vectors)
            x = jnp.dot(
                left_ref[o],
                jnp.concatenate([tau_ref[0, rows], tau_ref[1, rows]], axis=0),
                preferred_element_type=f32,
            )
            for c in range(spins):
                cols = slice(c * vectors, (c + 1) * vectors)
                y = jnp.dot(
                    jnp.concatenate([tau_ref[0, rows, cols], tau_ref[1, rows, cols]], axis=1),
                    right_ref[o],
                    preferred_element_type=f32,
                )
                x_r, x_i = x[:vectors, cols], x[vectors:, cols]
                y_r, y_i = y[:, :vectors], y[:, vectors:]
                real = real + fold(x_r * y_r + x_i * y_i)
                imag = imag + fold(x_i * y_r - x_r * y_i)
        scale = 1.0 / vectors
        corr_ref[0, o, 0] = jnp.where(live, jnp.sum(real) * scale, 0.0)
        corr_ref[0, o, 1] = jnp.where(live, jnp.sum(imag) * scale, 0.0)


def vmem_spec():
    return pl.BlockSpec(memory_space=pltpu.VMEM)


def smem_spec():
    return pl.BlockSpec(memory_space=pltpu.SMEM)


def hbm_spec():
    return pl.BlockSpec(memory_space=pltpu.HBM)


def in_hbm(x):
    return pltpu.with_memory_space_constraint(x, pltpu.HBM)


def local_call(body, name, outs, in_specs, out_specs, scratch=(), cost=None):
    return pl.pallas_call(
        body,
        out_shape=outs,
        in_specs=in_specs,
        out_specs=out_specs,
        scratch_shapes=list(scratch),
        compiler_params=pltpu.CompilerParams(vmem_limit_bytes=VMEM_LIMIT),
        cost_estimate=cost,
        name=name,
    )


def from_step(block, axis, step):
    count = lax.axis_size(axis)
    return lax.ppermute(block, axis, [((i + step) % count, i) for i in range(count)])


def per_device(eigvecs, links, op_dirs, op_moms, perams, pair_times, slot_counts):
    f32, bf16 = jnp.float32, jnp.bfloat16
    _, cells_x, cells_y, cells_z, colors, _, vectors = eigvecs.shape
    order = cells_z * colors * 2
    lines = cells_x * cells_y
    count_ops = op_dirs.shape[0]
    times, shares, groups = lax.axis_size("ta"), lax.axis_size("gx"), lax.axis_size("gy")
    levels = groups.bit_length() - 1
    own_ops = count_ops // groups
    own_rows = own_ops * 2 * vectors
    field = eigvecs.reshape(cells_x, cells_y, order, vectors)
    halo_x = from_step(field[0:1], "gx", 1)
    halo_y = from_step(field, "gy", 1)
    link_field = links[0].transpose(0, 1, 3, 5, 6, 4, 2).reshape(lines, 27, 2, cells_z)
    outside, inside = halo_fields(cells_x, cells_y), local_fields(cells_x, cells_y)
    inputs = [field, link_field, op_dirs, op_moms, wave_constants(cells_z)]
    inputs = [in_hbm(x) for x in inputs]
    held = [
        pltpu.SMEM(x.shape, x.dtype) if x.ndim == 1 else pltpu.VMEM(x.shape, x.dtype)
        for x in inputs
    ]
    matrices, local, left, phases = local_call(
        functools.partial(prepare_kernel, cells_x, cells_y),
        "prepare_lines",
        (
            jax.ShapeDtypeStruct((len(outside), order, 128), bf16),
            jax.ShapeDtypeStruct((len(inside), order, vectors), f32),
            jax.ShapeDtypeStruct((2, vectors, lines * order), bf16),
            jax.ShapeDtypeStruct((count_ops, order // 2, 2 * vectors), f32),
        ),
        [hbm_spec()] * len(inputs),
        (vmem_spec(),) * 4,
        held
        + [
            pltpu.VMEM((lines, LINK_COLS, cells_z), f32),
            pltpu.SemaphoreType.DMA((len(inputs),)),
        ],
    )(*inputs)
    part_shapes = [
        jax.ShapeDtypeStruct((groups >> (b + 1), own_rows, vectors), f32)
        for b in range(levels)
    ] + [jax.ShapeDtypeStruct((1, own_rows, vectors), f32)]
    parts = local_call(
        functools.partial(margin_kernel, cells_x, cells_y, groups),
        "partial_margins",
        tuple(part_shapes),
        [vmem_spec()] * 6 + [hbm_spec()],
        (vmem_spec(),) * len(part_shapes),
        [
            pltpu.VMEM((7, lines, order, vectors), f32),
            pltpu.VMEM((4, vectors, lines * order), bf16),
            pltpu.SMEM((count_ops,), jnp.int32),
            pltpu.SemaphoreType.DMA,
        ],
    )(matrices, local, left, phases, halo_x, halo_y, in_hbm(op_dirs))
    received = []
    for b in range(levels):
        sent = parts[b]
        if b:
            sent = local_call(
                functools.partial(fold_kernel, b),
                "fold_groups",
                jax.ShapeDtypeStruct(sent.shape, f32),
                [vmem_spec()] * (1 + b),
                vmem_spec(),
            )(sent, *received)
        received.append(lax.ppermute(sent, "gy", [(i, i ^ (1 << b)) for i in range(groups)]))
    norm_factor = 1.0 / math.sqrt(3.0 * cells_x * shares * cells_y * groups * cells_z)
    direct = shares <= DIRECT_LIMIT and own_rows % (16 * shares) == 0
    steps = shares if direct else 1
    rows = own_rows // steps
    chunk_shapes = [jax.ShapeDtypeStruct((rows, vectors), f32) for k in range(steps)]
    chunks = local_call(
        functools.partial(share_kernel, levels),
        "share_rows",
        tuple(chunk_shapes),
        [vmem_spec()] * (1 + levels),
        (vmem_spec(),) * steps,
    )(parts[levels], *received)
    if direct:
        arrived = [from_step(chunks[k], "gx", -k) for k in range(1, shares)]
        own = local_call(
            functools.partial(sum_kernel, norm_factor),
            "sum_shares",
            jax.ShapeDtypeStruct((rows, vectors), bf16),
            [vmem_spec()] * shares,
            vmem_spec(),
        )(chunks[0], *arrived)
        own = local_call(
            pack_kernel,
            "pack_rows",
            jax.ShapeDtypeStruct((own_rows, vectors), bf16),
            [vmem_spec()] * shares,
            vmem_spec(),
        )(own, *[from_step(own, "gx", k) for k in range(1, shares)])
    else:
        own = (lax.psum(chunks[0], "gx") * norm_factor).astype(bf16)
    every = [own] + [from_step(own, "ta", k) for k in range(1, times)]
    margins, correlators = local_call(
        functools.partial(contract_kernel, times),
        "contraction",
        (
            jax.ShapeDtypeStruct((1, own_ops, 2, vectors, vectors), f32),
            jax.ShapeDtypeStruct((1, own_ops, 2), f32),
        ),
        [hbm_spec(), smem_spec()] + [vmem_spec()] * (len(every) + 1),
        (vmem_spec(), smem_spec()),
        [
            pltpu.VMEM((times, own_rows, vectors), bf16),
            pltpu.VMEM((own_ops, 2 * vectors, 2 * vectors), bf16),
            pltpu.VMEM((own_ops, 2 * vectors, 2 * vectors), bf16),
            pltpu.SMEM((1, 2), jnp.int32),
            pltpu.SemaphoreType.DMA,
        ],
    )(in_hbm(pair_times), slot_counts, *every, perams[0])
    return (margins, correlators)


def solution(mesh):
    placed = (
        P("ta", "gx", "gy", None, None, None, None),
        P("ta", "gx", "gy", None, None, None, None, None),
        P(),
        P(),
        P(("ta", "gx"), None, None, None),
        P(("ta", "gx"), None),
        P(("ta", "gx")),
    )
    return jax.shard_map(
        per_device,
        mesh=mesh,
        in_specs=placed,
        out_specs=(P("ta", "gy", None, None, None), P(("ta", "gx"), "gy", None)),
        check_vma=False,
    )
```

```python
import functools
import math

import jax
import jax.numpy as jnp
import numpy as np
from jax import lax
from jax.experimental import pallas as pl
from jax.experimental.pallas import tpu as pltpu
from jax.sharding import PartitionSpec as P

VMEM_LIMIT = 24 * 1024 * 1024
MOMENTA = 3
LINK_COLS = 54
TAIL = 16
FIXED_BITS = 14.0
DIRECT_LIMIT = 8


def wave_constants(cells_z):
    z_row = np.arange(3 * cells_z) // 3
    columns = []
    for ahead in range(2):
        for momentum in range(MOMENTA):
            angle = 2.0 * math.pi * momentum * ((z_row + ahead) % cells_z) / cells_z
            columns.append(np.cos(angle))
            columns.append(np.sin(angle))
    left = np.stack(columns, axis=1).astype(np.float32)
    terms = []
    for _ in range(3):
        term = left.astype(jnp.bfloat16).astype(np.float32)
        terms.append(term)
        left = left - term
    return jnp.asarray(np.concatenate(terms, axis=1), jnp.bfloat16)


def iota(shape, axis):
    return lax.broadcasted_iota(jnp.int32, shape, axis)


def third(x):
    return (x * 21846) >> 16


def one_hot(condition):
    return condition.astype(jnp.float32).astype(jnp.bfloat16)


def planar_order(order):
    row, col = iota((order, order), 0), iota((order, order), 1)
    half = order // 2
    source = jnp.where(row < half, 2 * row, 2 * (row - half) + 1)
    return one_hot(col == source)


def side_by_side(planar):
    half = planar.shape[0] // 2
    return jnp.concatenate([planar[:half], planar[half:]], axis=1).astype(jnp.bfloat16)


def transport(matrix, pair, sign):
    half, vectors = matrix.shape[0] // 2, pair.shape[1] // 2
    parts = jnp.dot(matrix, pair, preferred_element_type=jnp.float32)
    real, imag = parts[:half], parts[half:]
    if sign > 0:
        return jnp.concatenate(
            [real[:, :vectors] - imag[:, vectors:], real[:, vectors:] + imag[:, :vectors]], axis=0
        )
    return jnp.concatenate(
        [real[:, :vectors] + imag[:, vectors:], real[:, vectors:] - imag[:, :vectors]], axis=0
    )


def halo_fields(cells_x, cells_y):
    pairs = [(0, (cells_x - 1) * cells_y + y) for y in range(cells_y)]
    return pairs + [(1, x * cells_y + cells_y - 1) for x in range(cells_x)]


def local_fields(cells_x, cells_y):
    lines = cells_x * cells_y
    outside = halo_fields(cells_x, cells_y)
    every = [(code, line) for code in range(7) for line in range(lines)]
    return [pair for pair in every if pair not in outside]


def prepare_kernel(cells_x, cells_y, *refs):
    inputs, refs = refs[:5], refs[5:]
    matrix_ref, local_ref, left_ref, phase_ref = refs[:4]
    held, link_rows_ref, sems = refs[4:9], refs[9], refs[10]
    copies = [
        pltpu.make_async_copy(src, dst, sems.at[k])
        for k, (src, dst) in enumerate(zip(inputs, held))
    ]
    for copy in copies:
        copy.start()
    v_ref, link_ref, dirs_ref, moms_ref, waves_ref = held
    f32, bf16 = jnp.float32, jnp.bfloat16
    order, vectors = v_ref.shape[2], v_ref.shape[3]
    half, cells_z = order // 2, order // 6
    lines = cells_x * cells_y
    spread = one_hot(third(iota((half, cells_z), 0)) == iota((half, cells_z), 1))
    row, col = iota((half, LINK_COLS), 0), iota((half, LINK_COLS), 1)
    row_color = row - 3 * third(row)
    pair_at = third(col >> 1)
    col_in, col_out = (col >> 1) - 3 * pair_at, pair_at - 3 * third(pair_at)
    pick = [(row_color == col_out).astype(f32), (row_color == col_in).astype(f32)]
    wide = (LINK_COLS, 6 * 128)
    row, col = iota(wide, 0), iota(wide, 1)
    block, place = col >> 7, col & 127
    color = place - 3 * third(place)
    pair_at = third(row >> 1)
    row_in, row_out = (row >> 1) - 3 * pair_at, pair_at - 3 * third(pair_at)
    fits = 2 * third(pair_at) + (row & 1) == block
    expand = [one_hot(fits & (row_in == color)), one_hot(fits & (row_out == color))]
    row, col = iota((half, 128), 0), iota((half, 128), 1)
    near = ((third(row) == third(col)) & (col < half)).astype(f32)
    planar = planar_order(order)
    for copy in copies:
        copy.wait()
    for line in range(lines):
        for k in range(LINK_COLS // 2):
            link_rows_ref[line, 2 * k : 2 * k + 2] = link_ref[line, k].astype(f32)
    outside = halo_fields(cells_x, cells_y)
    inside = local_fields(cells_x, cells_y)
    ordered = []
    for line in range(lines):
        here = jnp.dot(
            planar, v_ref[line // cells_y, line % cells_y], preferred_element_type=f32
        )
        ordered.append(here)
        local_ref[inside.index((6, line))] = here
    for line in range(lines):
        here = ordered[line]
        ahead_z = jnp.concatenate(
            [here[3:half], here[:3], here[half + 3 :], here[half : half + 3]], axis=0
        )
        columns = slice(line * order, (line + 1) * order)
        left_ref[0, :, columns] = here.T.astype(bf16)
        left_ref[1, :, columns] = ahead_z.T.astype(bf16)
        seen = lax.dot_general(
            spread,
            link_rows_ref[line].astype(bf16),
            (((1,), (1,)), ((), ())),
            preferred_element_type=f32,
        )
        pair = side_by_side(here)
        for way in range(2):
            blocks = jnp.dot(
                (seen * pick[way]).astype(bf16), expand[way], preferred_element_type=f32
            )
            for d in range(3):
                matrix = jnp.concatenate(
                    [
                        blocks[:, 256 * d : 256 * d + 128] * near,
                        blocks[:, 256 * d + 128 : 256 * d + 256] * near,
                    ],
                    axis=0,
                ).astype(bf16)
                if way == 1:
                    carried = transport(matrix[:, :half], pair, -1)
                    local_ref[inside.index((3 + d, line))] = carried.astype(bf16).astype(f32)
                elif (d, line) in outside:
                    matrix_ref[outside.index((d, line))] = matrix
                else:
                    ahead = ahead_z if d == 2 else ordered[line + (cells_y if d == 0 else 1)]
                    local_ref[inside.index((d, line))] = transport(
                        matrix[:, :half], side_by_side(ahead), 1
                    )
    wave_cols = waves_ref.shape[1]
    per_term = wave_cols // 3
    row, col = iota((wave_cols, 2 * vectors), 0), iota((wave_cols, 2 * vectors), 1)
    term = (row >= per_term).astype(jnp.int32) + (row >= 2 * per_term).astype(jnp.int32)
    wave_at = row - per_term * term - (col >= vectors).astype(jnp.int32)
    for o in range(phase_ref.shape[0]):
        column = 2 * (jnp.where(dirs_ref[o] == 5, MOMENTA, 0) + moms_ref[o])
        phase_ref[o] = jnp.dot(
            waves_ref[...], one_hot(wave_at == column), preferred_element_type=f32
        )


def low_bit(j):
    return (j & -j).bit_length() - 1


def margin_kernel(cells_x, cells_y, groups, *refs):
    matrix_ref, local_ref, left_ref, phase_ref, halo_x_ref, halo_y_ref, dirs_hbm = refs[:7]
    levels = groups.bit_length() - 1
    out_refs = refs[7 : 8 + levels]
    field_ref, side_ref, dirs_ref, sem = refs[8 + levels :]
    f32, bf16 = jnp.float32, jnp.bfloat16
    copy = pltpu.make_async_copy(dirs_hbm, dirs_ref, sem)
    copy.start()
    lines = cells_x * cells_y
    order, vectors = halo_x_ref.shape[2], halo_x_ref.shape[3]
    half = order // 2
    planar = planar_order(order)
    side_ref[0] = left_ref[0]
    side_ref[3] = left_ref[1]
    outside = halo_fields(cells_x, cells_y)
    for d in range(2):
        for line in range(lines):
            x, y = line // cells_y, line % cells_y
            columns = slice(line * order, (line + 1) * order)
            if (d, line) not in outside:
                ahead = line + (cells_y if d == 0 else 1)
                side_ref[1 + d, :, columns] = left_ref[0, :, ahead * order : (ahead + 1) * order]
                continue
            halo = halo_x_ref[0, y] if d == 0 else halo_y_ref[x, 0]
            ahead = jnp.dot(planar, halo, preferred_element_type=f32)
            side_ref[1 + d, :, columns] = ahead.T.astype(bf16)
            matrix = matrix_ref[outside.index((d, line))]
            field_ref[d, line] = transport(matrix[:, :half], side_by_side(ahead), 1)
    for k, (code, line) in enumerate(local_fields(cells_x, cells_y)):
        field_ref[code, line] = local_ref[k]
    copy.wait()
    count_ops = dirs_ref.shape[0]
    own_ops = count_ops // groups
    me = lax.axis_index("gy")
    for j in range(groups):
        for i in range(own_ops):
            o = (me ^ j) * own_ops + i
            code = dirs_ref[o]
            side = jnp.where((code >= 3) & (code < 6), code - 2, 0)
            cosine = phase_ref[o, :, 0:vectors]
            sine = phase_ref[o, :, vectors : 2 * vectors]
            pairs = []
            for line in range(lines):
                real, imag = field_ref[code, line, 0:half], field_ref[code, line, half:order]
                turned_r, turned_i = cosine * real - sine * imag, sine * real + cosine * imag
                pairs.append(jnp.concatenate([turned_r, turned_i], axis=1))
                pairs.append(jnp.concatenate([turned_i, -turned_r], axis=1))
            product = jnp.dot(
                side_ref[side],
                jnp.concatenate(pairs, axis=0).astype(bf16),
                preferred_element_type=f32,
            )
            level = levels if j == 0 else low_bit(j)
            out_ref = out_refs[level]
            place = 0 if j == 0 else j >> (level + 1)
            first = 2 * i * vectors
            out_ref[place, first : first + vectors] = product[:, :vectors]
            out_ref[place, first + vectors : first + 2 * vectors] = product[:, vectors:]


def scale_of(block):
    top = jnp.max(jnp.abs(block), axis=0, keepdims=True)
    return jnp.floor(jnp.log2(jnp.maximum(top, 1e-30))) + 1.0


def put_fixed(out_ref, blocks):
    rows, vectors = blocks[0].shape
    tail = iota((TAIL, vectors), 0)
    scales = jnp.zeros((TAIL, vectors), jnp.float32)
    for k, block in enumerate(blocks):
        scale = scale_of(block)
        scales = jnp.where(tail == k, scale, scales)
        fixed = jnp.floor(block * jnp.exp2(FIXED_BITS - scale) + 0.5)
        out_ref[k * rows : (k + 1) * rows] = fixed.astype(jnp.int32).astype(jnp.int16)
    out_ref[len(blocks) * rows :] = scales.astype(jnp.int32).astype(jnp.int16)


def from_fixed(ref, rows, k):
    scales = ref[ref.shape[0] - TAIL :].astype(jnp.int32).astype(jnp.float32)
    block = ref[k * rows : (k + 1) * rows].astype(jnp.int32).astype(jnp.float32)
    return block * jnp.exp2(scales[k : k + 1] - FIXED_BITS)


def fold_kernel(level, count_blocks, *refs):
    held_ref, received, out_ref = refs[0], refs[1:-1], refs[-1]
    rows = held_ref.shape[1] // count_blocks
    for k in range(held_ref.shape[0]):
        j = (2 * k + 1) << level
        blocks = []
        for p in range(count_blocks):
            total = held_ref[k, p * rows : (p + 1) * rows]
            for b, ref in enumerate(received):
                total = total + arrived_block(ref.at[j >> (b + 1)], b, rows, p)
            blocks.append(total)
        put_fixed(out_ref.at[k], blocks)


def arrived_block(ref, level, rows, p):
    return ref[p * rows : (p + 1) * rows] if level == 0 else from_fixed(ref, rows, p)


def share_kernel(levels, count_blocks, *refs):
    held_ref, received, refs = refs[0], refs[1 : 1 + levels], refs[1 + levels :]
    outs, total_ref = refs[:-1], refs[-1]
    span = held_ref.shape[1] // count_blocks
    for p in range(count_blocks):
        total = held_ref[0, p * span : (p + 1) * span]
        for b, ref in enumerate(received):
            total = total + arrived_block(ref.at[0], b, span, p)
        total_ref[p * span : (p + 1) * span] = total
    rows = outs[0].shape[0]
    me = lax.axis_index("gx")
    for step, out_ref in enumerate(outs):
        chunk = lax.rem(me + step, len(outs))
        total = total_ref[pl.ds(pl.multiple_of(chunk * rows, rows), rows)]
        if step:
            put_fixed(out_ref, [total])
        else:
            out_ref[...] = total


def sum_kernel(norm_factor, *refs):
    own_ref, received, out_ref = refs[0], refs[1:-1], refs[-1]
    total = own_ref[...]
    for ref in received:
        total = total + from_fixed(ref, total.shape[0], 0)
    out_ref[...] = (total * norm_factor).astype(out_ref.dtype)


def contract_kernel(times, steps, *refs):
    pair_hbm, live_ref = refs[:2]
    chunks, refs = refs[2 : 2 + times * steps], refs[2 + times * steps :]
    tau_ref, margin_ref, corr_ref = refs[:3]
    every_ref, left_ref, right_ref, pair_ref, sem = refs[3:]
    f32 = jnp.float32
    copy = pltpu.make_async_copy(pair_hbm, pair_ref, sem)
    copy.start()
    vectors = every_ref.shape[2]
    count_ops = margin_ref.shape[1]
    order = tau_ref.shape[2]
    spins = order // vectors
    me_t, me_x = lax.axis_index("ta"), lax.axis_index("gx")
    rows = chunks[0].shape[0]
    for k, ref in enumerate(chunks):
        at_t = lax.rem(me_t + k // steps, times)
        place = lax.rem(me_x + k % steps, steps) if steps > 1 else 0
        every_ref[at_t, pl.ds(pl.multiple_of(place * rows, rows), rows)] = ref[...]
    copy.wait()
    sink, source = pair_ref[0, 0], pair_ref[0, 1]
    live = live_ref[0] > 0
    for o in range(count_ops):
        first = 2 * o * vectors
        part = lambda t, k: every_ref[t, first + k * vectors : first + (k + 1) * vectors]
        margin_ref[0, o, 0] = part(me_t, 0).astype(f32)
        margin_ref[0, o, 1] = part(me_t, 1).astype(f32)
        a_r, a_i = part(sink, 0), part(sink, 1)
        b_r, b_i = part(source, 0).T, part(source, 1).T
        left_ref[o, 0:vectors, 0:vectors] = a_r
        left_ref[o, 0:vectors, vectors:] = -a_i
        left_ref[o, vectors:, 0:vectors] = a_i
        left_ref[o, vectors:, vectors:] = a_r
        right_ref[o, 0:vectors, 0:vectors] = b_r
        right_ref[o, 0:vectors, vectors:] = -b_i
        right_ref[o, vectors:, 0:vectors] = b_i
        right_ref[o, vectors:, vectors:] = b_r
        real = jnp.zeros((8, vectors), f32)
        imag = jnp.zeros((8, vectors), f32)
        fold = lambda t: jnp.sum(t.reshape(vectors // 8, 8, vectors), axis=0)
        for s in range(spins):
            rows = slice(s * vectors, (s + 1) * vectors)
            x = jnp.dot(
                left_ref[o],
                jnp.concatenate([tau_ref[0, rows], tau_ref[1, rows]], axis=0),
                preferred_element_type=f32,
            )
            for c in range(spins):
                cols = slice(c * vectors, (c + 1) * vectors)
                y = jnp.dot(
                    jnp.concatenate([tau_ref[0, rows, cols], tau_ref[1, rows, cols]], axis=1),
                    right_ref[o],
                    preferred_element_type=f32,
                )
                x_r, x_i = x[:vectors, cols], x[vectors:, cols]
                y_r, y_i = y[:, :vectors], y[:, vectors:]
                real = real + fold(x_r * y_r + x_i * y_i)
                imag = imag + fold(x_i * y_r - x_r * y_i)
        scale = 1.0 / vectors
        corr_ref[0, o, 0] = jnp.where(live, jnp.sum(real) * scale, 0.0)
        corr_ref[0, o, 1] = jnp.where(live, jnp.sum(imag) * scale, 0.0)


def vmem_spec():
    return pl.BlockSpec(memory_space=pltpu.VMEM)


def smem_spec():
    return pl.BlockSpec(memory_space=pltpu.SMEM)


def hbm_spec():
    return pl.BlockSpec(memory_space=pltpu.HBM)


def in_hbm(x):
    return pltpu.with_memory_space_constraint(x, pltpu.HBM)


def local_call(body, name, outs, in_specs, out_specs, scratch=(), cost=None):
    return pl.pallas_call(
        body,
        out_shape=outs,
        in_specs=in_specs,
        out_specs=out_specs,
        scratch_shapes=list(scratch),
        compiler_params=pltpu.CompilerParams(vmem_limit_bytes=VMEM_LIMIT),
        cost_estimate=cost,
        name=name,
    )


def from_step(block, axis, step):
    count = lax.axis_size(axis)
    return lax.ppermute(block, axis, [((i + step) % count, i) for i in range(count)])


def per_device(eigvecs, links, op_dirs, op_moms, perams, pair_times, slot_counts):
    f32, bf16 = jnp.float32, jnp.bfloat16
    _, cells_x, cells_y, cells_z, colors, _, vectors = eigvecs.shape
    order = cells_z * colors * 2
    lines = cells_x * cells_y
    count_ops = op_dirs.shape[0]
    times, shares, groups = lax.axis_size("ta"), lax.axis_size("gx"), lax.axis_size("gy")
    levels = groups.bit_length() - 1
    own_ops = count_ops // groups
    own_rows = own_ops * 2 * vectors
    field = eigvecs.reshape(cells_x, cells_y, order, vectors)
    halo_x = from_step(field[0:1], "gx", 1)
    halo_y = from_step(field, "gy", 1)
    link_field = links[0].transpose(0, 1, 3, 5, 6, 4, 2).reshape(lines, 27, 2, cells_z)
    outside, inside = halo_fields(cells_x, cells_y), local_fields(cells_x, cells_y)
    inputs = [field, link_field, op_dirs, op_moms, wave_constants(cells_z)]
    inputs = [in_hbm(x) for x in inputs]
    held = [
        pltpu.SMEM(x.shape, x.dtype) if x.ndim == 1 else pltpu.VMEM(x.shape, x.dtype)
        for x in inputs
    ]
    matrices, local, left, phases = local_call(
        functools.partial(prepare_kernel, cells_x, cells_y),
        "prepare_lines",
        (
            jax.ShapeDtypeStruct((len(outside), order, 128), bf16),
            jax.ShapeDtypeStruct((len(inside), order, vectors), f32),
            jax.ShapeDtypeStruct((2, vectors, lines * order), bf16),
            jax.ShapeDtypeStruct((count_ops, order // 2, 2 * vectors), f32),
        ),
        [hbm_spec()] * len(inputs),
        (vmem_spec(),) * 4,
        held
        + [
            pltpu.VMEM((lines, LINK_COLS, cells_z), f32),
            pltpu.SemaphoreType.DMA((len(inputs),)),
        ],
    )(*inputs)
    part_shapes = [
        jax.ShapeDtypeStruct((groups >> (b + 1), own_rows, vectors), f32)
        for b in range(levels)
    ] + [jax.ShapeDtypeStruct((1, own_rows, vectors), f32)]
    parts = local_call(
        functools.partial(margin_kernel, cells_x, cells_y, groups),
        "partial_margins",
        tuple(part_shapes),
        [vmem_spec()] * 6 + [hbm_spec()],
        (vmem_spec(),) * len(part_shapes),
        [
            pltpu.VMEM((7, lines, order, vectors), f32),
            pltpu.VMEM((4, vectors, lines * order), bf16),
            pltpu.SMEM((count_ops,), jnp.int32),
            pltpu.SemaphoreType.DMA,
        ],
    )(matrices, local, left, phases, halo_x, halo_y, in_hbm(op_dirs))
    received = []
    for b in range(levels):
        sent = parts[b]
        if b:
            sent = local_call(
                functools.partial(fold_kernel, b, 2 * own_ops),
                "fold_groups",
                jax.ShapeDtypeStruct((sent.shape[0], own_rows + TAIL, vectors), jnp.int16),
                [vmem_spec()] * (1 + b),
                vmem_spec(),
            )(sent, *received)
        received.append(lax.ppermute(sent, "gy", [(i, i ^ (1 << b)) for i in range(groups)]))
    norm_factor = 1.0 / math.sqrt(3.0 * cells_x * shares * cells_y * groups * cells_z)
    direct = shares <= DIRECT_LIMIT and own_rows % (16 * shares) == 0
    steps = shares if direct else 1
    rows = own_rows // steps
    chunk_shapes = [jax.ShapeDtypeStruct((rows, vectors), f32)]
    chunk_shapes += [jax.ShapeDtypeStruct((rows + TAIL, vectors), jnp.int16)] * (steps - 1)
    chunks = local_call(
        functools.partial(share_kernel, levels, 2 * own_ops),
        "share_rows",
        tuple(chunk_shapes),
        [vmem_spec()] * (1 + levels),
        (vmem_spec(),) * steps,
        [pltpu.VMEM((own_rows, vectors), f32)],
    )(parts[levels], *received)
    if direct:
        arrived = [from_step(chunks[k], "gx", -k) for k in range(1, shares)]
        own = local_call(
            functools.partial(sum_kernel, norm_factor),
            "sum_shares",
            jax.ShapeDtypeStruct((rows, vectors), bf16),
            [vmem_spec()] * shares,
            vmem_spec(),
        )(chunks[0], *arrived)
        every = [own] + [from_step(own, "gx", k) for k in range(1, shares)]
    else:
        every = [(lax.psum(chunks[0], "gx") * norm_factor).astype(bf16)]
    every += [from_step(every[k], "ta", t) for t in range(1, times) for k in range(steps)]
    margins, correlators = local_call(
        functools.partial(contract_kernel, times, steps),
        "contraction",
        (
            jax.ShapeDtypeStruct((1, own_ops, 2, vectors, vectors), f32),
            jax.ShapeDtypeStruct((1, own_ops, 2), f32),
        ),
        [hbm_spec(), smem_spec()] + [vmem_spec()] * (len(every) + 1),
        (vmem_spec(), smem_spec()),
        [
            pltpu.VMEM((times, own_rows, vectors), bf16),
            pltpu.VMEM((own_ops, 2 * vectors, 2 * vectors), bf16),
            pltpu.VMEM((own_ops, 2 * vectors, 2 * vectors), bf16),
            pltpu.SMEM((1, 2), jnp.int32),
            pltpu.SemaphoreType.DMA,
        ],
    )(in_hbm(pair_times), slot_counts, *every, perams[0])
    return (margins, correlators)


def solution(mesh):
    placed = (
        P("ta", "gx", "gy", None, None, None, None),
        P("ta", "gx", "gy", None, None, None, None, None),
        P(),
        P(),
        P(("ta", "gx"), None, None, None),
        P(("ta", "gx"), None),
        P(("ta", "gx")),
    )
    return jax.shard_map(
        per_device,
        mesh=mesh,
        in_specs=placed,
        out_specs=(P("ta", "gy", None, None, None), P(("ta", "gx"), "gy", None)),
        check_vma=False,
    )
```

```python
import functools
import math

import jax
import jax.numpy as jnp
import numpy as np
from jax import lax
from jax.experimental import pallas as pl
from jax.experimental.pallas import tpu as pltpu
from jax.sharding import PartitionSpec as P

VMEM_LIMIT = 24 * 1024 * 1024
MOMENTA = 3
LINK_COLS = 54
TAIL = 16
FIXED_BITS = 14.0
DIRECT_LIMIT = 8


def wave_constants(cells_z):
    z_row = np.arange(3 * cells_z) // 3
    columns = []
    for ahead in range(2):
        for momentum in range(MOMENTA):
            angle = 2.0 * math.pi * momentum * ((z_row + ahead) % cells_z) / cells_z
            columns.append(np.cos(angle))
            columns.append(np.sin(angle))
    left = np.stack(columns, axis=1).astype(np.float32)
    terms = []
    for _ in range(3):
        term = left.astype(jnp.bfloat16).astype(np.float32)
        terms.append(term)
        left = left - term
    return jnp.asarray(np.concatenate(terms, axis=1), jnp.bfloat16)


def iota(shape, axis):
    return lax.broadcasted_iota(jnp.int32, shape, axis)


def third(x):
    return (x * 21846) >> 16


def one_hot(condition):
    return condition.astype(jnp.float32).astype(jnp.bfloat16)


def planar_order(order):
    row, col = iota((order, order), 0), iota((order, order), 1)
    half = order // 2
    source = jnp.where(row < half, 2 * row, 2 * (row - half) + 1)
    return one_hot(col == source)


def side_by_side(planar):
    half = planar.shape[0] // 2
    return jnp.concatenate([planar[:half], planar[half:]], axis=1).astype(jnp.bfloat16)


def transport(matrix, pair, sign):
    half, vectors = matrix.shape[0] // 2, pair.shape[1] // 2
    parts = jnp.dot(matrix, pair, preferred_element_type=jnp.float32)
    real, imag = parts[:half], parts[half:]
    if sign > 0:
        return jnp.concatenate(
            [real[:, :vectors] - imag[:, vectors:], real[:, vectors:] + imag[:, :vectors]], axis=0
        )
    return jnp.concatenate(
        [real[:, :vectors] + imag[:, vectors:], real[:, vectors:] - imag[:, :vectors]], axis=0
    )


def halo_fields(cells_x, cells_y):
    pairs = [(0, (cells_x - 1) * cells_y + y) for y in range(cells_y)]
    return pairs + [(1, x * cells_y + cells_y - 1) for x in range(cells_x)]


def local_fields(cells_x, cells_y):
    lines = cells_x * cells_y
    outside = halo_fields(cells_x, cells_y)
    every = [(code, line) for code in range(7) for line in range(lines)]
    return [pair for pair in every if pair not in outside]


def prepare_kernel(cells_x, cells_y, *refs):
    inputs, refs = refs[:5], refs[5:]
    matrix_ref, local_ref, left_ref, phase_ref = refs[:4]
    held, link_rows_ref, sems = refs[4:9], refs[9], refs[10]
    copies = [
        pltpu.make_async_copy(src, dst, sems.at[k])
        for k, (src, dst) in enumerate(zip(inputs, held))
    ]
    for copy in copies:
        copy.start()
    v_ref, link_ref, dirs_ref, moms_ref, waves_ref = held
    f32, bf16 = jnp.float32, jnp.bfloat16
    order, vectors = v_ref.shape[2], v_ref.shape[3]
    half, cells_z = order // 2, order // 6
    lines = cells_x * cells_y
    spread = one_hot(third(iota((half, cells_z), 0)) == iota((half, cells_z), 1))
    row, col = iota((half, LINK_COLS), 0), iota((half, LINK_COLS), 1)
    row_color = row - 3 * third(row)
    pair_at = third(col >> 1)
    col_in, col_out = (col >> 1) - 3 * pair_at, pair_at - 3 * third(pair_at)
    pick = [(row_color == col_out).astype(f32), (row_color == col_in).astype(f32)]
    wide = (LINK_COLS, 6 * 128)
    row, col = iota(wide, 0), iota(wide, 1)
    block, place = col >> 7, col & 127
    color = place - 3 * third(place)
    pair_at = third(row >> 1)
    row_in, row_out = (row >> 1) - 3 * pair_at, pair_at - 3 * third(pair_at)
    fits = 2 * third(pair_at) + (row & 1) == block
    expand = [one_hot(fits & (row_in == color)), one_hot(fits & (row_out == color))]
    row, col = iota((half, 128), 0), iota((half, 128), 1)
    near = ((third(row) == third(col)) & (col < half)).astype(f32)
    planar = planar_order(order)
    for copy in copies:
        copy.wait()
    for line in range(lines):
        for k in range(LINK_COLS // 2):
            link_rows_ref[line, 2 * k : 2 * k + 2] = link_ref[line, k].astype(f32)
    outside = halo_fields(cells_x, cells_y)
    inside = local_fields(cells_x, cells_y)
    ordered = []
    for line in range(lines):
        here = jnp.dot(
            planar, v_ref[line // cells_y, line % cells_y], preferred_element_type=f32
        )
        ordered.append(here)
        local_ref[inside.index((6, line))] = here
    for line in range(lines):
        here = ordered[line]
        ahead_z = jnp.concatenate(
            [here[3:half], here[:3], here[half + 3 :], here[half : half + 3]], axis=0
        )
        columns = slice(line * order, (line + 1) * order)
        left_ref[0, :, columns] = here.T.astype(bf16)
        left_ref[1, :, columns] = ahead_z.T.astype(bf16)
        seen = lax.dot_general(
            spread,
            link_rows_ref[line].astype(bf16),
            (((1,), (1,)), ((), ())),
            preferred_element_type=f32,
        )
        pair = side_by_side(here)
        for way in range(2):
            blocks = jnp.dot(
                (seen * pick[way]).astype(bf16), expand[way], preferred_element_type=f32
            )
            for d in range(3):
                matrix = jnp.concatenate(
                    [
                        blocks[:, 256 * d : 256 * d + 128] * near,
                        blocks[:, 256 * d + 128 : 256 * d + 256] * near,
                    ],
                    axis=0,
                ).astype(bf16)
                if way == 1:
                    carried = transport(matrix[:, :half], pair, -1)
                    local_ref[inside.index((3 + d, line))] = carried.astype(bf16).astype(f32)
                elif (d, line) in outside:
                    matrix_ref[outside.index((d, line))] = matrix
                else:
                    ahead = ahead_z if d == 2 else ordered[line + (cells_y if d == 0 else 1)]
                    local_ref[inside.index((d, line))] = transport(
                        matrix[:, :half], side_by_side(ahead), 1
                    )
    wave_cols = waves_ref.shape[1]
    per_term = wave_cols // 3
    row, col = iota((wave_cols, 2 * vectors), 0), iota((wave_cols, 2 * vectors), 1)
    term = (row >= per_term).astype(jnp.int32) + (row >= 2 * per_term).astype(jnp.int32)
    wave_at = row - per_term * term - (col >= vectors).astype(jnp.int32)
    for o in range(phase_ref.shape[0]):
        column = 2 * (jnp.where(dirs_ref[o] == 5, MOMENTA, 0) + moms_ref[o])
        phase_ref[o] = jnp.dot(
            waves_ref[...], one_hot(wave_at == column), preferred_element_type=f32
        )


def low_bit(j):
    return (j & -j).bit_length() - 1


def margin_kernel(cells_x, cells_y, groups, *refs):
    matrix_ref, local_ref, left_ref, phase_ref, halo_x_ref, halo_y_ref, dirs_hbm = refs[:7]
    levels = groups.bit_length() - 1
    out_refs = refs[7 : 8 + levels]
    field_ref, side_ref, dirs_ref, sem = refs[8 + levels :]
    f32, bf16 = jnp.float32, jnp.bfloat16
    copy = pltpu.make_async_copy(dirs_hbm, dirs_ref, sem)
    copy.start()
    lines = cells_x * cells_y
    order, vectors = halo_x_ref.shape[2], halo_x_ref.shape[3]
    half = order // 2
    planar = planar_order(order)
    side_ref[0] = left_ref[0]
    side_ref[3] = left_ref[1]
    outside = halo_fields(cells_x, cells_y)
    for d in range(2):
        for line in range(lines):
            x, y = line // cells_y, line % cells_y
            columns = slice(line * order, (line + 1) * order)
            if (d, line) not in outside:
                ahead = line + (cells_y if d == 0 else 1)
                side_ref[1 + d, :, columns] = left_ref[0, :, ahead * order : (ahead + 1) * order]
                continue
            halo = halo_x_ref[0, y] if d == 0 else halo_y_ref[x, 0]
            ahead = jnp.dot(planar, halo, preferred_element_type=f32)
            side_ref[1 + d, :, columns] = ahead.T.astype(bf16)
            matrix = matrix_ref[outside.index((d, line))]
            field_ref[d, line] = transport(matrix[:, :half], side_by_side(ahead), 1)
    for k, (code, line) in enumerate(local_fields(cells_x, cells_y)):
        field_ref[code, line] = local_ref[k]
    copy.wait()
    count_ops = dirs_ref.shape[0]
    own_ops = count_ops // groups
    me = lax.axis_index("gy")
    for j in range(groups):
        for i in range(own_ops):
            o = (me ^ j) * own_ops + i
            code = dirs_ref[o]
            side = jnp.where((code >= 3) & (code < 6), code - 2, 0)
            cosine = phase_ref[o, :, 0:vectors]
            sine = phase_ref[o, :, vectors : 2 * vectors]
            pairs = []
            for line in range(lines):
                real, imag = field_ref[code, line, 0:half], field_ref[code, line, half:order]
                turned_r, turned_i = cosine * real - sine * imag, sine * real + cosine * imag
                pairs.append(jnp.concatenate([turned_r, turned_i], axis=1))
                pairs.append(jnp.concatenate([turned_i, -turned_r], axis=1))
            product = jnp.dot(
                side_ref[side],
                jnp.concatenate(pairs, axis=0).astype(bf16),
                preferred_element_type=f32,
            )
            level = levels if j == 0 else low_bit(j)
            out_ref = out_refs[level]
            place = 0 if j == 0 else j >> (level + 1)
            first = 2 * i * vectors
            out_ref[place, first : first + vectors] = product[:, :vectors]
            out_ref[place, first + vectors : first + 2 * vectors] = product[:, vectors:]


def scale_of(block):
    top = jnp.max(jnp.abs(block), axis=0, keepdims=True)
    return jnp.floor(jnp.log2(jnp.maximum(top, 1e-30))) + 1.0


def put_fixed(out_ref, blocks):
    rows, vectors = blocks[0].shape
    tail = iota((TAIL, vectors), 0)
    scales = jnp.zeros((TAIL, vectors), jnp.float32)
    for k, block in enumerate(blocks):
        scale = scale_of(block)
        scales = jnp.where(tail == k, scale, scales)
        fixed = jnp.floor(block * jnp.exp2(FIXED_BITS - scale) + 0.5)
        out_ref[k * rows : (k + 1) * rows] = fixed.astype(jnp.int32).astype(jnp.int16)
    out_ref[len(blocks) * rows :] = scales.astype(jnp.int32).astype(jnp.int16)


def from_fixed(ref, rows, k):
    scales = ref[ref.shape[0] - TAIL :].astype(jnp.int32).astype(jnp.float32)
    block = ref[k * rows : (k + 1) * rows].astype(jnp.int32).astype(jnp.float32)
    return block * jnp.exp2(scales[k : k + 1] - FIXED_BITS)


def fold_kernel(level, count_blocks, *refs):
    held_ref, received, out_ref = refs[0], refs[1:-1], refs[-1]
    rows = held_ref.shape[1] // count_blocks
    for k in range(held_ref.shape[0]):
        j = (2 * k + 1) << level
        blocks = []
        for p in range(count_blocks):
            total = held_ref[k, p * rows : (p + 1) * rows]
            for b, ref in enumerate(received):
                total = total + arrived_block(ref.at[j >> (b + 1)], b, rows, p)
            blocks.append(total)
        put_fixed(out_ref.at[k], blocks)


def arrived_block(ref, level, rows, p):
    return ref[p * rows : (p + 1) * rows] if level == 0 else from_fixed(ref, rows, p)


def share_kernel(levels, count_blocks, *refs):
    held_ref, received, refs = refs[0], refs[1 : 1 + levels], refs[1 + levels :]
    outs, total_ref = refs[:-1], refs[-1]
    span = held_ref.shape[1] // count_blocks
    for p in range(count_blocks):
        total = held_ref[0, p * span : (p + 1) * span]
        for b, ref in enumerate(received):
            total = total + arrived_block(ref.at[0], b, span, p)
        total_ref[p * span : (p + 1) * span] = total
    if len(outs) == 1:
        outs[0][...] = total_ref[...]
        return
    own_ref, sent_ref = outs
    rows, count = own_ref.shape[0], sent_ref.shape[0]
    me = lax.axis_index("gx")
    own_ref[...] = total_ref[pl.ds(pl.multiple_of(me * rows, rows), rows)]
    for chunk in range(count):
        put_fixed(sent_ref.at[chunk], [total_ref[chunk * rows : (chunk + 1) * rows]])


def sum_kernel(norm_factor, own_ref, arrived_ref, out_ref):
    total = own_ref[...]
    me = lax.axis_index("gx")
    count = arrived_ref.shape[0]
    for k in range(1, count):
        total = total + from_fixed(arrived_ref.at[lax.rem(me + k, count)], total.shape[0], 0)
    total = (total * norm_factor).astype(out_ref.dtype)
    for k in range(count):
        out_ref[k] = total


def contract_kernel(times, *refs):
    pair_hbm, live_ref = refs[:2]
    blocks, refs = refs[2 : 2 + times], refs[2 + times :]
    tau_ref, margin_ref, corr_ref = refs[:3]
    every_ref, left_ref, right_ref, pair_ref, sem = refs[3:]
    f32 = jnp.float32
    copy = pltpu.make_async_copy(pair_hbm, pair_ref, sem)
    copy.start()
    vectors = every_ref.shape[2]
    count_ops = margin_ref.shape[1]
    order = tau_ref.shape[2]
    spins = order // vectors
    me_t = lax.axis_index("ta")
    for k, ref in enumerate(blocks):
        every_ref[lax.rem(me_t + k, times)] = ref[...]
    copy.wait()
    sink, source = pair_ref[0, 0], pair_ref[0, 1]
    live = live_ref[0] > 0
    for o in range(count_ops):
        first = 2 * o * vectors
        part = lambda t, k: every_ref[t, first + k * vectors : first + (k + 1) * vectors]
        margin_ref[0, o, 0] = part(me_t, 0).astype(f32)
        margin_ref[0, o, 1] = part(me_t, 1).astype(f32)
        a_r, a_i = part(sink, 0), part(sink, 1)
        b_r, b_i = part(source, 0).T, part(source, 1).T
        left_ref[o, 0:vectors, 0:vectors] = a_r
        left_ref[o, 0:vectors, vectors:] = -a_i
        left_ref[o, vectors:, 0:vectors] = a_i
        left_ref[o, vectors:, vectors:] = a_r
        right_ref[o, 0:vectors, 0:vectors] = b_r
        right_ref[o, 0:vectors, vectors:] = -b_i
        right_ref[o, vectors:, 0:vectors] = b_i
        right_ref[o, vectors:, vectors:] = b_r
        real = jnp.zeros((8, vectors), f32)
        imag = jnp.zeros((8, vectors), f32)
        fold = lambda t: jnp.sum(t.reshape(vectors // 8, 8, vectors), axis=0)
        for s in range(spins):
            rows = slice(s * vectors, (s + 1) * vectors)
            x = jnp.dot(
                left_ref[o],
                jnp.concatenate([tau_ref[0, rows], tau_ref[1, rows]], axis=0),
                preferred_element_type=f32,
            )
            for c in range(spins):
                cols = slice(c * vectors, (c + 1) * vectors)
                y = jnp.dot(
                    jnp.concatenate([tau_ref[0, rows, cols], tau_ref[1, rows, cols]], axis=1),
                    right_ref[o],
                    preferred_element_type=f32,
                )
                x_r, x_i = x[:vectors, cols], x[vectors:, cols]
                y_r, y_i = y[:, :vectors], y[:, vectors:]
                real = real + fold(x_r * y_r + x_i * y_i)
                imag = imag + fold(x_i * y_r - x_r * y_i)
        scale = 1.0 / vectors
        corr_ref[0, o, 0] = jnp.where(live, jnp.sum(real) * scale, 0.0)
        corr_ref[0, o, 1] = jnp.where(live, jnp.sum(imag) * scale, 0.0)


def vmem_spec():
    return pl.BlockSpec(memory_space=pltpu.VMEM)


def smem_spec():
    return pl.BlockSpec(memory_space=pltpu.SMEM)


def hbm_spec():
    return pl.BlockSpec(memory_space=pltpu.HBM)


def in_hbm(x):
    return pltpu.with_memory_space_constraint(x, pltpu.HBM)


def local_call(body, name, outs, in_specs, out_specs, scratch=(), cost=None):
    return pl.pallas_call(
        body,
        out_shape=outs,
        in_specs=in_specs,
        out_specs=out_specs,
        scratch_shapes=list(scratch),
        compiler_params=pltpu.CompilerParams(vmem_limit_bytes=VMEM_LIMIT),
        cost_estimate=cost,
        name=name,
    )


def from_step(block, axis, step):
    count = lax.axis_size(axis)
    return lax.ppermute(block, axis, [((i + step) % count, i) for i in range(count)])


def per_device(eigvecs, links, op_dirs, op_moms, perams, pair_times, slot_counts):
    f32, bf16 = jnp.float32, jnp.bfloat16
    _, cells_x, cells_y, cells_z, colors, _, vectors = eigvecs.shape
    order = cells_z * colors * 2
    lines = cells_x * cells_y
    count_ops = op_dirs.shape[0]
    times, shares, groups = lax.axis_size("ta"), lax.axis_size("gx"), lax.axis_size("gy")
    levels = groups.bit_length() - 1
    own_ops = count_ops // groups
    own_rows = own_ops * 2 * vectors
    field = eigvecs.reshape(cells_x, cells_y, order, vectors)
    halo_x = from_step(field[0:1], "gx", 1)
    halo_y = from_step(field, "gy", 1)
    link_field = links[0].transpose(0, 1, 3, 5, 6, 4, 2).reshape(lines, 27, 2, cells_z)
    outside, inside = halo_fields(cells_x, cells_y), local_fields(cells_x, cells_y)
    inputs = [field, link_field, op_dirs, op_moms, wave_constants(cells_z)]
    inputs = [in_hbm(x) for x in inputs]
    held = [
        pltpu.SMEM(x.shape, x.dtype) if x.ndim == 1 else pltpu.VMEM(x.shape, x.dtype)
        for x in inputs
    ]
    matrices, local, left, phases = local_call(
        functools.partial(prepare_kernel, cells_x, cells_y),
        "prepare_lines",
        (
            jax.ShapeDtypeStruct((len(outside), order, 128), bf16),
            jax.ShapeDtypeStruct((len(inside), order, vectors), f32),
            jax.ShapeDtypeStruct((2, vectors, lines * order), bf16),
            jax.ShapeDtypeStruct((count_ops, order // 2, 2 * vectors), f32),
        ),
        [hbm_spec()] * len(inputs),
        (vmem_spec(),) * 4,
        held
        + [
            pltpu.VMEM((lines, LINK_COLS, cells_z), f32),
            pltpu.SemaphoreType.DMA((len(inputs),)),
        ],
    )(*inputs)
    part_shapes = [
        jax.ShapeDtypeStruct((groups >> (b + 1), own_rows, vectors), f32)
        for b in range(levels)
    ] + [jax.ShapeDtypeStruct((1, own_rows, vectors), f32)]
    parts = local_call(
        functools.partial(margin_kernel, cells_x, cells_y, groups),
        "partial_margins",
        tuple(part_shapes),
        [vmem_spec()] * 6 + [hbm_spec()],
        (vmem_spec(),) * len(part_shapes),
        [
            pltpu.VMEM((7, lines, order, vectors), f32),
            pltpu.VMEM((4, vectors, lines * order), bf16),
            pltpu.SMEM((count_ops,), jnp.int32),
            pltpu.SemaphoreType.DMA,
        ],
    )(matrices, local, left, phases, halo_x, halo_y, in_hbm(op_dirs))
    received = []
    for b in range(levels):
        sent = parts[b]
        if b:
            sent = local_call(
                functools.partial(fold_kernel, b, 2 * own_ops),
                "fold_groups",
                jax.ShapeDtypeStruct((sent.shape[0], own_rows + TAIL, vectors), jnp.int16),
                [vmem_spec()] * (1 + b),
                vmem_spec(),
            )(sent, *received)
        received.append(lax.ppermute(sent, "gy", [(i, i ^ (1 << b)) for i in range(groups)]))
    norm_factor = 1.0 / math.sqrt(3.0 * cells_x * shares * cells_y * groups * cells_z)
    direct = shares <= DIRECT_LIMIT and own_rows % (16 * shares) == 0
    steps = shares if direct else 1
    rows = own_rows // steps
    chunk_shapes = [jax.ShapeDtypeStruct((rows, vectors), f32)]
    if direct:
        chunk_shapes.append(jax.ShapeDtypeStruct((steps, rows + TAIL, vectors), jnp.int16))
    chunks = local_call(
        functools.partial(share_kernel, levels, 2 * own_ops),
        "share_rows",
        tuple(chunk_shapes),
        [vmem_spec()] * (1 + levels),
        (vmem_spec(),) * len(chunk_shapes),
        [pltpu.VMEM((own_rows, vectors), f32)],
    )(parts[levels], *received)
    if direct:
        own = local_call(
            functools.partial(sum_kernel, norm_factor),
            "sum_shares",
            jax.ShapeDtypeStruct((steps, rows, vectors), bf16),
            [vmem_spec()] * 2,
            vmem_spec(),
        )(chunks[0], lax.all_to_all(chunks[1], "gx", 0, 0, tiled=True))
        own = lax.all_to_all(own, "gx", 0, 0, tiled=True).reshape(own_rows, vectors)
    else:
        own = (lax.psum(chunks[0], "gx") * norm_factor).astype(bf16)
    every = [own] + [from_step(own, "ta", t) for t in range(1, times)]
    margins, correlators = local_call(
        functools.partial(contract_kernel, times),
        "contraction",
        (
            jax.ShapeDtypeStruct((1, own_ops, 2, vectors, vectors), f32),
            jax.ShapeDtypeStruct((1, own_ops, 2), f32),
        ),
        [hbm_spec(), smem_spec()] + [vmem_spec()] * (len(every) + 1),
        (vmem_spec(), smem_spec()),
        [
            pltpu.VMEM((times, own_rows, vectors), bf16),
            pltpu.VMEM((own_ops, 2 * vectors, 2 * vectors), bf16),
            pltpu.VMEM((own_ops, 2 * vectors, 2 * vectors), bf16),
            pltpu.SMEM((1, 2), jnp.int32),
            pltpu.SemaphoreType.DMA,
        ],
    )(in_hbm(pair_times), slot_counts, *every, perams[0])
    return (margins, correlators)


def solution(mesh):
    placed = (
        P("ta", "gx", "gy", None, None, None, None),
        P("ta", "gx", "gy", None, None, None, None, None),
        P(),
        P(),
        P(("ta", "gx"), None, None, None),
        P(("ta", "gx"), None),
        P(("ta", "gx")),
    )
    return jax.shard_map(
        per_device,
        mesh=mesh,
        in_specs=placed,
        out_specs=(P("ta", "gy", None, None, None), P(("ta", "gx"), "gy", None)),
        check_vma=False,
    )
```

```python
import functools
import math

import jax
import jax.numpy as jnp
import numpy as np
from jax import lax
from jax.experimental import pallas as pl
from jax.experimental.pallas import tpu as pltpu
from jax.sharding import PartitionSpec as P

VMEM_LIMIT = 24 * 1024 * 1024
MOMENTA = 3
LINK_COLS = 54
TAIL = 16
FIXED_BITS = 14.0
DIRECT_LIMIT = 8


def wave_constants(cells_z):
    z_row = np.arange(3 * cells_z) // 3
    columns = []
    for ahead in range(2):
        for momentum in range(MOMENTA):
            angle = 2.0 * math.pi * momentum * ((z_row + ahead) % cells_z) / cells_z
            columns.append(np.cos(angle))
            columns.append(np.sin(angle))
    left = np.stack(columns, axis=1).astype(np.float32)
    terms = []
    for _ in range(3):
        term = left.astype(jnp.bfloat16).astype(np.float32)
        terms.append(term)
        left = left - term
    return jnp.asarray(np.concatenate(terms, axis=1), jnp.bfloat16)


def iota(shape, axis):
    return lax.broadcasted_iota(jnp.int32, shape, axis)


def third(x):
    return (x * 21846) >> 16


def one_hot(condition):
    return condition.astype(jnp.float32).astype(jnp.bfloat16)


def planar_order(order):
    row, col = iota((order, order), 0), iota((order, order), 1)
    half = order // 2
    source = jnp.where(row < half, 2 * row, 2 * (row - half) + 1)
    return one_hot(col == source)


def side_by_side(planar):
    half = planar.shape[0] // 2
    return jnp.concatenate([planar[:half], planar[half:]], axis=1).astype(jnp.bfloat16)


def transport(matrix, pair, sign):
    half, vectors = matrix.shape[0] // 2, pair.shape[1] // 2
    parts = jnp.dot(matrix, pair, preferred_element_type=jnp.float32)
    real, imag = parts[:half], parts[half:]
    if sign > 0:
        return jnp.concatenate(
            [real[:, :vectors] - imag[:, vectors:], real[:, vectors:] + imag[:, :vectors]], axis=0
        )
    return jnp.concatenate(
        [real[:, :vectors] + imag[:, vectors:], real[:, vectors:] - imag[:, :vectors]], axis=0
    )


def halo_fields(cells_x, cells_y):
    pairs = [(0, (cells_x - 1) * cells_y + y) for y in range(cells_y)]
    return pairs + [(1, x * cells_y + cells_y - 1) for x in range(cells_x)]


def local_fields(cells_x, cells_y):
    lines = cells_x * cells_y
    outside = halo_fields(cells_x, cells_y)
    every = [(code, line) for code in range(7) for line in range(lines)]
    return [pair for pair in every if pair not in outside]


def prepare_kernel(cells_x, cells_y, *refs):
    inputs, refs = refs[:5], refs[5:]
    matrix_ref, local_ref, left_ref, phase_ref = refs[:4]
    held, link_rows_ref, sems = refs[4:9], refs[9], refs[10]
    copies = [
        pltpu.make_async_copy(src, dst, sems.at[k])
        for k, (src, dst) in enumerate(zip(inputs, held))
    ]
    for copy in copies:
        copy.start()
    v_ref, link_ref, dirs_ref, moms_ref, waves_ref = held
    f32, bf16 = jnp.float32, jnp.bfloat16
    order, vectors = v_ref.shape[2], v_ref.shape[3]
    half, cells_z = order // 2, order // 6
    lines = cells_x * cells_y
    spread = one_hot(third(iota((half, cells_z), 0)) == iota((half, cells_z), 1))
    row, col = iota((half, LINK_COLS), 0), iota((half, LINK_COLS), 1)
    row_color = row - 3 * third(row)
    pair_at = third(col >> 1)
    col_in, col_out = (col >> 1) - 3 * pair_at, pair_at - 3 * third(pair_at)
    pick = [(row_color == col_out).astype(f32), (row_color == col_in).astype(f32)]
    wide = (LINK_COLS, 6 * 128)
    row, col = iota(wide, 0), iota(wide, 1)
    block, place = col >> 7, col & 127
    color = place - 3 * third(place)
    pair_at = third(row >> 1)
    row_in, row_out = (row >> 1) - 3 * pair_at, pair_at - 3 * third(pair_at)
    fits = 2 * third(pair_at) + (row & 1) == block
    expand = [one_hot(fits & (row_in == color)), one_hot(fits & (row_out == color))]
    row, col = iota((half, 128), 0), iota((half, 128), 1)
    near = ((third(row) == third(col)) & (col < half)).astype(f32)
    planar = planar_order(order)
    for copy in copies:
        copy.wait()
    for line in range(lines):
        for k in range(LINK_COLS // 2):
            link_rows_ref[line, 2 * k : 2 * k + 2] = link_ref[line, k].astype(f32)
    outside = halo_fields(cells_x, cells_y)
    inside = local_fields(cells_x, cells_y)
    ordered = []
    for line in range(lines):
        here = jnp.dot(
            planar, v_ref[line // cells_y, line % cells_y], preferred_element_type=f32
        )
        ordered.append(here)
        local_ref[inside.index((6, line))] = here
    for line in range(lines):
        here = ordered[line]
        ahead_z = jnp.concatenate(
            [here[3:half], here[:3], here[half + 3 :], here[half : half + 3]], axis=0
        )
        columns = slice(line * order, (line + 1) * order)
        left_ref[0, :, columns] = here.T.astype(bf16)
        left_ref[1, :, columns] = ahead_z.T.astype(bf16)
        seen = lax.dot_general(
            spread,
            link_rows_ref[line].astype(bf16),
            (((1,), (1,)), ((), ())),
            preferred_element_type=f32,
        )
        pair = side_by_side(here)
        for way in range(2):
            blocks = jnp.dot(
                (seen * pick[way]).astype(bf16), expand[way], preferred_element_type=f32
            )
            for d in range(3):
                matrix = jnp.concatenate(
                    [
                        blocks[:, 256 * d : 256 * d + 128] * near,
                        blocks[:, 256 * d + 128 : 256 * d + 256] * near,
                    ],
                    axis=0,
                ).astype(bf16)
                if way == 1:
                    carried = transport(matrix[:, :half], pair, -1)
                    local_ref[inside.index((3 + d, line))] = carried.astype(bf16).astype(f32)
                elif (d, line) in outside:
                    matrix_ref[outside.index((d, line))] = matrix
                else:
                    ahead = ahead_z if d == 2 else ordered[line + (cells_y if d == 0 else 1)]
                    local_ref[inside.index((d, line))] = transport(
                        matrix[:, :half], side_by_side(ahead), 1
                    )
    wave_cols = waves_ref.shape[1]
    per_term = wave_cols // 3
    row, col = iota((wave_cols, 2 * vectors), 0), iota((wave_cols, 2 * vectors), 1)
    term = (row >= per_term).astype(jnp.int32) + (row >= 2 * per_term).astype(jnp.int32)
    wave_at = row - per_term * term - (col >= vectors).astype(jnp.int32)
    for o in range(phase_ref.shape[0]):
        column = 2 * (jnp.where(dirs_ref[o] == 5, MOMENTA, 0) + moms_ref[o])
        phase_ref[o] = jnp.dot(
            waves_ref[...], one_hot(wave_at == column), preferred_element_type=f32
        )


def write_margins(slots, own_ops, field_ref, side_ref, phase_ref, dirs_ref, lines):
    f32, bf16 = jnp.float32, jnp.bfloat16
    order, vectors = field_ref.shape[2], field_ref.shape[3]
    half = order // 2
    me = lax.axis_index("gy")
    for j, out_ref, place in slots:
        for i in range(own_ops):
            o = (me ^ j) * own_ops + i
            code = dirs_ref[o]
            side = jnp.where((code >= 3) & (code < 6), code - 2, 0)
            cosine = phase_ref[o, :, 0:vectors]
            sine = phase_ref[o, :, vectors : 2 * vectors]
            pairs = []
            for line in range(lines):
                real, imag = field_ref[code, line, 0:half], field_ref[code, line, half:order]
                turned_r, turned_i = cosine * real - sine * imag, sine * real + cosine * imag
                pairs.append(jnp.concatenate([turned_r, turned_i], axis=1))
                pairs.append(jnp.concatenate([turned_i, -turned_r], axis=1))
            product = jnp.dot(
                side_ref[side],
                jnp.concatenate(pairs, axis=0).astype(bf16),
                preferred_element_type=f32,
            )
            first = 2 * i * vectors
            out_ref[place, first : first + vectors] = product[:, :vectors]
            out_ref[place, first + vectors : first + 2 * vectors] = product[:, vectors:]


def low_bit(j):
    return (j & -j).bit_length() - 1


def first_margin_kernel(cells_x, cells_y, groups, own_ops, *refs):
    matrix_ref, local_ref, left_ref, phase_ref, halo_x_ref, halo_y_ref, dirs_hbm = refs[:7]
    swap_ref, hold_ref, field_ref, side_ref, dirs_ref, sem = refs[7:]
    f32, bf16 = jnp.float32, jnp.bfloat16
    copy = pltpu.make_async_copy(dirs_hbm, dirs_ref, sem)
    copy.start()
    lines = cells_x * cells_y
    order = halo_x_ref.shape[2]
    half = order // 2
    planar = planar_order(order)
    side_ref[0] = left_ref[0]
    side_ref[3] = left_ref[1]
    outside = halo_fields(cells_x, cells_y)
    for d in range(2):
        for line in range(lines):
            x, y = line // cells_y, line % cells_y
            columns = slice(line * order, (line + 1) * order)
            if (d, line) not in outside:
                ahead = line + (cells_y if d == 0 else 1)
                side_ref[1 + d, :, columns] = left_ref[0, :, ahead * order : (ahead + 1) * order]
                continue
            halo = halo_x_ref[0, y] if d == 0 else halo_y_ref[x, 0]
            ahead = jnp.dot(planar, halo, preferred_element_type=f32)
            side_ref[1 + d, :, columns] = ahead.T.astype(bf16)
            matrix = matrix_ref[outside.index((d, line))]
            field_ref[d, line] = transport(matrix[:, :half], side_by_side(ahead), 1)
    for k, (code, line) in enumerate(local_fields(cells_x, cells_y)):
        field_ref[code, line] = local_ref[k]
    copy.wait()
    slots = [(j, swap_ref if j & 1 else hold_ref, j >> 2) for j in range(groups) if j & 2]
    slots.sort(key=lambda slot: -(slot[0] & 1))
    write_margins(slots, own_ops, field_ref, side_ref, phase_ref, dirs_ref, lines)


def second_margin_kernel(lines, groups, own_ops, *refs):
    field_ref, side_ref, phase_ref, dirs_hbm, swap_ref = refs[:5]
    hold_refs, dirs_ref, sem = refs[5:-2], refs[-2], refs[-1]
    copy = pltpu.make_async_copy(dirs_hbm, dirs_ref, sem)
    copy.start()
    copy.wait()
    slots = [(j, swap_ref, j >> 2) for j in range(groups) if j & 3 == 1]
    for j in range(0, groups, 4):
        level = low_bit(j) if j else groups.bit_length() - 1
        slots.append((j, hold_refs[level - 2], j >> (level + 1)))
    write_margins(slots, own_ops, field_ref, side_ref, phase_ref, dirs_ref, lines)


def scale_of(block):
    top = jnp.max(jnp.abs(block), axis=0, keepdims=True)
    return jnp.floor(jnp.log2(jnp.maximum(top, 1e-30))) + 1.0


def put_fixed(out_ref, blocks):
    rows, vectors = blocks[0].shape
    tail = iota((TAIL, vectors), 0)
    scales = jnp.zeros((TAIL, vectors), jnp.float32)
    for k, block in enumerate(blocks):
        scale = scale_of(block)
        scales = jnp.where(tail == k, scale, scales)
        fixed = jnp.floor(block * jnp.exp2(FIXED_BITS - scale) + 0.5)
        out_ref[k * rows : (k + 1) * rows] = fixed.astype(jnp.int32).astype(jnp.int16)
    out_ref[len(blocks) * rows :] = scales.astype(jnp.int32).astype(jnp.int16)


def from_fixed(ref, rows, k):
    scales = ref[ref.shape[0] - TAIL :].astype(jnp.int32).astype(jnp.float32)
    block = ref[k * rows : (k + 1) * rows].astype(jnp.int32).astype(jnp.float32)
    return block * jnp.exp2(scales[k : k + 1] - FIXED_BITS)


def arrived_block(received, j, rows, p):
    total = received[0][j >> 2, p * rows : (p + 1) * rows]
    for b, ref in enumerate(received[1:], 1):
        total = total + from_fixed(ref.at[j >> (b + 1)], rows, p)
    return total


def fold_kernel(level, count_blocks, *refs):
    held_ref, received, out_ref = refs[0], refs[1:-1], refs[-1]
    rows = held_ref.shape[1] // count_blocks
    for k in range(held_ref.shape[0]):
        j = (2 * k + 1) << level
        blocks = [
            held_ref[k, p * rows : (p + 1) * rows] + arrived_block(received, j, rows, p)
            for p in range(count_blocks)
        ]
        put_fixed(out_ref.at[k], blocks)


def share_kernel(levels, count_blocks, *refs):
    held_ref, received, refs = refs[0], refs[1 : 1 + levels], refs[1 + levels :]
    outs, total_ref = refs[:-1], refs[-1]
    span = held_ref.shape[1] // count_blocks
    for p in range(count_blocks):
        here = slice(p * span, (p + 1) * span)
        total_ref[here] = held_ref[0, here] + arrived_block(received, 0, span, p)
    rows = outs[0].shape[0]
    me = lax.axis_index("gx")
    for step, out_ref in enumerate(outs):
        chunk = partner_of(me, step, len(outs))
        total = total_ref[pl.ds(pl.multiple_of(chunk * rows, rows), rows)]
        if step:
            put_fixed(out_ref, [total])
        else:
            out_ref[...] = total


def partner_of(me, step, count):
    if count & (count - 1) == 0:
        return me ^ step
    return (me + step) % count


def sum_kernel(norm_factor, *refs):
    own_ref, received, out_ref = refs[0], refs[1:-1], refs[-1]
    total = own_ref[...]
    for ref in received:
        total = total + from_fixed(ref, total.shape[0], 0)
    out_ref[...] = (total * norm_factor).astype(out_ref.dtype)


def contract_kernel(times, steps, *refs):
    pair_hbm, live_ref = refs[:2]
    chunks, refs = refs[2 : 2 + times * steps], refs[2 + times * steps :]
    tau_ref, margin_ref, corr_ref = refs[:3]
    every_ref, left_ref, right_ref, pair_ref, sem = refs[3:]
    f32 = jnp.float32
    copy = pltpu.make_async_copy(pair_hbm, pair_ref, sem)
    copy.start()
    vectors = every_ref.shape[2]
    count_ops = margin_ref.shape[1]
    order = tau_ref.shape[2]
    spins = order // vectors
    me_t, me_x = lax.axis_index("ta"), lax.axis_index("gx")
    rows = chunks[0].shape[0]
    for k, ref in enumerate(chunks):
        at_t = lax.rem(me_t + k // steps, times)
        place = partner_of(me_x, k % steps, steps)
        every_ref[at_t, pl.ds(pl.multiple_of(place * rows, rows), rows)] = ref[...]
    copy.wait()
    sink, source = pair_ref[0, 0], pair_ref[0, 1]
    live = live_ref[0] > 0
    for o in range(count_ops):
        first = 2 * o * vectors
        part = lambda t, k: every_ref[t, first + k * vectors : first + (k + 1) * vectors]
        margin_ref[0, o, 0] = part(me_t, 0).astype(f32)
        margin_ref[0, o, 1] = part(me_t, 1).astype(f32)
        a_r, a_i = part(sink, 0), part(sink, 1)
        b_r, b_i = part(source, 0).T, part(source, 1).T
        real, imag = slice(first, first + vectors), slice(first + vectors, first + 2 * vectors)
        left_ref[real, 0:vectors] = a_r
        left_ref[real, vectors:] = -a_i
        left_ref[imag, 0:vectors] = a_i
        left_ref[imag, vectors:] = a_r
        right_ref[0:vectors, real] = b_r
        right_ref[0:vectors, imag] = -b_i
        right_ref[vectors:, real] = b_i
        right_ref[vectors:, imag] = b_r
    lanes = 32
    fold = lambda t: jnp.sum(t.reshape(vectors // lanes, lanes, vectors), axis=0)
    sums = [[jnp.zeros((lanes, vectors), f32) for _ in range(2)] for _ in range(count_ops)]
    for s in range(spins):
        rows = slice(s * vectors, (s + 1) * vectors)
        x = jnp.dot(
            left_ref[...],
            jnp.concatenate([tau_ref[0, rows], tau_ref[1, rows]], axis=0),
            preferred_element_type=f32,
        )
        for c in range(spins):
            cols = slice(c * vectors, (c + 1) * vectors)
            y = jnp.dot(
                jnp.concatenate([tau_ref[0, rows, cols], tau_ref[1, rows, cols]], axis=1),
                right_ref[...],
                preferred_element_type=f32,
            )
            for o in range(count_ops):
                first = 2 * o * vectors
                x_r = x[first : first + vectors, cols]
                x_i = x[first + vectors : first + 2 * vectors, cols]
                y_r = y[:, first : first + vectors]
                y_i = y[:, first + vectors : first + 2 * vectors]
                sums[o][0] = sums[o][0] + fold(x_r * y_r + x_i * y_i)
                sums[o][1] = sums[o][1] + fold(x_i * y_r - x_r * y_i)
    scale = 1.0 / vectors
    for o in range(count_ops):
        for k in range(2):
            corr_ref[0, o, k] = jnp.where(live, jnp.sum(sums[o][k]) * scale, 0.0)


def vmem_spec():
    return pl.BlockSpec(memory_space=pltpu.VMEM)


def smem_spec():
    return pl.BlockSpec(memory_space=pltpu.SMEM)


def hbm_spec():
    return pl.BlockSpec(memory_space=pltpu.HBM)


def in_hbm(x):
    return pltpu.with_memory_space_constraint(x, pltpu.HBM)


def local_call(body, name, outs, in_specs, out_specs, scratch=(), cost=None):
    return pl.pallas_call(
        body,
        out_shape=outs,
        in_specs=in_specs,
        out_specs=out_specs,
        scratch_shapes=list(scratch),
        compiler_params=pltpu.CompilerParams(vmem_limit_bytes=VMEM_LIMIT),
        cost_estimate=cost,
        name=name,
    )


def from_step(block, axis, step):
    count = lax.axis_size(axis)
    return lax.ppermute(block, axis, [((i + step) % count, i) for i in range(count)])


def from_partner(block, axis, step):
    count = lax.axis_size(axis)
    return lax.ppermute(block, axis, [(partner_of(i, step, count), i) for i in range(count)])


def to_partner(block, axis, step):
    count = lax.axis_size(axis)
    return lax.ppermute(block, axis, [(i, partner_of(i, step, count)) for i in range(count)])


def per_device(eigvecs, links, op_dirs, op_moms, perams, pair_times, slot_counts):
    f32, bf16 = jnp.float32, jnp.bfloat16
    _, cells_x, cells_y, cells_z, colors, _, vectors = eigvecs.shape
    order = cells_z * colors * 2
    lines = cells_x * cells_y
    count_ops = op_dirs.shape[0]
    times, shares, groups = lax.axis_size("ta"), lax.axis_size("gx"), lax.axis_size("gy")
    levels = groups.bit_length() - 1
    own_ops = count_ops // groups
    own_rows = own_ops * 2 * vectors
    field = eigvecs.reshape(cells_x, cells_y, order, vectors)
    halo_x = from_step(field[0:1], "gx", 1)
    halo_y = from_step(field, "gy", 1)
    link_field = links[0].transpose(0, 1, 3, 5, 6, 4, 2).reshape(lines, 27, 2, cells_z)
    outside, inside = halo_fields(cells_x, cells_y), local_fields(cells_x, cells_y)
    inputs = [field, link_field, op_dirs, op_moms, wave_constants(cells_z)]
    inputs = [in_hbm(x) for x in inputs]
    held = [
        pltpu.SMEM(x.shape, x.dtype) if x.ndim == 1 else pltpu.VMEM(x.shape, x.dtype)
        for x in inputs
    ]
    matrices, local, left, phases = local_call(
        functools.partial(prepare_kernel, cells_x, cells_y),
        "prepare_lines",
        (
            jax.ShapeDtypeStruct((len(outside), order, 128), bf16),
            jax.ShapeDtypeStruct((len(inside), order, vectors), f32),
            jax.ShapeDtypeStruct((2, vectors, lines * order), bf16),
            jax.ShapeDtypeStruct((count_ops, order // 2, 2 * vectors), f32),
        ),
        [hbm_spec()] * len(inputs),
        (vmem_spec(),) * 4,
        held
        + [
            pltpu.VMEM((lines, LINK_COLS, cells_z), f32),
            pltpu.SemaphoreType.DMA((len(inputs),)),
        ],
    )(*inputs)
    part = lambda count: jax.ShapeDtypeStruct((count, own_rows, vectors), f32)
    dirs = in_hbm(op_dirs)
    dirs_scratch = [pltpu.SMEM((count_ops,), jnp.int32), pltpu.SemaphoreType.DMA]
    swap_a, hold_a, fields, sides = local_call(
        functools.partial(first_margin_kernel, cells_x, cells_y, groups, own_ops),
        "first_margins",
        (
            part(groups // 4),
            part(groups // 4),
            jax.ShapeDtypeStruct((7, lines, order, vectors), f32),
            jax.ShapeDtypeStruct((4, vectors, lines * order), bf16),
        ),
        [vmem_spec()] * 6 + [hbm_spec()],
        (vmem_spec(),) * 4,
        dirs_scratch,
    )(matrices, local, left, phases, halo_x, halo_y, dirs)
    swapped_a = from_partner(swap_a, "gy", 1)
    held_shapes = [part(groups >> (b + 1)) for b in range(2, levels)] + [part(1)]
    swap_b, *held = local_call(
        functools.partial(second_margin_kernel, lines, groups, own_ops),
        "second_margins",
        (part(groups // 4), *held_shapes),
        [vmem_spec()] * 3 + [hbm_spec()],
        (vmem_spec(),) * (1 + len(held_shapes)),
        dirs_scratch,
    )(fields, sides, phases, dirs)
    received = [from_partner(swap_b, "gy", 1)]
    for b in range(1, levels):
        inputs = (hold_a, swapped_a) if b == 1 else (held[b - 2], *received)
        sent = local_call(
            functools.partial(fold_kernel, b, 2 * own_ops),
            "fold_groups",
            jax.ShapeDtypeStruct((inputs[0].shape[0], own_rows + TAIL, vectors), jnp.int16),
            [vmem_spec()] * len(inputs),
            vmem_spec(),
        )(*inputs)
        received.append(from_partner(sent, "gy", 1 << b))
    norm_factor = 1.0 / math.sqrt(3.0 * cells_x * shares * cells_y * groups * cells_z)
    direct = shares <= DIRECT_LIMIT and own_rows % (16 * shares) == 0
    steps = shares if direct else 1
    rows = own_rows // steps
    chunk_shapes = [jax.ShapeDtypeStruct((rows, vectors), f32)]
    chunk_shapes += [jax.ShapeDtypeStruct((rows + TAIL, vectors), jnp.int16)] * (steps - 1)
    chunks = local_call(
        functools.partial(share_kernel, levels, 2 * own_ops),
        "share_rows",
        tuple(chunk_shapes),
        [vmem_spec()] * (1 + levels),
        (vmem_spec(),) * steps,
        [pltpu.VMEM((own_rows, vectors), f32)],
    )(held[-1], *received)
    if direct:
        arrived = [to_partner(chunks[k], "gx", k) for k in range(1, shares)]
        own = local_call(
            functools.partial(sum_kernel, norm_factor),
            "sum_shares",
            jax.ShapeDtypeStruct((rows, vectors), bf16),
            [vmem_spec()] * shares,
            vmem_spec(),
        )(chunks[0], *arrived)
        every = [own] + [from_partner(own, "gx", k) for k in range(1, shares)]
    else:
        every = [(lax.psum(chunks[0], "gx") * norm_factor).astype(bf16)]
    every += [from_step(every[k], "ta", t) for t in range(1, times) for k in range(steps)]
    margins, correlators = local_call(
        functools.partial(contract_kernel, times, steps),
        "contraction",
        (
            jax.ShapeDtypeStruct((1, own_ops, 2, vectors, vectors), f32),
            jax.ShapeDtypeStruct((1, own_ops, 2), f32),
        ),
        [hbm_spec(), smem_spec()] + [vmem_spec()] * (len(every) + 1),
        (vmem_spec(), smem_spec()),
        [
            pltpu.VMEM((times, own_rows, vectors), bf16),
            pltpu.VMEM((own_rows, 2 * vectors), bf16),
            pltpu.VMEM((2 * vectors, own_rows), bf16),
            pltpu.SMEM((1, 2), jnp.int32),
            pltpu.SemaphoreType.DMA,
        ],
    )(in_hbm(pair_times), slot_counts, *every, perams[0])
    return (margins, correlators)


def solution(mesh):
    placed = (
        P("ta", "gx", "gy", None, None, None, None),
        P("ta", "gx", "gy", None, None, None, None, None),
        P(),
        P(),
        P(("ta", "gx"), None, None, None),
        P(("ta", "gx"), None),
        P(("ta", "gx")),
    )
    return jax.shard_map(
        per_device,
        mesh=mesh,
        in_specs=placed,
        out_specs=(P("ta", "gy", None, None, None), P(("ta", "gx"), "gy", None)),
        check_vma=False,
    )
```

```python
import functools
import math

import jax
import jax.numpy as jnp
import numpy as np
from jax import lax
from jax.experimental import pallas as pl
from jax.experimental.pallas import tpu as pltpu
from jax.sharding import PartitionSpec as P

VMEM_LIMIT = 24 * 1024 * 1024
MOMENTA = 3
LINK_COLS = 54
TAIL = 16
FIXED_BITS = 14.0


def wave_constants(cells_z):
    z_row = np.arange(3 * cells_z) // 3
    columns = []
    for ahead in range(2):
        for momentum in range(MOMENTA):
            angle = 2.0 * math.pi * momentum * ((z_row + ahead) % cells_z) / cells_z
            columns.append(np.cos(angle))
            columns.append(np.sin(angle))
    left = np.stack(columns, axis=1).astype(np.float32)
    terms = []
    for _ in range(3):
        term = left.astype(jnp.bfloat16).astype(np.float32)
        terms.append(term)
        left = left - term
    return jnp.asarray(np.concatenate(terms, axis=1), jnp.bfloat16)


def iota(shape, axis):
    return lax.broadcasted_iota(jnp.int32, shape, axis)


def third(x):
    return (x * 21846) >> 16


def one_hot(condition):
    return condition.astype(jnp.float32).astype(jnp.bfloat16)


def planar_order(order):
    row, col = iota((order, order), 0), iota((order, order), 1)
    half = order // 2
    source = jnp.where(row < half, 2 * row, 2 * (row - half) + 1)
    return one_hot(col == source)


def side_by_side(planar):
    half = planar.shape[0] // 2
    return jnp.concatenate([planar[:half], planar[half:]], axis=1).astype(jnp.bfloat16)


def transport(matrix, pair, sign):
    half, vectors = matrix.shape[0] // 2, pair.shape[1] // 2
    parts = jnp.dot(matrix, pair, preferred_element_type=jnp.float32)
    real, imag = parts[:half], parts[half:]
    if sign > 0:
        return jnp.concatenate(
            [real[:, :vectors] - imag[:, vectors:], real[:, vectors:] + imag[:, :vectors]], axis=0
        )
    return jnp.concatenate(
        [real[:, :vectors] + imag[:, vectors:], real[:, vectors:] - imag[:, :vectors]], axis=0
    )


def halo_fields(cells_x, cells_y):
    pairs = [(0, (cells_x - 1) * cells_y + y) for y in range(cells_y)]
    return pairs + [(1, x * cells_y + cells_y - 1) for x in range(cells_x)]


def local_fields(cells_x, cells_y):
    lines = cells_x * cells_y
    outside = halo_fields(cells_x, cells_y)
    every = [(code, line) for code in range(7) for line in range(lines)]
    return [pair for pair in every if pair not in outside]


def prepare_kernel(cells_x, cells_y, *refs):
    inputs, live_ref, refs = refs[:6], refs[6], refs[7:]
    matrix_ref, local_ref, left_ref, phase_ref, weight_ref = refs[:5]
    held, link_rows_ref, sems = refs[5:11], refs[11], refs[12]
    copies = [
        pltpu.make_async_copy(src, dst, sems.at[k])
        for k, (src, dst) in enumerate(zip(inputs, held))
    ]
    for copy in copies:
        copy.start()
    v_ref, link_ref, dirs_ref, moms_ref, waves_ref, pair_ref = held
    f32, bf16 = jnp.float32, jnp.bfloat16
    order, vectors = v_ref.shape[2], v_ref.shape[3]
    half, cells_z = order // 2, order // 6
    lines = cells_x * cells_y
    times = weight_ref.shape[1]
    spread = one_hot(third(iota((half, cells_z), 0)) == iota((half, cells_z), 1))
    row, col = iota((half, LINK_COLS), 0), iota((half, LINK_COLS), 1)
    row_color = row - 3 * third(row)
    pair_at = third(col >> 1)
    col_in, col_out = (col >> 1) - 3 * pair_at, pair_at - 3 * third(pair_at)
    pick = [(row_color == col_out).astype(f32), (row_color == col_in).astype(f32)]
    wide = (LINK_COLS, 6 * 128)
    row, col = iota(wide, 0), iota(wide, 1)
    block, place = col >> 7, col & 127
    color = place - 3 * third(place)
    pair_at = third(row >> 1)
    row_in, row_out = (row >> 1) - 3 * pair_at, pair_at - 3 * third(pair_at)
    fits = 2 * third(pair_at) + (row & 1) == block
    expand = [one_hot(fits & (row_in == color)), one_hot(fits & (row_out == color))]
    row, col = iota((half, 128), 0), iota((half, 128), 1)
    near = ((third(row) == third(col)) & (col < half)).astype(f32)
    planar = planar_order(order)
    for copy in copies:
        copy.wait()
    for t in range(times):
        sink = (pair_ref[0, 0] == t) & (live_ref[0] > 0)
        source = pair_ref[0, 1] == t
        weight_ref[0, t] = jnp.full(weight_ref.shape[2:], jnp.where(sink, 1.0, 0.0), f32)
        weight_ref[1, t] = jnp.full(weight_ref.shape[2:], jnp.where(source, 1.0, 0.0), f32)
    for line in range(lines):
        for k in range(LINK_COLS // 2):
            link_rows_ref[line, 2 * k : 2 * k + 2] = link_ref[line, k].astype(f32)
    outside = halo_fields(cells_x, cells_y)
    inside = local_fields(cells_x, cells_y)
    ordered = []
    for line in range(lines):
        here = jnp.dot(
            planar, v_ref[line // cells_y, line % cells_y], preferred_element_type=f32
        )
        ordered.append(here)
        local_ref[inside.index((6, line))] = here
    for line in range(lines):
        here = ordered[line]
        ahead_z = jnp.concatenate(
            [here[3:half], here[:3], here[half + 3 :], here[half : half + 3]], axis=0
        )
        columns = slice(line * order, (line + 1) * order)
        left_ref[0, :, columns] = here.T.astype(bf16)
        left_ref[1, :, columns] = ahead_z.T.astype(bf16)
        seen = lax.dot_general(
            spread,
            link_rows_ref[line].astype(bf16),
            (((1,), (1,)), ((), ())),
            preferred_element_type=f32,
        )
        pair = side_by_side(here)
        for way in range(2):
            blocks = jnp.dot(
                (seen * pick[way]).astype(bf16), expand[way], preferred_element_type=f32
            )
            for d in range(3):
                matrix = jnp.concatenate(
                    [
                        blocks[:, 256 * d : 256 * d + 128] * near,
                        blocks[:, 256 * d + 128 : 256 * d + 256] * near,
                    ],
                    axis=0,
                ).astype(bf16)
                if way == 1:
                    carried = transport(matrix[:, :half], pair, -1)
                    local_ref[inside.index((3 + d, line))] = carried.astype(bf16).astype(f32)
                elif (d, line) in outside:
                    matrix_ref[outside.index((d, line))] = matrix
                else:
                    ahead = ahead_z if d == 2 else ordered[line + (cells_y if d == 0 else 1)]
                    local_ref[inside.index((d, line))] = transport(
                        matrix[:, :half], side_by_side(ahead), 1
                    )
    wave_cols = waves_ref.shape[1]
    per_term = wave_cols // 3
    row, col = iota((wave_cols, 2 * vectors), 0), iota((wave_cols, 2 * vectors), 1)
    term = (row >= per_term).astype(jnp.int32) + (row >= 2 * per_term).astype(jnp.int32)
    wave_at = row - per_term * term - (col >= vectors).astype(jnp.int32)
    for o in range(phase_ref.shape[0]):
        column = 2 * (jnp.where(dirs_ref[o] == 5, MOMENTA, 0) + moms_ref[o])
        phase_ref[o] = jnp.dot(
            waves_ref[...], one_hot(wave_at == column), preferred_element_type=f32
        )


def low_bit(j):
    return (j & -j).bit_length() - 1


def put_product(out_ref, place, i, side, pair):
    vectors = pair.shape[1] // 2
    product = jnp.dot(side, pair, preferred_element_type=jnp.float32)
    first = 2 * i * vectors
    out_ref[place, first : first + vectors] = product[:, :vectors]
    out_ref[place, first + vectors : first + 2 * vectors] = product[:, vectors:]


def first_groups(groups):
    return sorted((j for j in range(groups) if j & 2), key=lambda j: -(j & 1))


def second_groups(groups):
    return sorted((j for j in range(groups) if not j & 2), key=lambda j: -(j & 1))


def first_margin_kernel(cells_x, cells_y, groups, own_ops, *refs):
    matrix_ref, local_ref, left_ref, phase_ref, halo_x_ref, halo_y_ref, dirs_hbm = refs[:7]
    swap_ref, hold_ref, later_side_ref, later_pair_ref = refs[7:11]
    field_ref, side_ref, dirs_ref, sem = refs[11:]
    f32, bf16 = jnp.float32, jnp.bfloat16
    copy = pltpu.make_async_copy(dirs_hbm, dirs_ref, sem)
    copy.start()
    lines = cells_x * cells_y
    order, vectors = halo_x_ref.shape[2], halo_x_ref.shape[3]
    half = order // 2
    planar = planar_order(order)
    side_ref[0] = left_ref[0]
    side_ref[3] = left_ref[1]
    outside = halo_fields(cells_x, cells_y)
    for d in range(2):
        for line in range(lines):
            x, y = line // cells_y, line % cells_y
            columns = slice(line * order, (line + 1) * order)
            if (d, line) not in outside:
                ahead = line + (cells_y if d == 0 else 1)
                side_ref[1 + d, :, columns] = left_ref[0, :, ahead * order : (ahead + 1) * order]
                continue
            halo = halo_x_ref[0, y] if d == 0 else halo_y_ref[x, 0]
            ahead = jnp.dot(planar, halo, preferred_element_type=f32)
            side_ref[1 + d, :, columns] = ahead.T.astype(bf16)
            matrix = matrix_ref[outside.index((d, line))]
            field_ref[d, line] = transport(matrix[:, :half], side_by_side(ahead), 1)
    for k, (code, line) in enumerate(local_fields(cells_x, cells_y)):
        field_ref[code, line] = local_ref[k]
    copy.wait()
    me = lax.axis_index("gy")
    later = 0
    for j in first_groups(groups) + second_groups(groups):
        for i in range(own_ops):
            o = (me ^ j) * own_ops + i
            code = dirs_ref[o]
            side = jnp.where((code >= 3) & (code < 6), code - 2, 0)
            cosine = phase_ref[o, :, 0:vectors]
            sine = phase_ref[o, :, vectors : 2 * vectors]
            pairs = []
            for line in range(lines):
                real, imag = field_ref[code, line, 0:half], field_ref[code, line, half:order]
                turned_r, turned_i = cosine * real - sine * imag, sine * real + cosine * imag
                pairs.append(jnp.concatenate([turned_r, turned_i], axis=1))
                pairs.append(jnp.concatenate([turned_i, -turned_r], axis=1))
            pair = jnp.concatenate(pairs, axis=0).astype(bf16)
            if j & 2:
                put_product(swap_ref if j & 1 else hold_ref, j >> 2, i, side_ref[side], pair)
            else:
                later_side_ref[later] = side_ref[side]
                later_pair_ref[later] = pair
                later += 1


def second_margin_kernel(groups, own_ops, side_ref, pair_ref, swap_ref, *hold_refs):
    later = 0
    for j in second_groups(groups):
        level = low_bit(j) if j else groups.bit_length() - 1
        for i in range(own_ops):
            out_ref, place = (swap_ref, j >> 2) if j & 1 else (hold_refs[level - 2], j >> (level + 1))
            put_product(out_ref, place, i, side_ref[later], pair_ref[later])
            later += 1


def scale_of(block):
    top = jnp.max(jnp.abs(block), axis=0, keepdims=True)
    return jnp.floor(jnp.log2(jnp.maximum(top, 1e-30))) + 1.0


def put_fixed(out_ref, blocks):
    rows, vectors = blocks[0].shape
    tail = iota((TAIL, vectors), 0)
    scales = jnp.zeros((TAIL, vectors), jnp.float32)
    for k, block in enumerate(blocks):
        scale = scale_of(block)
        scales = jnp.where(tail == k, scale, scales)
        fixed = jnp.floor(block * jnp.exp2(FIXED_BITS - scale) + 0.5)
        out_ref[k * rows : (k + 1) * rows] = fixed.astype(jnp.int32).astype(jnp.int16)
    out_ref[len(blocks) * rows :] = scales.astype(jnp.int32).astype(jnp.int16)


def from_fixed(ref, rows, k):
    scales = ref[ref.shape[0] - TAIL :].astype(jnp.int32).astype(jnp.float32)
    block = ref[k * rows : (k + 1) * rows].astype(jnp.int32).astype(jnp.float32)
    return block * jnp.exp2(scales[k : k + 1] - FIXED_BITS)


def group_block(held_ref, received, k, j, start, rows):
    span = pl.ds(start, rows)
    total = held_ref[k, span] + received[0][j >> 2, span]
    for b, ref in enumerate(received[1:], 1):
        total = total + fixed_at(ref.at[j >> (b + 1)], start, rows)
    return total


def fixed_at(ref, start, rows):
    tail = ref[ref.shape[0] - TAIL :].astype(jnp.int32).astype(jnp.float32)
    scale = jnp.max(
        jnp.where(iota(tail.shape, 0) == start // rows, tail, -1000.0), axis=0, keepdims=True
    )
    block = ref[pl.ds(start, rows)].astype(jnp.int32).astype(jnp.float32)
    return block * jnp.exp2(scale - FIXED_BITS)


def fold_kernel(level, vectors, *refs):
    held_ref, received, out_ref = refs[0], refs[1:-1], refs[-1]
    for k in range(held_ref.shape[0]):
        j = (2 * k + 1) << level
        blocks = [
            group_block(held_ref, received, k, j, start, vectors)
            for start in range(0, held_ref.shape[1], vectors)
        ]
        put_fixed(out_ref.at[k], blocks)


def half_rows(held_ref, vectors, kept):
    me = lax.axis_index("gx") & 1
    half = held_ref.shape[1] // 2
    base = pl.multiple_of((me if kept else 1 - me) * half, half)
    return [base + step for step in range(0, half, vectors)]


def fold_halves_kernel(vectors, *refs):
    held_ref, received, outs = refs[0], refs[1:-2], refs[-2:]
    for kept, out_ref in enumerate(outs):
        starts = half_rows(held_ref, vectors, kept)
        blocks = [group_block(held_ref, received, 0, held_ref.shape[0], s, vectors) for s in starts]
        put_fixed(out_ref, blocks)


def half_kernel(vectors, kept, *refs):
    count = 3 if kept else 2
    held_ref, received, last, out_ref = refs[0], refs[1:-count], refs[-count:-1], refs[-1]
    blocks = []
    for p, start in enumerate(half_rows(held_ref, vectors, kept)):
        total = group_block(held_ref, received, 0, 0, start, vectors)
        for ref in last:
            total = total + from_fixed(ref, vectors, p)
        blocks.append(total)
    put_fixed(out_ref, blocks)


def both_kernel(vectors, norm_factor, own_ref, arrived_ref, out_ref):
    blocks = [
        from_fixed(own_ref, vectors, p) + from_fixed(arrived_ref, vectors, p)
        for p in range((own_ref.shape[0] - TAIL) // vectors)
    ]
    if norm_factor is None:
        put_fixed(out_ref, blocks)
        return
    for p, block in enumerate(blocks):
        out_ref[p * vectors : (p + 1) * vectors] = (block * norm_factor).astype(out_ref.dtype)


def contract(sums_ref, weight_ref, blocks, tau_ref, left_ref, right_ref):
    f32, bf16 = jnp.float32, jnp.bfloat16
    vectors = sums_ref.shape[2]
    count_ops = sums_ref.shape[0] // 2
    order = tau_ref.shape[2]
    spins = order // vectors
    me_t = lax.axis_index("ta")
    times = len(blocks)

    def chosen(end, k):
        total = jnp.zeros((vectors // 8, 8, vectors), f32)
        for t in range(times):
            weight = weight_ref[end, lax.rem(me_t + t, times)]
            total = total + blocks[t](k).astype(f32).reshape(total.shape) * weight
        return total.reshape(vectors, vectors)

    for o in range(count_ops):
        first = 2 * o * vectors
        a_r, a_i = chosen(0, 2 * o).astype(bf16), chosen(0, 2 * o + 1).astype(bf16)
        b_r, b_i = chosen(1, 2 * o).T.astype(bf16), chosen(1, 2 * o + 1).T.astype(bf16)
        real, imag = slice(first, first + vectors), slice(first + vectors, first + 2 * vectors)
        left_ref[real, 0:vectors] = a_r
        left_ref[real, vectors:] = -a_i
        left_ref[imag, 0:vectors] = a_i
        left_ref[imag, vectors:] = a_r
        right_ref[0:vectors, real] = b_r
        right_ref[0:vectors, imag] = -b_i
        right_ref[vectors:, real] = b_i
        right_ref[vectors:, imag] = b_r
    lanes = sums_ref.shape[1]
    fold = lambda t: jnp.sum(t.reshape(vectors // lanes, lanes, vectors), axis=0)
    sums = [jnp.zeros((lanes, vectors), f32) for _ in range(2 * count_ops)]
    for s in range(spins):
        rows = slice(s * vectors, (s + 1) * vectors)
        x = jnp.dot(
            left_ref[...],
            jnp.concatenate([tau_ref[0, rows], tau_ref[1, rows]], axis=0),
            preferred_element_type=f32,
        )
        for c in range(spins):
            cols = slice(c * vectors, (c + 1) * vectors)
            y = jnp.dot(
                jnp.concatenate([tau_ref[0, rows, cols], tau_ref[1, rows, cols]], axis=1),
                right_ref[...],
                preferred_element_type=f32,
            )
            for o in range(count_ops):
                first = 2 * o * vectors
                x_r = x[first : first + vectors, cols]
                x_i = x[first + vectors : first + 2 * vectors, cols]
                y_r = y[:, first : first + vectors]
                y_i = y[:, first + vectors : first + 2 * vectors]
                sums[2 * o] = sums[2 * o] + fold(x_r * y_r + x_i * y_i)
                sums[2 * o + 1] = sums[2 * o + 1] + fold(x_i * y_r - x_r * y_i)
    for k, total in enumerate(sums):
        sums_ref[k] = total


def part_of(ref, vectors):
    return lambda k: ref[k * vectors : (k + 1) * vectors]


def first_contract_kernel(times, weight_ref, tau_ref, *refs):
    blocks, (sums_ref, left_ref, right_ref) = refs[:times], refs[times:]
    vectors = sums_ref.shape[2]
    blocks = [part_of(ref, vectors) for ref in blocks]
    contract(sums_ref, weight_ref, blocks, tau_ref, left_ref, right_ref)


def second_contract_kernel(times, split, weight_ref, tau_ref, *refs):
    kept, other, refs = refs[:times], refs[times : 2 * times], refs[2 * times :]
    if split:
        first_sums_ref, refs = refs[0], refs[1:]
    margin_ref, corr_ref, sums_ref, left_ref, right_ref = refs
    vectors = sums_ref.shape[2]
    half = kept[0].shape[0]
    me = lax.axis_index("gx") & 1
    places = (me, 1 - me)
    for place, ref in zip(places, (kept[0], other[0])):
        span = pl.ds(pl.multiple_of(place * half, half), half)
        margin_ref[0, span] = ref[...].astype(jnp.float32)
    scale = 1.0 / vectors

    def put(sums, first):
        for k in range(sums.shape[0]):
            corr_ref[0, first + k // 2, k % 2] = jnp.sum(sums[k]) * scale

    if split:
        blocks = [part_of(ref, vectors) for ref in other]
        contract(sums_ref, weight_ref, blocks, tau_ref, left_ref, right_ref)
        own_ops = sums_ref.shape[0] // 2
        put(first_sums_ref, places[0] * own_ops)
        put(sums_ref, places[1] * own_ops)
        return
    parts_per_half = half // vectors

    def either(kept_ref, other_ref):
        def part(k):
            row = (k % parts_per_half) * vectors
            own, far = kept_ref[row : row + vectors], other_ref[row : row + vectors]
            mine = (k // parts_per_half == me).astype(jnp.float32)
            return own.astype(jnp.float32) * mine + far.astype(jnp.float32) * (1.0 - mine)

        return part

    blocks = [either(a, b) for a, b in zip(kept, other)]
    contract(sums_ref, weight_ref, blocks, tau_ref, left_ref, right_ref)
    put(sums_ref, 0)


def vmem_spec():
    return pl.BlockSpec(memory_space=pltpu.VMEM)


def smem_spec():
    return pl.BlockSpec(memory_space=pltpu.SMEM)


def hbm_spec():
    return pl.BlockSpec(memory_space=pltpu.HBM)


def in_hbm(x):
    return pltpu.with_memory_space_constraint(x, pltpu.HBM)


def local_call(body, name, outs, in_specs, out_specs, scratch=(), cost=None):
    return pl.pallas_call(
        body,
        out_shape=outs,
        in_specs=in_specs,
        out_specs=out_specs,
        scratch_shapes=list(scratch),
        compiler_params=pltpu.CompilerParams(vmem_limit_bytes=VMEM_LIMIT),
        cost_estimate=cost,
        name=name,
    )


def from_step(block, axis, step):
    count = lax.axis_size(axis)
    return lax.ppermute(block, axis, [((i + step) % count, i) for i in range(count)])


def from_partner(block, axis, step):
    count = lax.axis_size(axis)
    return lax.ppermute(block, axis, [(i ^ step, i) for i in range(count)])


def per_device(eigvecs, links, op_dirs, op_moms, perams, pair_times, slot_counts):
    f32, bf16 = jnp.float32, jnp.bfloat16
    _, cells_x, cells_y, cells_z, colors, _, vectors = eigvecs.shape
    order = cells_z * colors * 2
    lines = cells_x * cells_y
    count_ops = op_dirs.shape[0]
    times, shares, groups = lax.axis_size("ta"), lax.axis_size("gx"), lax.axis_size("gy")
    levels = groups.bit_length() - 1
    own_ops = count_ops // groups
    own_rows = own_ops * 2 * vectors
    field = eigvecs.reshape(cells_x, cells_y, order, vectors)
    halo_x = from_step(field[0:1], "gx", 1)
    halo_y = from_step(field, "gy", 1)
    link_field = links[0].transpose(0, 1, 3, 5, 6, 4, 2).reshape(lines, 27, 2, cells_z)
    outside, inside = halo_fields(cells_x, cells_y), local_fields(cells_x, cells_y)
    inputs = [field, link_field, op_dirs, op_moms, wave_constants(cells_z), pair_times]
    inputs = [in_hbm(x) for x in inputs]
    held = [
        pltpu.SMEM(x.shape, x.dtype) if x.dtype == jnp.int32 else pltpu.VMEM(x.shape, x.dtype)
        for x in inputs
    ]
    matrices, local, left, phases, weights = local_call(
        functools.partial(prepare_kernel, cells_x, cells_y),
        "prepare_lines",
        (
            jax.ShapeDtypeStruct((len(outside), order, 128), bf16),
            jax.ShapeDtypeStruct((len(inside), order, vectors), f32),
            jax.ShapeDtypeStruct((2, vectors, lines * order), bf16),
            jax.ShapeDtypeStruct((count_ops, order // 2, 2 * vectors), f32),
            jax.ShapeDtypeStruct((2, times, 8, vectors), f32),
        ),
        [hbm_spec()] * len(inputs) + [smem_spec()],
        (vmem_spec(),) * 5,
        held
        + [
            pltpu.VMEM((lines, LINK_COLS, cells_z), f32),
            pltpu.SemaphoreType.DMA((len(inputs),)),
        ],
    )(*inputs, slot_counts)
    part = lambda count: jax.ShapeDtypeStruct((count, own_rows, vectors), f32)
    later = count_ops // 2
    swap_a, hold_a, later_sides, later_pairs = local_call(
        functools.partial(first_margin_kernel, cells_x, cells_y, groups, own_ops),
        "first_margins",
        (
            part(groups // 4),
            part(groups // 4),
            jax.ShapeDtypeStruct((later, vectors, lines * order), bf16),
            jax.ShapeDtypeStruct((later, lines * order, 2 * vectors), bf16),
        ),
        [vmem_spec()] * 6 + [hbm_spec()],
        (vmem_spec(),) * 4,
        [
            pltpu.VMEM((7, lines, order, vectors), f32),
            pltpu.VMEM((4, vectors, lines * order), bf16),
            pltpu.SMEM((count_ops,), jnp.int32),
            pltpu.SemaphoreType.DMA,
        ],
    )(matrices, local, left, phases, halo_x, halo_y, in_hbm(op_dirs))
    swapped_a = from_partner(swap_a, "gy", 1)
    held_shapes = [part(groups >> (b + 1)) for b in range(2, levels)] + [part(1)]
    swap_b, *held = local_call(
        functools.partial(second_margin_kernel, groups, own_ops),
        "second_margins",
        (part(groups // 4), *held_shapes),
        [vmem_spec()] * 2,
        (vmem_spec(),) * (1 + len(held_shapes)),
    )(later_sides, later_pairs)
    received = [from_partner(swap_b, "gy", 1)]

    def packed(body, name, *inputs, rows=own_rows, lead=(), count=1):
        shape = jax.ShapeDtypeStruct((*lead, rows + TAIL, vectors), jnp.int16)
        outs = shape if count == 1 else (shape,) * count
        specs = vmem_spec() if count == 1 else (vmem_spec(),) * count
        return local_call(body, name, outs, [vmem_spec()] * len(inputs), specs)(*inputs)

    half = own_rows // 2
    for b in range(1, levels):
        inputs = (hold_a, swapped_a) if b == 1 else (held[b - 2], *received)
        if b < levels - 1:
            body = functools.partial(fold_kernel, b, vectors)
            sent = packed(body, "fold_groups", *inputs, lead=inputs[0].shape[:1])
            received.append(from_partner(sent, "gy", 1 << b))
            continue
        body = functools.partial(fold_halves_kernel, vectors)
        away, kept = packed(body, "fold_halves", *inputs, rows=half, count=2)
        away, kept = from_partner(away, "gy", 1 << b), from_partner(kept, "gy", 1 << b)
    body = functools.partial(half_kernel, vectors, False)
    sent = packed(body, "send_half", held[-1], *received, away, rows=half)
    arrived = from_partner(sent, "gx", 1)
    body = functools.partial(half_kernel, vectors, True)
    message = packed(body, "keep_half", held[-1], *received, kept, arrived, rows=half)
    norm_factor = 1.0 / math.sqrt(3.0 * cells_x * shares * cells_y * groups * cells_z)
    step = 2
    while step < shares:
        arrived = from_partner(message, "gx", step)
        step *= 2
        if step < shares:
            body = functools.partial(both_kernel, vectors, None)
            message = packed(body, "sum_both", message, arrived, rows=half)
    finished = local_call(
        functools.partial(both_kernel, vectors, norm_factor),
        "finish_half",
        jax.ShapeDtypeStruct((half, vectors), bf16),
        [vmem_spec()] * 2,
        vmem_spec(),
    )(message, arrived)
    kept = [finished] + [from_step(finished, "ta", t) for t in range(1, times)]
    other = [from_partner(block, "gx", 1) for block in kept]
    split = own_ops % 2 == 0
    now_ops = own_ops // 2 if split else own_ops
    sums_shape = (2 * now_ops, 32, vectors)
    scratch = [
        pltpu.VMEM((2 * now_ops * vectors, 2 * vectors), bf16),
        pltpu.VMEM((2 * vectors, 2 * now_ops * vectors), bf16),
    ]
    sums = []
    if split:
        sums = [
            local_call(
                functools.partial(first_contract_kernel, times),
                "first_contraction",
                jax.ShapeDtypeStruct(sums_shape, f32),
                [vmem_spec()] * (2 + times),
                vmem_spec(),
                scratch,
            )(weights, perams[0], *kept)
        ]
    margins, correlators = local_call(
        functools.partial(second_contract_kernel, times, split),
        "second_contraction",
        (
            jax.ShapeDtypeStruct((1, own_rows, vectors), f32),
            jax.ShapeDtypeStruct((1, own_ops, 2), f32),
        ),
        [vmem_spec()] * (2 + 2 * times + len(sums)),
        (vmem_spec(), smem_spec()),
        [pltpu.VMEM(sums_shape, f32)] + scratch,
    )(weights, perams[0], *kept, *other, *sums)
    return (margins.reshape(1, own_ops, 2, vectors, vectors), correlators)


def solution(mesh):
    placed = (
        P("ta", "gx", "gy", None, None, None, None),
        P("ta", "gx", "gy", None, None, None, None, None),
        P(),
        P(),
        P(("ta", "gx"), None, None, None),
        P(("ta", "gx"), None),
        P(("ta", "gx")),
    )
    return jax.shard_map(
        per_device,
        mesh=mesh,
        in_specs=placed,
        out_specs=(P("ta", "gy", None, None, None), P(("ta", "gx"), "gy", None)),
        check_vma=False,
    )
```

```python
import functools
import math

import jax
import jax.numpy as jnp
import numpy as np
from jax import lax
from jax.experimental import pallas as pl
from jax.experimental.pallas import tpu as pltpu
from jax.sharding import PartitionSpec as P

VMEM_LIMIT = 24 * 1024 * 1024
MOMENTA = 3
LINK_COLS = 54
TAIL = 16
FIXED_BITS = 14.0


def wave_constants(cells_z):
    z_row = np.arange(3 * cells_z) // 3
    columns = []
    for ahead in range(2):
        for momentum in range(MOMENTA):
            angle = 2.0 * math.pi * momentum * ((z_row + ahead) % cells_z) / cells_z
            columns.append(np.cos(angle))
            columns.append(np.sin(angle))
    left = np.stack(columns, axis=1).astype(np.float32)
    terms = []
    for _ in range(3):
        term = left.astype(jnp.bfloat16).astype(np.float32)
        terms.append(term)
        left = left - term
    return jnp.asarray(np.concatenate(terms, axis=1), jnp.bfloat16)


def iota(shape, axis):
    return lax.broadcasted_iota(jnp.int32, shape, axis)


def third(x):
    return (x * 21846) >> 16


def one_hot(condition):
    return condition.astype(jnp.float32).astype(jnp.bfloat16)


def planar_order(order):
    row, col = iota((order, order), 0), iota((order, order), 1)
    half = order // 2
    source = jnp.where(row < half, 2 * row, 2 * (row - half) + 1)
    return one_hot(col == source)


def side_by_side(planar):
    half = planar.shape[0] // 2
    return jnp.concatenate([planar[:half], planar[half:]], axis=1).astype(jnp.bfloat16)


def transport(matrix, pair, sign):
    half, vectors = matrix.shape[0] // 2, pair.shape[1] // 2
    parts = jnp.dot(matrix, pair, preferred_element_type=jnp.float32)
    real, imag = parts[:half], parts[half:]
    if sign > 0:
        return jnp.concatenate(
            [real[:, :vectors] - imag[:, vectors:], real[:, vectors:] + imag[:, :vectors]], axis=0
        )
    return jnp.concatenate(
        [real[:, :vectors] + imag[:, vectors:], real[:, vectors:] - imag[:, :vectors]], axis=0
    )


def leaves(cells_x, cells_y, code, line):
    if code in (0, 3):
        return line // cells_y == 0
    return code == 1 and line % cells_y == cells_y - 1


def local_fields(cells_x, cells_y):
    every = [(code, line) for code in range(7) for line in range(cells_x * cells_y)]
    return [pair for pair in every if not leaves(cells_x, cells_y, *pair)]


class LinkForms:
    def __init__(self, half):
        cells_z = half // 3
        self.half = half
        self.spread = one_hot(third(iota((half, cells_z), 0)) == iota((half, cells_z), 1))
        row, col = iota((half, LINK_COLS), 0), iota((half, LINK_COLS), 1)
        row_color = row - 3 * third(row)
        pair_at = third(col >> 1)
        col_in, col_out = (col >> 1) - 3 * pair_at, pair_at - 3 * third(pair_at)
        self.pick = [(row_color == c).astype(jnp.float32) for c in (col_out, col_in)]
        row, col = iota((LINK_COLS, 6 * 128), 0), iota((LINK_COLS, 6 * 128), 1)
        block, place = col >> 7, col & 127
        color = place - 3 * third(place)
        pair_at = third(row >> 1)
        row_in, row_out = (row >> 1) - 3 * pair_at, pair_at - 3 * third(pair_at)
        fits = 2 * third(pair_at) + (row & 1) == block
        self.expand = [one_hot(fits & (c == color)) for c in (row_in, row_out)]
        row, col = iota((half, 128), 0), iota((half, 128), 1)
        self.near = ((third(row) == third(col)) & (col < half)).astype(jnp.float32)

    def seen(self, link_ref, rows_ref):
        for k in range(LINK_COLS // 2):
            rows_ref[2 * k : 2 * k + 2] = link_ref[k].astype(jnp.float32)
        return lax.dot_general(
            self.spread,
            rows_ref[...].astype(jnp.bfloat16),
            (((1,), (1,)), ((), ())),
            preferred_element_type=jnp.float32,
        )

    def matrices(self, seen, way, directions):
        blocks = jnp.dot(
            (seen * self.pick[way]).astype(jnp.bfloat16),
            self.expand[way][:, : 256 * directions],
            preferred_element_type=jnp.float32,
        )
        cut = lambda k: blocks[:, 128 * k : 128 * k + 128] * self.near
        return [
            jnp.concatenate([cut(2 * d), cut(2 * d + 1)], axis=0).astype(jnp.bfloat16)
            for d in range(directions)
        ]


def prepare_kernel(cells_x, cells_y, *refs):
    inputs, live_ref, refs = refs[:6], refs[6], refs[7:]
    matrix_ref, local_ref, left_ref, phase_ref, weight_ref = refs[:5]
    held, link_rows_ref, sems = refs[5:11], refs[11], refs[12]
    copies = [
        pltpu.make_async_copy(src, dst, sems.at[k])
        for k, (src, dst) in enumerate(zip(inputs, held))
    ]
    for copy in copies:
        copy.start()
    v_ref, link_ref, dirs_ref, moms_ref, waves_ref, pair_ref = held
    f32, bf16 = jnp.float32, jnp.bfloat16
    order, vectors = v_ref.shape[2], v_ref.shape[3]
    half = order // 2
    lines = cells_x * cells_y
    times = weight_ref.shape[1]
    forms = LinkForms(half)
    planar = planar_order(order)
    for copy in copies:
        copy.wait()
    for t in range(times):
        sink = (pair_ref[0, 0] == t) & (live_ref[0] > 0)
        source = pair_ref[0, 1] == t
        weight_ref[0, t] = jnp.full(weight_ref.shape[2:], jnp.where(sink, 1.0, 0.0), f32)
        weight_ref[1, t] = jnp.full(weight_ref.shape[2:], jnp.where(source, 1.0, 0.0), f32)
    inside = local_fields(cells_x, cells_y)
    ordered = []
    for line in range(lines):
        here = jnp.dot(
            planar, v_ref[line // cells_y, line % cells_y], preferred_element_type=f32
        )
        ordered.append(here)
        local_ref[inside.index((6, line))] = here
    for line in range(lines):
        here = ordered[line]
        ahead_z = jnp.concatenate(
            [here[3:half], here[:3], here[half + 3 :], here[half : half + 3]], axis=0
        )
        columns = slice(line * order, (line + 1) * order)
        left_ref[0, :, columns] = here.T.astype(bf16)
        left_ref[1, :, columns] = ahead_z.T.astype(bf16)
        seen = forms.seen(link_ref.at[line], link_rows_ref.at[line])
        pair = side_by_side(here)
        on_x = line + cells_y if line + cells_y < lines else None
        for d, matrix in enumerate(forms.matrices(seen, 0, 3)):
            if d == 0 and on_x is None:
                continue
            if d == 1 and leaves(cells_x, cells_y, 1, line):
                matrix_ref[line // cells_y] = matrix
                continue
            ahead = (ordered[on_x] if d == 0 else ordered[line + 1]) if d < 2 else ahead_z
            local_ref[inside.index((d, on_x if d == 0 else line))] = transport(
                matrix[:, :half], side_by_side(ahead), 1
            )
        for d, matrix in enumerate(forms.matrices(seen, 1, 3)):
            if d == 0 and on_x is None:
                continue
            carried = transport(matrix[:, :half], pair, -1).astype(bf16).astype(f32)
            local_ref[inside.index((3 + d, on_x if d == 0 else line))] = carried
    wave_cols = waves_ref.shape[1]
    per_term = wave_cols // 3
    row, col = iota((wave_cols, 2 * vectors), 0), iota((wave_cols, 2 * vectors), 1)
    term = (row >= per_term).astype(jnp.int32) + (row >= 2 * per_term).astype(jnp.int32)
    wave_at = row - per_term * term - (col >= vectors).astype(jnp.int32)
    for o in range(phase_ref.shape[0]):
        column = 2 * (jnp.where(dirs_ref[o] == 5, MOMENTA, 0) + moms_ref[o])
        phase_ref[o] = jnp.dot(
            waves_ref[...], one_hot(wave_at == column), preferred_element_type=f32
        )


def behind_kernel(cells_x, cells_y, link_ref, local_ref, field_ref, matrix_ref, rows_ref):
    half = local_ref.shape[1] // 2
    forms = LinkForms(half)
    inside = local_fields(cells_x, cells_y)
    for y in range(cells_y):
        seen = forms.seen(link_ref.at[y], rows_ref.at[y])
        pair = side_by_side(local_ref[inside.index((6, y))])
        field_ref[y] = transport(forms.matrices(seen, 0, 1)[0][:, :half], pair, 1)
        matrix_ref[y] = forms.matrices(seen, 1, 1)[0]


def low_bit(j):
    return (j & -j).bit_length() - 1


def put_product(out_ref, place, i, side, pair):
    vectors = pair.shape[1] // 2
    product = jnp.dot(side, pair, preferred_element_type=jnp.float32)
    first = 2 * i * vectors
    out_ref[place, first : first + vectors] = product[:, :vectors]
    out_ref[place, first + vectors : first + 2 * vectors] = product[:, vectors:]


def first_groups(groups):
    return sorted((j for j in range(groups) if j & 2), key=lambda j: -(j & 1))


def second_groups(groups):
    return sorted((j for j in range(groups) if not j & 2), key=lambda j: -(j & 1))


def first_margin_kernel(cells_x, cells_y, groups, own_ops, *refs):
    matrix_ref, local_ref, left_ref, phase_ref, behind_ref, adjoint_ref = refs[:6]
    halo_x_ref, halo_y_ref, dirs_hbm = refs[6:9]
    swap_ref, hold_ref, later_side_ref, later_pair_ref = refs[9:13]
    field_ref, side_ref, dirs_ref, sem = refs[13:]
    f32, bf16 = jnp.float32, jnp.bfloat16
    copy = pltpu.make_async_copy(dirs_hbm, dirs_ref, sem)
    copy.start()
    lines = cells_x * cells_y
    order, vectors = halo_x_ref.shape[2], halo_x_ref.shape[3]
    half = order // 2
    planar = planar_order(order)
    side_ref[0] = left_ref[0]
    side_ref[3] = left_ref[1]
    for line in range(lines):
        x, y = line // cells_y, line % cells_y
        columns = slice(line * order, (line + 1) * order)
        if x:
            back = line - cells_y
            side_ref[1, :, columns] = left_ref[0, :, back * order : (back + 1) * order]
        else:
            back = jnp.dot(planar, halo_x_ref[0, y], preferred_element_type=f32)
            side_ref[1, :, columns] = back.T.astype(bf16)
            field_ref[0, line] = behind_ref[y]
            carried = transport(adjoint_ref[y, :, :half], side_by_side(back), -1)
            field_ref[3, line] = carried.astype(bf16).astype(f32)
        if y + 1 < cells_y:
            side_ref[2, :, columns] = left_ref[0, :, (line + 1) * order : (line + 2) * order]
        else:
            ahead = jnp.dot(planar, halo_y_ref[x, 0], preferred_element_type=f32)
            side_ref[2, :, columns] = ahead.T.astype(bf16)
            field_ref[1, line] = transport(matrix_ref[x, :, :half], side_by_side(ahead), 1)
    for k, (code, line) in enumerate(local_fields(cells_x, cells_y)):
        field_ref[code, line] = local_ref[k]
    copy.wait()
    me = lax.axis_index("gy")
    later = 0
    for j in first_groups(groups) + second_groups(groups):
        for i in range(own_ops):
            o = (me ^ j) * own_ops + i
            code = dirs_ref[o]
            side = jnp.where(code == 0, 1, jnp.where((code == 4) | (code == 5), code - 2, 0))
            cosine = phase_ref[o, :, 0:vectors]
            sine = phase_ref[o, :, vectors : 2 * vectors]
            pairs = []
            for line in range(lines):
                real, imag = field_ref[code, line, 0:half], field_ref[code, line, half:order]
                turned_r, turned_i = cosine * real - sine * imag, sine * real + cosine * imag
                pairs.append(jnp.concatenate([turned_r, turned_i], axis=1))
                pairs.append(jnp.concatenate([turned_i, -turned_r], axis=1))
            pair = jnp.concatenate(pairs, axis=0).astype(bf16)
            if j & 2:
                put_product(swap_ref if j & 1 else hold_ref, j >> 2, i, side_ref[side], pair)
            else:
                later_side_ref[later] = side_ref[side]
                later_pair_ref[later] = pair
                later += 1


def second_margin_kernel(groups, own_ops, side_ref, pair_ref, swap_ref, *hold_refs):
    later = 0
    for j in second_groups(groups):
        level = low_bit(j) if j else groups.bit_length() - 1
        for i in range(own_ops):
            out_ref, place = (swap_ref, j >> 2) if j & 1 else (hold_refs[level - 2], j >> (level + 1))
            put_product(out_ref, place, i, side_ref[later], pair_ref[later])
            later += 1


def scale_of(block):
    top = jnp.max(jnp.abs(block), axis=0, keepdims=True)
    return jnp.floor(jnp.log2(jnp.maximum(top, 1e-30))) + 1.0


def put_fixed(out_ref, blocks):
    rows, vectors = blocks[0].shape
    tail = iota((TAIL, vectors), 0)
    scales = jnp.zeros((TAIL, vectors), jnp.float32)
    for k, block in enumerate(blocks):
        scale = scale_of(block)
        scales = jnp.where(tail == k, scale, scales)
        fixed = jnp.floor(block * jnp.exp2(FIXED_BITS - scale) + 0.5)
        out_ref[k * rows : (k + 1) * rows] = fixed.astype(jnp.int32).astype(jnp.int16)
    out_ref[len(blocks) * rows :] = scales.astype(jnp.int32).astype(jnp.int16)


def from_fixed(ref, rows, k):
    scales = ref[ref.shape[0] - TAIL :].astype(jnp.int32).astype(jnp.float32)
    block = ref[k * rows : (k + 1) * rows].astype(jnp.int32).astype(jnp.float32)
    return block * jnp.exp2(scales[k : k + 1] - FIXED_BITS)


def group_block(held_ref, received, k, j, start, rows):
    span = pl.ds(start, rows)
    total = held_ref[k, span] + received[0][j >> 2, span]
    for b, ref in enumerate(received[1:], 1):
        total = total + fixed_at(ref.at[j >> (b + 1)], start, rows)
    return total


def fixed_at(ref, start, rows):
    tail = ref[ref.shape[0] - TAIL :].astype(jnp.int32).astype(jnp.float32)
    scale = jnp.max(
        jnp.where(iota(tail.shape, 0) == start // rows, tail, -1000.0), axis=0, keepdims=True
    )
    block = ref[pl.ds(start, rows)].astype(jnp.int32).astype(jnp.float32)
    return block * jnp.exp2(scale - FIXED_BITS)


def fold_kernel(level, vectors, *refs):
    held_ref, received, out_ref = refs[0], refs[1:-1], refs[-1]
    for k in range(held_ref.shape[0]):
        j = (2 * k + 1) << level
        blocks = [
            group_block(held_ref, received, k, j, start, vectors)
            for start in range(0, held_ref.shape[1], vectors)
        ]
        put_fixed(out_ref.at[k], blocks)


def half_rows(held_ref, vectors, kept):
    me = lax.axis_index("gx") & 1
    half = held_ref.shape[1] // 2
    base = pl.multiple_of((me if kept else 1 - me) * half, half)
    return [base + step for step in range(0, half, vectors)]


def fold_halves_kernel(vectors, *refs):
    held_ref, received, outs = refs[0], refs[1:-2], refs[-2:]
    for kept, out_ref in enumerate(outs):
        starts = half_rows(held_ref, vectors, kept)
        blocks = [group_block(held_ref, received, 0, held_ref.shape[0], s, vectors) for s in starts]
        put_fixed(out_ref, blocks)


def half_kernel(vectors, kept, *refs):
    count = 3 if kept else 2
    held_ref, received, last, out_ref = refs[0], refs[1:-count], refs[-count:-1], refs[-1]
    blocks = []
    for p, start in enumerate(half_rows(held_ref, vectors, kept)):
        total = group_block(held_ref, received, 0, 0, start, vectors)
        for ref in last:
            total = total + from_fixed(ref, vectors, p)
        blocks.append(total)
    put_fixed(out_ref, blocks)


def both_kernel(vectors, norm_factor, own_ref, arrived_ref, out_ref):
    blocks = [
        from_fixed(own_ref, vectors, p) + from_fixed(arrived_ref, vectors, p)
        for p in range((own_ref.shape[0] - TAIL) // vectors)
    ]
    if norm_factor is None:
        put_fixed(out_ref, blocks)
        return
    for p, block in enumerate(blocks):
        out_ref[p * vectors : (p + 1) * vectors] = (block * norm_factor).astype(out_ref.dtype)


def contract(sums_ref, weight_ref, blocks, tau_ref, left_ref, right_ref):
    f32, bf16 = jnp.float32, jnp.bfloat16
    vectors = sums_ref.shape[2]
    count_ops = sums_ref.shape[0] // 2
    order = tau_ref.shape[2]
    spins = order // vectors
    me_t = lax.axis_index("ta")
    times = len(blocks)

    def chosen(end, k):
        total = jnp.zeros((vectors // 8, 8, vectors), f32)
        for t in range(times):
            weight = weight_ref[end, lax.rem(me_t + t, times)]
            total = total + blocks[t](k).astype(f32).reshape(total.shape) * weight
        return total.reshape(vectors, vectors)

    for o in range(count_ops):
        first = 2 * o * vectors
        a_r, a_i = chosen(0, 2 * o).astype(bf16), chosen(0, 2 * o + 1).astype(bf16)
        b_r, b_i = chosen(1, 2 * o).T.astype(bf16), chosen(1, 2 * o + 1).T.astype(bf16)
        real, imag = slice(first, first + vectors), slice(first + vectors, first + 2 * vectors)
        left_ref[real, 0:vectors] = a_r
        left_ref[real, vectors:] = -a_i
        left_ref[imag, 0:vectors] = a_i
        left_ref[imag, vectors:] = a_r
        right_ref[0:vectors, real] = b_r
        right_ref[0:vectors, imag] = -b_i
        right_ref[vectors:, real] = b_i
        right_ref[vectors:, imag] = b_r
    lanes = sums_ref.shape[1]
    fold = lambda t: jnp.sum(t.reshape(vectors // lanes, lanes, vectors), axis=0)
    sums = [jnp.zeros((lanes, vectors), f32) for _ in range(2 * count_ops)]
    for s in range(spins):
        rows = slice(s * vectors, (s + 1) * vectors)
        x = jnp.dot(
            left_ref[...],
            jnp.concatenate([tau_ref[0, rows], tau_ref[1, rows]], axis=0),
            preferred_element_type=f32,
        )
        for c in range(spins):
            cols = slice(c * vectors, (c + 1) * vectors)
            y = jnp.dot(
                jnp.concatenate([tau_ref[0, rows, cols], tau_ref[1, rows, cols]], axis=1),
                right_ref[...],
                preferred_element_type=f32,
            )
            for o in range(count_ops):
                first = 2 * o * vectors
                x_r = x[first : first + vectors, cols]
                x_i = x[first + vectors : first + 2 * vectors, cols]
                y_r = y[:, first : first + vectors]
                y_i = y[:, first + vectors : first + 2 * vectors]
                sums[2 * o] = sums[2 * o] + fold(x_r * y_r + x_i * y_i)
                sums[2 * o + 1] = sums[2 * o + 1] + fold(x_i * y_r - x_r * y_i)
    for k, total in enumerate(sums):
        sums_ref[k] = total


def part_of(ref, vectors):
    return lambda k: ref[k * vectors : (k + 1) * vectors]


def half_copy(block_ref, wide_ref, margin_hbm, sem, place):
    half = block_ref.shape[0]
    wide_ref[...] = block_ref[...].astype(jnp.float32)
    rows = pl.ds(pl.multiple_of(place * half, half), half)
    copy = pltpu.make_async_copy(wide_ref, margin_hbm.at[0, rows], sem)
    copy.start()
    return copy


def first_contract_kernel(times, split, weight_ref, tau_ref, *refs):
    blocks, (margin_hbm, sums_ref, left_ref, right_ref, wide_ref, sem) = refs[:times], refs[times:]
    me = lax.axis_index("gx") & 1
    copy = half_copy(blocks[0], wide_ref, margin_hbm, sem, me)
    if split:
        vectors = sums_ref.shape[2]
        blocks = [part_of(ref, vectors) for ref in blocks]
        contract(sums_ref, weight_ref, blocks, tau_ref, left_ref, right_ref)
    else:
        sums_ref[...] = jnp.zeros_like(sums_ref)
    copy.wait()


def second_contract_kernel(times, split, weight_ref, tau_ref, *refs):
    kept, other, refs = refs[:times], refs[times : 2 * times], refs[2 * times :]
    first_sums_ref, _, margin_hbm, corr_ref, sums_ref, left_ref, right_ref, wide_ref, sem = refs
    vectors = sums_ref.shape[2]
    half = kept[0].shape[0]
    me = lax.axis_index("gx") & 1
    copy = half_copy(other[0], wide_ref, margin_hbm, sem, 1 - me)
    if split:
        blocks = [part_of(ref, vectors) for ref in other]
    else:
        parts_per_half = half // vectors

        def either(kept_ref, other_ref):
            def part(k):
                row = (k % parts_per_half) * vectors
                own, far = kept_ref[row : row + vectors], other_ref[row : row + vectors]
                mine = (k // parts_per_half == me).astype(jnp.float32)
                return own.astype(jnp.float32) * mine + far.astype(jnp.float32) * (1.0 - mine)

            return part

        blocks = [either(a, b) for a, b in zip(kept, other)]
    contract(sums_ref, weight_ref, blocks, tau_ref, left_ref, right_ref)
    shape = corr_ref.shape[1:]
    row, col = iota(shape, 0), iota(shape, 1)
    result = jnp.zeros(shape, jnp.float32)
    now_ops = sums_ref.shape[0] // 2
    for ref, place in ((first_sums_ref, me), (sums_ref, 1 - me)):
        first = place * now_ops if split else 0
        for k in range(2 * now_ops if split or ref is sums_ref else 0):
            total = jnp.sum(jnp.sum(ref[k], axis=0, keepdims=True), axis=1, keepdims=True)
            here = (row == first + k // 2) & (col == k % 2)
            result = jnp.where(here, total * (1.0 / vectors), result)
    corr_ref[0] = result
    copy.wait()


def vmem_spec():
    return pl.BlockSpec(memory_space=pltpu.VMEM)


def smem_spec():
    return pl.BlockSpec(memory_space=pltpu.SMEM)


def hbm_spec():
    return pl.BlockSpec(memory_space=pltpu.HBM)


def in_hbm(x):
    return pltpu.with_memory_space_constraint(x, pltpu.HBM)


def local_call(body, name, outs, in_specs, out_specs, scratch=(), aliases=None):
    return pl.pallas_call(
        body,
        out_shape=outs,
        in_specs=in_specs,
        out_specs=out_specs,
        scratch_shapes=list(scratch),
        compiler_params=pltpu.CompilerParams(vmem_limit_bytes=VMEM_LIMIT),
        input_output_aliases=aliases or {},
        name=name,
    )


def from_step(block, axis, step):
    count = lax.axis_size(axis)
    return lax.ppermute(block, axis, [((i + step) % count, i) for i in range(count)])


def from_partner(block, axis, step):
    count = lax.axis_size(axis)
    return lax.ppermute(block, axis, [(i ^ step, i) for i in range(count)])


def per_device(eigvecs, links, op_dirs, op_moms, perams, pair_times, slot_counts):
    f32, bf16 = jnp.float32, jnp.bfloat16
    _, cells_x, cells_y, cells_z, colors, _, vectors = eigvecs.shape
    order = cells_z * colors * 2
    lines = cells_x * cells_y
    count_ops = op_dirs.shape[0]
    times, shares, groups = lax.axis_size("ta"), lax.axis_size("gx"), lax.axis_size("gy")
    levels = groups.bit_length() - 1
    own_ops = count_ops // groups
    own_rows = own_ops * 2 * vectors
    field = eigvecs.reshape(cells_x, cells_y, order, vectors)
    link_field = links[0].transpose(0, 1, 3, 5, 6, 4, 2).reshape(lines, 27, 2, cells_z)
    links_x = from_step(link_field[lines - cells_y :], "gx", -1)
    halo_x = from_step(field[cells_x - 1 :], "gx", -1)
    halo_y = from_step(field, "gy", 1)
    inside = local_fields(cells_x, cells_y)
    inputs = [field, link_field, op_dirs, op_moms, wave_constants(cells_z), pair_times]
    inputs = [in_hbm(x) for x in inputs]
    held = [
        pltpu.SMEM(x.shape, x.dtype) if x.dtype == jnp.int32 else pltpu.VMEM(x.shape, x.dtype)
        for x in inputs
    ]
    matrices, local, left, phases, weights = local_call(
        functools.partial(prepare_kernel, cells_x, cells_y),
        "prepare_lines",
        (
            jax.ShapeDtypeStruct((cells_x, order, 128), bf16),
            jax.ShapeDtypeStruct((len(inside), order, vectors), f32),
            jax.ShapeDtypeStruct((2, vectors, lines * order), bf16),
            jax.ShapeDtypeStruct((count_ops, order // 2, 2 * vectors), f32),
            jax.ShapeDtypeStruct((2, times, 8, vectors), f32),
        ),
        [hbm_spec()] * len(inputs) + [smem_spec()],
        (vmem_spec(),) * 5,
        held
        + [
            pltpu.VMEM((lines, LINK_COLS, cells_z), f32),
            pltpu.SemaphoreType.DMA((len(inputs),)),
        ],
    )(*inputs, slot_counts)
    behind, adjoint = local_call(
        functools.partial(behind_kernel, cells_x, cells_y),
        "behind_lines",
        (
            jax.ShapeDtypeStruct((cells_y, order, vectors), f32),
            jax.ShapeDtypeStruct((cells_y, order, 128), bf16),
        ),
        [vmem_spec()] * 2,
        (vmem_spec(),) * 2,
        [pltpu.VMEM((cells_y, LINK_COLS, cells_z), f32)],
    )(links_x, local)
    part = lambda count: jax.ShapeDtypeStruct((count, own_rows, vectors), f32)
    later = count_ops // 2
    swap_a, hold_a, later_sides, later_pairs = local_call(
        functools.partial(first_margin_kernel, cells_x, cells_y, groups, own_ops),
        "first_margins",
        (
            part(groups // 4),
            part(groups // 4),
            jax.ShapeDtypeStruct((later, vectors, lines * order), bf16),
            jax.ShapeDtypeStruct((later, lines * order, 2 * vectors), bf16),
        ),
        [vmem_spec()] * 8 + [hbm_spec()],
        (vmem_spec(),) * 4,
        [
            pltpu.VMEM((7, lines, order, vectors), f32),
            pltpu.VMEM((4, vectors, lines * order), bf16),
            pltpu.SMEM((count_ops,), jnp.int32),
            pltpu.SemaphoreType.DMA,
        ],
    )(matrices, local, left, phases, behind, adjoint, halo_x, halo_y, in_hbm(op_dirs))
    swapped_a = from_partner(swap_a, "gy", 1)
    held_shapes = [part(groups >> (b + 1)) for b in range(2, levels)] + [part(1)]
    swap_b, *held = local_call(
        functools.partial(second_margin_kernel, groups, own_ops),
        "second_margins",
        (part(groups // 4), *held_shapes),
        [vmem_spec()] * 2,
        (vmem_spec(),) * (1 + len(held_shapes)),
    )(later_sides, later_pairs)
    received = [from_partner(swap_b, "gy", 1)]

    def packed(body, name, *inputs, rows=own_rows, lead=(), count=1):
        shape = jax.ShapeDtypeStruct((*lead, rows + TAIL, vectors), jnp.int16)
        outs = shape if count == 1 else (shape,) * count
        specs = vmem_spec() if count == 1 else (vmem_spec(),) * count
        return local_call(body, name, outs, [vmem_spec()] * len(inputs), specs)(*inputs)

    half = own_rows // 2
    for b in range(1, levels):
        inputs = (hold_a, swapped_a) if b == 1 else (held[b - 2], *received)
        if b < levels - 1:
            body = functools.partial(fold_kernel, b, vectors)
            sent = packed(body, "fold_groups", *inputs, lead=inputs[0].shape[:1])
            received.append(from_partner(sent, "gy", 1 << b))
            continue
        body = functools.partial(fold_halves_kernel, vectors)
        away, kept = packed(body, "fold_halves", *inputs, rows=half, count=2)
        away = from_partner(away, "gy", 1 << b)
    body = functools.partial(half_kernel, vectors, False)
    sent = packed(body, "send_half", held[-1], *received, away, rows=half)
    sent, kept = lax.optimization_barrier((sent, kept))
    kept = from_partner(kept, "gy", 1 << (levels - 1))
    arrived = from_partner(sent, "gx", 1)
    body = functools.partial(half_kernel, vectors, True)
    message = packed(body, "keep_half", held[-1], *received, kept, arrived, rows=half)
    norm_factor = 1.0 / math.sqrt(3.0 * cells_x * shares * cells_y * groups * cells_z)
    step = 2
    while step < shares:
        arrived = from_partner(message, "gx", step)
        step *= 2
        if step < shares:
            body = functools.partial(both_kernel, vectors, None)
            message = packed(body, "sum_both", message, arrived, rows=half)
    finished = local_call(
        functools.partial(both_kernel, vectors, norm_factor),
        "finish_half",
        jax.ShapeDtypeStruct((half, vectors), bf16),
        [vmem_spec()] * 2,
        vmem_spec(),
    )(message, arrived)
    kept = [finished] + [from_step(finished, "ta", t) for t in range(1, times)]
    other = [from_partner(block, "gx", 1) for block in kept]
    split = own_ops % 2 == 0
    now_ops = own_ops // 2 if split else own_ops
    sums_shape = (2 * now_ops, 32, vectors)
    scratch = [
        pltpu.VMEM((2 * now_ops * vectors, 2 * vectors), bf16),
        pltpu.VMEM((2 * vectors, 2 * now_ops * vectors), bf16),
    ]
    scratch += [pltpu.VMEM((half, vectors), f32), pltpu.SemaphoreType.DMA]
    margin_shape = jax.ShapeDtypeStruct((1, own_rows, vectors), f32)
    margins, sums = local_call(
        functools.partial(first_contract_kernel, times, split),
        "first_contraction",
        (margin_shape, jax.ShapeDtypeStruct(sums_shape, f32)),
        [vmem_spec()] * (2 + times),
        (hbm_spec(), vmem_spec()),
        scratch,
    )(weights, perams[0], *kept)
    margins, correlators = local_call(
        functools.partial(second_contract_kernel, times, split),
        "second_contraction",
        (margin_shape, jax.ShapeDtypeStruct((1, own_ops, 2), f32)),
        [vmem_spec()] * (3 + 2 * times) + [hbm_spec()],
        (hbm_spec(), vmem_spec()),
        [pltpu.VMEM(sums_shape, f32)] + scratch,
        {3 + 2 * times: 0},
    )(weights, perams[0], *kept, *other, sums, margins)
    return (margins.reshape(1, own_ops, 2, vectors, vectors), correlators)


def solution(mesh):
    placed = (
        P("ta", "gx", "gy", None, None, None, None),
        P("ta", "gx", "gy", None, None, None, None, None),
        P(),
        P(),
        P(("ta", "gx"), None, None, None),
        P(("ta", "gx"), None),
        P(("ta", "gx")),
    )
    return jax.shard_map(
        per_device,
        mesh=mesh,
        in_specs=placed,
        out_specs=(P("ta", "gy", None, None, None), P(("ta", "gx"), "gy", None)),
        check_vma=False,
    )
```

```python
import functools
import math

import jax
import jax.numpy as jnp
import numpy as np
from jax import lax
from jax.experimental import pallas as pl
from jax.experimental.pallas import tpu as pltpu
from jax.sharding import PartitionSpec as P

VMEM_LIMIT = 24 * 1024 * 1024
AXES = ("ta", "gx", "gy")
MOMENTA = 3
LINK_COLS = 54
TAIL = 16
FIXED_BITS = 14.0


def wave_constants(cells_z):
    z_row = np.arange(3 * cells_z) // 3
    columns = []
    for ahead in range(2):
        for momentum in range(MOMENTA):
            angle = 2.0 * math.pi * momentum * ((z_row + ahead) % cells_z) / cells_z
            columns.append(np.cos(angle))
            columns.append(np.sin(angle))
    left = np.stack(columns, axis=1).astype(np.float32)
    terms = []
    for _ in range(3):
        term = left.astype(jnp.bfloat16).astype(np.float32)
        terms.append(term)
        left = left - term
    return jnp.asarray(np.concatenate(terms, axis=1), jnp.bfloat16)


def iota(shape, axis):
    return lax.broadcasted_iota(jnp.int32, shape, axis)


def third(x):
    return (x * 21846) >> 16


def one_hot(condition):
    return condition.astype(jnp.float32).astype(jnp.bfloat16)


def planar_order(order):
    row, col = iota((order, order), 0), iota((order, order), 1)
    half = order // 2
    source = jnp.where(row < half, 2 * row, 2 * (row - half) + 1)
    return one_hot(col == source)


def side_by_side(planar):
    half = planar.shape[0] // 2
    return jnp.concatenate([planar[:half], planar[half:]], axis=1).astype(jnp.bfloat16)


def transport(matrix, pair, sign):
    half, vectors = matrix.shape[0] // 2, pair.shape[1] // 2
    parts = jnp.dot(matrix, pair, preferred_element_type=jnp.float32)
    real, imag = parts[:half], parts[half:]
    if sign > 0:
        return jnp.concatenate(
            [real[:, :vectors] - imag[:, vectors:], real[:, vectors:] + imag[:, :vectors]], axis=0
        )
    return jnp.concatenate(
        [real[:, :vectors] + imag[:, vectors:], real[:, vectors:] - imag[:, :vectors]], axis=0
    )


def halo_fields(cells_x, cells_y):
    pairs = [(0, (cells_x - 1) * cells_y + y) for y in range(cells_y)]
    return pairs + [(1, x * cells_y + cells_y - 1) for x in range(cells_x)]


def local_fields(cells_x, cells_y):
    lines = cells_x * cells_y
    outside = halo_fields(cells_x, cells_y)
    every = [(code, line) for code in range(7) for line in range(lines)]
    return [pair for pair in every if pair not in outside]


def prepare_kernel(cells_x, cells_y, *refs):
    inputs, live_ref, refs = refs[:6], refs[6], refs[7:]
    edge_ref, matrix_ref, local_ref, left_ref, phase_ref, weight_ref = refs[:6]
    held, link_rows_ref, sems = refs[6:12], refs[12], refs[13]
    copies = [
        pltpu.make_async_copy(src, dst, sems.at[k])
        for k, (src, dst) in enumerate(zip(inputs, held))
    ]
    for copy in copies:
        copy.start()
    v_ref, link_ref, dirs_ref, moms_ref, waves_ref, pair_ref = held
    f32, bf16 = jnp.float32, jnp.bfloat16
    order, vectors = v_ref.shape[2], v_ref.shape[3]
    half, cells_z = order // 2, order // 6
    lines = cells_x * cells_y
    times = weight_ref.shape[1]
    spread = one_hot(third(iota((half, cells_z), 0)) == iota((half, cells_z), 1))
    row, col = iota((half, LINK_COLS), 0), iota((half, LINK_COLS), 1)
    row_color = row - 3 * third(row)
    pair_at = third(col >> 1)
    col_in, col_out = (col >> 1) - 3 * pair_at, pair_at - 3 * third(pair_at)
    pick = [(row_color == col_out).astype(f32), (row_color == col_in).astype(f32)]
    wide = (LINK_COLS, 6 * 128)
    row, col = iota(wide, 0), iota(wide, 1)
    block, place = col >> 7, col & 127
    color = place - 3 * third(place)
    pair_at = third(row >> 1)
    row_in, row_out = (row >> 1) - 3 * pair_at, pair_at - 3 * third(pair_at)
    fits = 2 * third(pair_at) + (row & 1) == block
    expand = [one_hot(fits & (row_in == color)), one_hot(fits & (row_out == color))]
    row, col = iota((half, 128), 0), iota((half, 128), 1)
    near = ((third(row) == third(col)) & (col < half)).astype(f32)
    planar = planar_order(order)
    for copy in copies:
        copy.wait()
    edge_ref[...] = v_ref[:, 0:1]
    for t in range(times):
        sink = (pair_ref[0, 0] == t) & (live_ref[0] > 0)
        source = pair_ref[0, 1] == t
        weight_ref[0, t] = jnp.full(weight_ref.shape[2:], jnp.where(sink, 1.0, 0.0), f32)
        weight_ref[1, t] = jnp.full(weight_ref.shape[2:], jnp.where(source, 1.0, 0.0), f32)
    for line in range(lines):
        for k in range(LINK_COLS // 2):
            link_rows_ref[line, 2 * k : 2 * k + 2] = link_ref[line, k].astype(f32)
    outside = halo_fields(cells_x, cells_y)
    inside = local_fields(cells_x, cells_y)
    ordered = []
    for line in range(lines):
        here = jnp.dot(
            planar, v_ref[line // cells_y, line % cells_y], preferred_element_type=f32
        )
        ordered.append(here)
        local_ref[inside.index((6, line))] = here
    for line in range(lines):
        here = ordered[line]
        ahead_z = jnp.concatenate(
            [here[3:half], here[:3], here[half + 3 :], here[half : half + 3]], axis=0
        )
        columns = slice(line * order, (line + 1) * order)
        left_ref[0, :, columns] = here.T.astype(bf16)
        left_ref[1, :, columns] = ahead_z.T.astype(bf16)
        seen = lax.dot_general(
            spread,
            link_rows_ref[line].astype(bf16),
            (((1,), (1,)), ((), ())),
            preferred_element_type=f32,
        )
        pair = side_by_side(here)
        for way in range(2):
            blocks = jnp.dot(
                (seen * pick[way]).astype(bf16), expand[way], preferred_element_type=f32
            )
            for d in range(3):
                matrix = jnp.concatenate(
                    [
                        blocks[:, 256 * d : 256 * d + 128] * near,
                        blocks[:, 256 * d + 128 : 256 * d + 256] * near,
                    ],
                    axis=0,
                ).astype(bf16)
                if way == 1:
                    carried = transport(matrix[:, :half], pair, -1)
                    local_ref[inside.index((3 + d, line))] = carried.astype(bf16).astype(f32)
                elif (d, line) in outside:
                    matrix_ref[outside.index((d, line))] = matrix
                else:
                    ahead = ahead_z if d == 2 else ordered[line + (cells_y if d == 0 else 1)]
                    local_ref[inside.index((d, line))] = transport(
                        matrix[:, :half], side_by_side(ahead), 1
                    )
    wave_cols = waves_ref.shape[1]
    per_term = wave_cols // 3
    row, col = iota((wave_cols, 2 * vectors), 0), iota((wave_cols, 2 * vectors), 1)
    term = (row >= per_term).astype(jnp.int32) + (row >= 2 * per_term).astype(jnp.int32)
    wave_at = row - per_term * term - (col >= vectors).astype(jnp.int32)
    for o in range(phase_ref.shape[0]):
        column = 2 * (jnp.where(dirs_ref[o] == 5, MOMENTA, 0) + moms_ref[o])
        phase_ref[o] = jnp.dot(
            waves_ref[...], one_hot(wave_at == column), preferred_element_type=f32
        )


def put_product(out_ref, place, core, i, side, pair):
    vectors = pair.shape[1] // 2
    product = jnp.dot(side, pair, preferred_element_type=jnp.float32)
    own_ops = out_ref.shape[1] // (4 * vectors)
    for part in range(2):
        flat = 2 * i + part
        block = (flat // own_ops) * 2 * own_ops + core * own_ops + flat % own_ops
        out_ref[place, block * vectors : (block + 1) * vectors] = product[
            :, part * vectors : (part + 1) * vectors
        ]


def operators(pairs, own_ops, odd):
    mine = lax.axis_index("gy") >> 1
    for j in range(1 if odd else 0, pairs, 2):
        for core in range(2):
            for i in range(own_ops):
                yield j >> 1, core, i, (mine ^ j) * 2 * own_ops + core * own_ops + i


def first_margin_kernel(cells_x, cells_y, pairs, own_ops, *refs):
    matrix_ref, local_ref, left_ref, phase_ref, halo_x_ref, halo_y_ref, dirs_hbm = refs[:7]
    out_ref, later_side_ref, later_pair_ref = refs[7:10]
    field_ref, side_ref, dirs_ref, sem = refs[10:]
    f32, bf16 = jnp.float32, jnp.bfloat16
    copy = pltpu.make_async_copy(dirs_hbm, dirs_ref, sem)
    copy.start()
    lines = cells_x * cells_y
    order, vectors = halo_x_ref.shape[2], halo_x_ref.shape[3]
    half = order // 2
    planar = planar_order(order)
    side_ref[0] = left_ref[0]
    side_ref[3] = left_ref[1]
    outside = halo_fields(cells_x, cells_y)
    for d in range(2):
        for line in range(lines):
            x, y = line // cells_y, line % cells_y
            columns = slice(line * order, (line + 1) * order)
            if (d, line) not in outside:
                ahead = line + (cells_y if d == 0 else 1)
                side_ref[1 + d, :, columns] = left_ref[0, :, ahead * order : (ahead + 1) * order]
                continue
            halo = halo_x_ref[0, y] if d == 0 else halo_y_ref[x, 0]
            ahead = jnp.dot(planar, halo, preferred_element_type=f32)
            side_ref[1 + d, :, columns] = ahead.T.astype(bf16)
            matrix = matrix_ref[outside.index((d, line))]
            field_ref[d, line] = transport(matrix[:, :half], side_by_side(ahead), 1)
    for k, (code, line) in enumerate(local_fields(cells_x, cells_y)):
        field_ref[code, line] = local_ref[k]
    copy.wait()

    def factors(o):
        code = dirs_ref[o]
        side = jnp.where((code >= 3) & (code < 6), code - 2, 0)
        cosine = phase_ref[o, :, 0:vectors]
        sine = phase_ref[o, :, vectors : 2 * vectors]
        rows = []
        for line in range(lines):
            real, imag = field_ref[code, line, 0:half], field_ref[code, line, half:order]
            turned_r, turned_i = cosine * real - sine * imag, sine * real + cosine * imag
            rows.append(jnp.concatenate([turned_r, turned_i], axis=1))
            rows.append(jnp.concatenate([turned_i, -turned_r], axis=1))
        return side_ref[side], jnp.concatenate(rows, axis=0).astype(bf16)

    for place, core, i, o in operators(pairs, own_ops, True):
        put_product(out_ref, place, core, i, *factors(o))
    for k, (_, _, _, o) in enumerate(operators(pairs, own_ops, False)):
        later_side_ref[k], later_pair_ref[k] = factors(o)


def second_margin_kernel(pairs, own_ops, side_ref, pair_ref, out_ref):
    for k, (place, core, i, _) in enumerate(operators(pairs, own_ops, False)):
        put_product(out_ref, place, core, i, side_ref[k], pair_ref[k])


def scale_of(block):
    top = jnp.max(jnp.abs(block), axis=0, keepdims=True)
    return jnp.floor(jnp.log2(jnp.maximum(top, 1e-30))) + 1.0


def put_fixed(out_ref, blocks):
    rows, vectors = blocks[0].shape
    tail = iota((TAIL, vectors), 0)
    scales = jnp.zeros((TAIL, vectors), jnp.float32)
    for k, block in enumerate(blocks):
        scale = scale_of(block)
        scales = jnp.where(tail == k, scale, scales)
        fixed = jnp.floor(block * jnp.exp2(FIXED_BITS - scale) + 0.5)
        out_ref[k * rows : (k + 1) * rows] = fixed.astype(jnp.int32).astype(jnp.int16)
    out_ref[len(blocks) * rows :] = scales.astype(jnp.int32).astype(jnp.int16)


def from_fixed(ref, rows, k):
    scales = ref[ref.shape[0] - TAIL :].astype(jnp.int32).astype(jnp.float32)
    block = ref[k * rows : (k + 1) * rows].astype(jnp.int32).astype(jnp.float32)
    return block * jnp.exp2(scales[k : k + 1] - FIXED_BITS)


def group_block(bases, messages, j, start, rows):
    total = bases[0][j >> 1, pl.ds(start, rows)] + bases[1][j >> 1, pl.ds(start, rows)]
    for b, ref in enumerate(messages):
        total = total + fixed_at(ref.at[j >> (b + 1)], start, rows)
    return total


def fixed_at(ref, start, rows):
    tail = ref[ref.shape[0] - TAIL :].astype(jnp.int32).astype(jnp.float32)
    scale = jnp.max(
        jnp.where(iota(tail.shape, 0) == start // rows, tail, -1000.0), axis=0, keepdims=True
    )
    block = ref[pl.ds(start, rows)].astype(jnp.int32).astype(jnp.float32)
    return block * jnp.exp2(scale - FIXED_BITS)


def fold_kernel(level, vectors, own_ref, other_ref, *refs):
    messages, out_ref = refs[:-1], refs[-1]
    for k in range(out_ref.shape[0]):
        blocks = [
            group_block((own_ref, other_ref), messages, (2 * k + 1) << level, start, vectors)
            for start in range(0, own_ref.shape[1], vectors)
        ]
        put_fixed(out_ref.at[k], blocks)


def half_rows(half, vectors, kept):
    me = lax.axis_index("gx") & 1
    base = pl.multiple_of((me if kept else 1 - me) * half, half)
    return [base + step for step in range(0, half, vectors)]


def fold_halves_kernel(level, vectors, own_ref, other_ref, *refs):
    messages, outs = refs[:-2], refs[-2:]
    for kept, out_ref in enumerate(outs):
        starts = half_rows(own_ref.shape[1] // 2, vectors, kept)
        bases = (own_ref, other_ref)
        put_fixed(out_ref, [group_block(bases, messages, 1 << level, s, vectors) for s in starts])


def half_kernel(levels, vectors, kept, own_ref, other_ref, *refs):
    messages, last, out_ref = refs[: levels - 1], refs[levels - 1 : -1], refs[-1]
    blocks = []
    for p, start in enumerate(half_rows(own_ref.shape[1] // 2, vectors, kept)):
        total = group_block((own_ref, other_ref), messages, 0, start, vectors)
        for ref in last:
            total = total + from_fixed(ref, vectors, p)
        blocks.append(total)
    put_fixed(out_ref, blocks)


def both_kernel(vectors, norm_factor, own_ref, arrived_ref, out_ref):
    blocks = [
        from_fixed(own_ref, vectors, p) + from_fixed(arrived_ref, vectors, p)
        for p in range((own_ref.shape[0] - TAIL) // vectors)
    ]
    if norm_factor is None:
        put_fixed(out_ref, blocks)
        return
    for p, block in enumerate(blocks):
        out_ref[p * vectors : (p + 1) * vectors] = (block * norm_factor).astype(out_ref.dtype)


def contract(sums_ref, weight_ref, blocks, tau_ref, left_ref, right_ref):
    f32, bf16 = jnp.float32, jnp.bfloat16
    vectors = sums_ref.shape[2]
    count_ops = sums_ref.shape[0] // 2
    order = tau_ref.shape[2]
    spins = order // vectors
    me_t = lax.axis_index("ta")
    times = len(blocks)

    def chosen(end, k):
        total = jnp.zeros((vectors // 8, 8, vectors), f32)
        for t in range(times):
            weight = weight_ref[end, lax.rem(me_t + t, times)]
            total = total + blocks[t](k).astype(f32).reshape(total.shape) * weight
        return total.reshape(vectors, vectors)

    for o in range(count_ops):
        first = 2 * o * vectors
        a_r, a_i = chosen(0, 2 * o).astype(bf16), chosen(0, 2 * o + 1).astype(bf16)
        b_r, b_i = chosen(1, 2 * o).T.astype(bf16), chosen(1, 2 * o + 1).T.astype(bf16)
        real, imag = slice(first, first + vectors), slice(first + vectors, first + 2 * vectors)
        left_ref[real, 0:vectors] = a_r
        left_ref[real, vectors:] = -a_i
        left_ref[imag, 0:vectors] = a_i
        left_ref[imag, vectors:] = a_r
        right_ref[0:vectors, real] = b_r
        right_ref[0:vectors, imag] = -b_i
        right_ref[vectors:, real] = b_i
        right_ref[vectors:, imag] = b_r
    lanes = sums_ref.shape[1]
    fold = lambda t: jnp.sum(t.reshape(vectors // lanes, lanes, vectors), axis=0)
    sums = [jnp.zeros((lanes, vectors), f32) for _ in range(2 * count_ops)]
    for s in range(spins):
        rows = slice(s * vectors, (s + 1) * vectors)
        x = jnp.dot(
            left_ref[...],
            jnp.concatenate([tau_ref[0, rows], tau_ref[1, rows]], axis=0),
            preferred_element_type=f32,
        )
        for c in range(spins):
            cols = slice(c * vectors, (c + 1) * vectors)
            y = jnp.dot(
                jnp.concatenate([tau_ref[0, rows, cols], tau_ref[1, rows, cols]], axis=1),
                right_ref[...],
                preferred_element_type=f32,
            )
            for o in range(count_ops):
                first = 2 * o * vectors
                x_r = x[first : first + vectors, cols]
                x_i = x[first + vectors : first + 2 * vectors, cols]
                y_r = y[:, first : first + vectors]
                y_i = y[:, first + vectors : first + 2 * vectors]
                sums[2 * o] = sums[2 * o] + fold(x_r * y_r + x_i * y_i)
                sums[2 * o + 1] = sums[2 * o + 1] + fold(x_i * y_r - x_r * y_i)
    for k, total in enumerate(sums):
        sums_ref[k] = total


def hand_kernel(*refs):
    blocks, out_ref = refs[:-1], refs[-1]
    rows = blocks[0].shape[0] // 2
    for t, ref in enumerate(blocks):
        out_ref[t * rows : (t + 1) * rows] = ref[:rows]


def own_part(handed_ref, carried_ref, t, vectors):
    rows = carried_ref.shape[0] // 2
    second = (lax.axis_index("gy") & 1).astype(jnp.float32)

    def part(k):
        first = handed_ref[t * rows + k * vectors : t * rows + (k + 1) * vectors]
        mine = carried_ref[rows + k * vectors : rows + (k + 1) * vectors]
        return first.astype(jnp.float32) * (1.0 - second) + mine.astype(jnp.float32) * second

    return part


def first_contract_kernel(times, weight_ref, tau_ref, handed_ref, *refs):
    carried, (sums_ref, left_ref, right_ref) = refs[:times], refs[times:]
    vectors = sums_ref.shape[2]
    blocks = [own_part(handed_ref, ref, t, vectors) for t, ref in enumerate(carried)]
    contract(sums_ref, weight_ref, blocks, tau_ref, left_ref, right_ref)


def second_contract_kernel(times, split, weight_ref, tau_ref, *refs):
    handed, refs = refs[:2], refs[2:]
    kept, other, refs = refs[:times], refs[times : 2 * times], refs[2 * times :]
    if split:
        first_sums_ref, refs = refs[0], refs[1:]
    margin_ref, corr_ref, sums_ref, left_ref, right_ref = refs
    vectors = sums_ref.shape[2]
    half = kept[0].shape[0] // 2
    me = lax.axis_index("gx") & 1
    kept = [own_part(handed[0], ref, t, vectors) for t, ref in enumerate(kept)]
    other = [own_part(handed[1], ref, t, vectors) for t, ref in enumerate(other)]
    count_parts = half // vectors
    for place, part in ((me, kept[0]), (1 - me, other[0])):
        for k in range(count_parts):
            start = pl.multiple_of(place * half + k * vectors, vectors)
            margin_ref[0, pl.ds(start, vectors)] = part(k)

    def either(kept_part, other_part):
        def part(k):
            mine = (k // count_parts == me).astype(jnp.float32)
            k = k % count_parts
            return kept_part(k) * mine + other_part(k) * (1.0 - mine)

        return part

    blocks = other if split else [either(a, b) for a, b in zip(kept, other)]
    contract(sums_ref, weight_ref, blocks, tau_ref, left_ref, right_ref)
    now_ops = sums_ref.shape[0] // 2
    known = [(sums_ref, (1 - me) * now_ops)] if split else [(sums_ref, 0)]
    if split:
        known.append((first_sums_ref, me * now_ops))
    shape = corr_ref.shape[1:]
    row, col = iota(shape, 0), iota(shape, 1)
    result = jnp.zeros(shape, jnp.float32)
    for ref, first in known:
        for k in range(2 * now_ops):
            total = jnp.sum(jnp.sum(ref[k], axis=0, keepdims=True), axis=1, keepdims=True)
            here = (row == first + k // 2) & (col == k % 2)
            result = jnp.where(here, total * (1.0 / vectors), result)
    corr_ref[0] = result


def vmem_spec():
    return pl.BlockSpec(memory_space=pltpu.VMEM)


def smem_spec():
    return pl.BlockSpec(memory_space=pltpu.SMEM)


def hbm_spec():
    return pl.BlockSpec(memory_space=pltpu.HBM)


def in_hbm(x):
    return pltpu.with_memory_space_constraint(x, pltpu.HBM)


def local_call(body, name, outs, in_specs, out_specs, scratch=(), cost=None):
    return pl.pallas_call(
        body,
        out_shape=outs,
        in_specs=in_specs,
        out_specs=out_specs,
        scratch_shapes=list(scratch),
        compiler_params=pltpu.CompilerParams(vmem_limit_bytes=VMEM_LIMIT),
        cost_estimate=cost,
        name=name,
    )


def from_step(block, axis, step):
    count = lax.axis_size(axis)
    return lax.ppermute(block, axis, [((i + step) % count, i) for i in range(count)])


def moved(block, place):
    sizes = [lax.axis_size(axis) for axis in AXES]
    flat = lambda t, x, y: (t * sizes[1] + x) * sizes[2] + y
    perm = []
    for member in np.ndindex(*sizes):
        target = place(*member)
        if target is not None:
            perm.append((flat(*member), flat(*target)))
    return lax.ppermute(block, AXES, perm)


def to_carrier(block):
    return moved(block, lambda t, x, y: None if y & 1 else (t, x, y + 1))


def from_carrier(block):
    return moved(block, lambda t, x, y: (t, x, y - 1) if y & 1 else None)


def between(block, t_step=0, x_bits=0, y_bits=0):
    times = lax.axis_size("ta")
    target = lambda t, x, y: ((t + t_step) % times, x ^ x_bits, y ^ y_bits)
    return moved(block, lambda t, x, y: target(t, x, y) if y & 1 else None)


def per_device(eigvecs, links, op_dirs, op_moms, perams, pair_times, slot_counts):
    f32, bf16 = jnp.float32, jnp.bfloat16
    _, cells_x, cells_y, cells_z, colors, _, vectors = eigvecs.shape
    order = cells_z * colors * 2
    lines = cells_x * cells_y
    count_ops = op_dirs.shape[0]
    times, shares, groups = lax.axis_size("ta"), lax.axis_size("gx"), lax.axis_size("gy")
    pairs = groups // 2
    levels = pairs.bit_length() - 1
    own_ops = count_ops // groups
    own_rows = own_ops * 2 * vectors
    field = eigvecs.reshape(cells_x, cells_y, order, vectors)
    halo_x = from_step(field[0:1], "gx", 1)
    link_field = links[0].transpose(0, 1, 3, 5, 6, 4, 2).reshape(lines, 27, 2, cells_z)
    outside, inside = halo_fields(cells_x, cells_y), local_fields(cells_x, cells_y)
    inputs = [field, link_field, op_dirs, op_moms, wave_constants(cells_z), pair_times]
    inputs = [in_hbm(x) for x in inputs]
    held = [
        pltpu.SMEM(x.shape, x.dtype) if x.dtype == jnp.int32 else pltpu.VMEM(x.shape, x.dtype)
        for x in inputs
    ]
    edge, matrices, local, left, phases, weights = local_call(
        functools.partial(prepare_kernel, cells_x, cells_y),
        "prepare_lines",
        (
            jax.ShapeDtypeStruct((cells_x, 1, order, vectors), bf16),
            jax.ShapeDtypeStruct((len(outside), order, 128), bf16),
            jax.ShapeDtypeStruct((len(inside), order, vectors), f32),
            jax.ShapeDtypeStruct((2, vectors, lines * order), bf16),
            jax.ShapeDtypeStruct((count_ops, order // 2, 2 * vectors), f32),
            jax.ShapeDtypeStruct((2, times, 8, vectors), f32),
        ),
        [hbm_spec()] * len(inputs) + [smem_spec()],
        (vmem_spec(),) * 6,
        held
        + [
            pltpu.VMEM((lines, LINK_COLS, cells_z), f32),
            pltpu.SemaphoreType.DMA((len(inputs),)),
        ],
    )(*inputs, slot_counts)
    halo_y = from_step(edge, "gy", 1)
    pair_rows = 2 * own_rows
    part = jax.ShapeDtypeStruct((pairs // 2, pair_rows, vectors), f32)
    later = count_ops // 2
    part_a, later_sides, later_pairs = local_call(
        functools.partial(first_margin_kernel, cells_x, cells_y, pairs, own_ops),
        "first_margins",
        (
            part,
            jax.ShapeDtypeStruct((later, vectors, lines * order), bf16),
            jax.ShapeDtypeStruct((later, lines * order, 2 * vectors), bf16),
        ),
        [vmem_spec()] * 6 + [hbm_spec()],
        (vmem_spec(),) * 3,
        [
            pltpu.VMEM((7, lines, order, vectors), f32),
            pltpu.VMEM((4, vectors, lines * order), bf16),
            pltpu.SMEM((count_ops,), jnp.int32),
            pltpu.SemaphoreType.DMA,
        ],
    )(matrices, local, left, phases, halo_x, halo_y, in_hbm(op_dirs))
    bases_a = (part_a, to_carrier(part_a))
    part_b = local_call(
        functools.partial(second_margin_kernel, pairs, own_ops),
        "second_margins",
        part,
        [vmem_spec()] * 2,
        vmem_spec(),
    )(later_sides, later_pairs)
    bases_b = (part_b, to_carrier(part_b))

    def packed(body, name, *inputs, rows=pair_rows, lead=(), count=1):
        shape = jax.ShapeDtypeStruct((*lead, rows + TAIL, vectors), jnp.int16)
        outs = shape if count == 1 else (shape,) * count
        specs = vmem_spec() if count == 1 else (vmem_spec(),) * count
        return local_call(body, name, outs, [vmem_spec()] * len(inputs), specs)(*inputs)

    half = pair_rows // 2
    messages = []
    for b in range(levels):
        inputs = bases_b + tuple(messages) if b else bases_a
        if b < levels - 1:
            body = functools.partial(fold_kernel, b, vectors)
            sent = packed(body, "fold_pairs", *inputs, lead=(pairs >> (b + 1),))
            messages.append(between(sent, y_bits=2 << b))
            continue
        body = functools.partial(fold_halves_kernel, b, vectors)
        away, kept = packed(body, "fold_halves", *inputs, rows=half, count=2)
        away, kept = between(away, y_bits=2 << b), between(kept, y_bits=2 << b)
    body = functools.partial(half_kernel, levels, vectors, False)
    sent = packed(body, "send_half", *bases_b, *messages, away, rows=half)
    arrived = between(sent, x_bits=1)
    body = functools.partial(half_kernel, levels, vectors, True)
    message = packed(body, "keep_half", *bases_b, *messages, kept, arrived, rows=half)
    norm_factor = 1.0 / math.sqrt(3.0 * cells_x * shares * cells_y * groups * cells_z)
    step = 2
    while step < shares:
        arrived = between(message, x_bits=step)
        step *= 2
        if step < shares:
            body = functools.partial(both_kernel, vectors, None)
            message = packed(body, "sum_both", message, arrived, rows=half)
    finished = local_call(
        functools.partial(both_kernel, vectors, norm_factor),
        "finish_half",
        jax.ShapeDtypeStruct((half, vectors), bf16),
        [vmem_spec()] * 2,
        vmem_spec(),
    )(message, arrived)
    kept = [finished] + [between(finished, t_step=-t) for t in range(1, times)]
    other = [between(block, x_bits=1) for block in kept]

    def handed(blocks, name):
        shape = jax.ShapeDtypeStruct((times * half // 2, vectors), bf16)
        specs = [vmem_spec()] * times
        return from_carrier(local_call(hand_kernel, name, shape, specs, vmem_spec())(*blocks))

    hands = [handed(kept, "hand_kept"), handed(other, "hand_other")]
    split = own_ops % 2 == 0
    now_ops = own_ops // 2 if split else own_ops
    sums_shape = (2 * now_ops, 32, vectors)
    scratch = [
        pltpu.VMEM((2 * now_ops * vectors, 2 * vectors), bf16),
        pltpu.VMEM((2 * vectors, 2 * now_ops * vectors), bf16),
    ]
    sums = []
    if split:
        sums = [
            local_call(
                functools.partial(first_contract_kernel, times),
                "first_contraction",
                jax.ShapeDtypeStruct(sums_shape, f32),
                [vmem_spec()] * (3 + times),
                vmem_spec(),
                scratch,
            )(weights, perams[0], hands[0], *kept)
        ]
    margins, correlators = local_call(
        functools.partial(second_contract_kernel, times, split),
        "second_contraction",
        (
            jax.ShapeDtypeStruct((1, own_rows, vectors), f32),
            jax.ShapeDtypeStruct((1, own_ops, 2), f32),
        ),
        [vmem_spec()] * (4 + 2 * times + len(sums)),
        (vmem_spec(), vmem_spec()),
        [pltpu.VMEM(sums_shape, f32)] + scratch,
    )(weights, perams[0], *hands, *kept, *other, *sums)
    return (margins.reshape(1, own_ops, 2, vectors, vectors), correlators)


def solution(mesh):
    placed = (
        P("ta", "gx", "gy", None, None, None, None),
        P("ta", "gx", "gy", None, None, None, None, None),
        P(),
        P(),
        P(("ta", "gx"), None, None, None),
        P(("ta", "gx"), None),
        P(("ta", "gx")),
    )
    return jax.shard_map(
        per_device,
        mesh=mesh,
        in_specs=placed,
        out_specs=(P("ta", "gy", None, None, None), P(("ta", "gx"), "gy", None)),
        check_vma=False,
    )
```

```python
import functools
import math

import jax
import jax.numpy as jnp
import numpy as np
from jax import lax
from jax.experimental import pallas as pl
from jax.experimental.pallas import tpu as pltpu
from jax.sharding import PartitionSpec as P

VMEM_LIMIT = 24 * 1024 * 1024
AXES = ("ta", "gx", "gy")
MOMENTA = 3
LINK_COLS = 54
TAIL = 16
FIXED_BITS = 14.0


def wave_constants(cells_z):
    z_row = np.arange(3 * cells_z) // 3
    columns = []
    for ahead in range(2):
        for momentum in range(MOMENTA):
            angle = 2.0 * math.pi * momentum * ((z_row + ahead) % cells_z) / cells_z
            columns.append(np.cos(angle))
            columns.append(np.sin(angle))
    left = np.stack(columns, axis=1).astype(np.float32)
    terms = []
    for _ in range(3):
        term = left.astype(jnp.bfloat16).astype(np.float32)
        terms.append(term)
        left = left - term
    return jnp.asarray(np.concatenate(terms, axis=1), jnp.bfloat16)


def iota(shape, axis):
    return lax.broadcasted_iota(jnp.int32, shape, axis)


def third(x):
    return (x * 21846) >> 16


def one_hot(condition):
    return condition.astype(jnp.float32).astype(jnp.bfloat16)


def planar_order(order):
    row, col = iota((order, order), 0), iota((order, order), 1)
    half = order // 2
    source = jnp.where(row < half, 2 * row, 2 * (row - half) + 1)
    return one_hot(col == source)


def side_by_side(planar):
    half = planar.shape[0] // 2
    return jnp.concatenate([planar[:half], planar[half:]], axis=1).astype(jnp.bfloat16)


def transport(matrix, pair, sign):
    half, vectors = matrix.shape[0] // 2, pair.shape[1] // 2
    parts = jnp.dot(matrix, pair, preferred_element_type=jnp.float32)
    real, imag = parts[:half], parts[half:]
    if sign > 0:
        return jnp.concatenate(
            [real[:, :vectors] - imag[:, vectors:], real[:, vectors:] + imag[:, :vectors]], axis=0
        )
    return jnp.concatenate(
        [real[:, :vectors] + imag[:, vectors:], real[:, vectors:] - imag[:, :vectors]], axis=0
    )


def halo_fields(cells_x, cells_y):
    pairs = [(0, (cells_x - 1) * cells_y + y) for y in range(cells_y)]
    return pairs + [(1, x * cells_y + cells_y - 1) for x in range(cells_x)]


def local_fields(cells_x, cells_y):
    lines = cells_x * cells_y
    outside = halo_fields(cells_x, cells_y)
    every = [(code, line) for code in range(7) for line in range(lines)]
    return [pair for pair in every if pair not in outside]


def prepare_kernel(cells_x, cells_y, *refs):
    inputs, live_ref, refs = refs[:6], refs[6], refs[7:]
    edge_ref, matrix_ref, local_ref, left_ref, phase_ref, weight_ref = refs[:6]
    held, link_rows_ref, sems = refs[6:12], refs[12], refs[13]
    copies = [
        pltpu.make_async_copy(src, dst, sems.at[k])
        for k, (src, dst) in enumerate(zip(inputs, held))
    ]
    for copy in copies:
        copy.start()
    v_ref, link_ref, dirs_ref, moms_ref, waves_ref, pair_ref = held
    f32, bf16 = jnp.float32, jnp.bfloat16
    order, vectors = v_ref.shape[2], v_ref.shape[3]
    half, cells_z = order // 2, order // 6
    lines = cells_x * cells_y
    times = weight_ref.shape[1]
    spread = one_hot(third(iota((half, cells_z), 0)) == iota((half, cells_z), 1))
    row, col = iota((half, LINK_COLS), 0), iota((half, LINK_COLS), 1)
    row_color = row - 3 * third(row)
    pair_at = third(col >> 1)
    col_in, col_out = (col >> 1) - 3 * pair_at, pair_at - 3 * third(pair_at)
    pick = [(row_color == col_out).astype(f32), (row_color == col_in).astype(f32)]
    wide = (LINK_COLS, 6 * 128)
    row, col = iota(wide, 0), iota(wide, 1)
    block, place = col >> 7, col & 127
    color = place - 3 * third(place)
    pair_at = third(row >> 1)
    row_in, row_out = (row >> 1) - 3 * pair_at, pair_at - 3 * third(pair_at)
    fits = 2 * third(pair_at) + (row & 1) == block
    expand = [one_hot(fits & (row_in == color)), one_hot(fits & (row_out == color))]
    row, col = iota((half, 128), 0), iota((half, 128), 1)
    near = ((third(row) == third(col)) & (col < half)).astype(f32)
    planar = planar_order(order)
    for copy in copies:
        copy.wait()
    edge_ref[...] = v_ref[:, 0:1]
    for t in range(times):
        sink = (pair_ref[0, 0] == t) & (live_ref[0] > 0)
        source = pair_ref[0, 1] == t
        weight_ref[0, t] = jnp.full(weight_ref.shape[2:], jnp.where(sink, 1.0, 0.0), f32)
        weight_ref[1, t] = jnp.full(weight_ref.shape[2:], jnp.where(source, 1.0, 0.0), f32)
    for line in range(lines):
        for k in range(LINK_COLS // 2):
            link_rows_ref[line, 2 * k : 2 * k + 2] = link_ref[line, k].astype(f32)
    outside = halo_fields(cells_x, cells_y)
    inside = local_fields(cells_x, cells_y)
    ordered = []
    for line in range(lines):
        here = jnp.dot(
            planar, v_ref[line // cells_y, line % cells_y], preferred_element_type=f32
        )
        ordered.append(here)
        local_ref[inside.index((6, line))] = here
    for line in range(lines):
        here = ordered[line]
        ahead_z = jnp.concatenate(
            [here[3:half], here[:3], here[half + 3 :], here[half : half + 3]], axis=0
        )
        columns = slice(line * order, (line + 1) * order)
        left_ref[0, :, columns] = here.T.astype(bf16)
        left_ref[1, :, columns] = ahead_z.T.astype(bf16)
        seen = lax.dot_general(
            spread,
            link_rows_ref[line].astype(bf16),
            (((1,), (1,)), ((), ())),
            preferred_element_type=f32,
        )
        pair = side_by_side(here)
        for way in range(2):
            blocks = jnp.dot(
                (seen * pick[way]).astype(bf16), expand[way], preferred_element_type=f32
            )
            for d in range(3):
                matrix = jnp.concatenate(
                    [
                        blocks[:, 256 * d : 256 * d + 128] * near,
                        blocks[:, 256 * d + 128 : 256 * d + 256] * near,
                    ],
                    axis=0,
                ).astype(bf16)
                if way == 1:
                    carried = transport(matrix[:, :half], pair, -1)
                    local_ref[inside.index((3 + d, line))] = carried.astype(bf16).astype(f32)
                elif (d, line) in outside:
                    matrix_ref[outside.index((d, line))] = matrix
                else:
                    ahead = ahead_z if d == 2 else ordered[line + (cells_y if d == 0 else 1)]
                    local_ref[inside.index((d, line))] = transport(
                        matrix[:, :half], side_by_side(ahead), 1
                    )
    wave_cols = waves_ref.shape[1]
    per_term = wave_cols // 3
    row, col = iota((wave_cols, 2 * vectors), 0), iota((wave_cols, 2 * vectors), 1)
    term = (row >= per_term).astype(jnp.int32) + (row >= 2 * per_term).astype(jnp.int32)
    wave_at = row - per_term * term - (col >= vectors).astype(jnp.int32)
    for o in range(phase_ref.shape[0]):
        column = 2 * (jnp.where(dirs_ref[o] == 5, MOMENTA, 0) + moms_ref[o])
        phase_ref[o] = jnp.dot(
            waves_ref[...], one_hot(wave_at == column), preferred_element_type=f32
        )


def put_product(out_ref, place, core, i, side, pair):
    vectors = pair.shape[1] // 2
    product = jnp.dot(side, pair, preferred_element_type=jnp.float32)
    own_ops = out_ref.shape[1] // (4 * vectors)
    for part in range(2):
        flat = 2 * i + part
        block = (flat // own_ops) * 2 * own_ops + core * own_ops + flat % own_ops
        out_ref[place, block * vectors : (block + 1) * vectors] = product[
            :, part * vectors : (part + 1) * vectors
        ]


def operators(pairs, own_ops, odd):
    mine = lax.axis_index("gy") >> 1
    for j in range(1 if odd else 0, pairs, 2):
        for core in range(2):
            for i in range(own_ops):
                yield j >> 1, core, i, (mine ^ j) * 2 * own_ops + core * own_ops + i


def first_margin_kernel(cells_x, cells_y, pairs, own_ops, *refs):
    matrix_ref, local_ref, left_ref, phase_ref, halo_x_ref, halo_y_ref, dirs_hbm = refs[:7]
    out_ref, later_side_ref, later_pair_ref = refs[7:10]
    field_ref, side_ref, dirs_ref, sem = refs[10:]
    f32, bf16 = jnp.float32, jnp.bfloat16
    copy = pltpu.make_async_copy(dirs_hbm, dirs_ref, sem)
    copy.start()
    lines = cells_x * cells_y
    order, vectors = halo_x_ref.shape[2], halo_x_ref.shape[3]
    half = order // 2
    planar = planar_order(order)
    side_ref[0] = left_ref[0]
    side_ref[3] = left_ref[1]
    outside = halo_fields(cells_x, cells_y)
    for d in range(2):
        for line in range(lines):
            x, y = line // cells_y, line % cells_y
            columns = slice(line * order, (line + 1) * order)
            if (d, line) not in outside:
                ahead = line + (cells_y if d == 0 else 1)
                side_ref[1 + d, :, columns] = left_ref[0, :, ahead * order : (ahead + 1) * order]
                continue
            halo = halo_x_ref[0, y] if d == 0 else halo_y_ref[x, 0]
            ahead = jnp.dot(planar, halo, preferred_element_type=f32)
            side_ref[1 + d, :, columns] = ahead.T.astype(bf16)
            matrix = matrix_ref[outside.index((d, line))]
            field_ref[d, line] = transport(matrix[:, :half], side_by_side(ahead), 1)
    for k, (code, line) in enumerate(local_fields(cells_x, cells_y)):
        field_ref[code, line] = local_ref[k]
    copy.wait()

    def factors(o):
        code = dirs_ref[o]
        side = jnp.where((code >= 3) & (code < 6), code - 2, 0)
        cosine = phase_ref[o, :, 0:vectors]
        sine = phase_ref[o, :, vectors : 2 * vectors]
        rows = []
        for line in range(lines):
            real, imag = field_ref[code, line, 0:half], field_ref[code, line, half:order]
            turned_r, turned_i = cosine * real - sine * imag, sine * real + cosine * imag
            rows.append(jnp.concatenate([turned_r, turned_i], axis=1))
            rows.append(jnp.concatenate([turned_i, -turned_r], axis=1))
        return side_ref[side], jnp.concatenate(rows, axis=0).astype(bf16)

    for place, core, i, o in operators(pairs, own_ops, True):
        put_product(out_ref, place, core, i, *factors(o))
    for k, (_, _, _, o) in enumerate(operators(pairs, own_ops, False)):
        later_side_ref[k], later_pair_ref[k] = factors(o)


def second_margin_kernel(pairs, own_ops, side_ref, pair_ref, out_ref):
    for k, (place, core, i, _) in enumerate(operators(pairs, own_ops, False)):
        put_product(out_ref, place, core, i, side_ref[k], pair_ref[k])


def scale_of(block):
    top = jnp.max(jnp.abs(block), axis=0, keepdims=True)
    return jnp.floor(jnp.log2(jnp.maximum(top, 1e-30))) + 1.0


def put_fixed(out_ref, blocks):
    rows, vectors = blocks[0].shape
    tail = iota((TAIL, vectors), 0)
    scales = jnp.zeros((TAIL, vectors), jnp.float32)
    for k, block in enumerate(blocks):
        scale = scale_of(block)
        scales = jnp.where(tail == k, scale, scales)
        fixed = jnp.floor(block * jnp.exp2(FIXED_BITS - scale) + 0.5)
        out_ref[k * rows : (k + 1) * rows] = fixed.astype(jnp.int32).astype(jnp.int16)
    out_ref[len(blocks) * rows :] = scales.astype(jnp.int32).astype(jnp.int16)


def from_fixed(ref, rows, k):
    scales = ref[ref.shape[0] - TAIL :].astype(jnp.int32).astype(jnp.float32)
    block = ref[k * rows : (k + 1) * rows].astype(jnp.int32).astype(jnp.float32)
    return block * jnp.exp2(scales[k : k + 1] - FIXED_BITS)


def group_block(bases, messages, j, start, rows):
    total = bases[0][j >> 1, pl.ds(start, rows)] + bases[1][j >> 1, pl.ds(start, rows)]
    for b, ref in enumerate(messages):
        total = total + fixed_at(ref.at[j >> (b + 1)], start, rows)
    return total


def fixed_at(ref, start, rows):
    tail = ref[ref.shape[0] - TAIL :].astype(jnp.int32).astype(jnp.float32)
    scale = jnp.max(
        jnp.where(iota(tail.shape, 0) == start // rows, tail, -1000.0), axis=0, keepdims=True
    )
    block = ref[pl.ds(start, rows)].astype(jnp.int32).astype(jnp.float32)
    return block * jnp.exp2(scale - FIXED_BITS)


def fold_kernel(level, vectors, own_ref, other_ref, *refs):
    messages, out_ref = refs[:-1], refs[-1]
    for k in range(out_ref.shape[0]):
        blocks = [
            group_block((own_ref, other_ref), messages, (2 * k + 1) << level, start, vectors)
            for start in range(0, own_ref.shape[1], vectors)
        ]
        put_fixed(out_ref.at[k], blocks)


def half_rows(half, vectors, kept):
    me = lax.axis_index("gx") & 1
    base = pl.multiple_of((me if kept else 1 - me) * half, half)
    return [base + step for step in range(0, half, vectors)]


def fold_halves_kernel(level, vectors, own_ref, other_ref, *refs):
    messages, outs = refs[:-2], refs[-2:]
    for kept, out_ref in enumerate(outs):
        starts = half_rows(own_ref.shape[1] // 2, vectors, kept)
        bases = (own_ref, other_ref)
        put_fixed(out_ref, [group_block(bases, messages, 1 << level, s, vectors) for s in starts])


def half_kernel(levels, vectors, kept, own_ref, other_ref, *refs):
    messages, last, out_ref = refs[: levels - 1], refs[levels - 1 : -1], refs[-1]
    blocks = []
    for p, start in enumerate(half_rows(own_ref.shape[1] // 2, vectors, kept)):
        total = group_block((own_ref, other_ref), messages, 0, start, vectors)
        for ref in last:
            total = total + from_fixed(ref, vectors, p)
        blocks.append(total)
    put_fixed(out_ref, blocks)


def both_kernel(vectors, norm_factor, own_ref, arrived_ref, out_ref):
    blocks = [
        from_fixed(own_ref, vectors, p) + from_fixed(arrived_ref, vectors, p)
        for p in range((own_ref.shape[0] - TAIL) // vectors)
    ]
    if norm_factor is None:
        put_fixed(out_ref, blocks)
        return
    for p, block in enumerate(blocks):
        out_ref[p * vectors : (p + 1) * vectors] = (block * norm_factor).astype(out_ref.dtype)


def contract(sums_ref, weight_ref, blocks, tau_ref, left_ref, right_ref):
    f32, bf16 = jnp.float32, jnp.bfloat16
    vectors = sums_ref.shape[2]
    count_ops = sums_ref.shape[0] // 2
    order = tau_ref.shape[2]
    spins = order // vectors
    me_t = lax.axis_index("ta")
    times = len(blocks)

    def chosen(end, k):
        total = jnp.zeros((vectors // 8, 8, vectors), f32)
        for t in range(times):
            weight = weight_ref[end, lax.rem(me_t + t, times)]
            total = total + blocks[t](k).astype(f32).reshape(total.shape) * weight
        return total.reshape(vectors, vectors)

    for o in range(count_ops):
        first = 2 * o * vectors
        a_r, a_i = chosen(0, 2 * o).astype(bf16), chosen(0, 2 * o + 1).astype(bf16)
        b_r, b_i = chosen(1, 2 * o).T.astype(bf16), chosen(1, 2 * o + 1).T.astype(bf16)
        real, imag = slice(first, first + vectors), slice(first + vectors, first + 2 * vectors)
        left_ref[real, 0:vectors] = a_r
        left_ref[real, vectors:] = -a_i
        left_ref[imag, 0:vectors] = a_i
        left_ref[imag, vectors:] = a_r
        right_ref[0:vectors, real] = b_r
        right_ref[0:vectors, imag] = -b_i
        right_ref[vectors:, real] = b_i
        right_ref[vectors:, imag] = b_r
    lanes = sums_ref.shape[1]
    fold = lambda t: jnp.sum(t.reshape(vectors // lanes, lanes, vectors), axis=0)
    sums = [jnp.zeros((lanes, vectors), f32) for _ in range(2 * count_ops)]
    for s in range(spins):
        rows = slice(s * vectors, (s + 1) * vectors)
        x = jnp.dot(
            left_ref[...],
            jnp.concatenate([tau_ref[0, rows], tau_ref[1, rows]], axis=0),
            preferred_element_type=f32,
        )
        for c in range(spins):
            cols = slice(c * vectors, (c + 1) * vectors)
            y = jnp.dot(
                jnp.concatenate([tau_ref[0, rows, cols], tau_ref[1, rows, cols]], axis=1),
                right_ref[...],
                preferred_element_type=f32,
            )
            for o in range(count_ops):
                first = 2 * o * vectors
                x_r = x[first : first + vectors, cols]
                x_i = x[first + vectors : first + 2 * vectors, cols]
                y_r = y[:, first : first + vectors]
                y_i = y[:, first + vectors : first + 2 * vectors]
                sums[2 * o] = sums[2 * o] + fold(x_r * y_r + x_i * y_i)
                sums[2 * o + 1] = sums[2 * o + 1] + fold(x_i * y_r - x_r * y_i)
    for k, total in enumerate(sums):
        sums_ref[k] = total


def hand_kernel(*refs):
    blocks, out_ref = refs[:-1], refs[-1]
    rows = blocks[0].shape[0] // 2
    for t, ref in enumerate(blocks):
        out_ref[t * rows : (t + 1) * rows] = ref[:rows]


def own_part(handed_ref, carried_ref, t, vectors):
    rows = carried_ref.shape[0] // 2
    second = (lax.axis_index("gy") & 1).astype(jnp.float32)

    def part(k):
        first = handed_ref[t * rows + k * vectors : t * rows + (k + 1) * vectors]
        mine = carried_ref[rows + k * vectors : rows + (k + 1) * vectors]
        return first.astype(jnp.float32) * (1.0 - second) + mine.astype(jnp.float32) * second

    return part


def first_contract_kernel(times, weight_ref, tau_ref, handed_ref, *refs):
    carried, (sums_ref, left_ref, right_ref) = refs[:times], refs[times:]
    vectors = sums_ref.shape[2]
    blocks = [own_part(handed_ref, ref, t, vectors) for t, ref in enumerate(carried)]
    contract(sums_ref, weight_ref, blocks, tau_ref, left_ref, right_ref)


def second_contract_kernel(times, split, weight_ref, tau_ref, *refs):
    handed, refs = refs[:2], refs[2:]
    kept, other, refs = refs[:times], refs[times : 2 * times], refs[2 * times :]
    if split:
        first_sums_ref, refs = refs[0], refs[1:]
    margin_ref, corr_ref, sums_ref, left_ref, right_ref = refs
    vectors = sums_ref.shape[2]
    half = kept[0].shape[0] // 2
    me = lax.axis_index("gx") & 1
    kept = [own_part(handed[0], ref, t, vectors) for t, ref in enumerate(kept)]
    other = [own_part(handed[1], ref, t, vectors) for t, ref in enumerate(other)]
    count_parts = half // vectors
    for place, part in ((me, kept[0]), (1 - me, other[0])):
        for k in range(count_parts):
            start = pl.multiple_of(place * half + k * vectors, vectors)
            margin_ref[0, pl.ds(start, vectors)] = part(k)

    def either(kept_part, other_part):
        def part(k):
            mine = (k // count_parts == me).astype(jnp.float32)
            k = k % count_parts
            return kept_part(k) * mine + other_part(k) * (1.0 - mine)

        return part

    blocks = other if split else [either(a, b) for a, b in zip(kept, other)]
    contract(sums_ref, weight_ref, blocks, tau_ref, left_ref, right_ref)
    now_ops = sums_ref.shape[0] // 2
    known = [(sums_ref, (1 - me) * now_ops)] if split else [(sums_ref, 0)]
    if split:
        known.append((first_sums_ref, me * now_ops))
    shape = corr_ref.shape[1:]
    row, col = iota(shape, 0), iota(shape, 1)
    result = jnp.zeros(shape, jnp.float32)
    for ref, first in known:
        for k in range(2 * now_ops):
            total = jnp.sum(jnp.sum(ref[k], axis=0, keepdims=True), axis=1, keepdims=True)
            here = (row == first + k // 2) & (col == k % 2)
            result = jnp.where(here, total * (1.0 / vectors), result)
    corr_ref[0] = result


def vmem_spec():
    return pl.BlockSpec(memory_space=pltpu.VMEM)


def smem_spec():
    return pl.BlockSpec(memory_space=pltpu.SMEM)


def hbm_spec():
    return pl.BlockSpec(memory_space=pltpu.HBM)


def in_hbm(x):
    return pltpu.with_memory_space_constraint(x, pltpu.HBM)


def local_call(body, name, outs, in_specs, out_specs, scratch=(), cost=None):
    return pl.pallas_call(
        body,
        out_shape=outs,
        in_specs=in_specs,
        out_specs=out_specs,
        scratch_shapes=list(scratch),
        compiler_params=pltpu.CompilerParams(vmem_limit_bytes=VMEM_LIMIT),
        cost_estimate=cost,
        name=name,
    )


def from_step(block, axis, step):
    count = lax.axis_size(axis)
    return lax.ppermute(block, axis, [((i + step) % count, i) for i in range(count)])


def moved(block, place):
    sizes = [lax.axis_size(axis) for axis in AXES]
    flat = lambda t, x, y: (t * sizes[1] + x) * sizes[2] + y
    perm = []
    for member in np.ndindex(*sizes):
        perm.append((flat(*member), flat(*place(*member))))
    return lax.ppermute(block, AXES, perm)


def swapped(block):
    return moved(block, lambda t, x, y: (t, x, y ^ 1))


def between(block, t_step=0, x_bits=0, y_bits=0):
    times = lax.axis_size("ta")
    target = lambda t, x, y: ((t + t_step) % times, x ^ x_bits, y ^ y_bits)
    return moved(block, lambda t, x, y: target(t, x, y) if y & 1 else (t, x, y))


def per_device(eigvecs, links, op_dirs, op_moms, perams, pair_times, slot_counts):
    f32, bf16 = jnp.float32, jnp.bfloat16
    _, cells_x, cells_y, cells_z, colors, _, vectors = eigvecs.shape
    order = cells_z * colors * 2
    lines = cells_x * cells_y
    count_ops = op_dirs.shape[0]
    times, shares, groups = lax.axis_size("ta"), lax.axis_size("gx"), lax.axis_size("gy")
    pairs = groups // 2
    levels = pairs.bit_length() - 1
    own_ops = count_ops // groups
    own_rows = own_ops * 2 * vectors
    field = eigvecs.reshape(cells_x, cells_y, order, vectors)
    halo_x = from_step(field[0:1], "gx", 1)
    link_field = links[0].transpose(0, 1, 3, 5, 6, 4, 2).reshape(lines, 27, 2, cells_z)
    outside, inside = halo_fields(cells_x, cells_y), local_fields(cells_x, cells_y)
    inputs = [field, link_field, op_dirs, op_moms, wave_constants(cells_z), pair_times]
    inputs = [in_hbm(x) for x in inputs]
    held = [
        pltpu.SMEM(x.shape, x.dtype) if x.dtype == jnp.int32 else pltpu.VMEM(x.shape, x.dtype)
        for x in inputs
    ]
    edge, matrices, local, left, phases, weights = local_call(
        functools.partial(prepare_kernel, cells_x, cells_y),
        "prepare_lines",
        (
            jax.ShapeDtypeStruct((cells_x, 1, order, vectors), bf16),
            jax.ShapeDtypeStruct((len(outside), order, 128), bf16),
            jax.ShapeDtypeStruct((len(inside), order, vectors), f32),
            jax.ShapeDtypeStruct((2, vectors, lines * order), bf16),
            jax.ShapeDtypeStruct((count_ops, order // 2, 2 * vectors), f32),
            jax.ShapeDtypeStruct((2, times, 8, vectors), f32),
        ),
        [hbm_spec()] * len(inputs) + [smem_spec()],
        (vmem_spec(),) * 6,
        held
        + [
            pltpu.VMEM((lines, LINK_COLS, cells_z), f32),
            pltpu.SemaphoreType.DMA((len(inputs),)),
        ],
    )(*inputs, slot_counts)
    halo_y = from_step(edge, "gy", 1)
    pair_rows = 2 * own_rows
    part = jax.ShapeDtypeStruct((pairs // 2, pair_rows, vectors), f32)
    later = count_ops // 2
    part_a, later_sides, later_pairs = local_call(
        functools.partial(first_margin_kernel, cells_x, cells_y, pairs, own_ops),
        "first_margins",
        (
            part,
            jax.ShapeDtypeStruct((later, vectors, lines * order), bf16),
            jax.ShapeDtypeStruct((later, lines * order, 2 * vectors), bf16),
        ),
        [vmem_spec()] * 6 + [hbm_spec()],
        (vmem_spec(),) * 3,
        [
            pltpu.VMEM((7, lines, order, vectors), f32),
            pltpu.VMEM((4, vectors, lines * order), bf16),
            pltpu.SMEM((count_ops,), jnp.int32),
            pltpu.SemaphoreType.DMA,
        ],
    )(matrices, local, left, phases, halo_x, halo_y, in_hbm(op_dirs))
    bases_a = (part_a, swapped(part_a))
    part_b = local_call(
        functools.partial(second_margin_kernel, pairs, own_ops),
        "second_margins",
        part,
        [vmem_spec()] * 2,
        vmem_spec(),
    )(later_sides, later_pairs)
    bases_b = (part_b, swapped(part_b))

    def packed(body, name, *inputs, rows=pair_rows, lead=(), count=1):
        shape = jax.ShapeDtypeStruct((*lead, rows + TAIL, vectors), jnp.int16)
        outs = shape if count == 1 else (shape,) * count
        specs = vmem_spec() if count == 1 else (vmem_spec(),) * count
        return local_call(body, name, outs, [vmem_spec()] * len(inputs), specs)(*inputs)

    half = pair_rows // 2
    messages = []
    for b in range(levels):
        inputs = bases_b + tuple(messages) if b else bases_a
        if b < levels - 1:
            body = functools.partial(fold_kernel, b, vectors)
            sent = packed(body, "fold_pairs", *inputs, lead=(pairs >> (b + 1),))
            messages.append(between(sent, y_bits=2 << b))
            continue
        body = functools.partial(fold_halves_kernel, b, vectors)
        away, kept = packed(body, "fold_halves", *inputs, rows=half, count=2)
        away, kept = between(away, y_bits=2 << b), between(kept, y_bits=2 << b)
    body = functools.partial(half_kernel, levels, vectors, False)
    sent = packed(body, "send_half", *bases_b, *messages, away, rows=half)
    arrived = between(sent, x_bits=1)
    body = functools.partial(half_kernel, levels, vectors, True)
    message = packed(body, "keep_half", *bases_b, *messages, kept, arrived, rows=half)
    norm_factor = 1.0 / math.sqrt(3.0 * cells_x * shares * cells_y * groups * cells_z)
    step = 2
    while step < shares:
        arrived = between(message, x_bits=step)
        step *= 2
        if step < shares:
            body = functools.partial(both_kernel, vectors, None)
            message = packed(body, "sum_both", message, arrived, rows=half)
    finished = local_call(
        functools.partial(both_kernel, vectors, norm_factor),
        "finish_half",
        jax.ShapeDtypeStruct((half, vectors), bf16),
        [vmem_spec()] * 2,
        vmem_spec(),
    )(message, arrived)
    kept = [finished] + [between(finished, t_step=-t) for t in range(1, times)]
    other = [between(block, x_bits=1) for block in kept]

    def handed(blocks, name):
        shape = jax.ShapeDtypeStruct((times * half // 2, vectors), bf16)
        specs = [vmem_spec()] * times
        return swapped(local_call(hand_kernel, name, shape, specs, vmem_spec())(*blocks))

    hands = [handed(kept, "hand_kept"), handed(other, "hand_other")]
    split = own_ops % 2 == 0
    now_ops = own_ops // 2 if split else own_ops
    sums_shape = (2 * now_ops, 32, vectors)
    scratch = [
        pltpu.VMEM((2 * now_ops * vectors, 2 * vectors), bf16),
        pltpu.VMEM((2 * vectors, 2 * now_ops * vectors), bf16),
    ]
    sums = []
    if split:
        sums = [
            local_call(
                functools.partial(first_contract_kernel, times),
                "first_contraction",
                jax.ShapeDtypeStruct(sums_shape, f32),
                [vmem_spec()] * (3 + times),
                vmem_spec(),
                scratch,
            )(weights, perams[0], hands[0], *kept)
        ]
    margins, correlators = local_call(
        functools.partial(second_contract_kernel, times, split),
        "second_contraction",
        (
            jax.ShapeDtypeStruct((1, own_rows, vectors), f32),
            jax.ShapeDtypeStruct((1, own_ops, 2), f32),
        ),
        [vmem_spec()] * (4 + 2 * times + len(sums)),
        (vmem_spec(), vmem_spec()),
        [pltpu.VMEM(sums_shape, f32)] + scratch,
    )(weights, perams[0], *hands, *kept, *other, *sums)
    return (margins.reshape(1, own_ops, 2, vectors, vectors), correlators)


def solution(mesh):
    placed = (
        P("ta", "gx", "gy", None, None, None, None),
        P("ta", "gx", "gy", None, None, None, None, None),
        P(),
        P(),
        P(("ta", "gx"), None, None, None),
        P(("ta", "gx"), None),
        P(("ta", "gx")),
    )
    return jax.shard_map(
        per_device,
        mesh=mesh,
        in_specs=placed,
        out_specs=(P("ta", "gy", None, None, None), P(("ta", "gx"), "gy", None)),
        check_vma=False,
    )
```

```python
import functools
import math

import jax
import jax.numpy as jnp
import numpy as np
from jax import lax
from jax.experimental import pallas as pl
from jax.experimental.pallas import tpu as pltpu
from jax.sharding import PartitionSpec as P

VMEM_LIMIT = 24 * 1024 * 1024
MOMENTA = 3
LINK_COLS = 54
TAIL = 16
FIXED_BITS = 14.0


def wave_constants(cells_z):
    z_row = np.arange(3 * cells_z) // 3
    columns = []
    for ahead in range(2):
        for momentum in range(MOMENTA):
            angle = 2.0 * math.pi * momentum * ((z_row + ahead) % cells_z) / cells_z
            columns.append(np.cos(angle))
            columns.append(np.sin(angle))
    left = np.stack(columns, axis=1).astype(np.float32)
    terms = []
    for _ in range(3):
        term = left.astype(jnp.bfloat16).astype(np.float32)
        terms.append(term)
        left = left - term
    return jnp.asarray(np.concatenate(terms, axis=1), jnp.bfloat16)


def iota(shape, axis):
    return lax.broadcasted_iota(jnp.int32, shape, axis)


def third(x):
    return (x * 21846) >> 16


def one_hot(condition):
    return condition.astype(jnp.float32).astype(jnp.bfloat16)


def planar_order(order):
    row, col = iota((order, order), 0), iota((order, order), 1)
    half = order // 2
    source = jnp.where(row < half, 2 * row, 2 * (row - half) + 1)
    return one_hot(col == source)


def side_by_side(planar):
    half = planar.shape[0] // 2
    return jnp.concatenate([planar[:half], planar[half:]], axis=1).astype(jnp.bfloat16)


def transport(matrix, pair, sign):
    half, vectors = matrix.shape[0] // 2, pair.shape[1] // 2
    parts = jnp.dot(matrix, pair, preferred_element_type=jnp.float32)
    real, imag = parts[:half], parts[half:]
    if sign > 0:
        return jnp.concatenate(
            [real[:, :vectors] - imag[:, vectors:], real[:, vectors:] + imag[:, :vectors]], axis=0
        )
    return jnp.concatenate(
        [real[:, :vectors] + imag[:, vectors:], real[:, vectors:] - imag[:, :vectors]], axis=0
    )


def halo_fields(cells_x, cells_y):
    pairs = [(0, (cells_x - 1) * cells_y + y) for y in range(cells_y)]
    return pairs + [(1, x * cells_y + cells_y - 1) for x in range(cells_x)]


def local_fields(cells_x, cells_y):
    lines = cells_x * cells_y
    outside = halo_fields(cells_x, cells_y)
    every = [(code, line) for code in range(7) for line in range(lines)]
    return [pair for pair in every if pair not in outside]


def prepare_kernel(cells_x, cells_y, *refs):
    inputs, live_ref, refs = refs[:6], refs[6], refs[7:]
    matrix_ref, local_ref, left_ref, phase_ref, weight_ref = refs[:5]
    held, link_rows_ref, sems = refs[5:11], refs[11], refs[12]
    copies = [
        pltpu.make_async_copy(src, dst, sems.at[k])
        for k, (src, dst) in enumerate(zip(inputs, held))
    ]
    for copy in copies:
        copy.start()
    v_ref, link_ref, dirs_ref, moms_ref, waves_ref, pair_ref = held
    f32, bf16 = jnp.float32, jnp.bfloat16
    order, vectors = v_ref.shape[2], v_ref.shape[3]
    half, cells_z = order // 2, order // 6
    lines = cells_x * cells_y
    times = weight_ref.shape[1]
    spread = one_hot(third(iota((half, cells_z), 0)) == iota((half, cells_z), 1))
    row, col = iota((half, LINK_COLS), 0), iota((half, LINK_COLS), 1)
    row_color = row - 3 * third(row)
    pair_at = third(col >> 1)
    col_in, col_out = (col >> 1) - 3 * pair_at, pair_at - 3 * third(pair_at)
    pick = [(row_color == col_out).astype(f32), (row_color == col_in).astype(f32)]
    wide = (LINK_COLS, 6 * 128)
    row, col = iota(wide, 0), iota(wide, 1)
    block, place = col >> 7, col & 127
    color = place - 3 * third(place)
    pair_at = third(row >> 1)
    row_in, row_out = (row >> 1) - 3 * pair_at, pair_at - 3 * third(pair_at)
    fits = 2 * third(pair_at) + (row & 1) == block
    expand = [one_hot(fits & (row_in == color)), one_hot(fits & (row_out == color))]
    row, col = iota((half, 128), 0), iota((half, 128), 1)
    near = ((third(row) == third(col)) & (col < half)).astype(f32)
    planar = planar_order(order)
    for copy in copies:
        copy.wait()
    for t in range(times):
        sink = (pair_ref[0, 0] == t) & (live_ref[0] > 0)
        source = pair_ref[0, 1] == t
        weight_ref[0, t] = jnp.full(weight_ref.shape[2:], jnp.where(sink, 1.0, 0.0), f32)
        weight_ref[1, t] = jnp.full(weight_ref.shape[2:], jnp.where(source, 1.0, 0.0), f32)
    for line in range(lines):
        for k in range(LINK_COLS // 2):
            link_rows_ref[line, 2 * k : 2 * k + 2] = link_ref[line, k].astype(f32)
    outside = halo_fields(cells_x, cells_y)
    inside = local_fields(cells_x, cells_y)
    ordered = []
    for line in range(lines):
        here = jnp.dot(
            planar, v_ref[line // cells_y, line % cells_y], preferred_element_type=f32
        )
        ordered.append(here)
        local_ref[inside.index((6, line))] = here
    for line in range(lines):
        here = ordered[line]
        ahead_z = jnp.concatenate(
            [here[3:half], here[:3], here[half + 3 :], here[half : half + 3]], axis=0
        )
        columns = slice(line * order, (line + 1) * order)
        left_ref[0, :, columns] = here.T.astype(bf16)
        left_ref[1, :, columns] = ahead_z.T.astype(bf16)
        seen = lax.dot_general(
            spread,
            link_rows_ref[line].astype(bf16),
            (((1,), (1,)), ((), ())),
            preferred_element_type=f32,
        )
        pair = side_by_side(here)
        for way in range(2):
            blocks = jnp.dot(
                (seen * pick[way]).astype(bf16), expand[way], preferred_element_type=f32
            )
            for d in range(3):
                matrix = jnp.concatenate(
                    [
                        blocks[:, 256 * d : 256 * d + 128] * near,
                        blocks[:, 256 * d + 128 : 256 * d + 256] * near,
                    ],
                    axis=0,
                ).astype(bf16)
                if way == 1:
                    carried = transport(matrix[:, :half], pair, -1)
                    local_ref[inside.index((3 + d, line))] = carried.astype(bf16).astype(f32)
                elif (d, line) in outside:
                    matrix_ref[outside.index((d, line))] = matrix
                else:
                    ahead = ahead_z if d == 2 else ordered[line + (cells_y if d == 0 else 1)]
                    local_ref[inside.index((d, line))] = transport(
                        matrix[:, :half], side_by_side(ahead), 1
                    )
    wave_cols = waves_ref.shape[1]
    per_term = wave_cols // 3
    row, col = iota((wave_cols, 2 * vectors), 0), iota((wave_cols, 2 * vectors), 1)
    term = (row >= per_term).astype(jnp.int32) + (row >= 2 * per_term).astype(jnp.int32)
    wave_at = row - per_term * term - (col >= vectors).astype(jnp.int32)
    for o in range(phase_ref.shape[0]):
        column = 2 * (jnp.where(dirs_ref[o] == 5, MOMENTA, 0) + moms_ref[o])
        phase_ref[o] = jnp.dot(
            waves_ref[...], one_hot(wave_at == column), preferred_element_type=f32
        )


def low_bit(j):
    return (j & -j).bit_length() - 1


def put_product(out_ref, place, i, side, pair):
    vectors = pair.shape[1] // 2
    product = jnp.dot(side, pair, preferred_element_type=jnp.float32)
    first = 2 * i * vectors
    out_ref[place, first : first + vectors] = product[:, :vectors]
    out_ref[place, first + vectors : first + 2 * vectors] = product[:, vectors:]


def first_groups(groups):
    return sorted((j for j in range(groups) if j & 2), key=lambda j: -(j & 1))


def second_groups(groups):
    return sorted((j for j in range(groups) if not j & 2), key=lambda j: -(j & 1))


def first_margin_kernel(cells_x, cells_y, groups, own_ops, *refs):
    matrix_ref, local_ref, left_ref, phase_ref, halo_y_ref, halo_x_ref, dirs_hbm = refs[:7]
    swap_ref, hold_ref, later_side_ref, later_pair_ref = refs[7:11]
    field_ref, side_ref, dirs_ref, sem = refs[11:]
    f32, bf16 = jnp.float32, jnp.bfloat16
    copy = pltpu.make_async_copy(dirs_hbm, dirs_ref, sem)
    copy.start()
    lines = cells_x * cells_y
    order, vectors = halo_x_ref.shape[2], halo_x_ref.shape[3]
    half = order // 2
    planar = planar_order(order)
    side_ref[0] = left_ref[0]
    side_ref[3] = left_ref[1]
    outside = halo_fields(cells_x, cells_y)
    for d in range(2):
        for line in range(lines):
            x, y = line // cells_y, line % cells_y
            columns = slice(line * order, (line + 1) * order)
            if (d, line) not in outside:
                ahead = line + (cells_y if d == 0 else 1)
                side_ref[1 + d, :, columns] = left_ref[0, :, ahead * order : (ahead + 1) * order]
                continue
            halo = halo_x_ref[0, y] if d == 0 else halo_y_ref[x, 0]
            ahead = jnp.dot(planar, halo, preferred_element_type=f32)
            side_ref[1 + d, :, columns] = ahead.T.astype(bf16)
            matrix = matrix_ref[outside.index((d, line))]
            field_ref[d, line] = transport(matrix[:, :half], side_by_side(ahead), 1)
    for k, (code, line) in enumerate(local_fields(cells_x, cells_y)):
        field_ref[code, line] = local_ref[k]
    copy.wait()
    me = lax.axis_index("gy")
    later = 0
    for j in first_groups(groups) + second_groups(groups):
        for i in range(own_ops):
            o = (me ^ j) * own_ops + i
            code = dirs_ref[o]
            side = jnp.where((code >= 3) & (code < 6), code - 2, 0)
            cosine = phase_ref[o, :, 0:vectors]
            sine = phase_ref[o, :, vectors : 2 * vectors]
            pairs = []
            for line in range(lines):
                real, imag = field_ref[code, line, 0:half], field_ref[code, line, half:order]
                turned_r, turned_i = cosine * real - sine * imag, sine * real + cosine * imag
                pairs.append(jnp.concatenate([turned_r, turned_i], axis=1))
                pairs.append(jnp.concatenate([turned_i, -turned_r], axis=1))
            pair = jnp.concatenate(pairs, axis=0).astype(bf16)
            if j & 2:
                put_product(swap_ref if j & 1 else hold_ref, j >> 2, i, side_ref[side], pair)
            else:
                later_side_ref[later] = side_ref[side]
                later_pair_ref[later] = pair
                later += 1


def second_margin_kernel(groups, own_ops, side_ref, pair_ref, swap_ref, *hold_refs):
    later = 0
    for j in second_groups(groups):
        level = low_bit(j) if j else groups.bit_length() - 1
        for i in range(own_ops):
            out_ref, place = (swap_ref, j >> 2) if j & 1 else (hold_refs[level - 2], j >> (level + 1))
            put_product(out_ref, place, i, side_ref[later], pair_ref[later])
            later += 1


def scale_of(block):
    top = jnp.max(jnp.abs(block), axis=0, keepdims=True)
    return jnp.floor(jnp.log2(jnp.maximum(top, 1e-30))) + 1.0


def put_fixed(out_ref, blocks):
    rows, vectors = blocks[0].shape
    tail = iota((TAIL, vectors), 0)
    scales = jnp.zeros((TAIL, vectors), jnp.float32)
    for k, block in enumerate(blocks):
        scale = scale_of(block)
        scales = jnp.where(tail == k, scale, scales)
        fixed = jnp.floor(block * jnp.exp2(FIXED_BITS - scale) + 0.5)
        out_ref[k * rows : (k + 1) * rows] = fixed.astype(jnp.int32).astype(jnp.int16)
    out_ref[len(blocks) * rows :] = scales.astype(jnp.int32).astype(jnp.int16)


def from_fixed(ref, rows, k):
    scales = ref[ref.shape[0] - TAIL :].astype(jnp.int32).astype(jnp.float32)
    block = ref[k * rows : (k + 1) * rows].astype(jnp.int32).astype(jnp.float32)
    return block * jnp.exp2(scales[k : k + 1] - FIXED_BITS)


def group_block(held_ref, received, k, j, start, rows):
    span = pl.ds(start, rows)
    total = held_ref[k, span] + received[0][j >> 2, span]
    for b, ref in enumerate(received[1:], 1):
        total = total + fixed_at(ref.at[j >> (b + 1)], start, rows)
    return total


def fixed_at(ref, start, rows):
    tail = ref[ref.shape[0] - TAIL :].astype(jnp.int32).astype(jnp.float32)
    scale = jnp.max(
        jnp.where(iota(tail.shape, 0) == start // rows, tail, -1000.0), axis=0, keepdims=True
    )
    block = ref[pl.ds(start, rows)].astype(jnp.int32).astype(jnp.float32)
    return block * jnp.exp2(scale - FIXED_BITS)


def fold_kernel(level, vectors, *refs):
    held_ref, received, out_ref = refs[0], refs[1:-1], refs[-1]
    for k in range(held_ref.shape[0]):
        j = (2 * k + 1) << level
        blocks = [
            group_block(held_ref, received, k, j, start, vectors)
            for start in range(0, held_ref.shape[1], vectors)
        ]
        put_fixed(out_ref.at[k], blocks)


def half_rows(held_ref, vectors, kept):
    me = lax.axis_index("gx") & 1
    half = held_ref.shape[1] // 2
    base = pl.multiple_of((me if kept else 1 - me) * half, half)
    return [base + step for step in range(0, half, vectors)]


def fold_halves_kernel(vectors, *refs):
    held_ref, received, outs = refs[0], refs[1:-2], refs[-2:]
    for kept, out_ref in enumerate(outs):
        starts = half_rows(held_ref, vectors, kept)
        blocks = [group_block(held_ref, received, 0, held_ref.shape[0], s, vectors) for s in starts]
        put_fixed(out_ref, blocks)


def half_kernel(vectors, kept, *refs):
    count = 3 if kept else 2
    held_ref, received, last, out_ref = refs[0], refs[1:-count], refs[-count:-1], refs[-1]
    blocks = []
    for p, start in enumerate(half_rows(held_ref, vectors, kept)):
        total = group_block(held_ref, received, 0, 0, start, vectors)
        for ref in last:
            total = total + from_fixed(ref, vectors, p)
        blocks.append(total)
    put_fixed(out_ref, blocks)


def both_kernel(vectors, norm_factor, own_ref, arrived_ref, out_ref):
    blocks = [
        from_fixed(own_ref, vectors, p) + from_fixed(arrived_ref, vectors, p)
        for p in range((own_ref.shape[0] - TAIL) // vectors)
    ]
    if norm_factor is None:
        put_fixed(out_ref, blocks)
        return
    for p, block in enumerate(blocks):
        out_ref[p * vectors : (p + 1) * vectors] = (block * norm_factor).astype(out_ref.dtype)


def contract(sums_ref, weight_ref, blocks, tau_ref, left_ref, right_ref):
    f32, bf16 = jnp.float32, jnp.bfloat16
    vectors = sums_ref.shape[2]
    count_ops = sums_ref.shape[0] // 2
    order = tau_ref.shape[2]
    spins = order // vectors
    me_t = lax.axis_index("ta")
    times = len(blocks)

    def chosen(end, k):
        total = jnp.zeros((vectors // 8, 8, vectors), f32)
        for t in range(times):
            weight = weight_ref[end, lax.rem(me_t + t, times)]
            total = total + blocks[t](k).astype(f32).reshape(total.shape) * weight
        return total.reshape(vectors, vectors)

    for o in range(count_ops):
        first = 2 * o * vectors
        a_r, a_i = chosen(0, 2 * o).astype(bf16), chosen(0, 2 * o + 1).astype(bf16)
        b_r, b_i = chosen(1, 2 * o).T.astype(bf16), chosen(1, 2 * o + 1).T.astype(bf16)
        real, imag = slice(first, first + vectors), slice(first + vectors, first + 2 * vectors)
        left_ref[real, 0:vectors] = a_r
        left_ref[real, vectors:] = -a_i
        left_ref[imag, 0:vectors] = a_i
        left_ref[imag, vectors:] = a_r
        right_ref[0:vectors, real] = b_r
        right_ref[0:vectors, imag] = -b_i
        right_ref[vectors:, real] = b_i
        right_ref[vectors:, imag] = b_r
    lanes = sums_ref.shape[1]
    fold = lambda t: jnp.sum(t.reshape(vectors // lanes, lanes, vectors), axis=0)
    sums = [jnp.zeros((lanes, vectors), f32) for _ in range(2 * count_ops)]
    for s in range(spins):
        rows = slice(s * vectors, (s + 1) * vectors)
        x = jnp.dot(
            left_ref[...],
            jnp.concatenate([tau_ref[0, rows], tau_ref[1, rows]], axis=0),
            preferred_element_type=f32,
        )
        for c in range(spins):
            cols = slice(c * vectors, (c + 1) * vectors)
            y = jnp.dot(
                jnp.concatenate([tau_ref[0, rows, cols], tau_ref[1, rows, cols]], axis=1),
                right_ref[...],
                preferred_element_type=f32,
            )
            for o in range(count_ops):
                first = 2 * o * vectors
                x_r = x[first : first + vectors, cols]
                x_i = x[first + vectors : first + 2 * vectors, cols]
                y_r = y[:, first : first + vectors]
                y_i = y[:, first + vectors : first + 2 * vectors]
                sums[2 * o] = sums[2 * o] + fold(x_r * y_r + x_i * y_i)
                sums[2 * o + 1] = sums[2 * o + 1] + fold(x_i * y_r - x_r * y_i)
    for k, total in enumerate(sums):
        sums_ref[k] = total


def part_of(ref, vectors):
    return lambda k: ref[k * vectors : (k + 1) * vectors]


def first_contract_kernel(times, weight_ref, tau_ref, *refs):
    blocks, (sums_ref, left_ref, right_ref) = refs[:times], refs[times:]
    vectors = sums_ref.shape[2]
    blocks = [part_of(ref, vectors) for ref in blocks]
    contract(sums_ref, weight_ref, blocks, tau_ref, left_ref, right_ref)


def second_contract_kernel(times, split, weight_ref, tau_ref, *refs):
    kept, other, refs = refs[:times], refs[times : 2 * times], refs[2 * times :]
    if split:
        first_sums_ref, refs = refs[0], refs[1:]
    margin_hbm, corr_ref, sums_ref, left_ref, right_ref, wide_ref, sems = refs
    vectors = sums_ref.shape[2]
    half = kept[0].shape[0]
    me = lax.axis_index("gx") & 1
    copies = []
    for k, (place, ref) in enumerate(((me, kept[0]), (1 - me, other[0]))):
        wide_ref[k] = ref[...].astype(jnp.float32)
        rows = pl.ds(pl.multiple_of(place * half, half), half)
        copies.append(pltpu.make_async_copy(wide_ref.at[k], margin_hbm.at[0, rows], sems.at[k]))
        copies[k].start()
    parts_per_half = half // vectors

    def either(kept_ref, other_ref):
        def part(k):
            row = (k % parts_per_half) * vectors
            own, far = kept_ref[row : row + vectors], other_ref[row : row + vectors]
            mine = (k // parts_per_half == me).astype(jnp.float32)
            return own.astype(jnp.float32) * mine + far.astype(jnp.float32) * (1.0 - mine)

        return part

    blocks = [part_of(ref, vectors) for ref in other]
    if not split:
        blocks = [either(a, b) for a, b in zip(kept, other)]
    contract(sums_ref, weight_ref, blocks, tau_ref, left_ref, right_ref)
    now_ops = sums_ref.shape[0] // 2
    known = [(sums_ref, (1 - me) * now_ops)] if split else [(sums_ref, 0)]
    if split:
        known.append((first_sums_ref, me * now_ops))
    shape = corr_ref.shape[1:]
    row, col = iota(shape, 0), iota(shape, 1)
    result = jnp.zeros(shape, jnp.float32)
    for ref, first in known:
        for k in range(2 * now_ops):
            total = jnp.sum(jnp.sum(ref[k], axis=0, keepdims=True), axis=1, keepdims=True)
            here = (row == first + k // 2) & (col == k % 2)
            result = jnp.where(here, total * (1.0 / vectors), result)
    corr_ref[0] = result
    for copy in copies:
        copy.wait()


def vmem_spec():
    return pl.BlockSpec(memory_space=pltpu.VMEM)


def smem_spec():
    return pl.BlockSpec(memory_space=pltpu.SMEM)


def hbm_spec():
    return pl.BlockSpec(memory_space=pltpu.HBM)


def in_hbm(x):
    return pltpu.with_memory_space_constraint(x, pltpu.HBM)


def local_call(body, name, outs, in_specs, out_specs, scratch=(), cost=None):
    return pl.pallas_call(
        body,
        out_shape=outs,
        in_specs=in_specs,
        out_specs=out_specs,
        scratch_shapes=list(scratch),
        compiler_params=pltpu.CompilerParams(vmem_limit_bytes=VMEM_LIMIT),
        cost_estimate=cost,
        name=name,
    )


def from_step(block, axis, step):
    count = lax.axis_size(axis)
    return lax.ppermute(block, axis, [((i + step) % count, i) for i in range(count)])


def from_partner(block, axis, step):
    count = lax.axis_size(axis)
    return lax.ppermute(block, axis, [(i ^ step, i) for i in range(count)])


def per_device(eigvecs, links, op_dirs, op_moms, perams, pair_times, slot_counts):
    f32, bf16 = jnp.float32, jnp.bfloat16
    _, cells_x, cells_y, cells_z, colors, _, vectors = eigvecs.shape
    order = cells_z * colors * 2
    lines = cells_x * cells_y
    count_ops = op_dirs.shape[0]
    times, shares, groups = lax.axis_size("ta"), lax.axis_size("gx"), lax.axis_size("gy")
    levels = groups.bit_length() - 1
    own_ops = count_ops // groups
    own_rows = own_ops * 2 * vectors
    field = eigvecs.reshape(cells_x, cells_y, order, vectors)
    halo_x = from_step(field[0:1], "gx", 1)
    halo_y = from_step(field, "gy", 1)
    link_field = links[0].transpose(0, 1, 3, 5, 6, 4, 2).reshape(lines, 27, 2, cells_z)
    outside, inside = halo_fields(cells_x, cells_y), local_fields(cells_x, cells_y)
    inputs = [field, link_field, op_dirs, op_moms, wave_constants(cells_z), pair_times]
    inputs = [in_hbm(x) for x in inputs]
    held = [
        pltpu.SMEM(x.shape, x.dtype) if x.dtype == jnp.int32 else pltpu.VMEM(x.shape, x.dtype)
        for x in inputs
    ]
    matrices, local, left, phases, weights = local_call(
        functools.partial(prepare_kernel, cells_x, cells_y),
        "prepare_lines",
        (
            jax.ShapeDtypeStruct((len(outside), order, 128), bf16),
            jax.ShapeDtypeStruct((len(inside), order, vectors), f32),
            jax.ShapeDtypeStruct((2, vectors, lines * order), bf16),
            jax.ShapeDtypeStruct((count_ops, order // 2, 2 * vectors), f32),
            jax.ShapeDtypeStruct((2, times, 8, vectors), f32),
        ),
        [hbm_spec()] * len(inputs) + [smem_spec()],
        (vmem_spec(),) * 5,
        held
        + [
            pltpu.VMEM((lines, LINK_COLS, cells_z), f32),
            pltpu.SemaphoreType.DMA((len(inputs),)),
        ],
    )(*inputs, slot_counts)
    part = lambda count: jax.ShapeDtypeStruct((count, own_rows, vectors), f32)
    later = count_ops // 2
    swap_a, hold_a, later_sides, later_pairs = local_call(
        functools.partial(first_margin_kernel, cells_x, cells_y, groups, own_ops),
        "first_margins",
        (
            part(groups // 4),
            part(groups // 4),
            jax.ShapeDtypeStruct((later, vectors, lines * order), bf16),
            jax.ShapeDtypeStruct((later, lines * order, 2 * vectors), bf16),
        ),
        [vmem_spec()] * 6 + [hbm_spec()],
        (vmem_spec(),) * 4,
        [
            pltpu.VMEM((7, lines, order, vectors), f32),
            pltpu.VMEM((4, vectors, lines * order), bf16),
            pltpu.SMEM((count_ops,), jnp.int32),
            pltpu.SemaphoreType.DMA,
        ],
    )(matrices, local, left, phases, halo_y, halo_x, in_hbm(op_dirs))
    swapped_a = from_partner(swap_a, "gy", 1)
    held_shapes = [part(groups >> (b + 1)) for b in range(2, levels)] + [part(1)]
    swap_b, *held = local_call(
        functools.partial(second_margin_kernel, groups, own_ops),
        "second_margins",
        (part(groups // 4), *held_shapes),
        [vmem_spec()] * 2,
        (vmem_spec(),) * (1 + len(held_shapes)),
    )(later_sides, later_pairs)
    received = [from_partner(swap_b, "gy", 1)]

    def packed(body, name, *inputs, rows=own_rows, lead=(), count=1):
        shape = jax.ShapeDtypeStruct((*lead, rows + TAIL, vectors), jnp.int16)
        outs = shape if count == 1 else (shape,) * count
        specs = vmem_spec() if count == 1 else (vmem_spec(),) * count
        return local_call(body, name, outs, [vmem_spec()] * len(inputs), specs)(*inputs)

    half = own_rows // 2
    for b in range(1, levels):
        inputs = (hold_a, swapped_a) if b == 1 else (held[b - 2], *received)
        if b < levels - 1:
            body = functools.partial(fold_kernel, b, vectors)
            sent = packed(body, "fold_groups", *inputs, lead=inputs[0].shape[:1])
            received.append(from_partner(sent, "gy", 1 << b))
            continue
        body = functools.partial(fold_halves_kernel, vectors)
        away, kept = packed(body, "fold_halves", *inputs, rows=half, count=2)
        away, kept = from_partner(away, "gy", 1 << b), from_partner(kept, "gy", 1 << b)
    body = functools.partial(half_kernel, vectors, False)
    sent = packed(body, "send_half", held[-1], *received, away, rows=half)
    arrived = from_partner(sent, "gx", 1)
    body = functools.partial(half_kernel, vectors, True)
    message = packed(body, "keep_half", held[-1], *received, kept, arrived, rows=half)
    norm_factor = 1.0 / math.sqrt(3.0 * cells_x * shares * cells_y * groups * cells_z)
    step = 2
    while step < shares:
        arrived = from_partner(message, "gx", step)
        step *= 2
        if step < shares:
            body = functools.partial(both_kernel, vectors, None)
            message = packed(body, "sum_both", message, arrived, rows=half)
    finished = local_call(
        functools.partial(both_kernel, vectors, norm_factor),
        "finish_half",
        jax.ShapeDtypeStruct((half, vectors), bf16),
        [vmem_spec()] * 2,
        vmem_spec(),
    )(message, arrived)
    kept = [finished] + [from_step(finished, "ta", t) for t in range(1, times)]
    other = [from_partner(block, "gx", 1) for block in kept]
    split = own_ops % 2 == 0
    now_ops = own_ops // 2 if split else own_ops
    sums_shape = (2 * now_ops, 32, vectors)
    scratch = [
        pltpu.VMEM((2 * now_ops * vectors, 2 * vectors), bf16),
        pltpu.VMEM((2 * vectors, 2 * now_ops * vectors), bf16),
    ]
    sums = []
    if split:
        sums = [
            local_call(
                functools.partial(first_contract_kernel, times),
                "first_contraction",
                jax.ShapeDtypeStruct(sums_shape, f32),
                [vmem_spec()] * (2 + times),
                vmem_spec(),
                scratch,
            )(weights, perams[0], *kept)
        ]
    margins, correlators = local_call(
        functools.partial(second_contract_kernel, times, split),
        "second_contraction",
        (
            jax.ShapeDtypeStruct((1, own_rows, vectors), f32),
            jax.ShapeDtypeStruct((1, own_ops, 2), f32),
        ),
        [vmem_spec()] * (2 + 2 * times + len(sums)),
        (hbm_spec(), vmem_spec()),
        [pltpu.VMEM(sums_shape, f32)]
        + scratch
        + [pltpu.VMEM((2, half, vectors), f32), pltpu.SemaphoreType.DMA((2,))],
    )(weights, perams[0], *kept, *other, *sums)
    return (margins.reshape(1, own_ops, 2, vectors, vectors), correlators)


def solution(mesh):
    placed = (
        P("ta", "gx", "gy", None, None, None, None),
        P("ta", "gx", "gy", None, None, None, None, None),
        P(),
        P(),
        P(("ta", "gx"), None, None, None),
        P(("ta", "gx"), None),
        P(("ta", "gx")),
    )
    return jax.shard_map(
        per_device,
        mesh=mesh,
        in_specs=placed,
        out_specs=(P("ta", "gy", None, None, None), P(("ta", "gx"), "gy", None)),
        check_vma=False,
    )
```

```python
import functools
import math

import jax
import jax.numpy as jnp
import numpy as np
from jax import lax
from jax.experimental import pallas as pl
from jax.experimental.pallas import tpu as pltpu
from jax.sharding import PartitionSpec as P

VMEM_LIMIT = 24 * 1024 * 1024
MOMENTA = 3
LINK_COLS = 54
TAIL = 16
FIXED_BITS = 14.0


def wave_constants(cells_z):
    z_row = np.arange(3 * cells_z) // 3
    columns = []
    for ahead in range(2):
        for momentum in range(MOMENTA):
            angle = 2.0 * math.pi * momentum * ((z_row + ahead) % cells_z) / cells_z
            columns.append(np.cos(angle))
            columns.append(np.sin(angle))
    left = np.stack(columns, axis=1).astype(np.float32)
    terms = []
    for _ in range(3):
        term = left.astype(jnp.bfloat16).astype(np.float32)
        terms.append(term)
        left = left - term
    return jnp.asarray(np.concatenate(terms, axis=1), jnp.bfloat16)


def iota(shape, axis):
    return lax.broadcasted_iota(jnp.int32, shape, axis)


def third(x):
    return (x * 21846) >> 16


def one_hot(condition):
    return condition.astype(jnp.float32).astype(jnp.bfloat16)


def planar_order(order):
    row, col = iota((order, order), 0), iota((order, order), 1)
    half = order // 2
    source = jnp.where(row < half, 2 * row, 2 * (row - half) + 1)
    return one_hot(col == source)


def side_by_side(planar):
    half = planar.shape[0] // 2
    return jnp.concatenate([planar[:half], planar[half:]], axis=1).astype(jnp.bfloat16)


def transport(matrix, pair, sign):
    half, vectors = matrix.shape[0] // 2, pair.shape[1] // 2
    parts = jnp.dot(matrix, pair, preferred_element_type=jnp.float32)
    real, imag = parts[:half], parts[half:]
    if sign > 0:
        return jnp.concatenate(
            [real[:, :vectors] - imag[:, vectors:], real[:, vectors:] + imag[:, :vectors]], axis=0
        )
    return jnp.concatenate(
        [real[:, :vectors] + imag[:, vectors:], real[:, vectors:] - imag[:, :vectors]], axis=0
    )


def halo_fields(cells_x, cells_y):
    pairs = [(0, (cells_x - 1) * cells_y + y) for y in range(cells_y)]
    return pairs + [(1, x * cells_y + cells_y - 1) for x in range(cells_x)]


def local_fields(cells_x, cells_y):
    lines = cells_x * cells_y
    outside = halo_fields(cells_x, cells_y)
    every = [(code, line) for code in range(7) for line in range(lines)]
    return [pair for pair in every if pair not in outside]


def prepare_kernel(cells_x, cells_y, *refs):
    inputs, refs = refs[:6], refs[6:]
    matrix_ref, local_ref, left_ref, phase_ref, weight_ref = refs[:5]
    held, link_rows_ref, sems = refs[5:11], refs[11], refs[12]
    copies = [
        pltpu.make_async_copy(src, dst, sems.at[k])
        for k, (src, dst) in enumerate(zip(inputs, held))
    ]
    for copy in copies:
        copy.start()
    v_ref, link_ref, dirs_ref, moms_ref, waves_ref, pair_ref = held
    f32, bf16 = jnp.float32, jnp.bfloat16
    order, vectors = v_ref.shape[2], v_ref.shape[3]
    half, cells_z = order // 2, order // 6
    lines = cells_x * cells_y
    times = weight_ref.shape[1]
    spread = one_hot(third(iota((half, cells_z), 0)) == iota((half, cells_z), 1))
    row, col = iota((half, LINK_COLS), 0), iota((half, LINK_COLS), 1)
    row_color = row - 3 * third(row)
    pair_at = third(col >> 1)
    col_in, col_out = (col >> 1) - 3 * pair_at, pair_at - 3 * third(pair_at)
    pick = [(row_color == col_out).astype(f32), (row_color == col_in).astype(f32)]
    wide = (LINK_COLS, 6 * 128)
    row, col = iota(wide, 0), iota(wide, 1)
    block, place = col >> 7, col & 127
    color = place - 3 * third(place)
    pair_at = third(row >> 1)
    row_in, row_out = (row >> 1) - 3 * pair_at, pair_at - 3 * third(pair_at)
    fits = 2 * third(pair_at) + (row & 1) == block
    expand = [one_hot(fits & (row_in == color)), one_hot(fits & (row_out == color))]
    row, col = iota((half, 128), 0), iota((half, 128), 1)
    near = ((third(row) == third(col)) & (col < half)).astype(f32)
    planar = planar_order(order)
    for copy in copies:
        copy.wait()
    for t in range(times):
        sink = pair_ref[0, 0] == t
        source = pair_ref[0, 1] == t
        weight_ref[0, t] = jnp.full(weight_ref.shape[2:], jnp.where(sink, 1.0, 0.0), f32)
        weight_ref[1, t] = jnp.full(weight_ref.shape[2:], jnp.where(source, 1.0, 0.0), f32)
    for line in range(lines):
        for k in range(LINK_COLS // 2):
            link_rows_ref[line, 2 * k : 2 * k + 2] = link_ref[line, k].astype(f32)
    outside = halo_fields(cells_x, cells_y)
    inside = local_fields(cells_x, cells_y)
    ordered = []
    for line in range(lines):
        here = jnp.dot(
            planar, v_ref[line // cells_y, line % cells_y], preferred_element_type=f32
        )
        ordered.append(here)
        local_ref[inside.index((6, line))] = here
    for line in range(lines):
        here = ordered[line]
        ahead_z = jnp.concatenate(
            [here[3:half], here[:3], here[half + 3 :], here[half : half + 3]], axis=0
        )
        columns = slice(line * order, (line + 1) * order)
        left_ref[0, :, columns] = here.T.astype(bf16)
        left_ref[1, :, columns] = ahead_z.T.astype(bf16)
        seen = lax.dot_general(
            spread,
            link_rows_ref[line].astype(bf16),
            (((1,), (1,)), ((), ())),
            preferred_element_type=f32,
        )
        pair = side_by_side(here)
        for way in range(2):
            blocks = jnp.dot(
                (seen * pick[way]).astype(bf16), expand[way], preferred_element_type=f32
            )
            for d in range(3):
                matrix = jnp.concatenate(
                    [
                        blocks[:, 256 * d : 256 * d + 128] * near,
                        blocks[:, 256 * d + 128 : 256 * d + 256] * near,
                    ],
                    axis=0,
                ).astype(bf16)
                if way == 1:
                    carried = transport(matrix[:, :half], pair, -1)
                    local_ref[inside.index((3 + d, line))] = carried.astype(bf16).astype(f32)
                elif (d, line) in outside:
                    matrix_ref[outside.index((d, line))] = matrix
                else:
                    ahead = ahead_z if d == 2 else ordered[line + (cells_y if d == 0 else 1)]
                    local_ref[inside.index((d, line))] = transport(
                        matrix[:, :half], side_by_side(ahead), 1
                    )
    wave_cols = waves_ref.shape[1]
    per_term = wave_cols // 3
    row, col = iota((wave_cols, 2 * vectors), 0), iota((wave_cols, 2 * vectors), 1)
    term = (row >= per_term).astype(jnp.int32) + (row >= 2 * per_term).astype(jnp.int32)
    wave_at = row - per_term * term - (col >= vectors).astype(jnp.int32)
    for o in range(phase_ref.shape[0]):
        column = 2 * (jnp.where(dirs_ref[o] == 5, MOMENTA, 0) + moms_ref[o])
        phase_ref[o] = jnp.dot(
            waves_ref[...], one_hot(wave_at == column), preferred_element_type=f32
        )


def low_bit(j):
    return (j & -j).bit_length() - 1


def parts_of_product(side, pair):
    vectors = pair.shape[1] // 2
    product = jnp.dot(side, pair, preferred_element_type=jnp.float32)
    return [product[:, :vectors], product[:, vectors:]]


def put_product(out_ref, place, i, side, pair):
    for k, block in enumerate(parts_of_product(side, pair)):
        rows = block.shape[0]
        out_ref[place, (2 * i + k) * rows : (2 * i + k + 1) * rows] = block


def first_groups(groups):
    return sorted((j for j in range(groups) if j & 2), key=lambda j: -(j & 1))


def second_groups(groups):
    return sorted((j for j in range(groups) if not j & 2), key=lambda j: -(j & 1))


def first_margin_kernel(cells_x, cells_y, groups, own_ops, *refs):
    matrix_ref, local_ref, left_ref, phase_ref, halo_x_ref, halo_y_ref, dirs_hbm = refs[:7]
    swap_ref, hold_ref, later_side_ref, later_pair_ref = refs[7:11]
    field_ref, side_ref, dirs_ref, sem = refs[11:]
    f32, bf16 = jnp.float32, jnp.bfloat16
    copy = pltpu.make_async_copy(dirs_hbm, dirs_ref, sem)
    copy.start()
    lines = cells_x * cells_y
    order, vectors = halo_x_ref.shape[2], halo_x_ref.shape[3]
    half = order // 2
    planar = planar_order(order)
    side_ref[0] = left_ref[0]
    side_ref[3] = left_ref[1]
    outside = halo_fields(cells_x, cells_y)
    for d in range(2):
        for line in range(lines):
            x, y = line // cells_y, line % cells_y
            columns = slice(line * order, (line + 1) * order)
            if (d, line) not in outside:
                ahead = line + (cells_y if d == 0 else 1)
                side_ref[1 + d, :, columns] = left_ref[0, :, ahead * order : (ahead + 1) * order]
                continue
            halo = halo_x_ref[0, y] if d == 0 else halo_y_ref[x, 0]
            ahead = jnp.dot(planar, halo, preferred_element_type=f32)
            side_ref[1 + d, :, columns] = ahead.T.astype(bf16)
            matrix = matrix_ref[outside.index((d, line))]
            field_ref[d, line] = transport(matrix[:, :half], side_by_side(ahead), 1)
    for k, (code, line) in enumerate(local_fields(cells_x, cells_y)):
        field_ref[code, line] = local_ref[k]
    copy.wait()
    me = lax.axis_index("gy")
    later = 0
    for j in first_groups(groups) + second_groups(groups):
        for i in range(own_ops):
            o = (me ^ j) * own_ops + i
            code = dirs_ref[o]
            side = jnp.where((code >= 3) & (code < 6), code - 2, 0)
            cosine = phase_ref[o, :, 0:vectors]
            sine = phase_ref[o, :, vectors : 2 * vectors]
            pairs = []
            for line in range(lines):
                real, imag = field_ref[code, line, 0:half], field_ref[code, line, half:order]
                turned_r, turned_i = cosine * real - sine * imag, sine * real + cosine * imag
                pairs.append(jnp.concatenate([turned_r, turned_i], axis=1))
                pairs.append(jnp.concatenate([turned_i, -turned_r], axis=1))
            pair = jnp.concatenate(pairs, axis=0).astype(bf16)
            if j & 2:
                put_product(swap_ref if j & 1 else hold_ref, j >> 2, i, side_ref[side], pair)
            else:
                later_side_ref[later] = side_ref[side]
                later_pair_ref[later] = pair
                later += 1


def second_margin_kernel(groups, own_ops, side_ref, pair_ref, swap_ref, *hold_refs):
    later = 0
    for j in second_groups(groups):
        level = low_bit(j) if j else groups.bit_length() - 1
        for i in range(own_ops):
            out_ref, place = (swap_ref, j >> 2) if j & 1 else (hold_refs[level - 2], j >> (level + 1))
            put_product(out_ref, place, i, side_ref[later], pair_ref[later])
            later += 1


def scale_of(block):
    top = jnp.max(jnp.abs(block), axis=0, keepdims=True)
    return jnp.floor(jnp.log2(jnp.maximum(top, 1e-30))) + 1.0


def put_fixed(out_ref, blocks):
    rows, vectors = blocks[0].shape
    tail = iota((TAIL, vectors), 0)
    scales = jnp.zeros((TAIL, vectors), jnp.float32)
    for k, block in enumerate(blocks):
        scale = scale_of(block)
        scales = jnp.where(tail == k, scale, scales)
        fixed = jnp.floor(block * jnp.exp2(FIXED_BITS - scale) + 0.5)
        out_ref[k * rows : (k + 1) * rows] = fixed.astype(jnp.int32).astype(jnp.int16)
    out_ref[len(blocks) * rows :] = scales.astype(jnp.int32).astype(jnp.int16)


def from_fixed(ref, rows, k):
    scales = ref[ref.shape[0] - TAIL :].astype(jnp.int32).astype(jnp.float32)
    block = ref[k * rows : (k + 1) * rows].astype(jnp.int32).astype(jnp.float32)
    return block * jnp.exp2(scales[k : k + 1] - FIXED_BITS)


def group_block(held_ref, swapped_ref, messages, k, j, start, rows):
    span = pl.ds(start, rows)
    total = held_ref[k, span] + swapped_ref[j >> 2, span]
    for b, ref in enumerate(messages, 1):
        total = total + fixed_at(ref.at[j >> (b + 1)], start, rows)
    return total


def fixed_at(ref, start, rows):
    tail = ref[ref.shape[0] - TAIL :].astype(jnp.int32).astype(jnp.float32)
    scale = jnp.max(
        jnp.where(iota(tail.shape, 0) == start // rows, tail, -1000.0), axis=0, keepdims=True
    )
    block = ref[pl.ds(start, rows)].astype(jnp.int32).astype(jnp.float32)
    return block * jnp.exp2(scale - FIXED_BITS)


def fold_kernel(level, vectors, held_ref, swapped_ref, *refs):
    messages, out_ref = refs[:-1], refs[-1]
    for k in range(held_ref.shape[0]):
        blocks = [
            group_block(held_ref, swapped_ref, messages, k, (2 * k + 1) << level, start, vectors)
            for start in range(0, held_ref.shape[1], vectors)
        ]
        put_fixed(out_ref.at[k], blocks)


def half_rows(rows, vectors, kept):
    me = lax.axis_index("gx") & 1
    half = rows // 2
    base = pl.multiple_of((me if kept else 1 - me) * half, half)
    return [base + step for step in range(0, half, vectors)]


def fold_halves_kernel(level, vectors, held_ref, swapped_ref, *refs):
    messages, outs = refs[:-2], refs[-2:]
    group = 1 << level
    for kept, out_ref in enumerate(outs):
        starts = half_rows(held_ref.shape[1], vectors, kept)
        put_fixed(
            out_ref,
            [group_block(held_ref, swapped_ref, messages, 0, group, s, vectors) for s in starts],
        )


def half_kernel(levels, vectors, kept, own_ref, swapped_ref, *refs):
    messages, came, out_ref = refs[: levels - 2], refs[levels - 2 : -1], refs[-1]
    blocks = []
    for p, start in enumerate(half_rows(own_ref.shape[1], vectors, kept)):
        total = group_block(own_ref, swapped_ref, messages, 0, 0, start, vectors)
        for ref in came:
            total = total + from_fixed(ref, vectors, p)
        blocks.append(total)
    put_fixed(out_ref, blocks)


def both_kernel(vectors, norm_factor, own_ref, arrived_ref, out_ref):
    blocks = [
        from_fixed(own_ref, vectors, p) + from_fixed(arrived_ref, vectors, p)
        for p in range((own_ref.shape[0] - TAIL) // vectors)
    ]
    if norm_factor is None:
        put_fixed(out_ref, blocks)
        return
    for p, block in enumerate(blocks):
        out_ref[p * vectors : (p + 1) * vectors] = (block * norm_factor).astype(out_ref.dtype)


def contract(sums_ref, weight_ref, blocks, tau_ref, left_ref, right_ref):
    f32, bf16 = jnp.float32, jnp.bfloat16
    vectors = sums_ref.shape[2]
    count_ops = sums_ref.shape[0] // 2
    order = tau_ref.shape[2]
    spins = order // vectors
    me_t = lax.axis_index("ta")
    times = len(blocks)

    def chosen(end, k):
        total = jnp.zeros((vectors // 8, 8, vectors), f32)
        for t in range(times):
            weight = weight_ref[end, lax.rem(me_t + t, times)]
            total = total + blocks[t](k).astype(f32).reshape(total.shape) * weight
        return total.reshape(vectors, vectors)

    for o in range(count_ops):
        first = 2 * o * vectors
        a_r, a_i = chosen(0, 2 * o).astype(bf16), chosen(0, 2 * o + 1).astype(bf16)
        b_r, b_i = chosen(1, 2 * o).T.astype(bf16), chosen(1, 2 * o + 1).T.astype(bf16)
        real, imag = slice(first, first + vectors), slice(first + vectors, first + 2 * vectors)
        left_ref[real, 0:vectors] = a_r
        left_ref[real, vectors:] = -a_i
        left_ref[imag, 0:vectors] = a_i
        left_ref[imag, vectors:] = a_r
        right_ref[0:vectors, real] = b_r
        right_ref[0:vectors, imag] = -b_i
        right_ref[vectors:, real] = b_i
        right_ref[vectors:, imag] = b_r
    lanes = sums_ref.shape[1]
    fold = lambda t: jnp.sum(t.reshape(vectors // lanes, lanes, vectors), axis=0)
    sums = [jnp.zeros((lanes, vectors), f32) for _ in range(2 * count_ops)]
    for s in range(spins):
        rows = slice(s * vectors, (s + 1) * vectors)
        x = jnp.dot(
            left_ref[...],
            jnp.concatenate([tau_ref[0, rows], tau_ref[1, rows]], axis=0),
            preferred_element_type=f32,
        )
        for c in range(spins):
            cols = slice(c * vectors, (c + 1) * vectors)
            y = jnp.dot(
                jnp.concatenate([tau_ref[0, rows, cols], tau_ref[1, rows, cols]], axis=1),
                right_ref[...],
                preferred_element_type=f32,
            )
            for o in range(count_ops):
                first = 2 * o * vectors
                x_r = x[first : first + vectors, cols]
                x_i = x[first + vectors : first + 2 * vectors, cols]
                y_r = y[:, first : first + vectors]
                y_i = y[:, first + vectors : first + 2 * vectors]
                sums[2 * o] = sums[2 * o] + fold(x_r * y_r + x_i * y_i)
                sums[2 * o + 1] = sums[2 * o + 1] + fold(x_i * y_r - x_r * y_i)
    for k, total in enumerate(sums):
        sums_ref[k] = total


def part_of(ref, vectors):
    return lambda k: ref[k * vectors : (k + 1) * vectors]


def first_contract_kernel(times, split, live_ref, weight_ref, tau_ref, *refs):
    blocks, (live_out_ref, sums_ref, left_ref, right_ref) = refs[:times], refs[times:]
    live = jnp.where(live_ref[0] > 0, 1.0, 0.0)
    live_out_ref[...] = jnp.full(live_out_ref.shape, live, jnp.float32)
    if split:
        vectors = sums_ref.shape[2]
        blocks = [part_of(ref, vectors) for ref in blocks]
        contract(sums_ref, weight_ref, blocks, tau_ref, left_ref, right_ref)
    else:
        sums_ref[...] = jnp.zeros_like(sums_ref)


def margins_kernel(kept_ref, other_ref, margin_ref):
    half = kept_ref.shape[0]
    me = lax.axis_index("gx") & 1
    for place, ref in ((me, kept_ref), (1 - me, other_ref)):
        rows = pl.ds(pl.multiple_of(place * half, half), half)
        margin_ref[0, rows] = ref[...].astype(jnp.float32)


def second_contract_kernel(times, split, weight_ref, tau_ref, *refs):
    kept, other, refs = refs[:times], refs[times : 2 * times], refs[2 * times :]
    live_ref, first_sums_ref, corr_ref, sums_ref, left_ref, right_ref = refs
    vectors = sums_ref.shape[2]
    half = kept[0].shape[0]
    me = lax.axis_index("gx") & 1
    parts_per_half = half // vectors

    def either(kept_ref, other_ref):
        def part(k):
            row = (k % parts_per_half) * vectors
            own, far = kept_ref[row : row + vectors], other_ref[row : row + vectors]
            mine = (k // parts_per_half == me).astype(jnp.float32)
            return own.astype(jnp.float32) * mine + far.astype(jnp.float32) * (1.0 - mine)

        return part

    blocks = [part_of(ref, vectors) for ref in other]
    if not split:
        blocks = [either(a, b) for a, b in zip(kept, other)]
    contract(sums_ref, weight_ref, blocks, tau_ref, left_ref, right_ref)
    now_ops = sums_ref.shape[0] // 2
    known = [(sums_ref, (1 - me) * now_ops)] if split else [(sums_ref, 0)]
    if split:
        known.append((first_sums_ref, me * now_ops))
    shape = corr_ref.shape[1:]
    row, col = iota(shape, 0), iota(shape, 1)
    result = jnp.zeros(shape, jnp.float32)
    for ref, first in known:
        for k in range(2 * now_ops):
            total = jnp.sum(jnp.sum(ref[k], axis=0, keepdims=True), axis=1, keepdims=True)
            here = (row == first + k // 2) & (col == k % 2)
            result = jnp.where(here, total * (1.0 / vectors), result)
    corr_ref[0] = result * live_ref[0 : shape[0], 0 : shape[1]]


def vmem_spec():
    return pl.BlockSpec(memory_space=pltpu.VMEM)


def smem_spec():
    return pl.BlockSpec(memory_space=pltpu.SMEM)


def hbm_spec():
    return pl.BlockSpec(memory_space=pltpu.HBM)


def in_hbm(x):
    return pltpu.with_memory_space_constraint(x, pltpu.HBM)


def local_call(body, name, outs, in_specs, out_specs, scratch=(), cost=None):
    return pl.pallas_call(
        body,
        out_shape=outs,
        in_specs=in_specs,
        out_specs=out_specs,
        scratch_shapes=list(scratch),
        compiler_params=pltpu.CompilerParams(vmem_limit_bytes=VMEM_LIMIT),
        cost_estimate=cost,
        name=name,
    )


def from_step(block, axis, step):
    count = lax.axis_size(axis)
    return lax.ppermute(block, axis, [((i + step) % count, i) for i in range(count)])


def from_partner(block, axis, step):
    count = lax.axis_size(axis)
    return lax.ppermute(block, axis, [(i ^ step, i) for i in range(count)])


def per_device(eigvecs, links, op_dirs, op_moms, perams, pair_times, slot_counts):
    f32, bf16 = jnp.float32, jnp.bfloat16
    _, cells_x, cells_y, cells_z, colors, _, vectors = eigvecs.shape
    order = cells_z * colors * 2
    lines = cells_x * cells_y
    count_ops = op_dirs.shape[0]
    times, shares, groups = lax.axis_size("ta"), lax.axis_size("gx"), lax.axis_size("gy")
    levels = groups.bit_length() - 1
    own_ops = count_ops // groups
    own_rows = own_ops * 2 * vectors
    field = eigvecs.reshape(cells_x, cells_y, order, vectors)
    halo_x = from_step(field[0:1], "gx", 1)
    halo_y = from_step(field, "gy", 1)
    link_field = links[0].transpose(0, 1, 3, 5, 6, 4, 2).reshape(lines, 27, 2, cells_z)
    outside, inside = halo_fields(cells_x, cells_y), local_fields(cells_x, cells_y)
    inputs = [field, link_field, op_dirs, op_moms, wave_constants(cells_z), pair_times]
    inputs = [in_hbm(x) for x in inputs]
    held = [
        pltpu.SMEM(x.shape, x.dtype) if x.dtype == jnp.int32 else pltpu.VMEM(x.shape, x.dtype)
        for x in inputs
    ]
    matrices, local, left, phases, weights = local_call(
        functools.partial(prepare_kernel, cells_x, cells_y),
        "prepare_lines",
        (
            jax.ShapeDtypeStruct((len(outside), order, 128), bf16),
            jax.ShapeDtypeStruct((len(inside), order, vectors), f32),
            jax.ShapeDtypeStruct((2, vectors, lines * order), bf16),
            jax.ShapeDtypeStruct((count_ops, order // 2, 2 * vectors), f32),
            jax.ShapeDtypeStruct((2, times, 8, vectors), f32),
        ),
        [hbm_spec()] * len(inputs),
        (vmem_spec(),) * 5,
        held
        + [
            pltpu.VMEM((lines, LINK_COLS, cells_z), f32),
            pltpu.SemaphoreType.DMA((len(inputs),)),
        ],
    )(*inputs)
    part = lambda count: jax.ShapeDtypeStruct((count, own_rows, vectors), f32)
    later = count_ops // 2
    swap_a, hold_a, later_sides, later_pairs = local_call(
        functools.partial(first_margin_kernel, cells_x, cells_y, groups, own_ops),
        "first_margins",
        (
            part(groups // 4),
            part(groups // 4),
            jax.ShapeDtypeStruct((later, vectors, lines * order), bf16),
            jax.ShapeDtypeStruct((later, lines * order, 2 * vectors), bf16),
        ),
        [vmem_spec()] * 6 + [hbm_spec()],
        (vmem_spec(),) * 4,
        [
            pltpu.VMEM((7, lines, order, vectors), f32),
            pltpu.VMEM((4, vectors, lines * order), bf16),
            pltpu.SMEM((count_ops,), jnp.int32),
            pltpu.SemaphoreType.DMA,
        ],
    )(matrices, local, left, phases, halo_x, halo_y, in_hbm(op_dirs))
    swapped_a = from_partner(swap_a, "gy", 1)
    held_shapes = [part(groups >> (b + 1)) for b in range(2, levels)] + [part(1)]
    swap_b, *held = local_call(
        functools.partial(second_margin_kernel, groups, own_ops),
        "second_margins",
        (part(groups // 4), *held_shapes),
        [vmem_spec()] * 2,
        (vmem_spec(),) * (1 + len(held_shapes)),
        cost=pl.CostEstimate(
            flops=later * 4 * lines * order * vectors * vectors,
            bytes_accessed=later * 6 * lines * order * vectors + later * 8 * vectors * vectors,
            transcendentals=0,
        ),
    )(later_sides, later_pairs)
    swapped_b = from_partner(swap_b, "gy", 1)

    def packed(body, name, *inputs, rows=own_rows, lead=(), count=1):
        shape = jax.ShapeDtypeStruct((*lead, rows + TAIL, vectors), jnp.int16)
        outs = shape if count == 1 else (shape,) * count
        specs = vmem_spec() if count == 1 else (vmem_spec(),) * count
        return local_call(body, name, outs, [vmem_spec()] * len(inputs), specs)(*inputs)

    half = own_rows // 2
    messages = []
    for b in range(1, levels):
        inputs = (hold_a, swapped_a) if b == 1 else (held[b - 2], swapped_b, *messages)
        if b < levels - 1:
            body = functools.partial(fold_kernel, b, vectors)
            sent = packed(body, "fold_groups", *inputs, lead=inputs[0].shape[:1])
            messages.append(from_partner(sent, "gy", 1 << b))
            continue
        body = functools.partial(fold_halves_kernel, b, vectors)
        away, kept = packed(body, "fold_halves", *inputs, rows=half, count=2)
        away, kept = from_partner(away, "gy", 1 << b), from_partner(kept, "gy", 1 << b)
    inputs = (held[-1], swapped_b, *messages)
    body = functools.partial(half_kernel, levels, vectors, False)
    arrived = from_partner(packed(body, "send_half", *inputs, away, rows=half), "gx", 1)
    body = functools.partial(half_kernel, levels, vectors, True)
    message = packed(body, "keep_half", *inputs, kept, arrived, rows=half)
    norm_factor = 1.0 / math.sqrt(3.0 * cells_x * shares * cells_y * groups * cells_z)
    step = 2
    while step < shares:
        arrived = from_partner(message, "gx", step)
        step *= 2
        if step < shares:
            body = functools.partial(both_kernel, vectors, None)
            message = packed(body, "sum_both", message, arrived, rows=half)
    finished = local_call(
        functools.partial(both_kernel, vectors, norm_factor),
        "finish_half",
        jax.ShapeDtypeStruct((half, vectors), bf16),
        [vmem_spec()] * 2,
        vmem_spec(),
    )(message, arrived)
    kept = [finished] + [from_step(finished, "ta", t) for t in range(1, times)]
    other = [from_partner(block, "gx", 1) for block in kept]
    split = own_ops % 2 == 0
    now_ops = own_ops // 2 if split else own_ops
    sums_shape = (2 * now_ops, 32, vectors)
    scratch = [
        pltpu.VMEM((2 * now_ops * vectors, 2 * vectors), bf16),
        pltpu.VMEM((2 * vectors, 2 * now_ops * vectors), bf16),
    ]
    margins = local_call(
        margins_kernel,
        "margins_out",
        jax.ShapeDtypeStruct((1, own_rows, vectors), f32),
        [vmem_spec()] * 2,
        vmem_spec(),
    )(kept[0], other[0])
    live, sums = local_call(
        functools.partial(first_contract_kernel, times, split),
        "first_contraction",
        (jax.ShapeDtypeStruct((8, vectors), f32), jax.ShapeDtypeStruct(sums_shape, f32)),
        [smem_spec()] + [vmem_spec()] * (2 + times),
        (vmem_spec(),) * 2,
        scratch,
    )(slot_counts, weights, perams[0], *kept)
    correlators = local_call(
        functools.partial(second_contract_kernel, times, split),
        "second_contraction",
        jax.ShapeDtypeStruct((1, own_ops, 2), f32),
        [vmem_spec()] * (4 + 2 * times),
        vmem_spec(),
        [pltpu.VMEM(sums_shape, f32)] + scratch,
    )(weights, perams[0], *kept, *other, live, sums)
    return (margins.reshape(1, own_ops, 2, vectors, vectors), correlators)


def solution(mesh):
    placed = (
        P("ta", "gx", "gy", None, None, None, None),
        P("ta", "gx", "gy", None, None, None, None, None),
        P(),
        P(),
        P(("ta", "gx"), None, None, None),
        P(("ta", "gx"), None),
        P(("ta", "gx")),
    )
    return jax.shard_map(
        per_device,
        mesh=mesh,
        in_specs=placed,
        out_specs=(P("ta", "gy", None, None, None), P(("ta", "gx"), "gy", None)),
        check_vma=False,
    )
```

```python
import functools
import math

import jax
import jax.numpy as jnp
import numpy as np
from jax import lax
from jax.experimental import pallas as pl
from jax.experimental.pallas import tpu as pltpu
from jax.sharding import PartitionSpec as P

VMEM_LIMIT = 24 * 1024 * 1024
MOMENTA = 3
LINK_COLS = 54
TAIL = 16
FIXED_BITS = 14.0


def wave_constants(cells_z):
    z_row = np.arange(3 * cells_z) // 3
    columns = []
    for ahead in range(2):
        for momentum in range(MOMENTA):
            angle = 2.0 * math.pi * momentum * ((z_row + ahead) % cells_z) / cells_z
            columns.append(np.cos(angle))
            columns.append(np.sin(angle))
    left = np.stack(columns, axis=1).astype(np.float32)
    terms = []
    for _ in range(3):
        term = left.astype(jnp.bfloat16).astype(np.float32)
        terms.append(term)
        left = left - term
    return jnp.asarray(np.concatenate(terms, axis=1), jnp.bfloat16)


def iota(shape, axis):
    return lax.broadcasted_iota(jnp.int32, shape, axis)


def third(x):
    return (x * 21846) >> 16


def one_hot(condition):
    return condition.astype(jnp.float32).astype(jnp.bfloat16)


def planar_order(order):
    row, col = iota((order, order), 0), iota((order, order), 1)
    half = order // 2
    source = jnp.where(row < half, 2 * row, 2 * (row - half) + 1)
    return one_hot(col == source)


def side_by_side(planar):
    half = planar.shape[0] // 2
    return jnp.concatenate([planar[:half], planar[half:]], axis=1).astype(jnp.bfloat16)


def transport(matrix, pair, sign):
    half, vectors = matrix.shape[0] // 2, pair.shape[1] // 2
    parts = jnp.dot(matrix, pair, preferred_element_type=jnp.float32)
    real, imag = parts[:half], parts[half:]
    if sign > 0:
        return jnp.concatenate(
            [real[:, :vectors] - imag[:, vectors:], real[:, vectors:] + imag[:, :vectors]], axis=0
        )
    return jnp.concatenate(
        [real[:, :vectors] + imag[:, vectors:], real[:, vectors:] - imag[:, :vectors]], axis=0
    )


def halo_fields(cells_x, cells_y):
    pairs = [(0, (cells_x - 1) * cells_y + y) for y in range(cells_y)]
    return pairs + [(1, x * cells_y + cells_y - 1) for x in range(cells_x)]


def local_fields(cells_x, cells_y):
    lines = cells_x * cells_y
    outside = halo_fields(cells_x, cells_y)
    every = [(code, line) for code in range(7) for line in range(lines)]
    return [pair for pair in every if pair not in outside]


def prepare_kernel(cells_x, cells_y, *refs):
    inputs, refs = refs[:6], refs[6:]
    matrix_ref, local_ref, left_ref, phase_ref, weight_ref = refs[:5]
    held, link_rows_ref, sems = refs[5:11], refs[11], refs[12]
    copies = [
        pltpu.make_async_copy(src, dst, sems.at[k])
        for k, (src, dst) in enumerate(zip(inputs, held))
    ]
    for copy in copies:
        copy.start()
    v_ref, link_ref, dirs_ref, moms_ref, waves_ref, pair_ref = held
    f32, bf16 = jnp.float32, jnp.bfloat16
    order, vectors = v_ref.shape[2], v_ref.shape[3]
    half, cells_z = order // 2, order // 6
    lines = cells_x * cells_y
    times = weight_ref.shape[1]
    spread = one_hot(third(iota((half, cells_z), 0)) == iota((half, cells_z), 1))
    row, col = iota((half, LINK_COLS), 0), iota((half, LINK_COLS), 1)
    row_color = row - 3 * third(row)
    pair_at = third(col >> 1)
    col_in, col_out = (col >> 1) - 3 * pair_at, pair_at - 3 * third(pair_at)
    pick = [(row_color == col_out).astype(f32), (row_color == col_in).astype(f32)]
    wide = (LINK_COLS, 6 * 128)
    row, col = iota(wide, 0), iota(wide, 1)
    block, place = col >> 7, col & 127
    color = place - 3 * third(place)
    pair_at = third(row >> 1)
    row_in, row_out = (row >> 1) - 3 * pair_at, pair_at - 3 * third(pair_at)
    fits = 2 * third(pair_at) + (row & 1) == block
    expand = [one_hot(fits & (row_in == color)), one_hot(fits & (row_out == color))]
    row, col = iota((half, 128), 0), iota((half, 128), 1)
    near = ((third(row) == third(col)) & (col < half)).astype(f32)
    planar = planar_order(order)
    for copy in copies:
        copy.wait()
    for t in range(times):
        sink = pair_ref[0, 0] == t
        source = pair_ref[0, 1] == t
        weight_ref[0, t] = jnp.full(weight_ref.shape[2:], jnp.where(sink, 1.0, 0.0), f32)
        weight_ref[1, t] = jnp.full(weight_ref.shape[2:], jnp.where(source, 1.0, 0.0), f32)
    for line in range(lines):
        for k in range(LINK_COLS // 2):
            link_rows_ref[line, 2 * k : 2 * k + 2] = link_ref[line, k].astype(f32)
    outside = halo_fields(cells_x, cells_y)
    inside = local_fields(cells_x, cells_y)
    ordered = []
    for line in range(lines):
        here = jnp.dot(
            planar, v_ref[line // cells_y, line % cells_y], preferred_element_type=f32
        )
        ordered.append(here)
        local_ref[inside.index((6, line))] = here
    for line in range(lines):
        here = ordered[line]
        ahead_z = jnp.concatenate(
            [here[3:half], here[:3], here[half + 3 :], here[half : half + 3]], axis=0
        )
        columns = slice(line * order, (line + 1) * order)
        left_ref[0, :, columns] = here.T.astype(bf16)
        left_ref[1, :, columns] = ahead_z.T.astype(bf16)
        seen = lax.dot_general(
            spread,
            link_rows_ref[line].astype(bf16),
            (((1,), (1,)), ((), ())),
            preferred_element_type=f32,
        )
        pair = side_by_side(here)
        for way in range(2):
            blocks = jnp.dot(
                (seen * pick[way]).astype(bf16), expand[way], preferred_element_type=f32
            )
            for d in range(3):
                matrix = jnp.concatenate(
                    [
                        blocks[:, 256 * d : 256 * d + 128] * near,
                        blocks[:, 256 * d + 128 : 256 * d + 256] * near,
                    ],
                    axis=0,
                ).astype(bf16)
                if way == 1:
                    carried = transport(matrix[:, :half], pair, -1)
                    local_ref[inside.index((3 + d, line))] = carried.astype(bf16).astype(f32)
                elif (d, line) in outside:
                    matrix_ref[outside.index((d, line))] = matrix
                else:
                    ahead = ahead_z if d == 2 else ordered[line + (cells_y if d == 0 else 1)]
                    local_ref[inside.index((d, line))] = transport(
                        matrix[:, :half], side_by_side(ahead), 1
                    )
    wave_cols = waves_ref.shape[1]
    per_term = wave_cols // 3
    row, col = iota((wave_cols, 2 * vectors), 0), iota((wave_cols, 2 * vectors), 1)
    term = (row >= per_term).astype(jnp.int32) + (row >= 2 * per_term).astype(jnp.int32)
    wave_at = row - per_term * term - (col >= vectors).astype(jnp.int32)
    for o in range(phase_ref.shape[0]):
        column = 2 * (jnp.where(dirs_ref[o] == 5, MOMENTA, 0) + moms_ref[o])
        phase_ref[o] = jnp.dot(
            waves_ref[...], one_hot(wave_at == column), preferred_element_type=f32
        )


def low_bit(j):
    return (j & -j).bit_length() - 1


def parts_of_product(side, pair):
    vectors = pair.shape[1] // 2
    product = jnp.dot(side, pair, preferred_element_type=jnp.float32)
    return [product[:, :vectors], product[:, vectors:]]


def put_product(out_ref, place, i, side, pair):
    for k, block in enumerate(parts_of_product(side, pair)):
        rows = block.shape[0]
        out_ref[place, (2 * i + k) * rows : (2 * i + k + 1) * rows] = block


def first_groups(groups):
    return sorted((j for j in range(groups) if j & 2), key=lambda j: -(j & 1))


def second_groups(groups):
    return sorted((j for j in range(groups) if not j & 2), key=lambda j: -(j & 1))


def first_margin_kernel(cells_x, cells_y, groups, own_ops, *refs):
    matrix_ref, local_ref, left_ref, phase_ref, halo_x_ref, halo_y_ref, dirs_hbm = refs[:7]
    swap_ref, hold_ref, later_side_ref, later_pair_ref = refs[7:11]
    field_ref, side_ref, dirs_ref, sem = refs[11:]
    f32, bf16 = jnp.float32, jnp.bfloat16
    copy = pltpu.make_async_copy(dirs_hbm, dirs_ref, sem)
    copy.start()
    lines = cells_x * cells_y
    order, vectors = halo_x_ref.shape[2], halo_x_ref.shape[3]
    half = order // 2
    planar = planar_order(order)
    side_ref[0] = left_ref[0]
    side_ref[3] = left_ref[1]
    outside = halo_fields(cells_x, cells_y)
    for d in range(2):
        for line in range(lines):
            x, y = line // cells_y, line % cells_y
            columns = slice(line * order, (line + 1) * order)
            if (d, line) not in outside:
                ahead = line + (cells_y if d == 0 else 1)
                side_ref[1 + d, :, columns] = left_ref[0, :, ahead * order : (ahead + 1) * order]
                continue
            halo = halo_x_ref[0, y] if d == 0 else halo_y_ref[x, 0]
            ahead = jnp.dot(planar, halo, preferred_element_type=f32)
            side_ref[1 + d, :, columns] = ahead.T.astype(bf16)
            matrix = matrix_ref[outside.index((d, line))]
            field_ref[d, line] = transport(matrix[:, :half], side_by_side(ahead), 1)
    for k, (code, line) in enumerate(local_fields(cells_x, cells_y)):
        field_ref[code, line] = local_ref[k]
    copy.wait()
    me = lax.axis_index("gy")
    later = 0
    for j in first_groups(groups) + second_groups(groups):
        for i in range(own_ops):
            o = (me ^ j) * own_ops + i
            code = dirs_ref[o]
            side = jnp.where((code >= 3) & (code < 6), code - 2, 0)
            cosine = phase_ref[o, :, 0:vectors]
            sine = phase_ref[o, :, vectors : 2 * vectors]
            pairs = []
            for line in range(lines):
                real, imag = field_ref[code, line, 0:half], field_ref[code, line, half:order]
                turned_r, turned_i = cosine * real - sine * imag, sine * real + cosine * imag
                pairs.append(jnp.concatenate([turned_r, turned_i], axis=1))
                pairs.append(jnp.concatenate([turned_i, -turned_r], axis=1))
            pair = jnp.concatenate(pairs, axis=0).astype(bf16)
            if j & 2:
                put_product(swap_ref if j & 1 else hold_ref, j >> 2, i, side_ref[side], pair)
            else:
                later_side_ref[later] = side_ref[side]
                later_pair_ref[later] = pair
                later += 1


def second_margin_kernel(groups, own_ops, side_ref, pair_ref, swap_ref, *hold_refs):
    later = 0
    for j in second_groups(groups):
        level = low_bit(j) if j else groups.bit_length() - 1
        for i in range(own_ops):
            out_ref, place = (swap_ref, j >> 2) if j & 1 else (hold_refs[level - 2], j >> (level + 1))
            put_product(out_ref, place, i, side_ref[later], pair_ref[later])
            later += 1


def scale_of(block):
    top = jnp.max(jnp.abs(block), axis=0, keepdims=True)
    return jnp.floor(jnp.log2(jnp.maximum(top, 1e-30))) + 1.0


def put_fixed(out_ref, blocks):
    rows, vectors = blocks[0].shape
    tail = iota((TAIL, vectors), 0)
    scales = jnp.zeros((TAIL, vectors), jnp.float32)
    for k, block in enumerate(blocks):
        scale = scale_of(block)
        scales = jnp.where(tail == k, scale, scales)
        fixed = jnp.floor(block * jnp.exp2(FIXED_BITS - scale) + 0.5)
        out_ref[k * rows : (k + 1) * rows] = fixed.astype(jnp.int32).astype(jnp.int16)
    out_ref[len(blocks) * rows :] = scales.astype(jnp.int32).astype(jnp.int16)


def from_fixed(ref, rows, k):
    scales = ref[ref.shape[0] - TAIL :].astype(jnp.int32).astype(jnp.float32)
    block = ref[k * rows : (k + 1) * rows].astype(jnp.int32).astype(jnp.float32)
    return block * jnp.exp2(scales[k : k + 1] - FIXED_BITS)


def group_block(held_ref, swapped_ref, messages, k, j, start, rows):
    span = pl.ds(start, rows)
    total = held_ref[k, span] + swapped_ref[j >> 2, span]
    for b, ref in enumerate(messages, 1):
        total = total + fixed_at(ref.at[j >> (b + 1)], start, rows)
    return total


def fixed_at(ref, start, rows):
    tail = ref[ref.shape[0] - TAIL :].astype(jnp.int32).astype(jnp.float32)
    scale = jnp.max(
        jnp.where(iota(tail.shape, 0) == start // rows, tail, -1000.0), axis=0, keepdims=True
    )
    block = ref[pl.ds(start, rows)].astype(jnp.int32).astype(jnp.float32)
    return block * jnp.exp2(scale - FIXED_BITS)


def fold_kernel(level, vectors, held_ref, swapped_ref, *refs):
    messages, out_ref = refs[:-1], refs[-1]
    for k in range(held_ref.shape[0]):
        blocks = [
            group_block(held_ref, swapped_ref, messages, k, (2 * k + 1) << level, start, vectors)
            for start in range(0, held_ref.shape[1], vectors)
        ]
        put_fixed(out_ref.at[k], blocks)


def half_rows(rows, vectors, kept):
    me = lax.axis_index("gx") & 1
    half = rows // 2
    base = pl.multiple_of((me if kept else 1 - me) * half, half)
    return [base + step for step in range(0, half, vectors)]


def fold_halves_kernel(level, vectors, held_ref, swapped_ref, *refs):
    messages, outs = refs[:-2], refs[-2:]
    group = 1 << level
    for kept, out_ref in enumerate(outs):
        starts = half_rows(held_ref.shape[1], vectors, kept)
        put_fixed(
            out_ref,
            [group_block(held_ref, swapped_ref, messages, 0, group, s, vectors) for s in starts],
        )


def half_kernel(levels, vectors, kept, own_ref, swapped_ref, *refs):
    messages, came, out_ref = refs[: levels - 2], refs[levels - 2 : -1], refs[-1]
    blocks = []
    for p, start in enumerate(half_rows(own_ref.shape[1], vectors, kept)):
        total = group_block(own_ref, swapped_ref, messages, 0, 0, start, vectors)
        for ref in came:
            total = total + from_fixed(ref, vectors, p)
        blocks.append(total)
    put_fixed(out_ref, blocks)


def both_kernel(vectors, norm_factor, own_ref, arrived_ref, out_ref):
    blocks = [
        from_fixed(own_ref, vectors, p) + from_fixed(arrived_ref, vectors, p)
        for p in range((own_ref.shape[0] - TAIL) // vectors)
    ]
    if norm_factor is None:
        put_fixed(out_ref, blocks)
        return
    for p, block in enumerate(blocks):
        out_ref[p * vectors : (p + 1) * vectors] = (block * norm_factor).astype(out_ref.dtype)


def contract(sums_ref, weight_ref, blocks, tau_ref, left_ref, right_ref):
    f32, bf16 = jnp.float32, jnp.bfloat16
    vectors = sums_ref.shape[2]
    count_ops = sums_ref.shape[0] // 2
    order = tau_ref.shape[2]
    spins = order // vectors
    me_t = lax.axis_index("ta")
    times = len(blocks)

    def chosen(end, k):
        total = jnp.zeros((vectors // 8, 8, vectors), f32)
        for t in range(times):
            weight = weight_ref[end, lax.rem(me_t + t, times)]
            total = total + blocks[t](k).astype(f32).reshape(total.shape) * weight
        return total.reshape(vectors, vectors)

    for o in range(count_ops):
        first = 2 * o * vectors
        a_r, a_i = chosen(0, 2 * o).astype(bf16), chosen(0, 2 * o + 1).astype(bf16)
        b_r, b_i = chosen(1, 2 * o).T.astype(bf16), chosen(1, 2 * o + 1).T.astype(bf16)
        real, imag = slice(first, first + vectors), slice(first + vectors, first + 2 * vectors)
        left_ref[real, 0:vectors] = a_r
        left_ref[real, vectors:] = -a_i
        left_ref[imag, 0:vectors] = a_i
        left_ref[imag, vectors:] = a_r
        right_ref[0:vectors, real] = b_r
        right_ref[0:vectors, imag] = -b_i
        right_ref[vectors:, real] = b_i
        right_ref[vectors:, imag] = b_r
    lanes = sums_ref.shape[1]
    fold = lambda t: jnp.sum(t.reshape(vectors // lanes, lanes, vectors), axis=0)
    sums = [jnp.zeros((lanes, vectors), f32) for _ in range(2 * count_ops)]
    for s in range(spins):
        rows = slice(s * vectors, (s + 1) * vectors)
        x = jnp.dot(
            left_ref[...],
            jnp.concatenate([tau_ref[0, rows], tau_ref[1, rows]], axis=0),
            preferred_element_type=f32,
        )
        for c in range(spins):
            cols = slice(c * vectors, (c + 1) * vectors)
            y = jnp.dot(
                jnp.concatenate([tau_ref[0, rows, cols], tau_ref[1, rows, cols]], axis=1),
                right_ref[...],
                preferred_element_type=f32,
            )
            for o in range(count_ops):
                first = 2 * o * vectors
                x_r = x[first : first + vectors, cols]
                x_i = x[first + vectors : first + 2 * vectors, cols]
                y_r = y[:, first : first + vectors]
                y_i = y[:, first + vectors : first + 2 * vectors]
                sums[2 * o] = sums[2 * o] + fold(x_r * y_r + x_i * y_i)
                sums[2 * o + 1] = sums[2 * o + 1] + fold(x_i * y_r - x_r * y_i)
    for k, total in enumerate(sums):
        sums_ref[k] = total


def part_of(ref, vectors):
    return lambda k: ref[k * vectors : (k + 1) * vectors]


def first_contract_kernel(times, split, live_ref, weight_ref, tau_ref, *refs):
    blocks, (live_out_ref, sums_ref, left_ref, right_ref) = refs[:times], refs[times:]
    live = jnp.where(live_ref[0] > 0, 1.0, 0.0)
    live_out_ref[...] = jnp.full(live_out_ref.shape, live, jnp.float32)
    if split:
        vectors = sums_ref.shape[2]
        blocks = [part_of(ref, vectors) for ref in blocks]
        contract(sums_ref, weight_ref, blocks, tau_ref, left_ref, right_ref)
    else:
        sums_ref[...] = jnp.zeros_like(sums_ref)


def margins_kernel(kept_ref, other_ref, margin_ref):
    half = kept_ref.shape[0]
    me = lax.axis_index("gx") & 1
    for place, ref in ((me, kept_ref), (1 - me, other_ref)):
        rows = pl.ds(pl.multiple_of(place * half, half), half)
        margin_ref[0, rows] = ref[...].astype(jnp.float32)


def second_contract_kernel(times, split, weight_ref, tau_ref, *refs):
    other, kept, refs = refs[:times], refs[times : 2 * times], refs[2 * times :]
    live_ref, first_sums_ref, corr_ref, sums_ref, left_ref, right_ref = refs
    vectors = sums_ref.shape[2]
    half = kept[0].shape[0]
    me = lax.axis_index("gx") & 1
    parts_per_half = half // vectors

    def either(kept_ref, other_ref):
        def part(k):
            row = (k % parts_per_half) * vectors
            own, far = kept_ref[row : row + vectors], other_ref[row : row + vectors]
            mine = (k // parts_per_half == me).astype(jnp.float32)
            return own.astype(jnp.float32) * mine + far.astype(jnp.float32) * (1.0 - mine)

        return part

    blocks = [part_of(ref, vectors) for ref in other]
    if not split:
        blocks = [either(a, b) for a, b in zip(kept, other)]
    contract(sums_ref, weight_ref, blocks, tau_ref, left_ref, right_ref)
    now_ops = sums_ref.shape[0] // 2
    known = [(sums_ref, (1 - me) * now_ops)] if split else [(sums_ref, 0)]
    if split:
        known.append((first_sums_ref, me * now_ops))
    shape = corr_ref.shape[1:]
    row, col = iota(shape, 0), iota(shape, 1)
    result = jnp.zeros(shape, jnp.float32)
    for ref, first in known:
        for k in range(2 * now_ops):
            total = jnp.sum(jnp.sum(ref[k], axis=0, keepdims=True), axis=1, keepdims=True)
            here = (row == first + k // 2) & (col == k % 2)
            result = jnp.where(here, total * (1.0 / vectors), result)
    corr_ref[0] = result * live_ref[0 : shape[0], 0 : shape[1]]


def vmem_spec():
    return pl.BlockSpec(memory_space=pltpu.VMEM)


def smem_spec():
    return pl.BlockSpec(memory_space=pltpu.SMEM)


def hbm_spec():
    return pl.BlockSpec(memory_space=pltpu.HBM)


def in_hbm(x):
    return pltpu.with_memory_space_constraint(x, pltpu.HBM)


def local_call(body, name, outs, in_specs, out_specs, scratch=(), cost=None):
    return pl.pallas_call(
        body,
        out_shape=outs,
        in_specs=in_specs,
        out_specs=out_specs,
        scratch_shapes=list(scratch),
        compiler_params=pltpu.CompilerParams(vmem_limit_bytes=VMEM_LIMIT),
        cost_estimate=cost,
        name=name,
    )


def from_step(block, axis, step):
    count = lax.axis_size(axis)
    return lax.ppermute(block, axis, [((i + step) % count, i) for i in range(count)])


def from_partner(block, axis, step):
    count = lax.axis_size(axis)
    return lax.ppermute(block, axis, [(i ^ step, i) for i in range(count)])


def from_diagonal(block, axes, sources):
    rows, columns = (lax.axis_size(axis) for axis in axes)
    perm = []
    for row in range(rows):
        for column in range(columns):
            from_row, from_column = sources(row, column)
            perm.append((from_row * columns + from_column, row * columns + column))
    return lax.ppermute(block, axes, perm)


def per_device(eigvecs, links, op_dirs, op_moms, perams, pair_times, slot_counts):
    f32, bf16 = jnp.float32, jnp.bfloat16
    _, cells_x, cells_y, cells_z, colors, _, vectors = eigvecs.shape
    order = cells_z * colors * 2
    lines = cells_x * cells_y
    count_ops = op_dirs.shape[0]
    times, shares, groups = lax.axis_size("ta"), lax.axis_size("gx"), lax.axis_size("gy")
    levels = groups.bit_length() - 1
    own_ops = count_ops // groups
    own_rows = own_ops * 2 * vectors
    field = eigvecs.reshape(cells_x, cells_y, order, vectors)
    halo_x = from_step(field[0:1], "gx", 1)
    halo_y = from_step(field, "gy", 1)
    link_field = links[0].transpose(0, 1, 3, 5, 6, 4, 2).reshape(lines, 27, 2, cells_z)
    outside, inside = halo_fields(cells_x, cells_y), local_fields(cells_x, cells_y)
    inputs = [field, link_field, op_dirs, op_moms, wave_constants(cells_z), pair_times]
    inputs = [in_hbm(x) for x in inputs]
    held = [
        pltpu.SMEM(x.shape, x.dtype) if x.dtype == jnp.int32 else pltpu.VMEM(x.shape, x.dtype)
        for x in inputs
    ]
    matrices, local, left, phases, weights = local_call(
        functools.partial(prepare_kernel, cells_x, cells_y),
        "prepare_lines",
        (
            jax.ShapeDtypeStruct((len(outside), order, 128), bf16),
            jax.ShapeDtypeStruct((len(inside), order, vectors), f32),
            jax.ShapeDtypeStruct((2, vectors, lines * order), bf16),
            jax.ShapeDtypeStruct((count_ops, order // 2, 2 * vectors), f32),
            jax.ShapeDtypeStruct((2, times, 8, vectors), f32),
        ),
        [hbm_spec()] * len(inputs),
        (vmem_spec(),) * 5,
        held
        + [
            pltpu.VMEM((lines, LINK_COLS, cells_z), f32),
            pltpu.SemaphoreType.DMA((len(inputs),)),
        ],
    )(*inputs)
    part = lambda count: jax.ShapeDtypeStruct((count, own_rows, vectors), f32)
    later = count_ops // 2
    swap_a, hold_a, later_sides, later_pairs = local_call(
        functools.partial(first_margin_kernel, cells_x, cells_y, groups, own_ops),
        "first_margins",
        (
            part(groups // 4),
            part(groups // 4),
            jax.ShapeDtypeStruct((later, vectors, lines * order), bf16),
            jax.ShapeDtypeStruct((later, lines * order, 2 * vectors), bf16),
        ),
        [vmem_spec()] * 6 + [hbm_spec()],
        (vmem_spec(),) * 4,
        [
            pltpu.VMEM((7, lines, order, vectors), f32),
            pltpu.VMEM((4, vectors, lines * order), bf16),
            pltpu.SMEM((count_ops,), jnp.int32),
            pltpu.SemaphoreType.DMA,
        ],
    )(matrices, local, left, phases, halo_x, halo_y, in_hbm(op_dirs))
    swapped_a = from_partner(swap_a, "gy", 1)
    held_shapes = [part(groups >> (b + 1)) for b in range(2, levels)] + [part(1)]
    swap_b, *held = local_call(
        functools.partial(second_margin_kernel, groups, own_ops),
        "second_margins",
        (part(groups // 4), *held_shapes),
        [vmem_spec()] * 2,
        (vmem_spec(),) * (1 + len(held_shapes)),
        cost=pl.CostEstimate(
            flops=later * 4 * lines * order * vectors * vectors,
            bytes_accessed=later * 6 * lines * order * vectors + later * 8 * vectors * vectors,
            transcendentals=0,
        ),
    )(later_sides, later_pairs)
    swapped_b = from_partner(swap_b, "gy", 1)

    def packed(body, name, *inputs, rows=own_rows, lead=(), count=1):
        shape = jax.ShapeDtypeStruct((*lead, rows + TAIL, vectors), jnp.int16)
        outs = shape if count == 1 else (shape,) * count
        specs = vmem_spec() if count == 1 else (vmem_spec(),) * count
        return local_call(body, name, outs, [vmem_spec()] * len(inputs), specs)(*inputs)

    half = own_rows // 2
    messages = []
    for b in range(1, levels):
        inputs = (hold_a, swapped_a) if b == 1 else (held[b - 2], swapped_b, *messages)
        if b < levels - 1:
            body = functools.partial(fold_kernel, b, vectors)
            sent = packed(body, "fold_groups", *inputs, lead=inputs[0].shape[:1])
            messages.append(from_partner(sent, "gy", 1 << b))
            continue
        body = functools.partial(fold_halves_kernel, b, vectors)
        away, kept = packed(body, "fold_halves", *inputs, rows=half, count=2)
        away = from_diagonal(away, ("gx", "gy"), lambda x, y: (x ^ 1, y ^ (1 << b)))
        kept = from_partner(kept, "gy", 1 << b)
    inputs = (held[-1], swapped_b, *messages)
    body = functools.partial(half_kernel, levels, vectors, False)
    arrived = from_partner(packed(body, "send_half", *inputs, rows=half), "gx", 1)
    body = functools.partial(half_kernel, levels, vectors, True)
    message = packed(body, "keep_half", *inputs, arrived, away, kept, rows=half)
    norm_factor = 1.0 / math.sqrt(3.0 * cells_x * shares * cells_y * groups * cells_z)
    step = 2
    while step < shares:
        arrived = from_partner(message, "gx", step)
        step *= 2
        if step < shares:
            body = functools.partial(both_kernel, vectors, None)
            message = packed(body, "sum_both", message, arrived, rows=half)
    finished = local_call(
        functools.partial(both_kernel, vectors, norm_factor),
        "finish_half",
        jax.ShapeDtypeStruct((half, vectors), bf16),
        [vmem_spec()] * 2,
        vmem_spec(),
    )(message, arrived)
    kept = [finished] + [from_step(finished, "ta", t) for t in range(1, times)]
    other = [from_partner(finished, "gx", 1)]
    for t in range(1, times):
        source = lambda row, x: ((row + t) % times, x ^ 1)
        other.append(from_diagonal(finished, ("ta", "gx"), source))
    split = own_ops % 2 == 0
    now_ops = own_ops // 2 if split else own_ops
    sums_shape = (2 * now_ops, 32, vectors)
    scratch = [
        pltpu.VMEM((2 * now_ops * vectors, 2 * vectors), bf16),
        pltpu.VMEM((2 * vectors, 2 * now_ops * vectors), bf16),
    ]
    live, sums = local_call(
        functools.partial(first_contract_kernel, times, split),
        "first_contraction",
        (jax.ShapeDtypeStruct((8, vectors), f32), jax.ShapeDtypeStruct(sums_shape, f32)),
        [smem_spec()] + [vmem_spec()] * (2 + times),
        (vmem_spec(),) * 2,
        scratch,
    )(slot_counts, weights, perams[0], *kept)
    margins = local_call(
        margins_kernel,
        "margins_out",
        jax.ShapeDtypeStruct((1, own_rows, vectors), f32),
        [vmem_spec()] * 2,
        vmem_spec(),
    )(*lax.optimization_barrier((kept[0], other[0], sums))[:2])
    correlators = local_call(
        functools.partial(second_contract_kernel, times, split),
        "second_contraction",
        jax.ShapeDtypeStruct((1, own_ops, 2), f32),
        [vmem_spec()] * (4 + 2 * times),
        vmem_spec(),
        [pltpu.VMEM(sums_shape, f32)] + scratch,
    )(weights, perams[0], *other, *kept, live, sums)
    return (margins.reshape(1, own_ops, 2, vectors, vectors), correlators)


def solution(mesh):
    placed = (
        P("ta", "gx", "gy", None, None, None, None),
        P("ta", "gx", "gy", None, None, None, None, None),
        P(),
        P(),
        P(("ta", "gx"), None, None, None),
        P(("ta", "gx"), None),
        P(("ta", "gx")),
    )
    return jax.shard_map(
        per_device,
        mesh=mesh,
        in_specs=placed,
        out_specs=(P("ta", "gy", None, None, None), P(("ta", "gx"), "gy", None)),
        check_vma=False,
    )
```

```python
import functools
import math

import jax
import jax.numpy as jnp
import numpy as np
from jax import lax
from jax.experimental import pallas as pl
from jax.experimental.pallas import tpu as pltpu
from jax.sharding import PartitionSpec as P

VMEM_LIMIT = 24 * 1024 * 1024
MOMENTA = 3
LINK_COLS = 54
TAIL = 16
FIXED_BITS = 14.0


def wave_constants(cells_z):
    z_row = np.arange(3 * cells_z) // 3
    columns = []
    for ahead in range(2):
        for momentum in range(MOMENTA):
            angle = 2.0 * math.pi * momentum * ((z_row + ahead) % cells_z) / cells_z
            columns.append(np.cos(angle))
            columns.append(np.sin(angle))
    left = np.stack(columns, axis=1).astype(np.float32)
    terms = []
    for _ in range(3):
        term = left.astype(jnp.bfloat16).astype(np.float32)
        terms.append(term)
        left = left - term
    return jnp.asarray(np.concatenate(terms, axis=1), jnp.bfloat16)


def iota(shape, axis):
    return lax.broadcasted_iota(jnp.int32, shape, axis)


def third(x):
    return (x * 21846) >> 16


def one_hot(condition):
    return condition.astype(jnp.float32).astype(jnp.bfloat16)


def planar_order(order):
    row, col = iota((order, order), 0), iota((order, order), 1)
    half = order // 2
    source = jnp.where(row < half, 2 * row, 2 * (row - half) + 1)
    return one_hot(col == source)


def side_by_side(planar):
    half = planar.shape[0] // 2
    return jnp.concatenate([planar[:half], planar[half:]], axis=1).astype(jnp.bfloat16)


def transport(matrix, pair, sign):
    half, vectors = matrix.shape[0] // 2, pair.shape[1] // 2
    parts = jnp.dot(matrix, pair, preferred_element_type=jnp.float32)
    real, imag = parts[:half], parts[half:]
    if sign > 0:
        return jnp.concatenate(
            [real[:, :vectors] - imag[:, vectors:], real[:, vectors:] + imag[:, :vectors]], axis=0
        )
    return jnp.concatenate(
        [real[:, :vectors] + imag[:, vectors:], real[:, vectors:] - imag[:, :vectors]], axis=0
    )


def halo_fields(cells_x, cells_y):
    pairs = [(0, (cells_x - 1) * cells_y + y) for y in range(cells_y)]
    return pairs + [(1, x * cells_y + cells_y - 1) for x in range(cells_x)]


def local_fields(cells_x, cells_y):
    lines = cells_x * cells_y
    outside = halo_fields(cells_x, cells_y)
    every = [(code, line) for code in range(7) for line in range(lines)]
    return [pair for pair in every if pair not in outside]


def prepare_kernel(cells_x, cells_y, *refs):
    inputs, refs = refs[:6], refs[6:]
    matrix_ref, local_ref, left_ref, phase_ref, weight_ref = refs[:5]
    held, link_rows_ref, sems = refs[5:11], refs[11], refs[12]
    copies = [
        pltpu.make_async_copy(src, dst, sems.at[k])
        for k, (src, dst) in enumerate(zip(inputs, held))
    ]
    for copy in copies:
        copy.start()
    v_ref, link_ref, dirs_ref, moms_ref, waves_ref, pair_ref = held
    f32, bf16 = jnp.float32, jnp.bfloat16
    order, vectors = v_ref.shape[2], v_ref.shape[3]
    half, cells_z = order // 2, order // 6
    lines = cells_x * cells_y
    times = weight_ref.shape[1]
    spread = one_hot(third(iota((half, cells_z), 0)) == iota((half, cells_z), 1))
    row, col = iota((half, LINK_COLS), 0), iota((half, LINK_COLS), 1)
    row_color = row - 3 * third(row)
    pair_at = third(col >> 1)
    col_in, col_out = (col >> 1) - 3 * pair_at, pair_at - 3 * third(pair_at)
    pick = [(row_color == col_out).astype(f32), (row_color == col_in).astype(f32)]
    wide = (LINK_COLS, 6 * 128)
    row, col = iota(wide, 0), iota(wide, 1)
    block, place = col >> 7, col & 127
    color = place - 3 * third(place)
    pair_at = third(row >> 1)
    row_in, row_out = (row >> 1) - 3 * pair_at, pair_at - 3 * third(pair_at)
    fits = 2 * third(pair_at) + (row & 1) == block
    expand = [one_hot(fits & (row_in == color)), one_hot(fits & (row_out == color))]
    row, col = iota((half, 128), 0), iota((half, 128), 1)
    near = ((third(row) == third(col)) & (col < half)).astype(f32)
    planar = planar_order(order)
    for copy in copies:
        copy.wait()
    for t in range(times):
        sink = pair_ref[0, 0] == t
        source = pair_ref[0, 1] == t
        weight_ref[0, t] = jnp.full(weight_ref.shape[2:], jnp.where(sink, 1.0, 0.0), f32)
        weight_ref[1, t] = jnp.full(weight_ref.shape[2:], jnp.where(source, 1.0, 0.0), f32)
    for line in range(lines):
        for k in range(LINK_COLS // 2):
            link_rows_ref[line, 2 * k : 2 * k + 2] = link_ref[line, k].astype(f32)
    outside = halo_fields(cells_x, cells_y)
    inside = local_fields(cells_x, cells_y)
    ordered = []
    for line in range(lines):
        here = jnp.dot(
            planar, v_ref[line // cells_y, line % cells_y], preferred_element_type=f32
        )
        ordered.append(here)
        local_ref[inside.index((6, line))] = here
    for line in range(lines):
        here = ordered[line]
        ahead_z = jnp.concatenate(
            [here[3:half], here[:3], here[half + 3 :], here[half : half + 3]], axis=0
        )
        columns = slice(line * order, (line + 1) * order)
        left_ref[0, :, columns] = here.T.astype(bf16)
        left_ref[1, :, columns] = ahead_z.T.astype(bf16)
        seen = lax.dot_general(
            spread,
            link_rows_ref[line].astype(bf16),
            (((1,), (1,)), ((), ())),
            preferred_element_type=f32,
        )
        pair = side_by_side(here)
        for way in range(2):
            blocks = jnp.dot(
                (seen * pick[way]).astype(bf16), expand[way], preferred_element_type=f32
            )
            for d in range(3):
                matrix = jnp.concatenate(
                    [
                        blocks[:, 256 * d : 256 * d + 128] * near,
                        blocks[:, 256 * d + 128 : 256 * d + 256] * near,
                    ],
                    axis=0,
                ).astype(bf16)
                if way == 1:
                    carried = transport(matrix[:, :half], pair, -1)
                    local_ref[inside.index((3 + d, line))] = carried.astype(bf16).astype(f32)
                elif (d, line) in outside:
                    matrix_ref[outside.index((d, line))] = matrix
                else:
                    ahead = ahead_z if d == 2 else ordered[line + (cells_y if d == 0 else 1)]
                    local_ref[inside.index((d, line))] = transport(
                        matrix[:, :half], side_by_side(ahead), 1
                    )
    wave_cols = waves_ref.shape[1]
    per_term = wave_cols // 3
    row, col = iota((wave_cols, 2 * vectors), 0), iota((wave_cols, 2 * vectors), 1)
    term = (row >= per_term).astype(jnp.int32) + (row >= 2 * per_term).astype(jnp.int32)
    wave_at = row - per_term * term - (col >= vectors).astype(jnp.int32)
    for o in range(phase_ref.shape[0]):
        column = 2 * (jnp.where(dirs_ref[o] == 5, MOMENTA, 0) + moms_ref[o])
        phase_ref[o] = jnp.dot(
            waves_ref[...], one_hot(wave_at == column), preferred_element_type=f32
        )


def margin_kernel(cells_x, cells_y, groups, own_ops, *refs):
    matrix_ref, local_ref, left_ref, phase_ref, halo_x_ref, halo_y_ref, dirs_hbm = refs[:7]
    swap_ref, hold_ref = refs[7:9]
    field_ref, side_ref, dirs_ref, sem = refs[9:]
    f32, bf16 = jnp.float32, jnp.bfloat16
    copy = pltpu.make_async_copy(dirs_hbm, dirs_ref, sem)
    copy.start()
    lines = cells_x * cells_y
    order, vectors = halo_x_ref.shape[2], halo_x_ref.shape[3]
    half = order // 2
    planar = planar_order(order)
    side_ref[0] = left_ref[0]
    side_ref[3] = left_ref[1]
    outside = halo_fields(cells_x, cells_y)
    for d in range(2):
        for line in range(lines):
            x, y = line // cells_y, line % cells_y
            columns = slice(line * order, (line + 1) * order)
            if (d, line) not in outside:
                ahead = line + (cells_y if d == 0 else 1)
                side_ref[1 + d, :, columns] = left_ref[0, :, ahead * order : (ahead + 1) * order]
                continue
            halo = halo_x_ref[0, y] if d == 0 else halo_y_ref[x, 0]
            ahead = jnp.dot(planar, halo, preferred_element_type=f32)
            side_ref[1 + d, :, columns] = ahead.T.astype(bf16)
            matrix = matrix_ref[outside.index((d, line))]
            field_ref[d, line] = transport(matrix[:, :half], side_by_side(ahead), 1)
    for k, (code, line) in enumerate(local_fields(cells_x, cells_y)):
        field_ref[code, line] = local_ref[k]
    copy.wait()
    me = lax.axis_index("gy")
    for j in sorted(range(groups), key=lambda j: -(j & 1)):
        blocks = []
        for i in range(own_ops):
            o = (me ^ j) * own_ops + i
            code = dirs_ref[o]
            side = jnp.where((code >= 3) & (code < 6), code - 2, 0)
            cosine = phase_ref[o, :, 0:vectors]
            sine = phase_ref[o, :, vectors : 2 * vectors]
            pairs = []
            for line in range(lines):
                real, imag = field_ref[code, line, 0:half], field_ref[code, line, half:order]
                turned_r, turned_i = cosine * real - sine * imag, sine * real + cosine * imag
                pairs.append(jnp.concatenate([turned_r, turned_i], axis=1))
                pairs.append(jnp.concatenate([turned_i, -turned_r], axis=1))
            pair = jnp.concatenate(pairs, axis=0).astype(bf16)
            product = jnp.dot(side_ref[side], pair, preferred_element_type=f32)
            blocks += [product[:, :vectors], product[:, vectors:]]
        if j & 1:
            put_fixed(swap_ref.at[j >> 1], blocks)
            continue
        for k, block in enumerate(blocks):
            hold_ref[j >> 1, k * vectors : (k + 1) * vectors] = block


def scale_of(block):
    top = jnp.max(jnp.abs(block), axis=0, keepdims=True)
    return jnp.floor(jnp.log2(jnp.maximum(top, 1e-30))) + 1.0


def put_fixed(out_ref, blocks):
    rows, vectors = blocks[0].shape
    tail = iota((TAIL, vectors), 0)
    scales = jnp.zeros((TAIL, vectors), jnp.float32)
    for k, block in enumerate(blocks):
        scale = scale_of(block)
        scales = jnp.where(tail == k, scale, scales)
        fixed = jnp.floor(block * jnp.exp2(FIXED_BITS - scale) + 0.5)
        out_ref[k * rows : (k + 1) * rows] = fixed.astype(jnp.int32).astype(jnp.int16)
    out_ref[len(blocks) * rows :] = scales.astype(jnp.int32).astype(jnp.int16)


def from_fixed(ref, rows, k):
    scales = ref[ref.shape[0] - TAIL :].astype(jnp.int32).astype(jnp.float32)
    block = ref[k * rows : (k + 1) * rows].astype(jnp.int32).astype(jnp.float32)
    return block * jnp.exp2(scales[k : k + 1] - FIXED_BITS)


def group_block(held_ref, messages, j, start, rows):
    total = held_ref[j >> 1, pl.ds(start, rows)]
    for b, ref in enumerate(messages):
        total = total + fixed_at(ref.at[j >> (b + 1)], start, rows)
    return total


def fixed_at(ref, start, rows):
    tail = ref[ref.shape[0] - TAIL :].astype(jnp.int32).astype(jnp.float32)
    scale = jnp.max(
        jnp.where(iota(tail.shape, 0) == start // rows, tail, -1000.0), axis=0, keepdims=True
    )
    block = ref[pl.ds(start, rows)].astype(jnp.int32).astype(jnp.float32)
    return block * jnp.exp2(scale - FIXED_BITS)


def fold_kernel(level, vectors, held_ref, *refs):
    messages, out_ref = refs[:-1], refs[-1]
    for k in range(out_ref.shape[0]):
        blocks = [
            group_block(held_ref, messages, (2 * k + 1) << level, start, vectors)
            for start in range(0, held_ref.shape[1], vectors)
        ]
        put_fixed(out_ref.at[k], blocks)


def half_blocks(held_ref, messages, j, kept, vectors):
    me = lax.axis_index("gx") & 1
    half = held_ref.shape[1] // 2
    base = pl.multiple_of((me if kept else 1 - me) * half, half)
    steps = range(0, half, vectors)
    return [group_block(held_ref, messages, j, base + step, vectors) for step in steps]


def spread_kernel(level, vectors, held_ref, *refs):
    messages, (y_ref, diagonal_ref, x_ref) = refs[:-3], refs[-3:]
    put_fixed(y_ref, half_blocks(held_ref, messages, 1 << level, True, vectors))
    put_fixed(diagonal_ref, half_blocks(held_ref, messages, 1 << level, False, vectors))
    put_fixed(x_ref, half_blocks(held_ref, messages, 0, False, vectors))


def keep_kernel(vectors, held_ref, *refs):
    messages, came, out_ref = refs[:-4], refs[-4:-1], refs[-1]
    blocks = half_blocks(held_ref, messages, 0, True, vectors)
    for p in range(len(blocks)):
        for ref in came:
            blocks[p] = blocks[p] + from_fixed(ref, vectors, p)
    put_fixed(out_ref, blocks)


def both_kernel(vectors, norm_factor, own_ref, arrived_ref, out_ref):
    blocks = [
        from_fixed(own_ref, vectors, p) + from_fixed(arrived_ref, vectors, p)
        for p in range((own_ref.shape[0] - TAIL) // vectors)
    ]
    if norm_factor is None:
        put_fixed(out_ref, blocks)
        return
    for p, block in enumerate(blocks):
        out_ref[p * vectors : (p + 1) * vectors] = (block * norm_factor).astype(out_ref.dtype)


def contract(sums_ref, weight_ref, blocks, tau_ref, left_ref, right_ref):
    f32, bf16 = jnp.float32, jnp.bfloat16
    vectors = sums_ref.shape[2]
    count_ops = sums_ref.shape[0] // 2
    order = tau_ref.shape[2]
    spins = order // vectors
    me_t = lax.axis_index("ta")
    times = len(blocks)

    def chosen(end, k):
        total = jnp.zeros((vectors // 8, 8, vectors), f32)
        for t in range(times):
            weight = weight_ref[end, lax.rem(me_t + t, times)]
            total = total + blocks[t](k).astype(f32).reshape(total.shape) * weight
        return total.reshape(vectors, vectors)

    for o in range(count_ops):
        first = 2 * o * vectors
        a_r, a_i = chosen(0, 2 * o).astype(bf16), chosen(0, 2 * o + 1).astype(bf16)
        b_r, b_i = chosen(1, 2 * o).T.astype(bf16), chosen(1, 2 * o + 1).T.astype(bf16)
        real, imag = slice(first, first + vectors), slice(first + vectors, first + 2 * vectors)
        left_ref[real, 0:vectors] = a_r
        left_ref[real, vectors:] = -a_i
        left_ref[imag, 0:vectors] = a_i
        left_ref[imag, vectors:] = a_r
        right_ref[0:vectors, real] = b_r
        right_ref[0:vectors, imag] = -b_i
        right_ref[vectors:, real] = b_i
        right_ref[vectors:, imag] = b_r
    lanes = sums_ref.shape[1]
    fold = lambda t: jnp.sum(t.reshape(vectors // lanes, lanes, vectors), axis=0)
    sums = [jnp.zeros((lanes, vectors), f32) for _ in range(2 * count_ops)]
    for s in range(spins):
        rows = slice(s * vectors, (s + 1) * vectors)
        x = jnp.dot(
            left_ref[...],
            jnp.concatenate([tau_ref[0, rows], tau_ref[1, rows]], axis=0),
            preferred_element_type=f32,
        )
        for c in range(spins):
            cols = slice(c * vectors, (c + 1) * vectors)
            y = jnp.dot(
                jnp.concatenate([tau_ref[0, rows, cols], tau_ref[1, rows, cols]], axis=1),
                right_ref[...],
                preferred_element_type=f32,
            )
            for o in range(count_ops):
                first = 2 * o * vectors
                x_r = x[first : first + vectors, cols]
                x_i = x[first + vectors : first + 2 * vectors, cols]
                y_r = y[:, first : first + vectors]
                y_i = y[:, first + vectors : first + 2 * vectors]
                sums[2 * o] = sums[2 * o] + fold(x_r * y_r + x_i * y_i)
                sums[2 * o + 1] = sums[2 * o + 1] + fold(x_i * y_r - x_r * y_i)
    for k, total in enumerate(sums):
        sums_ref[k] = total


def part_of(ref, vectors):
    return lambda k: ref[k * vectors : (k + 1) * vectors]


def first_contract_kernel(times, split, live_ref, weight_ref, tau_ref, *refs):
    blocks, (live_out_ref, sums_ref, left_ref, right_ref) = refs[:times], refs[times:]
    live = jnp.where(live_ref[0] > 0, 1.0, 0.0)
    live_out_ref[...] = jnp.full(live_out_ref.shape, live, jnp.float32)
    if split:
        vectors = sums_ref.shape[2]
        blocks = [part_of(ref, vectors) for ref in blocks]
        contract(sums_ref, weight_ref, blocks, tau_ref, left_ref, right_ref)
    else:
        sums_ref[...] = jnp.zeros_like(sums_ref)


def margins_kernel(kept_ref, other_ref, margin_ref):
    half = kept_ref.shape[0]
    me = lax.axis_index("gx") & 1
    for place, ref in ((me, kept_ref), (1 - me, other_ref)):
        rows = pl.ds(pl.multiple_of(place * half, half), half)
        margin_ref[0, rows] = ref[...].astype(jnp.float32)


def second_contract_kernel(times, split, weight_ref, tau_ref, *refs):
    other, kept, refs = refs[:times], refs[times : 2 * times], refs[2 * times :]
    live_ref, first_sums_ref, corr_ref, sums_ref, left_ref, right_ref = refs
    vectors = sums_ref.shape[2]
    half = kept[0].shape[0]
    me = lax.axis_index("gx") & 1
    parts_per_half = half // vectors

    def either(kept_ref, other_ref):
        def part(k):
            row = (k % parts_per_half) * vectors
            own, far = kept_ref[row : row + vectors], other_ref[row : row + vectors]
            mine = (k // parts_per_half == me).astype(jnp.float32)
            return own.astype(jnp.float32) * mine + far.astype(jnp.float32) * (1.0 - mine)

        return part

    blocks = [part_of(ref, vectors) for ref in other]
    if not split:
        blocks = [either(a, b) for a, b in zip(kept, other)]
    contract(sums_ref, weight_ref, blocks, tau_ref, left_ref, right_ref)
    now_ops = sums_ref.shape[0] // 2
    known = [(sums_ref, (1 - me) * now_ops)] if split else [(sums_ref, 0)]
    if split:
        known.append((first_sums_ref, me * now_ops))
    shape = corr_ref.shape[1:]
    row, col = iota(shape, 0), iota(shape, 1)
    result = jnp.zeros(shape, jnp.float32)
    for ref, first in known:
        for k in range(2 * now_ops):
            total = jnp.sum(jnp.sum(ref[k], axis=0, keepdims=True), axis=1, keepdims=True)
            here = (row == first + k // 2) & (col == k % 2)
            result = jnp.where(here, total * (1.0 / vectors), result)
    corr_ref[0] = result * live_ref[0 : shape[0], 0 : shape[1]]


def vmem_spec():
    return pl.BlockSpec(memory_space=pltpu.VMEM)


def smem_spec():
    return pl.BlockSpec(memory_space=pltpu.SMEM)


def hbm_spec():
    return pl.BlockSpec(memory_space=pltpu.HBM)


def in_hbm(x):
    return pltpu.with_memory_space_constraint(x, pltpu.HBM)


def local_call(body, name, outs, in_specs, out_specs, scratch=(), cost=None):
    return pl.pallas_call(
        body,
        out_shape=outs,
        in_specs=in_specs,
        out_specs=out_specs,
        scratch_shapes=list(scratch),
        compiler_params=pltpu.CompilerParams(vmem_limit_bytes=VMEM_LIMIT),
        cost_estimate=cost,
        name=name,
    )


def from_step(block, axis, step):
    count = lax.axis_size(axis)
    return lax.ppermute(block, axis, [((i + step) % count, i) for i in range(count)])


def from_partner(block, axis, step):
    count = lax.axis_size(axis)
    return lax.ppermute(block, axis, [(i ^ step, i) for i in range(count)])


def from_diagonal(block, axes, sources):
    rows, columns = (lax.axis_size(axis) for axis in axes)
    perm = []
    for row in range(rows):
        for column in range(columns):
            from_row, from_column = sources(row, column)
            perm.append((from_row * columns + from_column, row * columns + column))
    return lax.ppermute(block, axes, perm)


def per_device(eigvecs, links, op_dirs, op_moms, perams, pair_times, slot_counts):
    f32, bf16 = jnp.float32, jnp.bfloat16
    _, cells_x, cells_y, cells_z, colors, _, vectors = eigvecs.shape
    order = cells_z * colors * 2
    lines = cells_x * cells_y
    count_ops = op_dirs.shape[0]
    times, shares, groups = lax.axis_size("ta"), lax.axis_size("gx"), lax.axis_size("gy")
    levels = groups.bit_length() - 1
    own_ops = count_ops // groups
    own_rows = own_ops * 2 * vectors
    field = eigvecs.reshape(cells_x, cells_y, order, vectors)
    halo_x = from_step(field[0:1], "gx", 1)
    halo_y = from_step(field, "gy", 1)
    link_field = links[0].transpose(0, 1, 3, 5, 6, 4, 2).reshape(lines, 27, 2, cells_z)
    outside, inside = halo_fields(cells_x, cells_y), local_fields(cells_x, cells_y)
    inputs = [field, link_field, op_dirs, op_moms, wave_constants(cells_z), pair_times]
    inputs = [in_hbm(x) for x in inputs]
    held = [
        pltpu.SMEM(x.shape, x.dtype) if x.dtype == jnp.int32 else pltpu.VMEM(x.shape, x.dtype)
        for x in inputs
    ]
    matrices, local, left, phases, weights = local_call(
        functools.partial(prepare_kernel, cells_x, cells_y),
        "prepare_lines",
        (
            jax.ShapeDtypeStruct((len(outside), order, 128), bf16),
            jax.ShapeDtypeStruct((len(inside), order, vectors), f32),
            jax.ShapeDtypeStruct((2, vectors, lines * order), bf16),
            jax.ShapeDtypeStruct((count_ops, order // 2, 2 * vectors), f32),
            jax.ShapeDtypeStruct((2, times, 8, vectors), f32),
        ),
        [hbm_spec()] * len(inputs),
        (vmem_spec(),) * 5,
        held
        + [
            pltpu.VMEM((lines, LINK_COLS, cells_z), f32),
            pltpu.SemaphoreType.DMA((len(inputs),)),
        ],
    )(*inputs)
    message = lambda rows, *lead: jax.ShapeDtypeStruct((*lead, rows + TAIL, vectors), jnp.int16)
    swap, held = local_call(
        functools.partial(margin_kernel, cells_x, cells_y, groups, own_ops),
        "partial_margins",
        (
            message(own_rows, groups // 2),
            jax.ShapeDtypeStruct((groups // 2, own_rows, vectors), f32),
        ),
        [vmem_spec()] * 6 + [hbm_spec()],
        (vmem_spec(),) * 2,
        [
            pltpu.VMEM((7, lines, order, vectors), f32),
            pltpu.VMEM((4, vectors, lines * order), bf16),
            pltpu.SMEM((count_ops,), jnp.int32),
            pltpu.SemaphoreType.DMA,
        ],
    )(matrices, local, left, phases, halo_x, halo_y, in_hbm(op_dirs))

    def in_vmem(body, name, outs, *inputs):
        outs = outs if isinstance(outs, tuple) else (outs,)
        specs = (vmem_spec(),) * len(outs)
        return local_call(body, name, outs, [vmem_spec()] * len(inputs), specs)(*inputs)

    half = own_rows // 2
    messages = [from_partner(swap, "gy", 1)]
    last = levels - 1
    for b in range(1, last):
        body = functools.partial(fold_kernel, b, vectors)
        shape = message(own_rows, groups >> (b + 1))
        (sent,) = in_vmem(body, "fold_groups", shape, held, *messages)
        messages.append(from_partner(sent, "gy", 1 << b))
    body = functools.partial(spread_kernel, last, vectors)
    for_y, for_both, for_x = in_vmem(body, "spread_halves", (message(half),) * 3, held, *messages)
    came = [
        from_partner(for_y, "gy", 1 << last),
        from_diagonal(for_both, ("gx", "gy"), lambda x, y: (x ^ 1, y ^ (1 << last))),
        from_partner(for_x, "gx", 1),
    ]
    body = functools.partial(keep_kernel, vectors)
    (packed,) = in_vmem(body, "keep_half", message(half), held, *messages, *came)
    norm_factor = 1.0 / math.sqrt(3.0 * cells_x * shares * cells_y * groups * cells_z)
    step = 2
    while step < shares:
        arrived = from_partner(packed, "gx", step)
        step *= 2
        last_one = step >= shares
        body = functools.partial(both_kernel, vectors, norm_factor if last_one else None)
        shape = jax.ShapeDtypeStruct((half, vectors), bf16) if last_one else message(half)
        (packed,) = in_vmem(body, "finish_half" if last_one else "sum_both", shape, packed, arrived)
    finished = packed
    kept = [finished] + [from_step(finished, "ta", t) for t in range(1, times)]
    other = [from_partner(finished, "gx", 1)]
    for t in range(1, times):
        source = lambda row, x: ((row + t) % times, x ^ 1)
        other.append(from_diagonal(finished, ("ta", "gx"), source))
    split = own_ops % 2 == 0
    now_ops = own_ops // 2 if split else own_ops
    sums_shape = (2 * now_ops, 32, vectors)
    scratch = [
        pltpu.VMEM((2 * now_ops * vectors, 2 * vectors), bf16),
        pltpu.VMEM((2 * vectors, 2 * now_ops * vectors), bf16),
    ]
    live, sums = local_call(
        functools.partial(first_contract_kernel, times, split),
        "first_contraction",
        (jax.ShapeDtypeStruct((8, vectors), f32), jax.ShapeDtypeStruct(sums_shape, f32)),
        [smem_spec()] + [vmem_spec()] * (2 + times),
        (vmem_spec(),) * 2,
        scratch,
    )(slot_counts, weights, perams[0], *kept)
    margins = local_call(
        margins_kernel,
        "margins_out",
        jax.ShapeDtypeStruct((1, own_rows, vectors), f32),
        [vmem_spec()] * 2,
        vmem_spec(),
    )(*lax.optimization_barrier((kept[0], other[0], sums))[:2])
    correlators = local_call(
        functools.partial(second_contract_kernel, times, split),
        "second_contraction",
        jax.ShapeDtypeStruct((1, own_ops, 2), f32),
        [vmem_spec()] * (4 + 2 * times),
        vmem_spec(),
        [pltpu.VMEM(sums_shape, f32)] + scratch,
    )(weights, perams[0], *other, *kept, live, sums)
    return (margins.reshape(1, own_ops, 2, vectors, vectors), correlators)


def solution(mesh):
    placed = (
        P("ta", "gx", "gy", None, None, None, None),
        P("ta", "gx", "gy", None, None, None, None, None),
        P(),
        P(),
        P(("ta", "gx"), None, None, None),
        P(("ta", "gx"), None),
        P(("ta", "gx")),
    )
    return jax.shard_map(
        per_device,
        mesh=mesh,
        in_specs=placed,
        out_specs=(P("ta", "gy", None, None, None), P(("ta", "gx"), "gy", None)),
        check_vma=False,
    )
```

```python
import functools
import math

import jax
import jax.numpy as jnp
import numpy as np
from jax import lax
from jax.experimental import pallas as pl
from jax.experimental.pallas import tpu as pltpu
from jax.sharding import PartitionSpec as P

VMEM_LIMIT = 24 * 1024 * 1024
MOMENTA = 3
LINK_COLS = 54
TAIL = 16
FIXED_BITS = 14.0


def wave_constants(cells_z):
    z_row = np.arange(3 * cells_z) // 3
    columns = []
    for ahead in range(2):
        for momentum in range(MOMENTA):
            angle = 2.0 * math.pi * momentum * ((z_row + ahead) % cells_z) / cells_z
            columns.append(np.cos(angle))
            columns.append(np.sin(angle))
    left = np.stack(columns, axis=1).astype(np.float32)
    terms = []
    for _ in range(3):
        term = left.astype(jnp.bfloat16).astype(np.float32)
        terms.append(term)
        left = left - term
    return jnp.asarray(np.concatenate(terms, axis=1), jnp.bfloat16)


def iota(shape, axis):
    return lax.broadcasted_iota(jnp.int32, shape, axis)


def third(x):
    return (x * 21846) >> 16


def one_hot(condition):
    return condition.astype(jnp.float32).astype(jnp.bfloat16)


def planar_order(order):
    row, col = iota((order, order), 0), iota((order, order), 1)
    half = order // 2
    source = jnp.where(row < half, 2 * row, 2 * (row - half) + 1)
    return one_hot(col == source)


def side_by_side(planar):
    half = planar.shape[0] // 2
    return jnp.concatenate([planar[:half], planar[half:]], axis=1).astype(jnp.bfloat16)


def transport(matrix, pair, sign):
    half, vectors = matrix.shape[0] // 2, pair.shape[1] // 2
    parts = jnp.dot(matrix, pair, preferred_element_type=jnp.float32)
    real, imag = parts[:half], parts[half:]
    if sign > 0:
        return jnp.concatenate(
            [real[:, :vectors] - imag[:, vectors:], real[:, vectors:] + imag[:, :vectors]], axis=0
        )
    return jnp.concatenate(
        [real[:, :vectors] + imag[:, vectors:], real[:, vectors:] - imag[:, :vectors]], axis=0
    )


def halo_fields(cells_x, cells_y):
    pairs = [(0, (cells_x - 1) * cells_y + y) for y in range(cells_y)]
    return pairs + [(1, x * cells_y + cells_y - 1) for x in range(cells_x)]


def local_fields(cells_x, cells_y):
    lines = cells_x * cells_y
    outside = halo_fields(cells_x, cells_y)
    every = [(code, line) for code in range(7) for line in range(lines)]
    return [pair for pair in every if pair not in outside]


def prepare_kernel(cells_x, cells_y, *refs):
    inputs, refs = refs[:6], refs[6:]
    matrix_ref, local_ref, left_ref, phase_ref, weight_ref = refs[:5]
    held, link_rows_ref, sems = refs[5:11], refs[11], refs[12]
    copies = [
        pltpu.make_async_copy(src, dst, sems.at[k])
        for k, (src, dst) in enumerate(zip(inputs, held))
    ]
    for copy in copies:
        copy.start()
    v_ref, link_ref, dirs_ref, moms_ref, waves_ref, pair_ref = held
    f32, bf16 = jnp.float32, jnp.bfloat16
    order, vectors = v_ref.shape[2], v_ref.shape[3]
    half, cells_z = order // 2, order // 6
    lines = cells_x * cells_y
    times = weight_ref.shape[1]
    spread = one_hot(third(iota((half, cells_z), 0)) == iota((half, cells_z), 1))
    row, col = iota((half, LINK_COLS), 0), iota((half, LINK_COLS), 1)
    row_color = row - 3 * third(row)
    pair_at = third(col >> 1)
    col_in, col_out = (col >> 1) - 3 * pair_at, pair_at - 3 * third(pair_at)
    pick = [(row_color == col_out).astype(f32), (row_color == col_in).astype(f32)]
    wide = (LINK_COLS, 6 * 128)
    row, col = iota(wide, 0), iota(wide, 1)
    block, place = col >> 7, col & 127
    color = place - 3 * third(place)
    pair_at = third(row >> 1)
    row_in, row_out = (row >> 1) - 3 * pair_at, pair_at - 3 * third(pair_at)
    fits = 2 * third(pair_at) + (row & 1) == block
    expand = [one_hot(fits & (row_in == color)), one_hot(fits & (row_out == color))]
    row, col = iota((half, 128), 0), iota((half, 128), 1)
    near = ((third(row) == third(col)) & (col < half)).astype(f32)
    planar = planar_order(order)
    for copy in copies:
        copy.wait()
    for t in range(times):
        sink = pair_ref[0, 0] == t
        source = pair_ref[0, 1] == t
        weight_ref[0, t] = jnp.full(weight_ref.shape[2:], jnp.where(sink, 1.0, 0.0), f32)
        weight_ref[1, t] = jnp.full(weight_ref.shape[2:], jnp.where(source, 1.0, 0.0), f32)
    for line in range(lines):
        for k in range(LINK_COLS // 2):
            link_rows_ref[line, 2 * k : 2 * k + 2] = link_ref[line, k].astype(f32)
    outside = halo_fields(cells_x, cells_y)
    inside = local_fields(cells_x, cells_y)
    ordered = []
    for line in range(lines):
        here = jnp.dot(
            planar, v_ref[line // cells_y, line % cells_y], preferred_element_type=f32
        )
        ordered.append(here)
        local_ref[inside.index((6, line))] = here
    for line in range(lines):
        here = ordered[line]
        ahead_z = jnp.concatenate(
            [here[3:half], here[:3], here[half + 3 :], here[half : half + 3]], axis=0
        )
        columns = slice(line * order, (line + 1) * order)
        left_ref[0, :, columns] = here.T.astype(bf16)
        left_ref[1, :, columns] = ahead_z.T.astype(bf16)
        seen = lax.dot_general(
            spread,
            link_rows_ref[line].astype(bf16),
            (((1,), (1,)), ((), ())),
            preferred_element_type=f32,
        )
        pair = side_by_side(here)
        for way in range(2):
            blocks = jnp.dot(
                (seen * pick[way]).astype(bf16), expand[way], preferred_element_type=f32
            )
            for d in range(3):
                matrix = jnp.concatenate(
                    [
                        blocks[:, 256 * d : 256 * d + 128] * near,
                        blocks[:, 256 * d + 128 : 256 * d + 256] * near,
                    ],
                    axis=0,
                ).astype(bf16)
                if way == 1:
                    carried = transport(matrix[:, :half], pair, -1)
                    local_ref[inside.index((3 + d, line))] = carried.astype(bf16).astype(f32)
                elif (d, line) in outside:
                    matrix_ref[outside.index((d, line))] = matrix
                else:
                    ahead = ahead_z if d == 2 else ordered[line + (cells_y if d == 0 else 1)]
                    local_ref[inside.index((d, line))] = transport(
                        matrix[:, :half], side_by_side(ahead), 1
                    )
    wave_cols = waves_ref.shape[1]
    per_term = wave_cols // 3
    row, col = iota((wave_cols, 2 * vectors), 0), iota((wave_cols, 2 * vectors), 1)
    term = (row >= per_term).astype(jnp.int32) + (row >= 2 * per_term).astype(jnp.int32)
    wave_at = row - per_term * term - (col >= vectors).astype(jnp.int32)
    for o in range(phase_ref.shape[0]):
        column = 2 * (jnp.where(dirs_ref[o] == 5, MOMENTA, 0) + moms_ref[o])
        phase_ref[o] = jnp.dot(
            waves_ref[...], one_hot(wave_at == column), preferred_element_type=f32
        )


def margin_kernel(cells_x, cells_y, groups, own_ops, *refs):
    matrix_ref, local_ref, left_ref, phase_ref, halo_x_ref, halo_y_ref, dirs_hbm = refs[:7]
    swap_ref, hold_ref = refs[7:9]
    field_ref, side_ref, dirs_ref, sem = refs[9:]
    f32, bf16 = jnp.float32, jnp.bfloat16
    copy = pltpu.make_async_copy(dirs_hbm, dirs_ref, sem)
    copy.start()
    lines = cells_x * cells_y
    order, vectors = halo_x_ref.shape[2], halo_x_ref.shape[3]
    half = order // 2
    planar = planar_order(order)
    side_ref[0] = left_ref[0]
    side_ref[3] = left_ref[1]
    outside = halo_fields(cells_x, cells_y)
    for d in range(2):
        for line in range(lines):
            x, y = line // cells_y, line % cells_y
            columns = slice(line * order, (line + 1) * order)
            if (d, line) not in outside:
                ahead = line + (cells_y if d == 0 else 1)
                side_ref[1 + d, :, columns] = left_ref[0, :, ahead * order : (ahead + 1) * order]
                continue
            halo = halo_x_ref[0, y] if d == 0 else halo_y_ref[x, 0]
            ahead = jnp.dot(planar, halo, preferred_element_type=f32)
            side_ref[1 + d, :, columns] = ahead.T.astype(bf16)
            matrix = matrix_ref[outside.index((d, line))]
            field_ref[d, line] = transport(matrix[:, :half], side_by_side(ahead), 1)
    for k, (code, line) in enumerate(local_fields(cells_x, cells_y)):
        field_ref[code, line] = local_ref[k]
    copy.wait()
    me = lax.axis_index("gy")
    for j in sorted(range(groups), key=lambda j: -(j & 1)):
        blocks = []
        for i in range(own_ops):
            o = (me ^ j) * own_ops + i
            code = dirs_ref[o]
            side = jnp.where((code >= 3) & (code < 6), code - 2, 0)
            cosine = phase_ref[o, :, 0:vectors]
            sine = phase_ref[o, :, vectors : 2 * vectors]
            pairs = []
            for line in range(lines):
                real, imag = field_ref[code, line, 0:half], field_ref[code, line, half:order]
                turned_r, turned_i = cosine * real - sine * imag, sine * real + cosine * imag
                pairs.append(jnp.concatenate([turned_r, turned_i], axis=1))
                pairs.append(jnp.concatenate([turned_i, -turned_r], axis=1))
            pair = jnp.concatenate(pairs, axis=0).astype(bf16)
            product = jnp.dot(side_ref[side], pair, preferred_element_type=f32)
            blocks += [product[:, :vectors], product[:, vectors:]]
        if j & 1:
            put_fixed(swap_ref.at[j >> 1], blocks)
            continue
        for k, block in enumerate(blocks):
            hold_ref[j >> 1, k * vectors : (k + 1) * vectors] = block


def scale_of(block):
    top = jnp.max(jnp.abs(block), axis=0, keepdims=True)
    return jnp.floor(jnp.log2(jnp.maximum(top, 1e-30))) + 1.0


def put_fixed(out_ref, blocks):
    rows, vectors = blocks[0].shape
    tail = iota((TAIL, vectors), 0)
    scales = jnp.zeros((TAIL, vectors), jnp.float32)
    for k, block in enumerate(blocks):
        scale = scale_of(block)
        scales = jnp.where(tail == k, scale, scales)
        fixed = jnp.floor(block * jnp.exp2(FIXED_BITS - scale) + 0.5)
        out_ref[k * rows : (k + 1) * rows] = fixed.astype(jnp.int32).astype(jnp.int16)
    out_ref[len(blocks) * rows :] = scales.astype(jnp.int32).astype(jnp.int16)


def from_fixed(ref, rows, k):
    scales = ref[ref.shape[0] - TAIL :].astype(jnp.int32).astype(jnp.float32)
    block = ref[k * rows : (k + 1) * rows].astype(jnp.int32).astype(jnp.float32)
    return block * jnp.exp2(scales[k : k + 1] - FIXED_BITS)


def group_block(held_ref, messages, j, start, rows):
    total = held_ref[j >> 1, pl.ds(start, rows)]
    for b, ref in enumerate(messages):
        total = total + fixed_at(ref.at[j >> (b + 1)], start, rows)
    return total


def fixed_at(ref, start, rows):
    tail = ref[ref.shape[0] - TAIL :].astype(jnp.int32).astype(jnp.float32)
    scale = jnp.max(
        jnp.where(iota(tail.shape, 0) == start // rows, tail, -1000.0), axis=0, keepdims=True
    )
    block = ref[pl.ds(start, rows)].astype(jnp.int32).astype(jnp.float32)
    return block * jnp.exp2(scale - FIXED_BITS)


def fold_kernel(level, vectors, held_ref, *refs):
    messages, out_ref = refs[:-1], refs[-1]
    for k in range(out_ref.shape[0]):
        blocks = [
            group_block(held_ref, messages, (2 * k + 1) << level, start, vectors)
            for start in range(0, held_ref.shape[1], vectors)
        ]
        put_fixed(out_ref.at[k], blocks)


def half_blocks(held_ref, messages, j, kept, vectors):
    me = lax.axis_index("gx") & 1
    half = held_ref.shape[1] // 2
    base = pl.multiple_of((me if kept else 1 - me) * half, half)
    steps = range(0, half, vectors)
    return [group_block(held_ref, messages, j, base + step, vectors) for step in steps]


def spread_kernel(level, vectors, held_ref, *refs):
    messages, (y_ref, diagonal_ref, x_ref) = refs[:-3], refs[-3:]
    put_fixed(y_ref, half_blocks(held_ref, messages, 1 << level, True, vectors))
    put_fixed(diagonal_ref, half_blocks(held_ref, messages, 1 << level, False, vectors))
    put_fixed(x_ref, half_blocks(held_ref, messages, 0, False, vectors))


def keep_kernel(vectors, held_ref, *refs):
    messages, came, out_ref = refs[:-4], refs[-4:-1], refs[-1]
    blocks = half_blocks(held_ref, messages, 0, True, vectors)
    for p in range(len(blocks)):
        for ref in came:
            blocks[p] = blocks[p] + from_fixed(ref, vectors, p)
    put_fixed(out_ref, blocks)


def both_kernel(vectors, norm_factor, own_ref, arrived_ref, out_ref):
    blocks = [
        from_fixed(own_ref, vectors, p) + from_fixed(arrived_ref, vectors, p)
        for p in range((own_ref.shape[0] - TAIL) // vectors)
    ]
    if norm_factor is None:
        put_fixed(out_ref, blocks)
        return
    for p, block in enumerate(blocks):
        out_ref[p * vectors : (p + 1) * vectors] = (block * norm_factor).astype(out_ref.dtype)


def contract(sums_ref, weight_ref, blocks, tau_ref, left_ref, right_ref):
    f32, bf16 = jnp.float32, jnp.bfloat16
    vectors = sums_ref.shape[2]
    count_ops = sums_ref.shape[0] // 2
    order = tau_ref.shape[2]
    spins = order // vectors
    me_t = lax.axis_index("ta")
    times = len(blocks)

    def chosen(end, k):
        total = jnp.zeros((vectors // 8, 8, vectors), f32)
        for t in range(times):
            weight = weight_ref[end, lax.rem(me_t + t, times)]
            total = total + blocks[t](k).astype(f32).reshape(total.shape) * weight
        return total.reshape(vectors, vectors)

    for o in range(count_ops):
        first = 2 * o * vectors
        a_r, a_i = chosen(0, 2 * o).astype(bf16), chosen(0, 2 * o + 1).astype(bf16)
        b_r, b_i = chosen(1, 2 * o).T.astype(bf16), chosen(1, 2 * o + 1).T.astype(bf16)
        real, imag = slice(first, first + vectors), slice(first + vectors, first + 2 * vectors)
        left_ref[real, 0:vectors] = a_r
        left_ref[real, vectors:] = -a_i
        left_ref[imag, 0:vectors] = a_i
        left_ref[imag, vectors:] = a_r
        right_ref[0:vectors, real] = b_r
        right_ref[0:vectors, imag] = -b_i
        right_ref[vectors:, real] = b_i
        right_ref[vectors:, imag] = b_r
    lanes = sums_ref.shape[1]
    fold = lambda t: jnp.sum(t.reshape(vectors // lanes, lanes, vectors), axis=0)
    sums = [jnp.zeros((lanes, vectors), f32) for _ in range(2 * count_ops)]
    for s in range(spins):
        rows = slice(s * vectors, (s + 1) * vectors)
        x = jnp.dot(
            left_ref[...],
            jnp.concatenate([tau_ref[0, rows], tau_ref[1, rows]], axis=0),
            preferred_element_type=f32,
        )
        for c in range(spins):
            cols = slice(c * vectors, (c + 1) * vectors)
            y = jnp.dot(
                jnp.concatenate([tau_ref[0, rows, cols], tau_ref[1, rows, cols]], axis=1),
                right_ref[...],
                preferred_element_type=f32,
            )
            for o in range(count_ops):
                first = 2 * o * vectors
                x_r = x[first : first + vectors, cols]
                x_i = x[first + vectors : first + 2 * vectors, cols]
                y_r = y[:, first : first + vectors]
                y_i = y[:, first + vectors : first + 2 * vectors]
                sums[2 * o] = sums[2 * o] + fold(x_r * y_r + x_i * y_i)
                sums[2 * o + 1] = sums[2 * o + 1] + fold(x_i * y_r - x_r * y_i)
    for k, total in enumerate(sums):
        sums_ref[k] = total


def part_of(ref, vectors):
    return lambda k: ref[k * vectors : (k + 1) * vectors]


def traces(sums_ref, shape, first):
    vectors = sums_ref.shape[2]
    row, col = iota(shape, 0), iota(shape, 1)
    result = jnp.zeros(shape, jnp.float32)
    for k in range(sums_ref.shape[0]):
        total = jnp.sum(jnp.sum(sums_ref[k], axis=0, keepdims=True), axis=1, keepdims=True)
        here = (row == first + k // 2) & (col == k % 2)
        result = jnp.where(here, total * (1.0 / vectors), result)
    return result


def first_contract_kernel(times, split, live_ref, weight_ref, tau_ref, *refs):
    blocks, (live_out_ref, corr_ref, sums_ref, left_ref, right_ref) = refs[:times], refs[times:]
    live = jnp.where(live_ref[0] > 0, 1.0, 0.0)
    live_out_ref[...] = jnp.full(live_out_ref.shape, live, jnp.float32)
    if not split:
        corr_ref[...] = jnp.zeros_like(corr_ref)
        return
    blocks = [part_of(ref, sums_ref.shape[2]) for ref in blocks]
    contract(sums_ref, weight_ref, blocks, tau_ref, left_ref, right_ref)
    first = (lax.axis_index("gx") & 1) * (sums_ref.shape[0] // 2)
    corr_ref[...] = traces(sums_ref, corr_ref.shape, first)


def second_contract_kernel(times, split, weight_ref, tau_ref, *refs):
    other, kept, refs = refs[:times][::-1], refs[times : 2 * times], refs[2 * times :]
    live_ref, first_corr_ref, margin_ref, corr_ref, sums_ref, left_ref, right_ref = refs
    vectors = sums_ref.shape[2]
    half = kept[0].shape[0]
    me = lax.axis_index("gx") & 1
    for place, ref in ((me, kept[0]), (1 - me, other[0])):
        rows = pl.ds(pl.multiple_of(place * half, half), half)
        margin_ref[0, rows] = ref[...].astype(jnp.float32)
    parts_per_half = half // vectors

    def either(kept_ref, other_ref):
        def part(k):
            row = (k % parts_per_half) * vectors
            own, far = kept_ref[row : row + vectors], other_ref[row : row + vectors]
            mine = (k // parts_per_half == me).astype(jnp.float32)
            return own.astype(jnp.float32) * mine + far.astype(jnp.float32) * (1.0 - mine)

        return part

    blocks = [part_of(ref, vectors) for ref in other]
    if not split:
        blocks = [either(a, b) for a, b in zip(kept, other)]
    contract(sums_ref, weight_ref, blocks, tau_ref, left_ref, right_ref)
    shape = corr_ref.shape[1:]
    first = (1 - me) * (sums_ref.shape[0] // 2) if split else 0
    result = traces(sums_ref, shape, first) + first_corr_ref[...]
    corr_ref[0] = result * live_ref[0 : shape[0], 0 : shape[1]]


def vmem_spec():
    return pl.BlockSpec(memory_space=pltpu.VMEM)


def smem_spec():
    return pl.BlockSpec(memory_space=pltpu.SMEM)


def hbm_spec():
    return pl.BlockSpec(memory_space=pltpu.HBM)


def in_hbm(x):
    return pltpu.with_memory_space_constraint(x, pltpu.HBM)


def local_call(body, name, outs, in_specs, out_specs, scratch=(), cost=None):
    return pl.pallas_call(
        body,
        out_shape=outs,
        in_specs=in_specs,
        out_specs=out_specs,
        scratch_shapes=list(scratch),
        compiler_params=pltpu.CompilerParams(vmem_limit_bytes=VMEM_LIMIT),
        cost_estimate=cost,
        name=name,
    )


def from_step(block, axis, step):
    count = lax.axis_size(axis)
    return lax.ppermute(block, axis, [((i + step) % count, i) for i in range(count)])


def from_partner(block, axis, step):
    count = lax.axis_size(axis)
    return lax.ppermute(block, axis, [(i ^ step, i) for i in range(count)])


def from_diagonal(block, axes, sources):
    rows, columns = (lax.axis_size(axis) for axis in axes)
    perm = []
    for row in range(rows):
        for column in range(columns):
            from_row, from_column = sources(row, column)
            perm.append((from_row * columns + from_column, row * columns + column))
    return lax.ppermute(block, axes, perm)


def per_device(eigvecs, links, op_dirs, op_moms, perams, pair_times, slot_counts):
    f32, bf16 = jnp.float32, jnp.bfloat16
    _, cells_x, cells_y, cells_z, colors, _, vectors = eigvecs.shape
    order = cells_z * colors * 2
    lines = cells_x * cells_y
    count_ops = op_dirs.shape[0]
    times, shares, groups = lax.axis_size("ta"), lax.axis_size("gx"), lax.axis_size("gy")
    levels = groups.bit_length() - 1
    own_ops = count_ops // groups
    own_rows = own_ops * 2 * vectors
    field = eigvecs.reshape(cells_x, cells_y, order, vectors)
    halo_x = from_step(field[0:1], "gx", 1)
    halo_y = from_step(field, "gy", 1)
    link_field = links[0].transpose(0, 1, 3, 5, 6, 4, 2).reshape(lines, 27, 2, cells_z)
    outside, inside = halo_fields(cells_x, cells_y), local_fields(cells_x, cells_y)
    inputs = [field, link_field, op_dirs, op_moms, wave_constants(cells_z), pair_times]
    inputs = [in_hbm(x) for x in inputs]
    held = [
        pltpu.SMEM(x.shape, x.dtype) if x.dtype == jnp.int32 else pltpu.VMEM(x.shape, x.dtype)
        for x in inputs
    ]
    matrices, local, left, phases, weights = local_call(
        functools.partial(prepare_kernel, cells_x, cells_y),
        "prepare_lines",
        (
            jax.ShapeDtypeStruct((len(outside), order, 128), bf16),
            jax.ShapeDtypeStruct((len(inside), order, vectors), f32),
            jax.ShapeDtypeStruct((2, vectors, lines * order), bf16),
            jax.ShapeDtypeStruct((count_ops, order // 2, 2 * vectors), f32),
            jax.ShapeDtypeStruct((2, times, 8, vectors), f32),
        ),
        [hbm_spec()] * len(inputs),
        (vmem_spec(),) * 5,
        held
        + [
            pltpu.VMEM((lines, LINK_COLS, cells_z), f32),
            pltpu.SemaphoreType.DMA((len(inputs),)),
        ],
    )(*inputs)
    message = lambda rows, *lead: jax.ShapeDtypeStruct((*lead, rows + TAIL, vectors), jnp.int16)
    swap, held = local_call(
        functools.partial(margin_kernel, cells_x, cells_y, groups, own_ops),
        "partial_margins",
        (
            message(own_rows, groups // 2),
            jax.ShapeDtypeStruct((groups // 2, own_rows, vectors), f32),
        ),
        [vmem_spec()] * 6 + [hbm_spec()],
        (vmem_spec(),) * 2,
        [
            pltpu.VMEM((7, lines, order, vectors), f32),
            pltpu.VMEM((4, vectors, lines * order), bf16),
            pltpu.SMEM((count_ops,), jnp.int32),
            pltpu.SemaphoreType.DMA,
        ],
    )(matrices, local, left, phases, halo_x, halo_y, in_hbm(op_dirs))

    def in_vmem(body, name, outs, *inputs):
        outs = outs if isinstance(outs, tuple) else (outs,)
        specs = (vmem_spec(),) * len(outs)
        return local_call(body, name, outs, [vmem_spec()] * len(inputs), specs)(*inputs)

    half = own_rows // 2
    messages = [from_partner(swap, "gy", 1)]
    last = levels - 1
    for b in range(1, last):
        body = functools.partial(fold_kernel, b, vectors)
        shape = message(own_rows, groups >> (b + 1))
        (sent,) = in_vmem(body, "fold_groups", shape, held, *messages)
        messages.append(from_partner(sent, "gy", 1 << b))
    body = functools.partial(spread_kernel, last, vectors)
    for_y, for_both, for_x = in_vmem(body, "spread_halves", (message(half),) * 3, held, *messages)
    came = [
        from_partner(for_y, "gy", 1 << last),
        from_diagonal(for_both, ("gx", "gy"), lambda x, y: (x ^ 1, y ^ (1 << last))),
        from_partner(for_x, "gx", 1),
    ]
    body = functools.partial(keep_kernel, vectors)
    (packed,) = in_vmem(body, "keep_half", message(half), held, *messages, *came)
    norm_factor = 1.0 / math.sqrt(3.0 * cells_x * shares * cells_y * groups * cells_z)
    step = 2
    while step < shares:
        arrived = from_partner(packed, "gx", step)
        step *= 2
        last_one = step >= shares
        body = functools.partial(both_kernel, vectors, norm_factor if last_one else None)
        shape = jax.ShapeDtypeStruct((half, vectors), bf16) if last_one else message(half)
        (packed,) = in_vmem(body, "finish_half" if last_one else "sum_both", shape, packed, arrived)
    finished = packed
    kept = [finished] + [from_step(finished, "ta", t) for t in range(1, times)]
    other = [from_partner(finished, "gx", 1)]
    for t in range(1, times):
        source = lambda row, x: ((row + t) % times, x ^ 1)
        other.append(from_diagonal(finished, ("ta", "gx"), source))
    split = own_ops % 2 == 0
    now_ops = own_ops // 2 if split else own_ops
    sums_shape = (2 * now_ops, 32, vectors)
    scratch = [
        pltpu.VMEM((2 * now_ops * vectors, 2 * vectors), bf16),
        pltpu.VMEM((2 * vectors, 2 * now_ops * vectors), bf16),
    ]
    live, first_corr = local_call(
        functools.partial(first_contract_kernel, times, split),
        "first_contraction",
        (
            jax.ShapeDtypeStruct((8, vectors), f32),
            jax.ShapeDtypeStruct((own_ops, 2), f32),
        ),
        [smem_spec()] + [vmem_spec()] * (2 + times),
        (vmem_spec(),) * 2,
        [pltpu.VMEM(sums_shape, f32)] + scratch,
    )(slot_counts, weights, perams[0], *kept)
    margins, correlators = local_call(
        functools.partial(second_contract_kernel, times, split),
        "second_contraction",
        (
            jax.ShapeDtypeStruct((1, own_rows, vectors), f32),
            jax.ShapeDtypeStruct((1, own_ops, 2), f32),
        ),
        [vmem_spec()] * (4 + 2 * times),
        (vmem_spec(),) * 2,
        [pltpu.VMEM(sums_shape, f32)] + scratch,
    )(weights, perams[0], *other[::-1], *kept, live, first_corr)
    return (margins.reshape(1, own_ops, 2, vectors, vectors), correlators)


def solution(mesh):
    placed = (
        P("ta", "gx", "gy", None, None, None, None),
        P("ta", "gx", "gy", None, None, None, None, None),
        P(),
        P(),
        P(("ta", "gx"), None, None, None),
        P(("ta", "gx"), None),
        P(("ta", "gx")),
    )
    return jax.shard_map(
        per_device,
        mesh=mesh,
        in_specs=placed,
        out_specs=(P("ta", "gy", None, None, None), P(("ta", "gx"), "gy", None)),
        check_vma=False,
    )
```

```python
import functools
import math

import jax
import jax.numpy as jnp
import numpy as np
from jax import lax
from jax.experimental import pallas as pl
from jax.experimental.pallas import tpu as pltpu
from jax.sharding import PartitionSpec as P

VMEM_LIMIT = 24 * 1024 * 1024
MOMENTA = 3
LINK_COLS = 54
TAIL = 16
FIXED_BITS = 14.0


def wave_constants(cells_z):
    z_row = np.arange(3 * cells_z) // 3
    columns = []
    for ahead in range(2):
        for momentum in range(MOMENTA):
            angle = 2.0 * math.pi * momentum * ((z_row + ahead) % cells_z) / cells_z
            columns.append(np.cos(angle))
            columns.append(np.sin(angle))
    left = np.stack(columns, axis=1).astype(np.float32)
    terms = []
    for _ in range(3):
        term = left.astype(jnp.bfloat16).astype(np.float32)
        terms.append(term)
        left = left - term
    return jnp.asarray(np.concatenate(terms, axis=1), jnp.bfloat16)


def iota(shape, axis):
    return lax.broadcasted_iota(jnp.int32, shape, axis)


def third(x):
    return (x * 21846) >> 16


def one_hot(condition):
    return condition.astype(jnp.float32).astype(jnp.bfloat16)


def planar_order(order):
    row, col = iota((order, order), 0), iota((order, order), 1)
    half = order // 2
    source = jnp.where(row < half, 2 * row, 2 * (row - half) + 1)
    return one_hot(col == source)


def side_by_side(planar):
    half = planar.shape[0] // 2
    return jnp.concatenate([planar[:half], planar[half:]], axis=1).astype(jnp.bfloat16)


def transport(matrix, pair, sign):
    half, vectors = matrix.shape[0] // 2, pair.shape[1] // 2
    parts = jnp.dot(matrix, pair, preferred_element_type=jnp.float32)
    real, imag = parts[:half], parts[half:]
    if sign > 0:
        return jnp.concatenate(
            [real[:, :vectors] - imag[:, vectors:], real[:, vectors:] + imag[:, :vectors]], axis=0
        )
    return jnp.concatenate(
        [real[:, :vectors] + imag[:, vectors:], real[:, vectors:] - imag[:, :vectors]], axis=0
    )


def leaves(cells_x, cells_y, code, line):
    if code in (0, 3):
        return line // cells_y == 0
    return code == 1 and line % cells_y == cells_y - 1


def local_fields(cells_x, cells_y):
    every = [(code, line) for code in range(7) for line in range(cells_x * cells_y)]
    return [pair for pair in every if not leaves(cells_x, cells_y, *pair)]


class LinkForms:
    def __init__(self, half):
        cells_z = half // 3
        self.half = half
        self.spread = one_hot(third(iota((half, cells_z), 0)) == iota((half, cells_z), 1))
        row, col = iota((half, LINK_COLS), 0), iota((half, LINK_COLS), 1)
        row_color = row - 3 * third(row)
        pair_at = third(col >> 1)
        col_in, col_out = (col >> 1) - 3 * pair_at, pair_at - 3 * third(pair_at)
        self.pick = [(row_color == c).astype(jnp.float32) for c in (col_out, col_in)]
        row, col = iota((LINK_COLS, 6 * 128), 0), iota((LINK_COLS, 6 * 128), 1)
        block, place = col >> 7, col & 127
        color = place - 3 * third(place)
        pair_at = third(row >> 1)
        row_in, row_out = (row >> 1) - 3 * pair_at, pair_at - 3 * third(pair_at)
        fits = 2 * third(pair_at) + (row & 1) == block
        self.expand = [one_hot(fits & (c == color)) for c in (row_in, row_out)]
        row, col = iota((half, 128), 0), iota((half, 128), 1)
        self.near = ((third(row) == third(col)) & (col < half)).astype(jnp.float32)

    def seen(self, link_ref, rows_ref):
        for k in range(LINK_COLS // 2):
            rows_ref[2 * k : 2 * k + 2] = link_ref[k].astype(jnp.float32)
        return lax.dot_general(
            self.spread,
            rows_ref[...].astype(jnp.bfloat16),
            (((1,), (1,)), ((), ())),
            preferred_element_type=jnp.float32,
        )

    def matrices(self, seen, way, directions):
        blocks = jnp.dot(
            (seen * self.pick[way]).astype(jnp.bfloat16),
            self.expand[way][:, : 256 * directions],
            preferred_element_type=jnp.float32,
        )
        cut = lambda k: blocks[:, 128 * k : 128 * k + 128] * self.near
        return [
            jnp.concatenate([cut(2 * d), cut(2 * d + 1)], axis=0).astype(jnp.bfloat16)
            for d in range(directions)
        ]


def prepare_kernel(cells_x, cells_y, *refs):
    inputs, refs = refs[:6], refs[6:]
    matrix_ref, local_ref, left_ref, phase_ref, weight_ref = refs[:5]
    held, link_rows_ref, sems = refs[5:11], refs[11], refs[12]
    copies = [
        pltpu.make_async_copy(src, dst, sems.at[k])
        for k, (src, dst) in enumerate(zip(inputs, held))
    ]
    for copy in copies:
        copy.start()
    v_ref, link_ref, dirs_ref, moms_ref, waves_ref, pair_ref = held
    f32, bf16 = jnp.float32, jnp.bfloat16
    order, vectors = v_ref.shape[2], v_ref.shape[3]
    half = order // 2
    lines = cells_x * cells_y
    times = weight_ref.shape[1]
    forms = LinkForms(half)
    planar = planar_order(order)
    for copy in copies:
        copy.wait()
    for t in range(times):
        sink = pair_ref[0, 0] == t
        source = pair_ref[0, 1] == t
        weight_ref[0, t] = jnp.full(weight_ref.shape[2:], jnp.where(sink, 1.0, 0.0), f32)
        weight_ref[1, t] = jnp.full(weight_ref.shape[2:], jnp.where(source, 1.0, 0.0), f32)
    inside = local_fields(cells_x, cells_y)
    ordered = []
    for line in range(lines):
        here = jnp.dot(
            planar, v_ref[line // cells_y, line % cells_y], preferred_element_type=f32
        )
        ordered.append(here)
        local_ref[inside.index((6, line))] = here
    for line in range(lines):
        here = ordered[line]
        ahead_z = jnp.concatenate(
            [here[3:half], here[:3], here[half + 3 :], here[half : half + 3]], axis=0
        )
        columns = slice(line * order, (line + 1) * order)
        left_ref[0, :, columns] = here.T.astype(bf16)
        left_ref[1, :, columns] = ahead_z.T.astype(bf16)
        seen = forms.seen(link_ref.at[line], link_rows_ref.at[line])
        pair = side_by_side(here)
        on_x = line + cells_y if line + cells_y < lines else None
        for d, matrix in enumerate(forms.matrices(seen, 0, 3)):
            if d == 0 and on_x is None:
                continue
            if d == 1 and leaves(cells_x, cells_y, 1, line):
                matrix_ref[line // cells_y] = matrix
                continue
            ahead = (ordered[on_x] if d == 0 else ordered[line + 1]) if d < 2 else ahead_z
            local_ref[inside.index((d, on_x if d == 0 else line))] = transport(
                matrix[:, :half], side_by_side(ahead), 1
            )
        for d, matrix in enumerate(forms.matrices(seen, 1, 3)):
            if d == 0 and on_x is None:
                continue
            carried = transport(matrix[:, :half], pair, -1).astype(bf16).astype(f32)
            local_ref[inside.index((3 + d, on_x if d == 0 else line))] = carried
    wave_cols = waves_ref.shape[1]
    per_term = wave_cols // 3
    row, col = iota((wave_cols, 2 * vectors), 0), iota((wave_cols, 2 * vectors), 1)
    term = (row >= per_term).astype(jnp.int32) + (row >= 2 * per_term).astype(jnp.int32)
    wave_at = row - per_term * term - (col >= vectors).astype(jnp.int32)
    for o in range(phase_ref.shape[0]):
        column = 2 * (jnp.where(dirs_ref[o] == 5, MOMENTA, 0) + moms_ref[o])
        phase_ref[o] = jnp.dot(
            waves_ref[...], one_hot(wave_at == column), preferred_element_type=f32
        )


def margin_kernel(cells_x, cells_y, groups, own_ops, *refs):
    matrix_ref, local_ref, left_ref, phase_ref = refs[:4]
    links_x_ref, halo_x_ref, halo_y_ref, dirs_hbm = refs[4:8]
    swap_ref, hold_ref = refs[8:10]
    field_ref, side_ref, rows_ref, dirs_ref, sem = refs[10:]
    f32, bf16 = jnp.float32, jnp.bfloat16
    copy = pltpu.make_async_copy(dirs_hbm, dirs_ref, sem)
    copy.start()
    lines = cells_x * cells_y
    order, vectors = halo_x_ref.shape[2], halo_x_ref.shape[3]
    half = order // 2
    planar = planar_order(order)
    forms = LinkForms(half)
    inside = local_fields(cells_x, cells_y)
    side_ref[0] = left_ref[0]
    side_ref[3] = left_ref[1]
    for line in range(lines):
        x, y = line // cells_y, line % cells_y
        columns = slice(line * order, (line + 1) * order)
        if x:
            back = line - cells_y
            side_ref[1, :, columns] = left_ref[0, :, back * order : (back + 1) * order]
        else:
            seen = forms.seen(links_x_ref.at[y], rows_ref.at[y])
            here = side_by_side(local_ref[inside.index((6, line))])
            field_ref[0, line] = transport(forms.matrices(seen, 0, 1)[0][:, :half], here, 1)
            back = jnp.dot(planar, halo_x_ref[0, y], preferred_element_type=f32)
            side_ref[1, :, columns] = back.T.astype(bf16)
            adjoint = forms.matrices(seen, 1, 1)[0][:, :half]
            carried = transport(adjoint, side_by_side(back), -1)
            field_ref[3, line] = carried.astype(bf16).astype(f32)
        if y + 1 < cells_y:
            side_ref[2, :, columns] = left_ref[0, :, (line + 1) * order : (line + 2) * order]
        else:
            ahead = jnp.dot(planar, halo_y_ref[x, 0], preferred_element_type=f32)
            side_ref[2, :, columns] = ahead.T.astype(bf16)
            field_ref[1, line] = transport(matrix_ref[x, :, :half], side_by_side(ahead), 1)
    for k, (code, line) in enumerate(inside):
        field_ref[code, line] = local_ref[k]
    copy.wait()
    me = lax.axis_index("gy")
    for j in sorted(range(groups), key=lambda j: -(j & 1)):
        blocks = []
        for i in range(own_ops):
            o = (me ^ j) * own_ops + i
            code = dirs_ref[o]
            side = jnp.where(code == 0, 1, jnp.where((code == 4) | (code == 5), code - 2, 0))
            cosine = phase_ref[o, :, 0:vectors]
            sine = phase_ref[o, :, vectors : 2 * vectors]
            pairs = []
            for line in range(lines):
                real, imag = field_ref[code, line, 0:half], field_ref[code, line, half:order]
                turned_r, turned_i = cosine * real - sine * imag, sine * real + cosine * imag
                pairs.append(jnp.concatenate([turned_r, turned_i], axis=1))
                pairs.append(jnp.concatenate([turned_i, -turned_r], axis=1))
            pair = jnp.concatenate(pairs, axis=0).astype(bf16)
            product = jnp.dot(side_ref[side], pair, preferred_element_type=f32)
            blocks += [product[:, :vectors], product[:, vectors:]]
        if j & 1:
            put_fixed(swap_ref.at[j >> 1], blocks)
            continue
        for k, block in enumerate(blocks):
            hold_ref[j >> 1, k * vectors : (k + 1) * vectors] = block


def scale_of(block):
    top = jnp.max(jnp.abs(block), axis=0, keepdims=True)
    return jnp.floor(jnp.log2(jnp.maximum(top, 1e-30))) + 1.0


def put_fixed(out_ref, blocks):
    rows, vectors = blocks[0].shape
    tail = iota((TAIL, vectors), 0)
    scales = jnp.zeros((TAIL, vectors), jnp.float32)
    for k, block in enumerate(blocks):
        scale = scale_of(block)
        scales = jnp.where(tail == k, scale, scales)
        fixed = jnp.floor(block * jnp.exp2(FIXED_BITS - scale) + 0.5)
        out_ref[k * rows : (k + 1) * rows] = fixed.astype(jnp.int32).astype(jnp.int16)
    out_ref[len(blocks) * rows :] = scales.astype(jnp.int32).astype(jnp.int16)


def from_fixed(ref, rows, k):
    scales = ref[ref.shape[0] - TAIL :].astype(jnp.int32).astype(jnp.float32)
    block = ref[k * rows : (k + 1) * rows].astype(jnp.int32).astype(jnp.float32)
    return block * jnp.exp2(scales[k : k + 1] - FIXED_BITS)


def group_block(held_ref, messages, j, start, rows):
    total = held_ref[j >> 1, pl.ds(start, rows)]
    for b, ref in enumerate(messages):
        total = total + fixed_at(ref.at[j >> (b + 1)], start, rows)
    return total


def fixed_at(ref, start, rows):
    tail = ref[ref.shape[0] - TAIL :].astype(jnp.int32).astype(jnp.float32)
    scale = jnp.max(
        jnp.where(iota(tail.shape, 0) == start // rows, tail, -1000.0), axis=0, keepdims=True
    )
    block = ref[pl.ds(start, rows)].astype(jnp.int32).astype(jnp.float32)
    return block * jnp.exp2(scale - FIXED_BITS)


def fold_kernel(level, vectors, held_ref, *refs):
    messages, out_ref = refs[:-1], refs[-1]
    for k in range(out_ref.shape[0]):
        blocks = [
            group_block(held_ref, messages, (2 * k + 1) << level, start, vectors)
            for start in range(0, held_ref.shape[1], vectors)
        ]
        put_fixed(out_ref.at[k], blocks)


def half_blocks(held_ref, messages, j, kept, vectors):
    me = lax.axis_index("gx") & 1
    half = held_ref.shape[1] // 2
    base = pl.multiple_of((me if kept else 1 - me) * half, half)
    steps = range(0, half, vectors)
    return [group_block(held_ref, messages, j, base + step, vectors) for step in steps]


def spread_kernel(level, vectors, held_ref, *refs):
    messages, (y_ref, diagonal_ref, x_ref) = refs[:-3], refs[-3:]
    put_fixed(y_ref, half_blocks(held_ref, messages, 1 << level, True, vectors))
    put_fixed(diagonal_ref, half_blocks(held_ref, messages, 1 << level, False, vectors))
    put_fixed(x_ref, half_blocks(held_ref, messages, 0, False, vectors))


def keep_kernel(vectors, held_ref, *refs):
    messages, came, out_ref = refs[:-4], refs[-4:-1], refs[-1]
    blocks = half_blocks(held_ref, messages, 0, True, vectors)
    for p in range(len(blocks)):
        for ref in came:
            blocks[p] = blocks[p] + from_fixed(ref, vectors, p)
    put_fixed(out_ref, blocks)


def both_kernel(vectors, norm_factor, own_ref, arrived_ref, out_ref):
    blocks = [
        from_fixed(own_ref, vectors, p) + from_fixed(arrived_ref, vectors, p)
        for p in range((own_ref.shape[0] - TAIL) // vectors)
    ]
    if norm_factor is None:
        put_fixed(out_ref, blocks)
        return
    for p, block in enumerate(blocks):
        out_ref[p * vectors : (p + 1) * vectors] = (block * norm_factor).astype(out_ref.dtype)


def contract(sums_ref, weight_ref, blocks, tau_ref, left_ref, right_ref):
    f32, bf16 = jnp.float32, jnp.bfloat16
    vectors = sums_ref.shape[2]
    count_ops = sums_ref.shape[0] // 2
    order = tau_ref.shape[2]
    spins = order // vectors
    me_t = lax.axis_index("ta")
    times = len(blocks)

    def chosen(end, k):
        total = jnp.zeros((vectors // 8, 8, vectors), f32)
        for t in range(times):
            weight = weight_ref[end, lax.rem(me_t + t, times)]
            total = total + blocks[t](k).astype(f32).reshape(total.shape) * weight
        return total.reshape(vectors, vectors)

    for o in range(count_ops):
        first = 2 * o * vectors
        a_r, a_i = chosen(0, 2 * o).astype(bf16), chosen(0, 2 * o + 1).astype(bf16)
        b_r, b_i = chosen(1, 2 * o).T.astype(bf16), chosen(1, 2 * o + 1).T.astype(bf16)
        real, imag = slice(first, first + vectors), slice(first + vectors, first + 2 * vectors)
        left_ref[real, 0:vectors] = a_r
        left_ref[real, vectors:] = -a_i
        left_ref[imag, 0:vectors] = a_i
        left_ref[imag, vectors:] = a_r
        right_ref[0:vectors, real] = b_r
        right_ref[0:vectors, imag] = -b_i
        right_ref[vectors:, real] = b_i
        right_ref[vectors:, imag] = b_r
    lanes = sums_ref.shape[1]
    fold = lambda t: jnp.sum(t.reshape(vectors // lanes, lanes, vectors), axis=0)
    sums = [jnp.zeros((lanes, vectors), f32) for _ in range(2 * count_ops)]
    for s in range(spins):
        rows = slice(s * vectors, (s + 1) * vectors)
        x = jnp.dot(
            left_ref[...],
            jnp.concatenate([tau_ref[0, rows], tau_ref[1, rows]], axis=0),
            preferred_element_type=f32,
        )
        columns = [slice(c * vectors, (c + 1) * vectors) for c in range(spins)]
        side = [
            jnp.concatenate([tau_ref[0, rows, cols], tau_ref[1, rows, cols]], axis=1)
            for cols in columns
        ]
        whole_y = jnp.dot(
            jnp.concatenate(side, axis=0), right_ref[...], preferred_element_type=f32
        )
        for c, cols in enumerate(columns):
            y = whole_y[c * vectors : (c + 1) * vectors]
            for o in range(count_ops):
                first = 2 * o * vectors
                x_r = x[first : first + vectors, cols]
                x_i = x[first + vectors : first + 2 * vectors, cols]
                y_r = y[:, first : first + vectors]
                y_i = y[:, first + vectors : first + 2 * vectors]
                sums[2 * o] = sums[2 * o] + fold(x_r * y_r + x_i * y_i)
                sums[2 * o + 1] = sums[2 * o + 1] + fold(x_i * y_r - x_r * y_i)
    for k, total in enumerate(sums):
        sums_ref[k] = total


def part_of(ref, vectors):
    return lambda k: ref[k * vectors : (k + 1) * vectors]


def first_contract_kernel(times, split, live_ref, weight_ref, tau_ref, *refs):
    blocks, (live_out_ref, sums_ref, left_ref, right_ref) = refs[:times], refs[times:]
    live = jnp.where(live_ref[0] > 0, 1.0, 0.0)
    live_out_ref[...] = jnp.full(live_out_ref.shape, live, jnp.float32)
    if split:
        vectors = sums_ref.shape[2]
        blocks = [part_of(ref, vectors) for ref in blocks]
        contract(sums_ref, weight_ref, blocks, tau_ref, left_ref, right_ref)
    else:
        sums_ref[...] = jnp.zeros_like(sums_ref)


def margins_kernel(kept_ref, other_ref, margin_ref):
    half = kept_ref.shape[0]
    me = lax.axis_index("gx") & 1
    for place, ref in ((me, kept_ref), (1 - me, other_ref)):
        rows = pl.ds(pl.multiple_of(place * half, half), half)
        margin_ref[0, rows] = ref[...].astype(jnp.float32)


def second_contract_kernel(times, split, weight_ref, tau_ref, *refs):
    other, kept, refs = refs[:times], refs[times : 2 * times], refs[2 * times :]
    live_ref, first_sums_ref, corr_ref, sums_ref, left_ref, right_ref = refs
    vectors = sums_ref.shape[2]
    half = kept[0].shape[0]
    me = lax.axis_index("gx") & 1
    parts_per_half = half // vectors

    def either(kept_ref, other_ref):
        def part(k):
            row = (k % parts_per_half) * vectors
            own, far = kept_ref[row : row + vectors], other_ref[row : row + vectors]
            mine = (k // parts_per_half == me).astype(jnp.float32)
            return own.astype(jnp.float32) * mine + far.astype(jnp.float32) * (1.0 - mine)

        return part

    blocks = [part_of(ref, vectors) for ref in other]
    if not split:
        blocks = [either(a, b) for a, b in zip(kept, other)]
    contract(sums_ref, weight_ref, blocks, tau_ref, left_ref, right_ref)
    now_ops = sums_ref.shape[0] // 2
    known = [(sums_ref, (1 - me) * now_ops)] if split else [(sums_ref, 0)]
    if split:
        known.append((first_sums_ref, me * now_ops))
    shape = corr_ref.shape[1:]
    row, col = iota(shape, 0), iota(shape, 1)
    result = jnp.zeros(shape, jnp.float32)
    for ref, first in known:
        for k in range(2 * now_ops):
            total = jnp.sum(jnp.sum(ref[k], axis=0, keepdims=True), axis=1, keepdims=True)
            here = (row == first + k // 2) & (col == k % 2)
            result = jnp.where(here, total * (1.0 / vectors), result)
    corr_ref[0] = result * live_ref[0 : shape[0], 0 : shape[1]]


def vmem_spec():
    return pl.BlockSpec(memory_space=pltpu.VMEM)


def smem_spec():
    return pl.BlockSpec(memory_space=pltpu.SMEM)


def hbm_spec():
    return pl.BlockSpec(memory_space=pltpu.HBM)


def in_hbm(x):
    return pltpu.with_memory_space_constraint(x, pltpu.HBM)


def local_call(body, name, outs, in_specs, out_specs, scratch=(), cost=None):
    return pl.pallas_call(
        body,
        out_shape=outs,
        in_specs=in_specs,
        out_specs=out_specs,
        scratch_shapes=list(scratch),
        compiler_params=pltpu.CompilerParams(vmem_limit_bytes=VMEM_LIMIT),
        cost_estimate=cost,
        name=name,
    )


def from_step(block, axis, step):
    count = lax.axis_size(axis)
    return lax.ppermute(block, axis, [((i + step) % count, i) for i in range(count)])


def from_partner(block, axis, step):
    count = lax.axis_size(axis)
    return lax.ppermute(block, axis, [(i ^ step, i) for i in range(count)])


def from_diagonal(block, axes, sources):
    rows, columns = (lax.axis_size(axis) for axis in axes)
    perm = []
    for row in range(rows):
        for column in range(columns):
            from_row, from_column = sources(row, column)
            perm.append((from_row * columns + from_column, row * columns + column))
    return lax.ppermute(block, axes, perm)


def per_device(eigvecs, links, op_dirs, op_moms, perams, pair_times, slot_counts):
    f32, bf16 = jnp.float32, jnp.bfloat16
    _, cells_x, cells_y, cells_z, colors, _, vectors = eigvecs.shape
    order = cells_z * colors * 2
    lines = cells_x * cells_y
    count_ops = op_dirs.shape[0]
    times, shares, groups = lax.axis_size("ta"), lax.axis_size("gx"), lax.axis_size("gy")
    levels = groups.bit_length() - 1
    own_ops = count_ops // groups
    own_rows = own_ops * 2 * vectors
    field = eigvecs.reshape(cells_x, cells_y, order, vectors)
    link_field = links[0].transpose(0, 1, 3, 5, 6, 4, 2).reshape(lines, 27, 2, cells_z)
    links_x = from_step(link_field[lines - cells_y :], "gx", -1)
    halo_x = from_step(field[cells_x - 1 :], "gx", -1)
    halo_y = from_step(field, "gy", 1)
    inside = local_fields(cells_x, cells_y)
    inputs = [field, link_field, op_dirs, op_moms, wave_constants(cells_z), pair_times]
    inputs = [in_hbm(x) for x in inputs]
    held = [
        pltpu.SMEM(x.shape, x.dtype) if x.dtype == jnp.int32 else pltpu.VMEM(x.shape, x.dtype)
        for x in inputs
    ]
    matrices, local, left, phases, weights = local_call(
        functools.partial(prepare_kernel, cells_x, cells_y),
        "prepare_lines",
        (
            jax.ShapeDtypeStruct((cells_x, order, 128), bf16),
            jax.ShapeDtypeStruct((len(inside), order, vectors), f32),
            jax.ShapeDtypeStruct((2, vectors, lines * order), bf16),
            jax.ShapeDtypeStruct((count_ops, order // 2, 2 * vectors), f32),
            jax.ShapeDtypeStruct((2, times, 8, vectors), f32),
        ),
        [hbm_spec()] * len(inputs),
        (vmem_spec(),) * 5,
        held
        + [
            pltpu.VMEM((lines, LINK_COLS, cells_z), f32),
            pltpu.SemaphoreType.DMA((len(inputs),)),
        ],
    )(*inputs)
    message = lambda rows, *lead: jax.ShapeDtypeStruct((*lead, rows + TAIL, vectors), jnp.int16)
    swap, held = local_call(
        functools.partial(margin_kernel, cells_x, cells_y, groups, own_ops),
        "partial_margins",
        (
            message(own_rows, groups // 2),
            jax.ShapeDtypeStruct((groups // 2, own_rows, vectors), f32),
        ),
        [vmem_spec()] * 7 + [hbm_spec()],
        (vmem_spec(),) * 2,
        [
            pltpu.VMEM((7, lines, order, vectors), f32),
            pltpu.VMEM((4, vectors, lines * order), bf16),
            pltpu.VMEM((cells_y, LINK_COLS, cells_z), f32),
            pltpu.SMEM((count_ops,), jnp.int32),
            pltpu.SemaphoreType.DMA,
        ],
    )(matrices, local, left, phases, links_x, halo_x, halo_y, in_hbm(op_dirs))

    def in_vmem(body, name, outs, *inputs):
        outs = outs if isinstance(outs, tuple) else (outs,)
        specs = (vmem_spec(),) * len(outs)
        return local_call(body, name, outs, [vmem_spec()] * len(inputs), specs)(*inputs)

    half = own_rows // 2
    messages = [from_partner(swap, "gy", 1)]
    last = levels - 1
    for b in range(1, last):
        body = functools.partial(fold_kernel, b, vectors)
        shape = message(own_rows, groups >> (b + 1))
        (sent,) = in_vmem(body, "fold_groups", shape, held, *messages)
        messages.append(from_partner(sent, "gy", 1 << b))
    body = functools.partial(spread_kernel, last, vectors)
    for_y, for_both, for_x = in_vmem(body, "spread_halves", (message(half),) * 3, held, *messages)
    came = [
        from_partner(for_y, "gy", 1 << last),
        from_diagonal(for_both, ("gx", "gy"), lambda x, y: (x ^ 1, y ^ (1 << last))),
        from_partner(for_x, "gx", 1),
    ]
    body = functools.partial(keep_kernel, vectors)
    (packed,) = in_vmem(body, "keep_half", message(half), held, *messages, *came)
    norm_factor = 1.0 / math.sqrt(3.0 * cells_x * shares * cells_y * groups * cells_z)
    step = 2
    while step < shares:
        arrived = from_partner(packed, "gx", step)
        step *= 2
        last_one = step >= shares
        body = functools.partial(both_kernel, vectors, norm_factor if last_one else None)
        shape = jax.ShapeDtypeStruct((half, vectors), bf16) if last_one else message(half)
        (packed,) = in_vmem(body, "finish_half" if last_one else "sum_both", shape, packed, arrived)
    finished = packed
    kept = [finished] + [from_step(finished, "ta", t) for t in range(1, times)]
    other = [from_partner(finished, "gx", 1)]
    for t in range(1, times):
        source = lambda row, x: ((row + t) % times, x ^ 1)
        other.append(from_diagonal(finished, ("ta", "gx"), source))
    split = own_ops % 2 == 0
    now_ops = own_ops // 2 if split else own_ops
    sums_shape = (2 * now_ops, 32, vectors)
    scratch = [
        pltpu.VMEM((2 * now_ops * vectors, 2 * vectors), bf16),
        pltpu.VMEM((2 * vectors, 2 * now_ops * vectors), bf16),
    ]
    live, sums = local_call(
        functools.partial(first_contract_kernel, times, split),
        "first_contraction",
        (jax.ShapeDtypeStruct((8, vectors), f32), jax.ShapeDtypeStruct(sums_shape, f32)),
        [smem_spec()] + [vmem_spec()] * (2 + times),
        (vmem_spec(),) * 2,
        scratch,
    )(slot_counts, weights, perams[0], *kept)
    margins = local_call(
        margins_kernel,
        "margins_out",
        jax.ShapeDtypeStruct((1, own_rows, vectors), f32),
        [vmem_spec()] * 2,
        vmem_spec(),
    )(*lax.optimization_barrier((kept[0], other[0], sums))[:2])
    correlators = local_call(
        functools.partial(second_contract_kernel, times, split),
        "second_contraction",
        jax.ShapeDtypeStruct((1, own_ops, 2), f32),
        [vmem_spec()] * (4 + 2 * times),
        vmem_spec(),
        [pltpu.VMEM(sums_shape, f32)] + scratch,
    )(weights, perams[0], *other, *kept, live, sums)
    return (margins.reshape(1, own_ops, 2, vectors, vectors), correlators)


def solution(mesh):
    placed = (
        P("ta", "gx", "gy", None, None, None, None),
        P("ta", "gx", "gy", None, None, None, None, None),
        P(),
        P(),
        P(("ta", "gx"), None, None, None),
        P(("ta", "gx"), None),
        P(("ta", "gx")),
    )
    return jax.shard_map(
        per_device,
        mesh=mesh,
        in_specs=placed,
        out_specs=(P("ta", "gy", None, None, None), P(("ta", "gx"), "gy", None)),
        check_vma=False,
    )
```

```python
import functools
import math

import jax
import jax.numpy as jnp
import numpy as np
from jax import lax
from jax.experimental import pallas as pl
from jax.experimental.pallas import tpu as pltpu
from jax.sharding import PartitionSpec as P

VMEM_LIMIT = 24 * 1024 * 1024
MOMENTA = 3
LINK_COLS = 54
TAIL = 16
FIXED_BITS = 14.0


def wave_constants(cells_z):
    z_row = np.arange(3 * cells_z) // 3
    columns = []
    for ahead in range(2):
        for momentum in range(MOMENTA):
            angle = 2.0 * math.pi * momentum * ((z_row + ahead) % cells_z) / cells_z
            columns.append(np.cos(angle))
            columns.append(np.sin(angle))
    left = np.stack(columns, axis=1).astype(np.float32)
    terms = []
    for _ in range(3):
        term = left.astype(jnp.bfloat16).astype(np.float32)
        terms.append(term)
        left = left - term
    return jnp.asarray(np.concatenate(terms, axis=1), jnp.bfloat16)


def iota(shape, axis):
    return lax.broadcasted_iota(jnp.int32, shape, axis)


def third(x):
    return (x * 21846) >> 16


def one_hot(condition):
    return condition.astype(jnp.float32).astype(jnp.bfloat16)


def planar_order(order):
    row, col = iota((order, order), 0), iota((order, order), 1)
    half = order // 2
    source = jnp.where(row < half, 2 * row, 2 * (row - half) + 1)
    return one_hot(col == source)


def side_by_side(planar):
    half = planar.shape[0] // 2
    return jnp.concatenate([planar[:half], planar[half:]], axis=1).astype(jnp.bfloat16)


def transport(matrix, pair, sign):
    half, vectors = matrix.shape[0] // 2, pair.shape[1] // 2
    parts = jnp.dot(matrix, pair, preferred_element_type=jnp.float32)
    real, imag = parts[:half], parts[half:]
    if sign > 0:
        return jnp.concatenate(
            [real[:, :vectors] - imag[:, vectors:], real[:, vectors:] + imag[:, :vectors]], axis=0
        )
    return jnp.concatenate(
        [real[:, :vectors] + imag[:, vectors:], real[:, vectors:] - imag[:, :vectors]], axis=0
    )


def halo_fields(cells_x, cells_y):
    pairs = [(0, (cells_x - 1) * cells_y + y) for y in range(cells_y)]
    return pairs + [(1, x * cells_y + cells_y - 1) for x in range(cells_x)]


def local_fields(cells_x, cells_y):
    lines = cells_x * cells_y
    outside = halo_fields(cells_x, cells_y)
    every = [(code, line) for code in range(7) for line in range(lines)]
    return [pair for pair in every if pair not in outside]


def prepare_kernel(cells_x, cells_y, *refs):
    inputs, refs = refs[:6], refs[6:]
    matrix_ref, local_ref, left_ref, phase_ref, weight_ref = refs[:5]
    held, link_rows_ref, sems = refs[5:11], refs[11], refs[12]
    copies = [
        pltpu.make_async_copy(src, dst, sems.at[k])
        for k, (src, dst) in enumerate(zip(inputs, held))
    ]
    for copy in copies:
        copy.start()
    v_ref, link_ref, dirs_ref, moms_ref, waves_ref, pair_ref = held
    f32, bf16 = jnp.float32, jnp.bfloat16
    order, vectors = v_ref.shape[2], v_ref.shape[3]
    half, cells_z = order // 2, order // 6
    lines = cells_x * cells_y
    times = weight_ref.shape[1]
    spread = one_hot(third(iota((half, cells_z), 0)) == iota((half, cells_z), 1))
    row, col = iota((half, LINK_COLS), 0), iota((half, LINK_COLS), 1)
    row_color = row - 3 * third(row)
    pair_at = third(col >> 1)
    col_in, col_out = (col >> 1) - 3 * pair_at, pair_at - 3 * third(pair_at)
    pick = [(row_color == col_out).astype(f32), (row_color == col_in).astype(f32)]
    wide = (LINK_COLS, 6 * 128)
    row, col = iota(wide, 0), iota(wide, 1)
    block, place = col >> 7, col & 127
    color = place - 3 * third(place)
    pair_at = third(row >> 1)
    row_in, row_out = (row >> 1) - 3 * pair_at, pair_at - 3 * third(pair_at)
    fits = 2 * third(pair_at) + (row & 1) == block
    expand = [one_hot(fits & (row_in == color)), one_hot(fits & (row_out == color))]
    row, col = iota((half, 128), 0), iota((half, 128), 1)
    near = ((third(row) == third(col)) & (col < half)).astype(f32)
    planar = planar_order(order)
    for copy in copies:
        copy.wait()
    for t in range(times):
        sink = pair_ref[0, 0] == t
        source = pair_ref[0, 1] == t
        weight_ref[0, t] = jnp.full(weight_ref.shape[2:], jnp.where(sink, 1.0, 0.0), f32)
        weight_ref[1, t] = jnp.full(weight_ref.shape[2:], jnp.where(source, 1.0, 0.0), f32)
    for line in range(lines):
        for k in range(LINK_COLS // 2):
            link_rows_ref[line, 2 * k : 2 * k + 2] = link_ref[line, k].astype(f32)
    outside = halo_fields(cells_x, cells_y)
    inside = local_fields(cells_x, cells_y)
    ordered = []
    for line in range(lines):
        here = jnp.dot(
            planar, v_ref[line // cells_y, line % cells_y], preferred_element_type=f32
        )
        ordered.append(here)
        local_ref[inside.index((6, line))] = here
    for line in range(lines):
        here = ordered[line]
        ahead_z = jnp.concatenate(
            [here[3:half], here[:3], here[half + 3 :], here[half : half + 3]], axis=0
        )
        columns = slice(line * order, (line + 1) * order)
        left_ref[0, :, columns] = here.T.astype(bf16)
        left_ref[1, :, columns] = ahead_z.T.astype(bf16)
        seen = lax.dot_general(
            spread,
            link_rows_ref[line].astype(bf16),
            (((1,), (1,)), ((), ())),
            preferred_element_type=f32,
        )
        pair = side_by_side(here)
        for way in range(2):
            blocks = jnp.dot(
                (seen * pick[way]).astype(bf16), expand[way], preferred_element_type=f32
            )
            for d in range(3):
                matrix = jnp.concatenate(
                    [
                        blocks[:, 256 * d : 256 * d + 128] * near,
                        blocks[:, 256 * d + 128 : 256 * d + 256] * near,
                    ],
                    axis=0,
                ).astype(bf16)
                if way == 1:
                    carried = transport(matrix[:, :half], pair, -1)
                    local_ref[inside.index((3 + d, line))] = carried.astype(bf16).astype(f32)
                elif (d, line) in outside:
                    matrix_ref[outside.index((d, line))] = matrix
                else:
                    ahead = ahead_z if d == 2 else ordered[line + (cells_y if d == 0 else 1)]
                    local_ref[inside.index((d, line))] = transport(
                        matrix[:, :half], side_by_side(ahead), 1
                    )
    wave_cols = waves_ref.shape[1]
    per_term = wave_cols // 3
    row, col = iota((wave_cols, 2 * vectors), 0), iota((wave_cols, 2 * vectors), 1)
    term = (row >= per_term).astype(jnp.int32) + (row >= 2 * per_term).astype(jnp.int32)
    wave_at = row - per_term * term - (col >= vectors).astype(jnp.int32)
    for o in range(phase_ref.shape[0]):
        column = 2 * (jnp.where(dirs_ref[o] == 5, MOMENTA, 0) + moms_ref[o])
        phase_ref[o] = jnp.dot(
            waves_ref[...], one_hot(wave_at == column), preferred_element_type=f32
        )


def margin_kernel(cells_x, cells_y, groups, own_ops, *refs):
    matrix_ref, local_ref, left_ref, phase_ref, halo_x_ref, halo_y_ref, dirs_hbm = refs[:7]
    swap_ref, hold_ref = refs[7:9]
    field_ref, side_ref, dirs_ref, sem = refs[9:]
    f32, bf16 = jnp.float32, jnp.bfloat16
    copy = pltpu.make_async_copy(dirs_hbm, dirs_ref, sem)
    copy.start()
    lines = cells_x * cells_y
    order, vectors = halo_x_ref.shape[2], halo_x_ref.shape[3]
    half = order // 2
    planar = planar_order(order)
    side_ref[0] = left_ref[0]
    side_ref[3] = left_ref[1]
    outside = halo_fields(cells_x, cells_y)
    for d in range(2):
        for line in range(lines):
            x, y = line // cells_y, line % cells_y
            columns = slice(line * order, (line + 1) * order)
            if (d, line) not in outside:
                ahead = line + (cells_y if d == 0 else 1)
                side_ref[1 + d, :, columns] = left_ref[0, :, ahead * order : (ahead + 1) * order]
                continue
            halo = halo_x_ref[0, y] if d == 0 else halo_y_ref[x, 0]
            ahead = jnp.dot(planar, halo, preferred_element_type=f32)
            side_ref[1 + d, :, columns] = ahead.T.astype(bf16)
            matrix = matrix_ref[outside.index((d, line))]
            field_ref[d, line] = transport(matrix[:, :half], side_by_side(ahead), 1)
    for k, (code, line) in enumerate(local_fields(cells_x, cells_y)):
        field_ref[code, line] = local_ref[k]
    copy.wait()
    me = lax.axis_index("gy")
    for j in sorted(range(groups), key=lambda j: -(j & 1)):
        blocks = []
        for i in range(own_ops):
            o = (me ^ j) * own_ops + i
            code = dirs_ref[o]
            side = jnp.where((code >= 3) & (code < 6), code - 2, 0)
            cosine = phase_ref[o, :, 0:vectors]
            sine = phase_ref[o, :, vectors : 2 * vectors]
            pairs = []
            for line in range(lines):
                real, imag = field_ref[code, line, 0:half], field_ref[code, line, half:order]
                turned_r, turned_i = cosine * real - sine * imag, sine * real + cosine * imag
                pairs.append(jnp.concatenate([turned_r, turned_i], axis=1))
                pairs.append(jnp.concatenate([turned_i, -turned_r], axis=1))
            pair = jnp.concatenate(pairs, axis=0).astype(bf16)
            product = jnp.dot(side_ref[side], pair, preferred_element_type=f32)
            blocks += [product[:, :vectors], product[:, vectors:]]
        if j & 1:
            put_fixed(swap_ref.at[j >> 1], blocks)
            continue
        for k, block in enumerate(blocks):
            hold_ref[j >> 1, k * vectors : (k + 1) * vectors] = block


def scale_of(block):
    top = jnp.max(jnp.abs(block), axis=0, keepdims=True)
    return jnp.floor(jnp.log2(jnp.maximum(top, 1e-30))) + 1.0


def put_fixed(out_ref, blocks):
    rows, vectors = blocks[0].shape
    tail = iota((TAIL, vectors), 0)
    scales = jnp.zeros((TAIL, vectors), jnp.float32)
    for k, block in enumerate(blocks):
        scale = scale_of(block)
        scales = jnp.where(tail == k, scale, scales)
        fixed = jnp.floor(block * jnp.exp2(FIXED_BITS - scale) + 0.5)
        out_ref[k * rows : (k + 1) * rows] = fixed.astype(jnp.int32).astype(jnp.int16)
    out_ref[len(blocks) * rows :] = scales.astype(jnp.int32).astype(jnp.int16)


def from_fixed(ref, rows, k):
    scales = ref[ref.shape[0] - TAIL :].astype(jnp.int32).astype(jnp.float32)
    block = ref[k * rows : (k + 1) * rows].astype(jnp.int32).astype(jnp.float32)
    return block * jnp.exp2(scales[k : k + 1] - FIXED_BITS)


def group_block(held_ref, messages, j, start, rows):
    total = held_ref[j >> 1, pl.ds(start, rows)]
    for b, ref in enumerate(messages):
        total = total + fixed_at(ref.at[j >> (b + 1)], start, rows)
    return total


def fixed_at(ref, start, rows):
    tail = ref[ref.shape[0] - TAIL :].astype(jnp.int32).astype(jnp.float32)
    scale = jnp.max(
        jnp.where(iota(tail.shape, 0) == start // rows, tail, -1000.0), axis=0, keepdims=True
    )
    block = ref[pl.ds(start, rows)].astype(jnp.int32).astype(jnp.float32)
    return block * jnp.exp2(scale - FIXED_BITS)


def fold_kernel(level, vectors, held_ref, *refs):
    messages, out_ref = refs[:-1], refs[-1]
    for k in range(out_ref.shape[0]):
        blocks = [
            group_block(held_ref, messages, (2 * k + 1) << level, start, vectors)
            for start in range(0, held_ref.shape[1], vectors)
        ]
        put_fixed(out_ref.at[k], blocks)


def half_blocks(held_ref, messages, j, kept, vectors):
    me = lax.axis_index("gx") & 1
    half = held_ref.shape[1] // 2
    base = pl.multiple_of((me if kept else 1 - me) * half, half)
    steps = range(0, half, vectors)
    return [group_block(held_ref, messages, j, base + step, vectors) for step in steps]


def spread_kernel(level, vectors, held_ref, *refs):
    messages, (y_ref, diagonal_ref, x_ref) = refs[:-3], refs[-3:]
    put_fixed(y_ref, half_blocks(held_ref, messages, 1 << level, True, vectors))
    put_fixed(diagonal_ref, half_blocks(held_ref, messages, 1 << level, False, vectors))
    put_fixed(x_ref, half_blocks(held_ref, messages, 0, False, vectors))


def keep_kernel(vectors, held_ref, *refs):
    messages, came, out_ref = refs[:-4], refs[-4:-1], refs[-1]
    blocks = half_blocks(held_ref, messages, 0, True, vectors)
    for p in range(len(blocks)):
        for ref in came:
            blocks[p] = blocks[p] + from_fixed(ref, vectors, p)
    put_fixed(out_ref, blocks)


def both_kernel(vectors, norm_factor, own_ref, arrived_ref, out_ref):
    blocks = [
        from_fixed(own_ref, vectors, p) + from_fixed(arrived_ref, vectors, p)
        for p in range((own_ref.shape[0] - TAIL) // vectors)
    ]
    if norm_factor is None:
        put_fixed(out_ref, blocks)
        return
    for p, block in enumerate(blocks):
        out_ref[p * vectors : (p + 1) * vectors] = (block * norm_factor).astype(out_ref.dtype)


def contract(sums_ref, weight_ref, blocks, tau_ref, left_ref, right_ref):
    f32, bf16 = jnp.float32, jnp.bfloat16
    vectors = sums_ref.shape[2]
    count_ops = sums_ref.shape[0] // 2
    order = tau_ref.shape[2]
    spins = order // vectors
    me_t = lax.axis_index("ta")
    times = len(blocks)

    def chosen(end, k):
        total = jnp.zeros((vectors // 8, 8, vectors), f32)
        for t in range(times):
            weight = weight_ref[end, lax.rem(me_t + t, times)]
            total = total + blocks[t](k).astype(f32).reshape(total.shape) * weight
        return total.reshape(vectors, vectors)

    for o in range(count_ops):
        first = 2 * o * vectors
        a_r, a_i = chosen(0, 2 * o).astype(bf16), chosen(0, 2 * o + 1).astype(bf16)
        b_r, b_i = chosen(1, 2 * o).T.astype(bf16), chosen(1, 2 * o + 1).T.astype(bf16)
        real, imag = slice(first, first + vectors), slice(first + vectors, first + 2 * vectors)
        left_ref[real, 0:vectors] = a_r
        left_ref[real, vectors:] = -a_i
        left_ref[imag, 0:vectors] = a_i
        left_ref[imag, vectors:] = a_r
        right_ref[0:vectors, real] = b_r
        right_ref[0:vectors, imag] = -b_i
        right_ref[vectors:, real] = b_i
        right_ref[vectors:, imag] = b_r
    lanes = sums_ref.shape[1]
    fold = lambda t: jnp.sum(t.reshape(vectors // lanes, lanes, vectors), axis=0)
    sums = [jnp.zeros((lanes, vectors), f32) for _ in range(2 * count_ops)]
    for s in range(spins):
        rows = slice(s * vectors, (s + 1) * vectors)
        x = jnp.dot(
            left_ref[...],
            jnp.concatenate([tau_ref[0, rows], tau_ref[1, rows]], axis=0),
            preferred_element_type=f32,
        )
        for c in range(spins):
            cols = slice(c * vectors, (c + 1) * vectors)
            y = jnp.dot(
                jnp.concatenate([tau_ref[0, rows, cols], tau_ref[1, rows, cols]], axis=1),
                right_ref[...],
                preferred_element_type=f32,
            )
            for o in range(count_ops):
                first = 2 * o * vectors
                x_r = x[first : first + vectors, cols]
                x_i = x[first + vectors : first + 2 * vectors, cols]
                y_r = y[:, first : first + vectors]
                y_i = y[:, first + vectors : first + 2 * vectors]
                sums[2 * o] = sums[2 * o] + fold(x_r * y_r + x_i * y_i)
                sums[2 * o + 1] = sums[2 * o + 1] + fold(x_i * y_r - x_r * y_i)
    for k, total in enumerate(sums):
        sums_ref[k] = total


def part_of(ref, vectors):
    return lambda k: ref[k * vectors : (k + 1) * vectors]


def traces(sums_ref, shape, first):
    vectors = sums_ref.shape[2]
    row, col = iota(shape, 0), iota(shape, 1)
    result = jnp.zeros(shape, jnp.float32)
    for k in range(sums_ref.shape[0]):
        total = jnp.sum(jnp.sum(sums_ref[k], axis=0, keepdims=True), axis=1, keepdims=True)
        here = (row == first + k // 2) & (col == k % 2)
        result = jnp.where(here, total * (1.0 / vectors), result)
    return result


def first_contract_kernel(times, split, live_ref, weight_ref, tau_ref, *refs):
    blocks, (live_out_ref, corr_ref, sums_ref, left_ref, right_ref) = refs[:times], refs[times:]
    live = jnp.where(live_ref[0] > 0, 1.0, 0.0)
    live_out_ref[...] = jnp.full(live_out_ref.shape, live, jnp.float32)
    if not split:
        corr_ref[...] = jnp.zeros_like(corr_ref)
        return
    blocks = [part_of(ref, sums_ref.shape[2]) for ref in blocks]
    contract(sums_ref, weight_ref, blocks, tau_ref, left_ref, right_ref)
    first = (lax.axis_index("gx") & 1) * (sums_ref.shape[0] // 2)
    corr_ref[...] = traces(sums_ref, corr_ref.shape, first)


def second_contract_kernel(times, split, weight_ref, tau_ref, *refs):
    other, kept, refs = refs[:times][::-1], refs[times : 2 * times], refs[2 * times :]
    live_ref, first_corr_ref, margin_ref, corr_ref, sums_ref, left_ref, right_ref = refs
    vectors = sums_ref.shape[2]
    half = kept[0].shape[0]
    me = lax.axis_index("gx") & 1
    for place, ref in ((me, kept[0]), (1 - me, other[0])):
        rows = pl.ds(pl.multiple_of(place * half, half), half)
        margin_ref[0, rows] = ref[...].astype(jnp.float32)
    parts_per_half = half // vectors

    def either(kept_ref, other_ref):
        def part(k):
            row = (k % parts_per_half) * vectors
            own, far = kept_ref[row : row + vectors], other_ref[row : row + vectors]
            mine = (k // parts_per_half == me).astype(jnp.float32)
            return own.astype(jnp.float32) * mine + far.astype(jnp.float32) * (1.0 - mine)

        return part

    blocks = [part_of(ref, vectors) for ref in other]
    if not split:
        blocks = [either(a, b) for a, b in zip(kept, other)]
    contract(sums_ref, weight_ref, blocks, tau_ref, left_ref, right_ref)
    shape = corr_ref.shape[1:]
    first = (1 - me) * (sums_ref.shape[0] // 2) if split else 0
    result = traces(sums_ref, shape, first) + first_corr_ref[...]
    corr_ref[0] = result * live_ref[0 : shape[0], 0 : shape[1]]


def vmem_spec():
    return pl.BlockSpec(memory_space=pltpu.VMEM)


def smem_spec():
    return pl.BlockSpec(memory_space=pltpu.SMEM)


def hbm_spec():
    return pl.BlockSpec(memory_space=pltpu.HBM)


def in_hbm(x):
    return pltpu.with_memory_space_constraint(x, pltpu.HBM)


def local_call(body, name, outs, in_specs, out_specs, scratch=(), cost=None):
    return pl.pallas_call(
        body,
        out_shape=outs,
        in_specs=in_specs,
        out_specs=out_specs,
        scratch_shapes=list(scratch),
        compiler_params=pltpu.CompilerParams(vmem_limit_bytes=VMEM_LIMIT),
        cost_estimate=cost,
        name=name,
    )


def from_step(block, axis, step):
    count = lax.axis_size(axis)
    return lax.ppermute(block, axis, [((i + step) % count, i) for i in range(count)])


def from_partner(block, axis, step):
    count = lax.axis_size(axis)
    return lax.ppermute(block, axis, [(i ^ step, i) for i in range(count)])


def from_diagonal(block, axes, sources):
    rows, columns = (lax.axis_size(axis) for axis in axes)
    perm = []
    for row in range(rows):
        for column in range(columns):
            from_row, from_column = sources(row, column)
            perm.append((from_row * columns + from_column, row * columns + column))
    return lax.ppermute(block, axes, perm)


def per_device(eigvecs, links, op_dirs, op_moms, perams, pair_times, slot_counts):
    f32, bf16 = jnp.float32, jnp.bfloat16
    _, cells_x, cells_y, cells_z, colors, _, vectors = eigvecs.shape
    order = cells_z * colors * 2
    lines = cells_x * cells_y
    count_ops = op_dirs.shape[0]
    times, shares, groups = lax.axis_size("ta"), lax.axis_size("gx"), lax.axis_size("gy")
    levels = groups.bit_length() - 1
    own_ops = count_ops // groups
    own_rows = own_ops * 2 * vectors
    field = eigvecs.reshape(cells_x, cells_y, order, vectors)
    halo_x = from_step(field[0:1], "gx", 1)
    halo_y = from_step(field, "gy", 1)
    link_field = links[0].transpose(0, 1, 3, 5, 6, 4, 2).reshape(lines, 27, 2, cells_z)
    outside, inside = halo_fields(cells_x, cells_y), local_fields(cells_x, cells_y)
    inputs = [field, link_field, op_dirs, op_moms, wave_constants(cells_z), pair_times]
    inputs = [in_hbm(x) for x in inputs]
    held = [
        pltpu.SMEM(x.shape, x.dtype) if x.dtype == jnp.int32 else pltpu.VMEM(x.shape, x.dtype)
        for x in inputs
    ]
    matrices, local, left, phases, weights = local_call(
        functools.partial(prepare_kernel, cells_x, cells_y),
        "prepare_lines",
        (
            jax.ShapeDtypeStruct((len(outside), order, 128), bf16),
            jax.ShapeDtypeStruct((len(inside), order, vectors), f32),
            jax.ShapeDtypeStruct((2, vectors, lines * order), bf16),
            jax.ShapeDtypeStruct((count_ops, order // 2, 2 * vectors), f32),
            jax.ShapeDtypeStruct((2, times, 8, vectors), f32),
        ),
        [hbm_spec()] * len(inputs),
        (vmem_spec(),) * 5,
        held
        + [
            pltpu.VMEM((lines, LINK_COLS, cells_z), f32),
            pltpu.SemaphoreType.DMA((len(inputs),)),
        ],
    )(*inputs)
    message = lambda rows, *lead: jax.ShapeDtypeStruct((*lead, rows + TAIL, vectors), jnp.int16)
    swap, held = local_call(
        functools.partial(margin_kernel, cells_x, cells_y, groups, own_ops),
        "partial_margins",
        (
            message(own_rows, groups // 2),
            jax.ShapeDtypeStruct((groups // 2, own_rows, vectors), f32),
        ),
        [vmem_spec()] * 6 + [hbm_spec()],
        (vmem_spec(),) * 2,
        [
            pltpu.VMEM((7, lines, order, vectors), f32),
            pltpu.VMEM((4, vectors, lines * order), bf16),
            pltpu.SMEM((count_ops,), jnp.int32),
            pltpu.SemaphoreType.DMA,
        ],
    )(matrices, local, left, phases, halo_x, halo_y, in_hbm(op_dirs))

    def in_vmem(body, name, outs, *inputs):
        outs = outs if isinstance(outs, tuple) else (outs,)
        specs = (vmem_spec(),) * len(outs)
        return local_call(body, name, outs, [vmem_spec()] * len(inputs), specs)(*inputs)

    half = own_rows // 2
    messages = [from_partner(swap, "gy", 1)]
    last = levels - 1
    for b in range(1, last):
        body = functools.partial(fold_kernel, b, vectors)
        shape = message(own_rows, groups >> (b + 1))
        (sent,) = in_vmem(body, "fold_groups", shape, held, *messages)
        messages.append(from_partner(sent, "gy", 1 << b))
    body = functools.partial(spread_kernel, last, vectors)
    for_y, for_both, for_x = in_vmem(body, "spread_halves", (message(half),) * 3, held, *messages)
    came = [
        from_partner(for_y, "gy", 1 << last),
        from_diagonal(for_both, ("gx", "gy"), lambda x, y: (x ^ 1, y ^ (1 << last))),
        from_partner(for_x, "gx", 1),
    ]
    body = functools.partial(keep_kernel, vectors)
    (packed,) = in_vmem(body, "keep_half", message(half), held, *messages, *came)
    norm_factor = 1.0 / math.sqrt(3.0 * cells_x * shares * cells_y * groups * cells_z)
    step = 2
    while step < shares:
        arrived = from_partner(packed, "gx", step)
        step *= 2
        last_one = step >= shares
        body = functools.partial(both_kernel, vectors, norm_factor if last_one else None)
        shape = jax.ShapeDtypeStruct((half, vectors), bf16) if last_one else message(half)
        (packed,) = in_vmem(body, "finish_half" if last_one else "sum_both", shape, packed, arrived)
    finished = packed
    kept = [finished] + [from_step(finished, "ta", t) for t in range(1, times)]
    other = [from_partner(finished, "gx", 1)]
    for t in range(1, times):
        source = lambda row, x: ((row + t) % times, x ^ 1)
        other.append(from_diagonal(finished, ("ta", "gx"), source))
    arrivals = lax.optimization_barrier((*other[1:], *kept[1:]))
    other[1:], kept[1:] = arrivals[: times - 1], arrivals[times - 1 :]
    split = own_ops % 2 == 0
    now_ops = own_ops // 2 if split else own_ops
    sums_shape = (2 * now_ops, 32, vectors)
    scratch = [
        pltpu.VMEM((2 * now_ops * vectors, 2 * vectors), bf16),
        pltpu.VMEM((2 * vectors, 2 * now_ops * vectors), bf16),
    ]
    live, first_corr = local_call(
        functools.partial(first_contract_kernel, times, split),
        "first_contraction",
        (
            jax.ShapeDtypeStruct((8, vectors), f32),
            jax.ShapeDtypeStruct((own_ops, 2), f32),
        ),
        [smem_spec()] + [vmem_spec()] * (2 + times),
        (vmem_spec(),) * 2,
        [pltpu.VMEM(sums_shape, f32)] + scratch,
    )(slot_counts, weights, perams[0], *kept)
    margins, correlators = local_call(
        functools.partial(second_contract_kernel, times, split),
        "second_contraction",
        (
            jax.ShapeDtypeStruct((1, own_rows, vectors), f32),
            jax.ShapeDtypeStruct((1, own_ops, 2), f32),
        ),
        [vmem_spec()] * (4 + 2 * times),
        (vmem_spec(),) * 2,
        [pltpu.VMEM(sums_shape, f32)] + scratch,
    )(weights, perams[0], *other[::-1], *kept, live, first_corr)
    return (margins.reshape(1, own_ops, 2, vectors, vectors), correlators)


def solution(mesh):
    placed = (
        P("ta", "gx", "gy", None, None, None, None),
        P("ta", "gx", "gy", None, None, None, None, None),
        P(),
        P(),
        P(("ta", "gx"), None, None, None),
        P(("ta", "gx"), None),
        P(("ta", "gx")),
    )
    return jax.shard_map(
        per_device,
        mesh=mesh,
        in_specs=placed,
        out_specs=(P("ta", "gy", None, None, None), P(("ta", "gx"), "gy", None)),
        check_vma=False,
    )
```

```python
import functools
import math

import jax
import jax.numpy as jnp
import numpy as np
from jax import lax
from jax.experimental import pallas as pl
from jax.experimental.pallas import tpu as pltpu
from jax.sharding import PartitionSpec as P

VMEM_LIMIT = 24 * 1024 * 1024
MOMENTA = 3
LINK_COLS = 54
TAIL = 16
FIXED_BITS = 14.0


def wave_constants(cells_z):
    z_row = np.arange(3 * cells_z) // 3
    columns = []
    for ahead in range(2):
        for momentum in range(MOMENTA):
            angle = 2.0 * math.pi * momentum * ((z_row + ahead) % cells_z) / cells_z
            columns.append(np.cos(angle))
            columns.append(np.sin(angle))
    left = np.stack(columns, axis=1).astype(np.float32)
    terms = []
    for _ in range(3):
        term = left.astype(jnp.bfloat16).astype(np.float32)
        terms.append(term)
        left = left - term
    return jnp.asarray(np.concatenate(terms, axis=1), jnp.bfloat16)


def iota(shape, axis):
    return lax.broadcasted_iota(jnp.int32, shape, axis)


def third(x):
    return (x * 21846) >> 16


def one_hot(condition):
    return condition.astype(jnp.float32).astype(jnp.bfloat16)


def planar_order(order):
    row, col = iota((order, order), 0), iota((order, order), 1)
    half = order // 2
    source = jnp.where(row < half, 2 * row, 2 * (row - half) + 1)
    return one_hot(col == source)


def side_by_side(planar):
    half = planar.shape[0] // 2
    return jnp.concatenate([planar[:half], planar[half:]], axis=1).astype(jnp.bfloat16)


def transport(matrix, pair, sign):
    half, vectors = matrix.shape[0] // 2, pair.shape[1] // 2
    parts = jnp.dot(matrix, pair, preferred_element_type=jnp.float32)
    real, imag = parts[:half], parts[half:]
    if sign > 0:
        return jnp.concatenate(
            [real[:, :vectors] - imag[:, vectors:], real[:, vectors:] + imag[:, :vectors]], axis=0
        )
    return jnp.concatenate(
        [real[:, :vectors] + imag[:, vectors:], real[:, vectors:] - imag[:, :vectors]], axis=0
    )


def halo_fields(cells_x, cells_y):
    pairs = [(0, (cells_x - 1) * cells_y + y) for y in range(cells_y)]
    return pairs + [(1, x * cells_y + cells_y - 1) for x in range(cells_x)]


def local_fields(cells_x, cells_y):
    lines = cells_x * cells_y
    outside = halo_fields(cells_x, cells_y)
    every = [(code, line) for code in range(7) for line in range(lines)]
    return [pair for pair in every if pair not in outside]


def prepare_kernel(cells_x, cells_y, *refs):
    inputs, refs = refs[:6], refs[6:]
    matrix_ref, local_ref, left_ref, phase_ref, weight_ref = refs[:5]
    held, link_rows_ref, sems = refs[5:11], refs[11], refs[12]
    copies = [
        pltpu.make_async_copy(src, dst, sems.at[k])
        for k, (src, dst) in enumerate(zip(inputs, held))
    ]
    for copy in copies:
        copy.start()
    v_ref, link_ref, dirs_ref, moms_ref, waves_ref, pair_ref = held
    f32, bf16 = jnp.float32, jnp.bfloat16
    order, vectors = v_ref.shape[2], v_ref.shape[3]
    half, cells_z = order // 2, order // 6
    lines = cells_x * cells_y
    times = weight_ref.shape[1]
    spread = one_hot(third(iota((half, cells_z), 0)) == iota((half, cells_z), 1))
    row, col = iota((half, LINK_COLS), 0), iota((half, LINK_COLS), 1)
    row_color = row - 3 * third(row)
    pair_at = third(col >> 1)
    col_in, col_out = (col >> 1) - 3 * pair_at, pair_at - 3 * third(pair_at)
    pick = [(row_color == col_out).astype(f32), (row_color == col_in).astype(f32)]
    wide = (LINK_COLS, 6 * 128)
    row, col = iota(wide, 0), iota(wide, 1)
    block, place = col >> 7, col & 127
    color = place - 3 * third(place)
    pair_at = third(row >> 1)
    row_in, row_out = (row >> 1) - 3 * pair_at, pair_at - 3 * third(pair_at)
    fits = 2 * third(pair_at) + (row & 1) == block
    expand = [one_hot(fits & (row_in == color)), one_hot(fits & (row_out == color))]
    row, col = iota((half, 128), 0), iota((half, 128), 1)
    near = ((third(row) == third(col)) & (col < half)).astype(f32)
    planar = planar_order(order)
    for copy in copies:
        copy.wait()
    for t in range(times):
        sink = pair_ref[0, 0] == t
        source = pair_ref[0, 1] == t
        weight_ref[0, t] = jnp.full(weight_ref.shape[2:], jnp.where(sink, 1.0, 0.0), f32)
        weight_ref[1, t] = jnp.full(weight_ref.shape[2:], jnp.where(source, 1.0, 0.0), f32)
    for line in range(lines):
        for k in range(LINK_COLS // 2):
            link_rows_ref[line, 2 * k : 2 * k + 2] = link_ref[line, k].astype(f32)
    outside = halo_fields(cells_x, cells_y)
    inside = local_fields(cells_x, cells_y)
    ordered = []
    for line in range(lines):
        here = jnp.dot(
            planar, v_ref[line // cells_y, line % cells_y], preferred_element_type=f32
        )
        ordered.append(here)
        local_ref[inside.index((6, line))] = here
    for line in range(lines):
        here = ordered[line]
        ahead_z = jnp.concatenate(
            [here[3:half], here[:3], here[half + 3 :], here[half : half + 3]], axis=0
        )
        columns = slice(line * order, (line + 1) * order)
        left_ref[0, :, columns] = here.T.astype(bf16)
        left_ref[1, :, columns] = ahead_z.T.astype(bf16)
        seen = lax.dot_general(
            spread,
            link_rows_ref[line].astype(bf16),
            (((1,), (1,)), ((), ())),
            preferred_element_type=f32,
        )
        pair = side_by_side(here)
        for way in range(2):
            blocks = jnp.dot(
                (seen * pick[way]).astype(bf16), expand[way], preferred_element_type=f32
            )
            for d in range(3):
                matrix = jnp.concatenate(
                    [
                        blocks[:, 256 * d : 256 * d + 128] * near,
                        blocks[:, 256 * d + 128 : 256 * d + 256] * near,
                    ],
                    axis=0,
                ).astype(bf16)
                if way == 1:
                    carried = transport(matrix[:, :half], pair, -1)
                    local_ref[inside.index((3 + d, line))] = carried.astype(bf16).astype(f32)
                elif (d, line) in outside:
                    matrix_ref[outside.index((d, line))] = matrix
                else:
                    ahead = ahead_z if d == 2 else ordered[line + (cells_y if d == 0 else 1)]
                    local_ref[inside.index((d, line))] = transport(
                        matrix[:, :half], side_by_side(ahead), 1
                    )
    wave_cols = waves_ref.shape[1]
    per_term = wave_cols // 3
    row, col = iota((wave_cols, 2 * vectors), 0), iota((wave_cols, 2 * vectors), 1)
    term = (row >= per_term).astype(jnp.int32) + (row >= 2 * per_term).astype(jnp.int32)
    wave_at = row - per_term * term - (col >= vectors).astype(jnp.int32)
    for o in range(phase_ref.shape[0]):
        column = 2 * (jnp.where(dirs_ref[o] == 5, MOMENTA, 0) + moms_ref[o])
        phase_ref[o] = jnp.dot(
            waves_ref[...], one_hot(wave_at == column), preferred_element_type=f32
        )


def margin_kernel(cells_x, cells_y, groups, own_ops, *refs):
    matrix_ref, local_ref, left_ref, phase_ref, halo_x_ref, halo_y_ref, dirs_hbm = refs[:7]
    swap_ref, hold_ref = refs[7:9]
    field_ref, side_ref, dirs_ref, sem = refs[9:]
    f32, bf16 = jnp.float32, jnp.bfloat16
    copy = pltpu.make_async_copy(dirs_hbm, dirs_ref, sem)
    copy.start()
    lines = cells_x * cells_y
    order, vectors = halo_x_ref.shape[2], halo_x_ref.shape[3]
    half = order // 2
    planar = planar_order(order)
    side_ref[0] = left_ref[0]
    side_ref[3] = left_ref[1]
    outside = halo_fields(cells_x, cells_y)
    for d in range(2):
        for line in range(lines):
            x, y = line // cells_y, line % cells_y
            columns = slice(line * order, (line + 1) * order)
            if (d, line) not in outside:
                ahead = line + (cells_y if d == 0 else 1)
                side_ref[1 + d, :, columns] = left_ref[0, :, ahead * order : (ahead + 1) * order]
                continue
            halo = halo_x_ref[0, y] if d == 0 else halo_y_ref[x, 0]
            ahead = jnp.dot(planar, halo, preferred_element_type=f32)
            side_ref[1 + d, :, columns] = ahead.T.astype(bf16)
            matrix = matrix_ref[outside.index((d, line))]
            field_ref[d, line] = transport(matrix[:, :half], side_by_side(ahead), 1)
    for k, (code, line) in enumerate(local_fields(cells_x, cells_y)):
        field_ref[code, line] = local_ref[k]
    copy.wait()
    me = lax.axis_index("gy")
    for j in sorted(range(groups), key=lambda j: -(j & 1)):
        blocks = []
        for i in range(own_ops):
            o = (me ^ j) * own_ops + i
            code = dirs_ref[o]
            side = jnp.where((code >= 3) & (code < 6), code - 2, 0)
            cosine = phase_ref[o, :, 0:vectors]
            sine = phase_ref[o, :, vectors : 2 * vectors]
            pairs = []
            for line in range(lines):
                real, imag = field_ref[code, line, 0:half], field_ref[code, line, half:order]
                turned_r, turned_i = cosine * real - sine * imag, sine * real + cosine * imag
                pairs.append(jnp.concatenate([turned_r, turned_i], axis=1))
                pairs.append(jnp.concatenate([turned_i, -turned_r], axis=1))
            pair = jnp.concatenate(pairs, axis=0).astype(bf16)
            product = jnp.dot(side_ref[side], pair, preferred_element_type=f32)
            blocks += [product[:, :vectors], product[:, vectors:]]
        if j & 1:
            put_fixed(swap_ref.at[j >> 1], blocks)
            continue
        for k, block in enumerate(blocks):
            hold_ref[j >> 1, k * vectors : (k + 1) * vectors] = block


def scale_of(block):
    top = jnp.max(jnp.abs(block), axis=0, keepdims=True)
    return jnp.floor(jnp.log2(jnp.maximum(top, 1e-30))) + 1.0


def put_fixed(out_ref, blocks):
    rows, vectors = blocks[0].shape
    tail = iota((TAIL, vectors), 0)
    scales = jnp.zeros((TAIL, vectors), jnp.float32)
    for k, block in enumerate(blocks):
        scale = scale_of(block)
        scales = jnp.where(tail == k, scale, scales)
        fixed = jnp.floor(block * jnp.exp2(FIXED_BITS - scale) + 0.5)
        out_ref[k * rows : (k + 1) * rows] = fixed.astype(jnp.int32).astype(jnp.int16)
    out_ref[len(blocks) * rows :] = scales.astype(jnp.int32).astype(jnp.int16)


def from_fixed(ref, rows, k):
    scales = ref[ref.shape[0] - TAIL :].astype(jnp.int32).astype(jnp.float32)
    block = ref[k * rows : (k + 1) * rows].astype(jnp.int32).astype(jnp.float32)
    return block * jnp.exp2(scales[k : k + 1] - FIXED_BITS)


def group_block(held_ref, messages, j, start, rows):
    total = held_ref[j >> 1, pl.ds(start, rows)]
    for b, ref in enumerate(messages):
        total = total + fixed_at(ref.at[j >> (b + 1)], start, rows)
    return total


def fixed_at(ref, start, rows):
    tail = ref[ref.shape[0] - TAIL :].astype(jnp.int32).astype(jnp.float32)
    scale = jnp.max(
        jnp.where(iota(tail.shape, 0) == start // rows, tail, -1000.0), axis=0, keepdims=True
    )
    block = ref[pl.ds(start, rows)].astype(jnp.int32).astype(jnp.float32)
    return block * jnp.exp2(scale - FIXED_BITS)


def fold_kernel(level, vectors, held_ref, *refs):
    messages, out_ref = refs[:-1], refs[-1]
    for k in range(out_ref.shape[0]):
        blocks = [
            group_block(held_ref, messages, (2 * k + 1) << level, start, vectors)
            for start in range(0, held_ref.shape[1], vectors)
        ]
        put_fixed(out_ref.at[k], blocks)


def half_blocks(held_ref, messages, j, kept, vectors):
    me = lax.axis_index("gx") & 1
    half = held_ref.shape[1] // 2
    base = pl.multiple_of((me if kept else 1 - me) * half, half)
    steps = range(0, half, vectors)
    return [group_block(held_ref, messages, j, base + step, vectors) for step in steps]


def spread_kernel(level, vectors, held_ref, *refs):
    messages, (y_ref, diagonal_ref, x_ref) = refs[:-3], refs[-3:]
    put_fixed(y_ref, half_blocks(held_ref, messages, 1 << level, True, vectors))
    put_fixed(diagonal_ref, half_blocks(held_ref, messages, 1 << level, False, vectors))
    put_fixed(x_ref, half_blocks(held_ref, messages, 0, False, vectors))


def keep_kernel(vectors, held_ref, *refs):
    messages, came, out_ref = refs[:-4], refs[-4:-1], refs[-1]
    blocks = half_blocks(held_ref, messages, 0, True, vectors)
    for p in range(len(blocks)):
        for ref in came:
            blocks[p] = blocks[p] + from_fixed(ref, vectors, p)
    put_fixed(out_ref, blocks)


def both_kernel(vectors, norm_factor, own_ref, arrived_ref, out_ref):
    blocks = [
        from_fixed(own_ref, vectors, p) + from_fixed(arrived_ref, vectors, p)
        for p in range((own_ref.shape[0] - TAIL) // vectors)
    ]
    if norm_factor is None:
        put_fixed(out_ref, blocks)
        return
    for p, block in enumerate(blocks):
        out_ref[p * vectors : (p + 1) * vectors] = (block * norm_factor).astype(out_ref.dtype)


def contract(sums_ref, weight_ref, blocks, tau_ref, left_ref, right_ref):
    f32, bf16 = jnp.float32, jnp.bfloat16
    vectors = sums_ref.shape[2]
    count_ops = sums_ref.shape[0] // 2
    order = tau_ref.shape[2]
    spins = order // vectors
    me_t = lax.axis_index("ta")
    times = len(blocks)

    def chosen(end, k):
        total = jnp.zeros((vectors // 8, 8, vectors), f32)
        for t in range(times):
            weight = weight_ref[end, lax.rem(me_t + t, times)]
            total = total + blocks[t](k).astype(f32).reshape(total.shape) * weight
        return total.reshape(vectors, vectors)

    for o in range(count_ops):
        first = 2 * o * vectors
        a_r, a_i = chosen(0, 2 * o).astype(bf16), chosen(0, 2 * o + 1).astype(bf16)
        b_r, b_i = chosen(1, 2 * o).T.astype(bf16), chosen(1, 2 * o + 1).T.astype(bf16)
        real, imag = slice(first, first + vectors), slice(first + vectors, first + 2 * vectors)
        left_ref[real, 0:vectors] = a_r
        left_ref[real, vectors:] = -a_i
        left_ref[imag, 0:vectors] = a_i
        left_ref[imag, vectors:] = a_r
        right_ref[0:vectors, real] = b_r
        right_ref[0:vectors, imag] = -b_i
        right_ref[vectors:, real] = b_i
        right_ref[vectors:, imag] = b_r
    lanes = sums_ref.shape[1]
    fold = lambda t: jnp.sum(t.reshape(vectors // lanes, lanes, vectors), axis=0)
    sums = [jnp.zeros((lanes, vectors), f32) for _ in range(2 * count_ops)]
    for s in range(spins):
        rows = slice(s * vectors, (s + 1) * vectors)
        x = jnp.dot(
            left_ref[...],
            jnp.concatenate([tau_ref[0, rows], tau_ref[1, rows]], axis=0),
            preferred_element_type=f32,
        )
        for c in range(spins):
            cols = slice(c * vectors, (c + 1) * vectors)
            y = jnp.dot(
                jnp.concatenate([tau_ref[0, rows, cols], tau_ref[1, rows, cols]], axis=1),
                right_ref[...],
                preferred_element_type=f32,
            )
            for o in range(count_ops):
                first = 2 * o * vectors
                x_r = x[first : first + vectors, cols]
                x_i = x[first + vectors : first + 2 * vectors, cols]
                y_r = y[:, first : first + vectors]
                y_i = y[:, first + vectors : first + 2 * vectors]
                sums[2 * o] = sums[2 * o] + fold(x_r * y_r + x_i * y_i)
                sums[2 * o + 1] = sums[2 * o + 1] + fold(x_i * y_r - x_r * y_i)
    for k, total in enumerate(sums):
        sums_ref[k] = total


def part_of(ref, vectors):
    return lambda k: ref[k * vectors : (k + 1) * vectors]


def first_contract_kernel(times, split, live_ref, weight_ref, tau_ref, *refs):
    blocks, (live_out_ref, sums_ref, left_ref, right_ref) = refs[:times], refs[times:]
    live = jnp.where(live_ref[0] > 0, 1.0, 0.0)
    live_out_ref[...] = jnp.full(live_out_ref.shape, live, jnp.float32)
    if split:
        vectors = sums_ref.shape[2]
        blocks = [part_of(ref, vectors) for ref in blocks]
        contract(sums_ref, weight_ref, blocks, tau_ref, left_ref, right_ref)
    else:
        sums_ref[...] = jnp.zeros_like(sums_ref)


def margins_kernel(kept_ref, other_ref, margin_ref):
    half = kept_ref.shape[0]
    me = lax.axis_index("gx") & 1
    for place, ref in ((me, kept_ref), (1 - me, other_ref)):
        rows = pl.ds(pl.multiple_of(place * half, half), half)
        margin_ref[0, rows] = ref[...].astype(jnp.float32)


def second_contract_kernel(times, split, weight_ref, tau_ref, *refs):
    other, kept, refs = refs[:times], refs[times : 2 * times], refs[2 * times :]
    live_ref, first_sums_ref, corr_ref, sums_ref, left_ref, right_ref = refs
    vectors = sums_ref.shape[2]
    half = kept[0].shape[0]
    me = lax.axis_index("gx") & 1
    parts_per_half = half // vectors

    def either(kept_ref, other_ref):
        def part(k):
            row = (k % parts_per_half) * vectors
            own, far = kept_ref[row : row + vectors], other_ref[row : row + vectors]
            mine = (k // parts_per_half == me).astype(jnp.float32)
            return own.astype(jnp.float32) * mine + far.astype(jnp.float32) * (1.0 - mine)

        return part

    blocks = [part_of(ref, vectors) for ref in other]
    if not split:
        blocks = [either(a, b) for a, b in zip(kept, other)]
    contract(sums_ref, weight_ref, blocks, tau_ref, left_ref, right_ref)
    now_ops = sums_ref.shape[0] // 2
    known = [(sums_ref, (1 - me) * now_ops)] if split else [(sums_ref, 0)]
    if split:
        known.append((first_sums_ref, me * now_ops))
    shape = corr_ref.shape[1:]
    row, col = iota(shape, 0), iota(shape, 1)
    result = jnp.zeros(shape, jnp.float32)
    for ref, first in known:
        for k in range(2 * now_ops):
            total = jnp.sum(jnp.sum(ref[k], axis=0, keepdims=True), axis=1, keepdims=True)
            here = (row == first + k // 2) & (col == k % 2)
            result = jnp.where(here, total * (1.0 / vectors), result)
    corr_ref[0] = result * live_ref[0 : shape[0], 0 : shape[1]]


def vmem_spec():
    return pl.BlockSpec(memory_space=pltpu.VMEM)


def smem_spec():
    return pl.BlockSpec(memory_space=pltpu.SMEM)


def hbm_spec():
    return pl.BlockSpec(memory_space=pltpu.HBM)


def in_hbm(x):
    return pltpu.with_memory_space_constraint(x, pltpu.HBM)


def local_call(body, name, outs, in_specs, out_specs, scratch=(), cost=None):
    return pl.pallas_call(
        body,
        out_shape=outs,
        in_specs=in_specs,
        out_specs=out_specs,
        scratch_shapes=list(scratch),
        compiler_params=pltpu.CompilerParams(vmem_limit_bytes=VMEM_LIMIT),
        cost_estimate=cost,
        name=name,
    )


def from_step(block, axis, step):
    count = lax.axis_size(axis)
    return lax.ppermute(block, axis, [((i + step) % count, i) for i in range(count)])


def from_partner(block, axis, step):
    count = lax.axis_size(axis)
    return lax.ppermute(block, axis, [(i ^ step, i) for i in range(count)])


def from_diagonal(block, axes, sources):
    rows, columns = (lax.axis_size(axis) for axis in axes)
    perm = []
    for row in range(rows):
        for column in range(columns):
            from_row, from_column = sources(row, column)
            perm.append((from_row * columns + from_column, row * columns + column))
    return lax.ppermute(block, axes, perm)


def per_device(eigvecs, links, op_dirs, op_moms, perams, pair_times, slot_counts):
    f32, bf16 = jnp.float32, jnp.bfloat16
    _, cells_x, cells_y, cells_z, colors, _, vectors = eigvecs.shape
    order = cells_z * colors * 2
    lines = cells_x * cells_y
    count_ops = op_dirs.shape[0]
    times, shares, groups = lax.axis_size("ta"), lax.axis_size("gx"), lax.axis_size("gy")
    levels = groups.bit_length() - 1
    own_ops = count_ops // groups
    own_rows = own_ops * 2 * vectors
    field = eigvecs.reshape(cells_x, cells_y, order, vectors)
    halo_x = from_step(field[0:1], "gx", 1)
    halo_y = from_step(field, "gy", 1)
    link_field = links[0].transpose(0, 1, 3, 5, 6, 4, 2).reshape(lines, 27, 2, cells_z)
    outside, inside = halo_fields(cells_x, cells_y), local_fields(cells_x, cells_y)
    inputs = [field, link_field, op_dirs, op_moms, wave_constants(cells_z), pair_times]
    inputs = [in_hbm(x) for x in inputs]
    held = [
        pltpu.SMEM(x.shape, x.dtype) if x.dtype == jnp.int32 else pltpu.VMEM(x.shape, x.dtype)
        for x in inputs
    ]
    matrices, local, left, phases, weights = local_call(
        functools.partial(prepare_kernel, cells_x, cells_y),
        "prepare_lines",
        (
            jax.ShapeDtypeStruct((len(outside), order, 128), bf16),
            jax.ShapeDtypeStruct((len(inside), order, vectors), f32),
            jax.ShapeDtypeStruct((2, vectors, lines * order), bf16),
            jax.ShapeDtypeStruct((count_ops, order // 2, 2 * vectors), f32),
            jax.ShapeDtypeStruct((2, times, 8, vectors), f32),
        ),
        [hbm_spec()] * len(inputs),
        (vmem_spec(),) * 5,
        held
        + [
            pltpu.VMEM((lines, LINK_COLS, cells_z), f32),
            pltpu.SemaphoreType.DMA((len(inputs),)),
        ],
    )(*inputs)
    message = lambda rows, *lead: jax.ShapeDtypeStruct((*lead, rows + TAIL, vectors), jnp.int16)
    swap, held = local_call(
        functools.partial(margin_kernel, cells_x, cells_y, groups, own_ops),
        "partial_margins",
        (
            message(own_rows, groups // 2),
            jax.ShapeDtypeStruct((groups // 2, own_rows, vectors), f32),
        ),
        [vmem_spec()] * 6 + [hbm_spec()],
        (vmem_spec(),) * 2,
        [
            pltpu.VMEM((7, lines, order, vectors), f32),
            pltpu.VMEM((4, vectors, lines * order), bf16),
            pltpu.SMEM((count_ops,), jnp.int32),
            pltpu.SemaphoreType.DMA,
        ],
    )(matrices, local, left, phases, halo_x, halo_y, in_hbm(op_dirs))

    def in_vmem(body, name, outs, *inputs):
        outs = outs if isinstance(outs, tuple) else (outs,)
        specs = (vmem_spec(),) * len(outs)
        return local_call(body, name, outs, [vmem_spec()] * len(inputs), specs)(*inputs)

    half = own_rows // 2
    messages = [from_partner(swap, "gy", 1)]
    last = levels - 1
    for b in range(1, last):
        body = functools.partial(fold_kernel, b, vectors)
        shape = message(own_rows, groups >> (b + 1))
        (sent,) = in_vmem(body, "fold_groups", shape, held, *messages)
        messages.append(from_partner(sent, "gy", 1 << b))
    body = functools.partial(spread_kernel, last, vectors)
    for_y, for_both, for_x = in_vmem(body, "spread_halves", (message(half),) * 3, held, *messages)
    came = [
        from_partner(for_y, "gy", 1 << last),
        from_partner(for_x, "gx", 1),
        from_diagonal(for_both, ("gx", "gy"), lambda x, y: (x ^ 1, y ^ (1 << last))),
    ]
    body = functools.partial(keep_kernel, vectors)
    (packed,) = in_vmem(body, "keep_half", message(half), held, *messages, *came)
    norm_factor = 1.0 / math.sqrt(3.0 * cells_x * shares * cells_y * groups * cells_z)
    step = 2
    while step < shares:
        arrived = from_partner(packed, "gx", step)
        step *= 2
        last_one = step >= shares
        body = functools.partial(both_kernel, vectors, norm_factor if last_one else None)
        shape = jax.ShapeDtypeStruct((half, vectors), bf16) if last_one else message(half)
        (packed,) = in_vmem(body, "finish_half" if last_one else "sum_both", shape, packed, arrived)
    finished = packed
    kept = [finished] + [from_step(finished, "ta", t) for t in range(1, times)]
    other = [from_partner(finished, "gx", 1)]
    for t in range(1, times):
        source = lambda row, x: ((row + t) % times, x ^ 1)
        other.append(from_diagonal(finished, ("ta", "gx"), source))
    split = own_ops % 2 == 0
    now_ops = own_ops // 2 if split else own_ops
    sums_shape = (2 * now_ops, 32, vectors)
    scratch = [
        pltpu.VMEM((2 * now_ops * vectors, 2 * vectors), bf16),
        pltpu.VMEM((2 * vectors, 2 * now_ops * vectors), bf16),
    ]
    live, sums = local_call(
        functools.partial(first_contract_kernel, times, split),
        "first_contraction",
        (jax.ShapeDtypeStruct((8, vectors), f32), jax.ShapeDtypeStruct(sums_shape, f32)),
        [smem_spec()] + [vmem_spec()] * (2 + times),
        (vmem_spec(),) * 2,
        scratch,
    )(slot_counts, weights, perams[0], *kept)
    margins = local_call(
        margins_kernel,
        "margins_out",
        jax.ShapeDtypeStruct((1, own_rows, vectors), f32),
        [vmem_spec()] * 2,
        vmem_spec(),
    )(*lax.optimization_barrier((kept[0], other[0], sums))[:2])
    correlators = local_call(
        functools.partial(second_contract_kernel, times, split),
        "second_contraction",
        jax.ShapeDtypeStruct((1, own_ops, 2), f32),
        [vmem_spec()] * (4 + 2 * times),
        vmem_spec(),
        [pltpu.VMEM(sums_shape, f32)] + scratch,
    )(weights, perams[0], *other, *kept, live, sums)
    return (margins.reshape(1, own_ops, 2, vectors, vectors), correlators)


def solution(mesh):
    placed = (
        P("ta", "gx", "gy", None, None, None, None),
        P("ta", "gx", "gy", None, None, None, None, None),
        P(),
        P(),
        P(("ta", "gx"), None, None, None),
        P(("ta", "gx"), None),
        P(("ta", "gx")),
    )
    return jax.shard_map(
        per_device,
        mesh=mesh,
        in_specs=placed,
        out_specs=(P("ta", "gy", None, None, None), P(("ta", "gx"), "gy", None)),
        check_vma=False,
    )
```

```python
import functools
import math

import jax
import jax.numpy as jnp
import numpy as np
from jax import lax
from jax.experimental import pallas as pl
from jax.experimental.pallas import tpu as pltpu
from jax.sharding import PartitionSpec as P

VMEM_LIMIT = 24 * 1024 * 1024
MOMENTA = 3
LINK_COLS = 54
TAIL = 16
FIXED_BITS = 14.0


def wave_constants(cells_z):
    z_row = np.arange(3 * cells_z) // 3
    columns = []
    for ahead in range(2):
        for momentum in range(MOMENTA):
            angle = 2.0 * math.pi * momentum * ((z_row + ahead) % cells_z) / cells_z
            columns.append(np.cos(angle))
            columns.append(np.sin(angle))
    left = np.stack(columns, axis=1).astype(np.float32)
    terms = []
    for _ in range(3):
        term = left.astype(jnp.bfloat16).astype(np.float32)
        terms.append(term)
        left = left - term
    return jnp.asarray(np.concatenate(terms, axis=1), jnp.bfloat16)


def iota(shape, axis):
    return lax.broadcasted_iota(jnp.int32, shape, axis)


def third(x):
    return (x * 21846) >> 16


def one_hot(condition):
    return condition.astype(jnp.float32).astype(jnp.bfloat16)


def planar_order(order):
    row, col = iota((order, order), 0), iota((order, order), 1)
    half = order // 2
    source = jnp.where(row < half, 2 * row, 2 * (row - half) + 1)
    return one_hot(col == source)


def side_by_side(planar):
    half = planar.shape[0] // 2
    return jnp.concatenate([planar[:half], planar[half:]], axis=1).astype(jnp.bfloat16)


def transport(matrix, pair, sign):
    half, vectors = matrix.shape[0] // 2, pair.shape[1] // 2
    parts = jnp.dot(matrix, pair, preferred_element_type=jnp.float32)
    real, imag = parts[:half], parts[half:]
    if sign > 0:
        return jnp.concatenate(
            [real[:, :vectors] - imag[:, vectors:], real[:, vectors:] + imag[:, :vectors]], axis=0
        )
    return jnp.concatenate(
        [real[:, :vectors] + imag[:, vectors:], real[:, vectors:] - imag[:, :vectors]], axis=0
    )


def halo_fields(cells_x, cells_y):
    pairs = [(0, (cells_x - 1) * cells_y + y) for y in range(cells_y)]
    return pairs + [(1, x * cells_y + cells_y - 1) for x in range(cells_x)]


def local_fields(cells_x, cells_y):
    lines = cells_x * cells_y
    outside = halo_fields(cells_x, cells_y)
    every = [(code, line) for code in range(7) for line in range(lines)]
    return [pair for pair in every if pair not in outside]


def prepare_kernel(cells_x, cells_y, *refs):
    inputs, refs = refs[:6], refs[6:]
    matrix_ref, local_ref, left_ref, phase_ref, weight_ref = refs[:5]
    held, link_rows_ref, sems = refs[5:11], refs[11], refs[12]
    copies = [
        pltpu.make_async_copy(src, dst, sems.at[k])
        for k, (src, dst) in enumerate(zip(inputs, held))
    ]
    for copy in copies:
        copy.start()
    v_ref, link_ref, dirs_ref, moms_ref, waves_ref, pair_ref = held
    f32, bf16 = jnp.float32, jnp.bfloat16
    order, vectors = v_ref.shape[2], v_ref.shape[3]
    half, cells_z = order // 2, order // 6
    lines = cells_x * cells_y
    times = weight_ref.shape[1]
    spread = one_hot(third(iota((half, cells_z), 0)) == iota((half, cells_z), 1))
    row, col = iota((half, LINK_COLS), 0), iota((half, LINK_COLS), 1)
    row_color = row - 3 * third(row)
    pair_at = third(col >> 1)
    col_in, col_out = (col >> 1) - 3 * pair_at, pair_at - 3 * third(pair_at)
    pick = [(row_color == col_out).astype(f32), (row_color == col_in).astype(f32)]
    wide = (LINK_COLS, 6 * 128)
    row, col = iota(wide, 0), iota(wide, 1)
    block, place = col >> 7, col & 127
    color = place - 3 * third(place)
    pair_at = third(row >> 1)
    row_in, row_out = (row >> 1) - 3 * pair_at, pair_at - 3 * third(pair_at)
    fits = 2 * third(pair_at) + (row & 1) == block
    expand = [one_hot(fits & (row_in == color)), one_hot(fits & (row_out == color))]
    row, col = iota((half, 128), 0), iota((half, 128), 1)
    near = ((third(row) == third(col)) & (col < half)).astype(f32)
    planar = planar_order(order)
    for copy in copies:
        copy.wait()
    for t in range(times):
        sink = pair_ref[0, 0] == t
        source = pair_ref[0, 1] == t
        weight_ref[0, t] = jnp.full(weight_ref.shape[2:], jnp.where(sink, 1.0, 0.0), f32)
        weight_ref[1, t] = jnp.full(weight_ref.shape[2:], jnp.where(source, 1.0, 0.0), f32)
    for line in range(lines):
        for k in range(LINK_COLS // 2):
            link_rows_ref[line, 2 * k : 2 * k + 2] = link_ref[line, k].astype(f32)
    outside = halo_fields(cells_x, cells_y)
    inside = local_fields(cells_x, cells_y)
    ordered = []
    for line in range(lines):
        here = jnp.dot(
            planar, v_ref[line // cells_y, line % cells_y], preferred_element_type=f32
        )
        ordered.append(here)
        local_ref[inside.index((6, line))] = here
    for line in range(lines):
        here = ordered[line]
        ahead_z = jnp.concatenate(
            [here[3:half], here[:3], here[half + 3 :], here[half : half + 3]], axis=0
        )
        columns = slice(line * order, (line + 1) * order)
        left_ref[0, :, columns] = here.T.astype(bf16)
        left_ref[1, :, columns] = ahead_z.T.astype(bf16)
        seen = lax.dot_general(
            spread,
            link_rows_ref[line].astype(bf16),
            (((1,), (1,)), ((), ())),
            preferred_element_type=f32,
        )
        pair = side_by_side(here)
        for way in range(2):
            blocks = jnp.dot(
                (seen * pick[way]).astype(bf16), expand[way], preferred_element_type=f32
            )
            for d in range(3):
                matrix = jnp.concatenate(
                    [
                        blocks[:, 256 * d : 256 * d + 128] * near,
                        blocks[:, 256 * d + 128 : 256 * d + 256] * near,
                    ],
                    axis=0,
                ).astype(bf16)
                if way == 1:
                    carried = transport(matrix[:, :half], pair, -1)
                    local_ref[inside.index((3 + d, line))] = carried.astype(bf16).astype(f32)
                elif (d, line) in outside:
                    matrix_ref[outside.index((d, line))] = matrix
                else:
                    ahead = ahead_z if d == 2 else ordered[line + (cells_y if d == 0 else 1)]
                    local_ref[inside.index((d, line))] = transport(
                        matrix[:, :half], side_by_side(ahead), 1
                    )
    wave_cols = waves_ref.shape[1]
    per_term = wave_cols // 3
    row, col = iota((wave_cols, 2 * vectors), 0), iota((wave_cols, 2 * vectors), 1)
    term = (row >= per_term).astype(jnp.int32) + (row >= 2 * per_term).astype(jnp.int32)
    wave_at = row - per_term * term - (col >= vectors).astype(jnp.int32)
    for o in range(phase_ref.shape[0]):
        column = 2 * (jnp.where(dirs_ref[o] == 5, MOMENTA, 0) + moms_ref[o])
        phase_ref[o] = jnp.dot(
            waves_ref[...], one_hot(wave_at == column), preferred_element_type=f32
        )


def put_margins(slots, own_ops, field_ref, side_ref, phase_ref, dirs_ref):
    f32, bf16 = jnp.float32, jnp.bfloat16
    lines, order, vectors = field_ref.shape[1:]
    half = order // 2
    me = lax.axis_index("gy")
    for j, out_ref in slots:
        for i in range(own_ops):
            o = (me ^ j) * own_ops + i
            code = dirs_ref[o]
            side = jnp.where((code >= 3) & (code < 6), code - 2, 0)
            cosine = phase_ref[o, :, 0:vectors]
            sine = phase_ref[o, :, vectors : 2 * vectors]
            pairs = []
            for line in range(lines):
                real, imag = field_ref[code, line, 0:half], field_ref[code, line, half:order]
                turned_r, turned_i = cosine * real - sine * imag, sine * real + cosine * imag
                pairs.append(jnp.concatenate([turned_r, turned_i], axis=1))
                pairs.append(jnp.concatenate([turned_i, -turned_r], axis=1))
            pair = jnp.concatenate(pairs, axis=0).astype(bf16)
            product = jnp.dot(side_ref[side], pair, preferred_element_type=f32)
            first = 2 * i * vectors
            out_ref[j >> 2, first : first + vectors] = product[:, :vectors]
            out_ref[j >> 2, first + vectors : first + 2 * vectors] = product[:, vectors:]


def first_margin_kernel(cells_x, cells_y, groups, own_ops, *refs):
    matrix_ref, local_ref, left_ref, phase_ref, halo_x_ref, halo_y_ref, dirs_hbm = refs[:7]
    swap_ref, field_ref, side_ref, dirs_ref, sem = refs[7:]
    f32, bf16 = jnp.float32, jnp.bfloat16
    copy = pltpu.make_async_copy(dirs_hbm, dirs_ref, sem)
    copy.start()
    lines = cells_x * cells_y
    order, vectors = halo_x_ref.shape[2], halo_x_ref.shape[3]
    half = order // 2
    planar = planar_order(order)
    side_ref[0] = left_ref[0]
    side_ref[3] = left_ref[1]
    outside = halo_fields(cells_x, cells_y)
    for d in range(2):
        for line in range(lines):
            x, y = line // cells_y, line % cells_y
            columns = slice(line * order, (line + 1) * order)
            if (d, line) not in outside:
                ahead = line + (cells_y if d == 0 else 1)
                side_ref[1 + d, :, columns] = left_ref[0, :, ahead * order : (ahead + 1) * order]
                continue
            halo = halo_x_ref[0, y] if d == 0 else halo_y_ref[x, 0]
            ahead = jnp.dot(planar, halo, preferred_element_type=f32)
            side_ref[1 + d, :, columns] = ahead.T.astype(bf16)
            matrix = matrix_ref[outside.index((d, line))]
            field_ref[d, line] = transport(matrix[:, :half], side_by_side(ahead), 1)
    for k, (code, line) in enumerate(local_fields(cells_x, cells_y)):
        field_ref[code, line] = local_ref[k]
    copy.wait()
    slots = [(j, swap_ref) for j in range(groups) if j & 3 == 3]
    put_margins(slots, own_ops, field_ref, side_ref, phase_ref, dirs_ref)


def second_margin_kernel(groups, own_ops, *refs):
    field_ref, side_ref, phase_ref, dirs_hbm = refs[:4]
    hold_a_ref, swap_b_ref, hold_b_ref, dirs_ref, sem = refs[4:]
    copy = pltpu.make_async_copy(dirs_hbm, dirs_ref, sem)
    copy.start()
    copy.wait()
    for kind, out_ref in ((2, hold_a_ref), (1, swap_b_ref), (0, hold_b_ref)):
        slots = [(j, out_ref) for j in range(groups) if j & 3 == kind]
        put_margins(slots, own_ops, field_ref, side_ref, phase_ref, dirs_ref)


def scale_of(block):
    top = jnp.max(jnp.abs(block), axis=0, keepdims=True)
    return jnp.floor(jnp.log2(jnp.maximum(top, 1e-30))) + 1.0


def put_fixed(out_ref, blocks):
    rows, vectors = blocks[0].shape
    tail = iota((TAIL, vectors), 0)
    scales = jnp.zeros((TAIL, vectors), jnp.float32)
    for k, block in enumerate(blocks):
        scale = scale_of(block)
        scales = jnp.where(tail == k, scale, scales)
        fixed = jnp.floor(block * jnp.exp2(FIXED_BITS - scale) + 0.5)
        out_ref[k * rows : (k + 1) * rows] = fixed.astype(jnp.int32).astype(jnp.int16)
    out_ref[len(blocks) * rows :] = scales.astype(jnp.int32).astype(jnp.int16)


def from_fixed(ref, rows, k):
    scales = ref[ref.shape[0] - TAIL :].astype(jnp.int32).astype(jnp.float32)
    block = ref[k * rows : (k + 1) * rows].astype(jnp.int32).astype(jnp.float32)
    return block * jnp.exp2(scales[k : k + 1] - FIXED_BITS)


def group_block(held_ref, swapped_ref, messages, j, start, rows):
    span = pl.ds(start, rows)
    total = held_ref[j >> 2, span] + swapped_ref[j >> 2, span]
    for b, ref in enumerate(messages, 1):
        total = total + fixed_at(ref.at[j >> (b + 1)], start, rows)
    return total


def fixed_at(ref, start, rows):
    tail = ref[ref.shape[0] - TAIL :].astype(jnp.int32).astype(jnp.float32)
    scale = jnp.max(
        jnp.where(iota(tail.shape, 0) == start // rows, tail, -1000.0), axis=0, keepdims=True
    )
    block = ref[pl.ds(start, rows)].astype(jnp.int32).astype(jnp.float32)
    return block * jnp.exp2(scale - FIXED_BITS)


def fold_kernel(level, vectors, held_ref, swapped_ref, *refs):
    messages, out_ref = refs[:-1], refs[-1]
    for k in range(out_ref.shape[0]):
        j = (2 * k + 1) << level
        blocks = [
            group_block(held_ref, swapped_ref, messages, j, start, vectors)
            for start in range(0, held_ref.shape[1], vectors)
        ]
        put_fixed(out_ref.at[k], blocks)


def half_blocks(held_ref, swapped_ref, messages, j, kept, vectors):
    me = lax.axis_index("gx") & 1
    half = held_ref.shape[1] // 2
    base = pl.multiple_of((me if kept else 1 - me) * half, half)
    steps = range(0, half, vectors)
    return [
        group_block(held_ref, swapped_ref, messages, j, base + step, vectors) for step in steps
    ]


def spread_kernel(level, vectors, held_ref, swapped_ref, *refs):
    messages, (y_ref, diagonal_ref) = refs[:-2], refs[-2:]
    for kept, out_ref in ((True, y_ref), (False, diagonal_ref)):
        blocks = half_blocks(held_ref, swapped_ref, messages, 1 << level, kept, vectors)
        put_fixed(out_ref, blocks)


def send_kernel(vectors, held_ref, swapped_ref, *refs):
    messages, out_ref = refs[:-1], refs[-1]
    put_fixed(out_ref, half_blocks(held_ref, swapped_ref, messages, 0, False, vectors))


def keep_kernel(vectors, held_ref, swapped_ref, *refs):
    messages, came, out_ref = refs[:-4], refs[-4:-1], refs[-1]
    blocks = half_blocks(held_ref, swapped_ref, messages, 0, True, vectors)
    for p in range(len(blocks)):
        for ref in came:
            blocks[p] = blocks[p] + from_fixed(ref, vectors, p)
    put_fixed(out_ref, blocks)


def both_kernel(vectors, norm_factor, own_ref, arrived_ref, out_ref):
    blocks = [
        from_fixed(own_ref, vectors, p) + from_fixed(arrived_ref, vectors, p)
        for p in range((own_ref.shape[0] - TAIL) // vectors)
    ]
    if norm_factor is None:
        put_fixed(out_ref, blocks)
        return
    for p, block in enumerate(blocks):
        out_ref[p * vectors : (p + 1) * vectors] = (block * norm_factor).astype(out_ref.dtype)


def contract(sums_ref, weight_ref, blocks, tau_ref, left_ref, right_ref):
    f32, bf16 = jnp.float32, jnp.bfloat16
    vectors = sums_ref.shape[2]
    count_ops = sums_ref.shape[0] // 2
    order = tau_ref.shape[2]
    spins = order // vectors
    me_t = lax.axis_index("ta")
    times = len(blocks)

    def chosen(end, k):
        total = jnp.zeros((vectors // 8, 8, vectors), f32)
        for t in range(times):
            weight = weight_ref[end, lax.rem(me_t + t, times)]
            total = total + blocks[t](k).astype(f32).reshape(total.shape) * weight
        return total.reshape(vectors, vectors)

    for o in range(count_ops):
        first = 2 * o * vectors
        a_r, a_i = chosen(0, 2 * o).astype(bf16), chosen(0, 2 * o + 1).astype(bf16)
        b_r, b_i = chosen(1, 2 * o).T.astype(bf16), chosen(1, 2 * o + 1).T.astype(bf16)
        real, imag = slice(first, first + vectors), slice(first + vectors, first + 2 * vectors)
        left_ref[real, 0:vectors] = a_r
        left_ref[real, vectors:] = -a_i
        left_ref[imag, 0:vectors] = a_i
        left_ref[imag, vectors:] = a_r
        right_ref[0:vectors, real] = b_r
        right_ref[0:vectors, imag] = -b_i
        right_ref[vectors:, real] = b_i
        right_ref[vectors:, imag] = b_r
    lanes = sums_ref.shape[1]
    fold = lambda t: jnp.sum(t.reshape(vectors // lanes, lanes, vectors), axis=0)
    sums = [jnp.zeros((lanes, vectors), f32) for _ in range(2 * count_ops)]
    for s in range(spins):
        rows = slice(s * vectors, (s + 1) * vectors)
        x = jnp.dot(
            left_ref[...],
            jnp.concatenate([tau_ref[0, rows], tau_ref[1, rows]], axis=0),
            preferred_element_type=f32,
        )
        for c in range(spins):
            cols = slice(c * vectors, (c + 1) * vectors)
            y = jnp.dot(
                jnp.concatenate([tau_ref[0, rows, cols], tau_ref[1, rows, cols]], axis=1),
                right_ref[...],
                preferred_element_type=f32,
            )
            for o in range(count_ops):
                first = 2 * o * vectors
                x_r = x[first : first + vectors, cols]
                x_i = x[first + vectors : first + 2 * vectors, cols]
                y_r = y[:, first : first + vectors]
                y_i = y[:, first + vectors : first + 2 * vectors]
                sums[2 * o] = sums[2 * o] + fold(x_r * y_r + x_i * y_i)
                sums[2 * o + 1] = sums[2 * o + 1] + fold(x_i * y_r - x_r * y_i)
    for k, total in enumerate(sums):
        sums_ref[k] = total


def part_of(ref, vectors):
    return lambda k: ref[k * vectors : (k + 1) * vectors]


def first_contract_kernel(times, split, live_ref, weight_ref, tau_ref, *refs):
    blocks, (live_out_ref, sums_ref, left_ref, right_ref) = refs[:times], refs[times:]
    live = jnp.where(live_ref[0] > 0, 1.0, 0.0)
    live_out_ref[...] = jnp.full(live_out_ref.shape, live, jnp.float32)
    if split:
        vectors = sums_ref.shape[2]
        blocks = [part_of(ref, vectors) for ref in blocks]
        contract(sums_ref, weight_ref, blocks, tau_ref, left_ref, right_ref)
    else:
        sums_ref[...] = jnp.zeros_like(sums_ref)


def margins_kernel(kept_ref, other_ref, margin_ref):
    half = kept_ref.shape[0]
    me = lax.axis_index("gx") & 1
    for place, ref in ((me, kept_ref), (1 - me, other_ref)):
        rows = pl.ds(pl.multiple_of(place * half, half), half)
        margin_ref[0, rows] = ref[...].astype(jnp.float32)


def second_contract_kernel(times, split, weight_ref, tau_ref, *refs):
    other, kept, refs = refs[:times], refs[times : 2 * times], refs[2 * times :]
    live_ref, first_sums_ref, corr_ref, sums_ref, left_ref, right_ref = refs
    vectors = sums_ref.shape[2]
    half = kept[0].shape[0]
    me = lax.axis_index("gx") & 1
    parts_per_half = half // vectors

    def either(kept_ref, other_ref):
        def part(k):
            row = (k % parts_per_half) * vectors
            own, far = kept_ref[row : row + vectors], other_ref[row : row + vectors]
            mine = (k // parts_per_half == me).astype(jnp.float32)
            return own.astype(jnp.float32) * mine + far.astype(jnp.float32) * (1.0 - mine)

        return part

    blocks = [part_of(ref, vectors) for ref in other]
    if not split:
        blocks = [either(a, b) for a, b in zip(kept, other)]
    contract(sums_ref, weight_ref, blocks, tau_ref, left_ref, right_ref)
    now_ops = sums_ref.shape[0] // 2
    known = [(sums_ref, (1 - me) * now_ops)] if split else [(sums_ref, 0)]
    if split:
        known.append((first_sums_ref, me * now_ops))
    shape = corr_ref.shape[1:]
    row, col = iota(shape, 0), iota(shape, 1)
    result = jnp.zeros(shape, jnp.float32)
    for ref, first in known:
        for k in range(2 * now_ops):
            total = jnp.sum(jnp.sum(ref[k], axis=0, keepdims=True), axis=1, keepdims=True)
            here = (row == first + k // 2) & (col == k % 2)
            result = jnp.where(here, total * (1.0 / vectors), result)
    corr_ref[0] = result * live_ref[0 : shape[0], 0 : shape[1]]


def vmem_spec():
    return pl.BlockSpec(memory_space=pltpu.VMEM)


def smem_spec():
    return pl.BlockSpec(memory_space=pltpu.SMEM)


def hbm_spec():
    return pl.BlockSpec(memory_space=pltpu.HBM)


def in_hbm(x):
    return pltpu.with_memory_space_constraint(x, pltpu.HBM)


def local_call(body, name, outs, in_specs, out_specs, scratch=(), cost=None):
    return pl.pallas_call(
        body,
        out_shape=outs,
        in_specs=in_specs,
        out_specs=out_specs,
        scratch_shapes=list(scratch),
        compiler_params=pltpu.CompilerParams(vmem_limit_bytes=VMEM_LIMIT),
        cost_estimate=cost,
        name=name,
    )


def from_step(block, axis, step):
    count = lax.axis_size(axis)
    return lax.ppermute(block, axis, [((i + step) % count, i) for i in range(count)])


def from_partner(block, axis, step):
    count = lax.axis_size(axis)
    return lax.ppermute(block, axis, [(i ^ step, i) for i in range(count)])


def from_diagonal(block, axes, sources):
    rows, columns = (lax.axis_size(axis) for axis in axes)
    perm = []
    for row in range(rows):
        for column in range(columns):
            from_row, from_column = sources(row, column)
            perm.append((from_row * columns + from_column, row * columns + column))
    return lax.ppermute(block, axes, perm)


def per_device(eigvecs, links, op_dirs, op_moms, perams, pair_times, slot_counts):
    f32, bf16 = jnp.float32, jnp.bfloat16
    _, cells_x, cells_y, cells_z, colors, _, vectors = eigvecs.shape
    order = cells_z * colors * 2
    lines = cells_x * cells_y
    count_ops = op_dirs.shape[0]
    times, shares, groups = lax.axis_size("ta"), lax.axis_size("gx"), lax.axis_size("gy")
    levels = groups.bit_length() - 1
    own_ops = count_ops // groups
    own_rows = own_ops * 2 * vectors
    field = eigvecs.reshape(cells_x, cells_y, order, vectors)
    halo_x = from_step(field[0:1], "gx", 1)
    halo_y = from_step(field, "gy", 1)
    link_field = links[0].transpose(0, 1, 3, 5, 6, 4, 2).reshape(lines, 27, 2, cells_z)
    outside, inside = halo_fields(cells_x, cells_y), local_fields(cells_x, cells_y)
    inputs = [field, link_field, op_dirs, op_moms, wave_constants(cells_z), pair_times]
    inputs = [in_hbm(x) for x in inputs]
    held = [
        pltpu.SMEM(x.shape, x.dtype) if x.dtype == jnp.int32 else pltpu.VMEM(x.shape, x.dtype)
        for x in inputs
    ]
    matrices, local, left, phases, weights = local_call(
        functools.partial(prepare_kernel, cells_x, cells_y),
        "prepare_lines",
        (
            jax.ShapeDtypeStruct((len(outside), order, 128), bf16),
            jax.ShapeDtypeStruct((len(inside), order, vectors), f32),
            jax.ShapeDtypeStruct((2, vectors, lines * order), bf16),
            jax.ShapeDtypeStruct((count_ops, order // 2, 2 * vectors), f32),
            jax.ShapeDtypeStruct((2, times, 8, vectors), f32),
        ),
        [hbm_spec()] * len(inputs),
        (vmem_spec(),) * 5,
        held
        + [
            pltpu.VMEM((lines, LINK_COLS, cells_z), f32),
            pltpu.SemaphoreType.DMA((len(inputs),)),
        ],
    )(*inputs)
    message = lambda rows, *lead: jax.ShapeDtypeStruct((*lead, rows + TAIL, vectors), jnp.int16)
    part = jax.ShapeDtypeStruct((groups // 4, own_rows, vectors), f32)
    dirs = in_hbm(op_dirs)
    dirs_scratch = [pltpu.SMEM((count_ops,), jnp.int32), pltpu.SemaphoreType.DMA]
    swap_a, fields, sides = local_call(
        functools.partial(first_margin_kernel, cells_x, cells_y, groups, own_ops),
        "first_margins",
        (
            part,
            jax.ShapeDtypeStruct((7, lines, order, vectors), f32),
            jax.ShapeDtypeStruct((4, vectors, lines * order), bf16),
        ),
        [vmem_spec()] * 6 + [hbm_spec()],
        (vmem_spec(),) * 3,
        dirs_scratch,
    )(matrices, local, left, phases, halo_x, halo_y, dirs)
    swapped_a = from_partner(swap_a, "gy", 1)
    hold_a, swap_b, hold_b = local_call(
        functools.partial(second_margin_kernel, groups, own_ops),
        "second_margins",
        (part,) * 3,
        [vmem_spec()] * 3 + [hbm_spec()],
        (vmem_spec(),) * 3,
        dirs_scratch,
    )(fields, sides, phases, dirs)
    def in_vmem(body, name, outs, *inputs):
        outs = outs if isinstance(outs, tuple) else (outs,)
        specs = (vmem_spec(),) * len(outs)
        return local_call(body, name, outs, [vmem_spec()] * len(inputs), specs)(*inputs)

    half = own_rows // 2
    messages = []
    last = levels - 1
    if last > 1:
        swapped_b = from_partner(swap_b, "gy", 1)
    for b in range(1, last):
        body = functools.partial(fold_kernel, b, vectors)
        inputs = (hold_a, swapped_a) if b == 1 else (hold_b, swapped_b)
        (sent,) = in_vmem(body, "fold_groups", message(own_rows, groups >> (b + 1)), *inputs, *messages)
        messages.append(from_partner(sent, "gy", 1 << b))
    body = functools.partial(spread_kernel, last, vectors)
    inputs = (hold_a, swapped_a) if last == 1 else (hold_b, swapped_b)
    for_y, for_both = in_vmem(body, "spread_halves", (message(half),) * 2, *inputs, *messages)
    if last == 1:
        for_y, for_both, swap_b = lax.optimization_barrier((for_y, for_both, swap_b))
        swapped_b = from_partner(swap_b, "gy", 1)
    own = (hold_b, swapped_b, *messages)
    body = functools.partial(send_kernel, vectors)
    (for_x,) = in_vmem(body, "send_half", message(half), *own)
    came = [
        from_partner(for_y, "gy", 1 << last),
        from_diagonal(for_both, ("gx", "gy"), lambda x, y: (x ^ 1, y ^ (1 << last))),
        from_partner(for_x, "gx", 1),
    ]
    body = functools.partial(keep_kernel, vectors)
    (packed,) = in_vmem(body, "keep_half", message(half), *own, *came)
    norm_factor = 1.0 / math.sqrt(3.0 * cells_x * shares * cells_y * groups * cells_z)
    step = 2
    while step < shares:
        arrived = from_partner(packed, "gx", step)
        step *= 2
        last_one = step >= shares
        body = functools.partial(both_kernel, vectors, norm_factor if last_one else None)
        shape = jax.ShapeDtypeStruct((half, vectors), bf16) if last_one else message(half)
        (packed,) = in_vmem(body, "finish_half" if last_one else "sum_both", shape, packed, arrived)
    finished = packed
    kept = [finished] + [from_step(finished, "ta", t) for t in range(1, times)]
    other = [from_partner(finished, "gx", 1)]
    for t in range(1, times):
        source = lambda row, x: ((row + t) % times, x ^ 1)
        other.append(from_diagonal(finished, ("ta", "gx"), source))
    split = own_ops % 2 == 0
    now_ops = own_ops // 2 if split else own_ops
    sums_shape = (2 * now_ops, 32, vectors)
    scratch = [
        pltpu.VMEM((2 * now_ops * vectors, 2 * vectors), bf16),
        pltpu.VMEM((2 * vectors, 2 * now_ops * vectors), bf16),
    ]
    live, sums = local_call(
        functools.partial(first_contract_kernel, times, split),
        "first_contraction",
        (jax.ShapeDtypeStruct((8, vectors), f32), jax.ShapeDtypeStruct(sums_shape, f32)),
        [smem_spec()] + [vmem_spec()] * (2 + times),
        (vmem_spec(),) * 2,
        scratch,
    )(slot_counts, weights, perams[0], *kept)
    margins = local_call(
        margins_kernel,
        "margins_out",
        jax.ShapeDtypeStruct((1, own_rows, vectors), f32),
        [vmem_spec()] * 2,
        vmem_spec(),
    )(*lax.optimization_barrier((kept[0], other[0], sums))[:2])
    correlators = local_call(
        functools.partial(second_contract_kernel, times, split),
        "second_contraction",
        jax.ShapeDtypeStruct((1, own_ops, 2), f32),
        [vmem_spec()] * (4 + 2 * times),
        vmem_spec(),
        [pltpu.VMEM(sums_shape, f32)] + scratch,
    )(weights, perams[0], *other, *kept, live, sums)
    return (margins.reshape(1, own_ops, 2, vectors, vectors), correlators)


def solution(mesh):
    placed = (
        P("ta", "gx", "gy", None, None, None, None),
        P("ta", "gx", "gy", None, None, None, None, None),
        P(),
        P(),
        P(("ta", "gx"), None, None, None),
        P(("ta", "gx"), None),
        P(("ta", "gx")),
    )
    return jax.shard_map(
        per_device,
        mesh=mesh,
        in_specs=placed,
        out_specs=(P("ta", "gy", None, None, None), P(("ta", "gx"), "gy", None)),
        check_vma=False,
    )
```

```python
import functools
import math

import jax
import jax.numpy as jnp
import numpy as np
from jax import lax
from jax.experimental import pallas as pl
from jax.experimental.pallas import tpu as pltpu
from jax.sharding import PartitionSpec as P

VMEM_LIMIT = 24 * 1024 * 1024
MOMENTA = 3
LINK_COLS = 54
TAIL = 16
FIXED_BITS = 14.0


def wave_constants(cells_z):
    z_row = np.arange(3 * cells_z) // 3
    columns = []
    for ahead in range(2):
        for momentum in range(MOMENTA):
            angle = 2.0 * math.pi * momentum * ((z_row + ahead) % cells_z) / cells_z
            columns.append(np.cos(angle))
            columns.append(np.sin(angle))
    left = np.stack(columns, axis=1).astype(np.float32)
    terms = []
    for _ in range(3):
        term = left.astype(jnp.bfloat16).astype(np.float32)
        terms.append(term)
        left = left - term
    return jnp.asarray(np.concatenate(terms, axis=1), jnp.bfloat16)


def iota(shape, axis):
    return lax.broadcasted_iota(jnp.int32, shape, axis)


def third(x):
    return (x * 21846) >> 16


def one_hot(condition):
    return condition.astype(jnp.float32).astype(jnp.bfloat16)


def planar_order(order):
    row, col = iota((order, order), 0), iota((order, order), 1)
    half = order // 2
    source = jnp.where(row < half, 2 * row, 2 * (row - half) + 1)
    return one_hot(col == source)


def side_by_side(planar):
    half = planar.shape[0] // 2
    return jnp.concatenate([planar[:half], planar[half:]], axis=1).astype(jnp.bfloat16)


def transport(matrix, pair, sign):
    half, vectors = matrix.shape[0] // 2, pair.shape[1] // 2
    parts = jnp.dot(matrix, pair, preferred_element_type=jnp.float32)
    real, imag = parts[:half], parts[half:]
    if sign > 0:
        return jnp.concatenate(
            [real[:, :vectors] - imag[:, vectors:], real[:, vectors:] + imag[:, :vectors]], axis=0
        )
    return jnp.concatenate(
        [real[:, :vectors] + imag[:, vectors:], real[:, vectors:] - imag[:, :vectors]], axis=0
    )


def halo_fields(cells_x, cells_y):
    pairs = [(0, (cells_x - 1) * cells_y + y) for y in range(cells_y)]
    return pairs + [(1, x * cells_y + cells_y - 1) for x in range(cells_x)]


def local_fields(cells_x, cells_y):
    lines = cells_x * cells_y
    outside = halo_fields(cells_x, cells_y)
    every = [(code, line) for code in range(7) for line in range(lines)]
    return [pair for pair in every if pair not in outside]


def prepare_kernel(cells_x, cells_y, *refs):
    inputs, refs = refs[:6], refs[6:]
    matrix_ref, local_ref, left_ref, phase_ref, weight_ref, code_ref = refs[:6]
    held, link_rows_ref, sems = refs[6:12], refs[12], refs[13]
    copies = [
        pltpu.make_async_copy(src, dst, sems.at[k])
        for k, (src, dst) in enumerate(zip(inputs, held))
    ]
    for copy in copies:
        copy.start()
    v_ref, link_ref, dirs_ref, moms_ref, waves_ref, pair_ref = held
    f32, bf16 = jnp.float32, jnp.bfloat16
    order, vectors = v_ref.shape[2], v_ref.shape[3]
    half, cells_z = order // 2, order // 6
    lines = cells_x * cells_y
    times = weight_ref.shape[1]
    spread = one_hot(third(iota((half, cells_z), 0)) == iota((half, cells_z), 1))
    row, col = iota((half, LINK_COLS), 0), iota((half, LINK_COLS), 1)
    row_color = row - 3 * third(row)
    pair_at = third(col >> 1)
    col_in, col_out = (col >> 1) - 3 * pair_at, pair_at - 3 * third(pair_at)
    pick = [(row_color == col_out).astype(f32), (row_color == col_in).astype(f32)]
    wide = (LINK_COLS, 6 * 128)
    row, col = iota(wide, 0), iota(wide, 1)
    block, place = col >> 7, col & 127
    color = place - 3 * third(place)
    pair_at = third(row >> 1)
    row_in, row_out = (row >> 1) - 3 * pair_at, pair_at - 3 * third(pair_at)
    fits = 2 * third(pair_at) + (row & 1) == block
    expand = [one_hot(fits & (row_in == color)), one_hot(fits & (row_out == color))]
    row, col = iota((half, 128), 0), iota((half, 128), 1)
    near = ((third(row) == third(col)) & (col < half)).astype(f32)
    planar = planar_order(order)
    for copy in copies:
        copy.wait()
    for t in range(times):
        sink = pair_ref[0, 0] == t
        source = pair_ref[0, 1] == t
        weight_ref[0, t] = jnp.full(weight_ref.shape[2:], jnp.where(sink, 1.0, 0.0), f32)
        weight_ref[1, t] = jnp.full(weight_ref.shape[2:], jnp.where(source, 1.0, 0.0), f32)
    for line in range(lines):
        for k in range(LINK_COLS // 2):
            link_rows_ref[line, 2 * k : 2 * k + 2] = link_ref[line, k].astype(f32)
    outside = halo_fields(cells_x, cells_y)
    inside = local_fields(cells_x, cells_y)
    ordered = []
    for line in range(lines):
        here = jnp.dot(
            planar, v_ref[line // cells_y, line % cells_y], preferred_element_type=f32
        )
        ordered.append(here)
        local_ref[inside.index((6, line))] = here
    for line in range(lines):
        here = ordered[line]
        ahead_z = jnp.concatenate(
            [here[3:half], here[:3], here[half + 3 :], here[half : half + 3]], axis=0
        )
        columns = slice(line * order, (line + 1) * order)
        left_ref[0, :, columns] = here.T.astype(bf16)
        left_ref[1, :, columns] = ahead_z.T.astype(bf16)
        seen = lax.dot_general(
            spread,
            link_rows_ref[line].astype(bf16),
            (((1,), (1,)), ((), ())),
            preferred_element_type=f32,
        )
        pair = side_by_side(here)
        for way in range(2):
            blocks = jnp.dot(
                (seen * pick[way]).astype(bf16), expand[way], preferred_element_type=f32
            )
            for d in range(3):
                matrix = jnp.concatenate(
                    [
                        blocks[:, 256 * d : 256 * d + 128] * near,
                        blocks[:, 256 * d + 128 : 256 * d + 256] * near,
                    ],
                    axis=0,
                ).astype(bf16)
                if way == 1:
                    carried = transport(matrix[:, :half], pair, -1)
                    local_ref[inside.index((3 + d, line))] = carried.astype(bf16).astype(f32)
                elif (d, line) in outside:
                    matrix_ref[outside.index((d, line))] = matrix
                else:
                    ahead = ahead_z if d == 2 else ordered[line + (cells_y if d == 0 else 1)]
                    local_ref[inside.index((d, line))] = transport(
                        matrix[:, :half], side_by_side(ahead), 1
                    )
    wave_cols = waves_ref.shape[1]
    per_term = wave_cols // 3
    row, col = iota((wave_cols, 2 * vectors), 0), iota((wave_cols, 2 * vectors), 1)
    term = (row >= per_term).astype(jnp.int32) + (row >= 2 * per_term).astype(jnp.int32)
    wave_at = row - per_term * term - (col >= vectors).astype(jnp.int32)
    for o in range(phase_ref.shape[0]):
        code_ref[o] = jnp.full(code_ref.shape[1:], dirs_ref[o], jnp.int32).astype(f32)
        column = 2 * (jnp.where(dirs_ref[o] == 5, MOMENTA, 0) + moms_ref[o])
        phase_ref[o] = jnp.dot(
            waves_ref[...], one_hot(wave_at == column), preferred_element_type=f32
        )


def margin_kernel(cells_x, cells_y, groups, own_ops, *refs):
    matrix_ref, local_ref, left_ref, phase_ref, code_ref, halo_x_ref, halo_y_ref = refs[:7]
    swap_ref, hold_ref, field_ref, side_ref = refs[7:]
    f32, bf16 = jnp.float32, jnp.bfloat16
    me = lax.axis_index("gy")
    codes = {}
    for j in range(groups):
        for i in range(own_ops):
            codes[j, i] = jnp.max(code_ref[(me ^ j) * own_ops + i]).astype(jnp.int32)
    lines = cells_x * cells_y
    order, vectors = halo_x_ref.shape[2], halo_x_ref.shape[3]
    half = order // 2
    planar = planar_order(order)
    side_ref[0] = left_ref[0]
    side_ref[3] = left_ref[1]
    outside = halo_fields(cells_x, cells_y)
    for d in range(2):
        for line in range(lines):
            x, y = line // cells_y, line % cells_y
            columns = slice(line * order, (line + 1) * order)
            if (d, line) not in outside:
                ahead = line + (cells_y if d == 0 else 1)
                side_ref[1 + d, :, columns] = left_ref[0, :, ahead * order : (ahead + 1) * order]
                continue
            halo = halo_x_ref[0, y] if d == 0 else halo_y_ref[x, 0]
            ahead = jnp.dot(planar, halo, preferred_element_type=f32)
            side_ref[1 + d, :, columns] = ahead.T.astype(bf16)
            matrix = matrix_ref[outside.index((d, line))]
            field_ref[d, line] = transport(matrix[:, :half], side_by_side(ahead), 1)
    for k, (code, line) in enumerate(local_fields(cells_x, cells_y)):
        field_ref[code, line] = local_ref[k]
    for j in sorted(range(groups), key=lambda j: -(j & 1)):
        blocks = []
        for i in range(own_ops):
            o = (me ^ j) * own_ops + i
            code = codes[j, i]
            side = jnp.where((code >= 3) & (code < 6), code - 2, 0)
            cosine = phase_ref[o, :, 0:vectors]
            sine = phase_ref[o, :, vectors : 2 * vectors]
            pairs = []
            for line in range(lines):
                real, imag = field_ref[code, line, 0:half], field_ref[code, line, half:order]
                turned_r, turned_i = cosine * real - sine * imag, sine * real + cosine * imag
                pairs.append(jnp.concatenate([turned_r, turned_i], axis=1))
                pairs.append(jnp.concatenate([turned_i, -turned_r], axis=1))
            pair = jnp.concatenate(pairs, axis=0).astype(bf16)
            product = jnp.dot(side_ref[side], pair, preferred_element_type=f32)
            blocks += [product[:, :vectors], product[:, vectors:]]
        if j & 1:
            put_fixed(swap_ref.at[j >> 1], blocks)
            continue
        for k, block in enumerate(blocks):
            hold_ref[j >> 1, k * vectors : (k + 1) * vectors] = block


def scale_of(block):
    top = jnp.max(jnp.abs(block), axis=0, keepdims=True)
    return jnp.floor(jnp.log2(jnp.maximum(top, 1e-30))) + 1.0


def put_fixed(out_ref, blocks):
    rows, vectors = blocks[0].shape
    tail = iota((TAIL, vectors), 0)
    scales = jnp.zeros((TAIL, vectors), jnp.float32)
    for k, block in enumerate(blocks):
        scale = scale_of(block)
        scales = jnp.where(tail == k, scale, scales)
        fixed = jnp.floor(block * jnp.exp2(FIXED_BITS - scale) + 0.5)
        out_ref[k * rows : (k + 1) * rows] = fixed.astype(jnp.int32).astype(jnp.int16)
    out_ref[len(blocks) * rows :] = scales.astype(jnp.int32).astype(jnp.int16)


def from_fixed(ref, rows, k):
    scales = ref[ref.shape[0] - TAIL :].astype(jnp.int32).astype(jnp.float32)
    block = ref[k * rows : (k + 1) * rows].astype(jnp.int32).astype(jnp.float32)
    return block * jnp.exp2(scales[k : k + 1] - FIXED_BITS)


def group_block(held_ref, messages, j, start, rows):
    total = held_ref[j >> 1, pl.ds(start, rows)]
    for b, ref in enumerate(messages):
        total = total + fixed_at(ref.at[j >> (b + 1)], start, rows)
    return total


def fixed_at(ref, start, rows):
    tail = ref[ref.shape[0] - TAIL :].astype(jnp.int32).astype(jnp.float32)
    scale = jnp.max(
        jnp.where(iota(tail.shape, 0) == start // rows, tail, -1000.0), axis=0, keepdims=True
    )
    block = ref[pl.ds(start, rows)].astype(jnp.int32).astype(jnp.float32)
    return block * jnp.exp2(scale - FIXED_BITS)


def fold_kernel(level, vectors, held_ref, *refs):
    messages, out_ref = refs[:-1], refs[-1]
    for k in range(out_ref.shape[0]):
        blocks = [
            group_block(held_ref, messages, (2 * k + 1) << level, start, vectors)
            for start in range(0, held_ref.shape[1], vectors)
        ]
        put_fixed(out_ref.at[k], blocks)


def half_blocks(held_ref, messages, j, kept, vectors):
    me = lax.axis_index("gx") & 1
    half = held_ref.shape[1] // 2
    base = pl.multiple_of((me if kept else 1 - me) * half, half)
    steps = range(0, half, vectors)
    return [group_block(held_ref, messages, j, base + step, vectors) for step in steps]


def spread_kernel(level, vectors, held_ref, *refs):
    messages, (y_ref, diagonal_ref, x_ref) = refs[:-3], refs[-3:]
    put_fixed(y_ref, half_blocks(held_ref, messages, 1 << level, True, vectors))
    put_fixed(diagonal_ref, half_blocks(held_ref, messages, 1 << level, False, vectors))
    put_fixed(x_ref, half_blocks(held_ref, messages, 0, False, vectors))


def keep_kernel(vectors, held_ref, *refs):
    messages, came, out_ref = refs[:-4], refs[-4:-1], refs[-1]
    blocks = half_blocks(held_ref, messages, 0, True, vectors)
    for p in range(len(blocks)):
        for ref in came:
            blocks[p] = blocks[p] + from_fixed(ref, vectors, p)
    put_fixed(out_ref, blocks)


def both_kernel(vectors, norm_factor, own_ref, arrived_ref, out_ref):
    blocks = [
        from_fixed(own_ref, vectors, p) + from_fixed(arrived_ref, vectors, p)
        for p in range((own_ref.shape[0] - TAIL) // vectors)
    ]
    if norm_factor is None:
        put_fixed(out_ref, blocks)
        return
    for p, block in enumerate(blocks):
        out_ref[p * vectors : (p + 1) * vectors] = (block * norm_factor).astype(out_ref.dtype)


def contract(sums_ref, weight_ref, blocks, tau_ref, left_ref, right_ref):
    f32, bf16 = jnp.float32, jnp.bfloat16
    vectors = sums_ref.shape[2]
    count_ops = sums_ref.shape[0] // 2
    order = tau_ref.shape[2]
    spins = order // vectors
    me_t = lax.axis_index("ta")
    times = len(blocks)

    def chosen(end, k):
        total = jnp.zeros((vectors // 8, 8, vectors), f32)
        for t in range(times):
            weight = weight_ref[end, lax.rem(me_t + t, times)]
            total = total + blocks[t](k).astype(f32).reshape(total.shape) * weight
        return total.reshape(vectors, vectors)

    for o in range(count_ops):
        first = 2 * o * vectors
        a_r, a_i = chosen(0, 2 * o).astype(bf16), chosen(0, 2 * o + 1).astype(bf16)
        b_r, b_i = chosen(1, 2 * o).T.astype(bf16), chosen(1, 2 * o + 1).T.astype(bf16)
        real, imag = slice(first, first + vectors), slice(first + vectors, first + 2 * vectors)
        left_ref[real, 0:vectors] = a_r
        left_ref[real, vectors:] = -a_i
        left_ref[imag, 0:vectors] = a_i
        left_ref[imag, vectors:] = a_r
        right_ref[0:vectors, real] = b_r
        right_ref[0:vectors, imag] = -b_i
        right_ref[vectors:, real] = b_i
        right_ref[vectors:, imag] = b_r
    lanes = sums_ref.shape[1]
    fold = lambda t: jnp.sum(t.reshape(vectors // lanes, lanes, vectors), axis=0)
    sums = [jnp.zeros((lanes, vectors), f32) for _ in range(2 * count_ops)]
    for s in range(spins):
        rows = slice(s * vectors, (s + 1) * vectors)
        x = jnp.dot(
            left_ref[...],
            jnp.concatenate([tau_ref[0, rows], tau_ref[1, rows]], axis=0),
            preferred_element_type=f32,
        )
        for c in range(spins):
            cols = slice(c * vectors, (c + 1) * vectors)
            y = jnp.dot(
                jnp.concatenate([tau_ref[0, rows, cols], tau_ref[1, rows, cols]], axis=1),
                right_ref[...],
                preferred_element_type=f32,
            )
            for o in range(count_ops):
                first = 2 * o * vectors
                x_r = x[first : first + vectors, cols]
                x_i = x[first + vectors : first + 2 * vectors, cols]
                y_r = y[:, first : first + vectors]
                y_i = y[:, first + vectors : first + 2 * vectors]
                sums[2 * o] = sums[2 * o] + fold(x_r * y_r + x_i * y_i)
                sums[2 * o + 1] = sums[2 * o + 1] + fold(x_i * y_r - x_r * y_i)
    for k, total in enumerate(sums):
        sums_ref[k] = total


def part_of(ref, vectors):
    return lambda k: ref[k * vectors : (k + 1) * vectors]


def first_contract_kernel(times, split, live_ref, weight_ref, tau_ref, *refs):
    blocks, (live_out_ref, sums_ref, left_ref, right_ref) = refs[:times], refs[times:]
    live = jnp.where(live_ref[0] > 0, 1.0, 0.0)
    live_out_ref[...] = jnp.full(live_out_ref.shape, live, jnp.float32)
    if split:
        vectors = sums_ref.shape[2]
        blocks = [part_of(ref, vectors) for ref in blocks]
        contract(sums_ref, weight_ref, blocks, tau_ref, left_ref, right_ref)
    else:
        sums_ref[...] = jnp.zeros_like(sums_ref)


def margins_kernel(kept_ref, other_ref, margin_ref):
    half = kept_ref.shape[0]
    me = lax.axis_index("gx") & 1
    for place, ref in ((me, kept_ref), (1 - me, other_ref)):
        rows = pl.ds(pl.multiple_of(place * half, half), half)
        margin_ref[0, rows] = ref[...].astype(jnp.float32)


def second_contract_kernel(times, split, weight_ref, tau_ref, *refs):
    other, kept, refs = refs[:times], refs[times : 2 * times], refs[2 * times :]
    live_ref, first_sums_ref, corr_ref, sums_ref, left_ref, right_ref = refs
    vectors = sums_ref.shape[2]
    half = kept[0].shape[0]
    me = lax.axis_index("gx") & 1
    parts_per_half = half // vectors

    def either(kept_ref, other_ref):
        def part(k):
            row = (k % parts_per_half) * vectors
            own, far = kept_ref[row : row + vectors], other_ref[row : row + vectors]
            mine = (k // parts_per_half == me).astype(jnp.float32)
            return own.astype(jnp.float32) * mine + far.astype(jnp.float32) * (1.0 - mine)

        return part

    blocks = [part_of(ref, vectors) for ref in other]
    if not split:
        blocks = [either(a, b) for a, b in zip(kept, other)]
    contract(sums_ref, weight_ref, blocks, tau_ref, left_ref, right_ref)
    now_ops = sums_ref.shape[0] // 2
    known = [(sums_ref, (1 - me) * now_ops)] if split else [(sums_ref, 0)]
    if split:
        known.append((first_sums_ref, me * now_ops))
    shape = corr_ref.shape[1:]
    row, col = iota(shape, 0), iota(shape, 1)
    result = jnp.zeros(shape, jnp.float32)
    for ref, first in known:
        for k in range(2 * now_ops):
            total = jnp.sum(jnp.sum(ref[k], axis=0, keepdims=True), axis=1, keepdims=True)
            here = (row == first + k // 2) & (col == k % 2)
            result = jnp.where(here, total * (1.0 / vectors), result)
    corr_ref[0] = result * live_ref[0 : shape[0], 0 : shape[1]]


def vmem_spec():
    return pl.BlockSpec(memory_space=pltpu.VMEM)


def smem_spec():
    return pl.BlockSpec(memory_space=pltpu.SMEM)


def hbm_spec():
    return pl.BlockSpec(memory_space=pltpu.HBM)


def in_hbm(x):
    return pltpu.with_memory_space_constraint(x, pltpu.HBM)


def local_call(body, name, outs, in_specs, out_specs, scratch=(), cost=None):
    return pl.pallas_call(
        body,
        out_shape=outs,
        in_specs=in_specs,
        out_specs=out_specs,
        scratch_shapes=list(scratch),
        compiler_params=pltpu.CompilerParams(vmem_limit_bytes=VMEM_LIMIT),
        cost_estimate=cost,
        name=name,
    )


def from_step(block, axis, step):
    count = lax.axis_size(axis)
    return lax.ppermute(block, axis, [((i + step) % count, i) for i in range(count)])


def from_partner(block, axis, step):
    count = lax.axis_size(axis)
    return lax.ppermute(block, axis, [(i ^ step, i) for i in range(count)])


def from_diagonal(block, axes, sources):
    rows, columns = (lax.axis_size(axis) for axis in axes)
    perm = []
    for row in range(rows):
        for column in range(columns):
            from_row, from_column = sources(row, column)
            perm.append((from_row * columns + from_column, row * columns + column))
    return lax.ppermute(block, axes, perm)


def per_device(eigvecs, links, op_dirs, op_moms, perams, pair_times, slot_counts):
    f32, bf16 = jnp.float32, jnp.bfloat16
    _, cells_x, cells_y, cells_z, colors, _, vectors = eigvecs.shape
    order = cells_z * colors * 2
    lines = cells_x * cells_y
    count_ops = op_dirs.shape[0]
    times, shares, groups = lax.axis_size("ta"), lax.axis_size("gx"), lax.axis_size("gy")
    levels = groups.bit_length() - 1
    own_ops = count_ops // groups
    own_rows = own_ops * 2 * vectors
    field = eigvecs.reshape(cells_x, cells_y, order, vectors)
    halo_x = from_step(field[0:1], "gx", 1)
    halo_y = from_step(field, "gy", 1)
    link_field = links[0].transpose(0, 1, 3, 5, 6, 4, 2).reshape(lines, 27, 2, cells_z)
    outside, inside = halo_fields(cells_x, cells_y), local_fields(cells_x, cells_y)
    inputs = [field, link_field, op_dirs, op_moms, wave_constants(cells_z), pair_times]
    inputs = [in_hbm(x) for x in inputs]
    held = [
        pltpu.SMEM(x.shape, x.dtype) if x.dtype == jnp.int32 else pltpu.VMEM(x.shape, x.dtype)
        for x in inputs
    ]
    matrices, local, left, phases, weights, codes = local_call(
        functools.partial(prepare_kernel, cells_x, cells_y),
        "prepare_lines",
        (
            jax.ShapeDtypeStruct((len(outside), order, 128), bf16),
            jax.ShapeDtypeStruct((len(inside), order, vectors), f32),
            jax.ShapeDtypeStruct((2, vectors, lines * order), bf16),
            jax.ShapeDtypeStruct((count_ops, order // 2, 2 * vectors), f32),
            jax.ShapeDtypeStruct((2, times, 8, vectors), f32),
            jax.ShapeDtypeStruct((count_ops, 8, vectors), f32),
        ),
        [hbm_spec()] * len(inputs),
        (vmem_spec(),) * 6,
        held
        + [
            pltpu.VMEM((lines, LINK_COLS, cells_z), f32),
            pltpu.SemaphoreType.DMA((len(inputs),)),
        ],
    )(*inputs)
    message = lambda rows, *lead: jax.ShapeDtypeStruct((*lead, rows + TAIL, vectors), jnp.int16)
    swap, held = local_call(
        functools.partial(margin_kernel, cells_x, cells_y, groups, own_ops),
        "partial_margins",
        (
            message(own_rows, groups // 2),
            jax.ShapeDtypeStruct((groups // 2, own_rows, vectors), f32),
        ),
        [vmem_spec()] * 7,
        (vmem_spec(),) * 2,
        [
            pltpu.VMEM((7, lines, order, vectors), f32),
            pltpu.VMEM((4, vectors, lines * order), bf16),
        ],
    )(matrices, local, left, phases, codes, halo_x, halo_y)

    def in_vmem(body, name, outs, *inputs):
        outs = outs if isinstance(outs, tuple) else (outs,)
        specs = (vmem_spec(),) * len(outs)
        return local_call(body, name, outs, [vmem_spec()] * len(inputs), specs)(*inputs)

    half = own_rows // 2
    messages = [from_partner(swap, "gy", 1)]
    last = levels - 1
    for b in range(1, last):
        body = functools.partial(fold_kernel, b, vectors)
        shape = message(own_rows, groups >> (b + 1))
        (sent,) = in_vmem(body, "fold_groups", shape, held, *messages)
        messages.append(from_partner(sent, "gy", 1 << b))
    body = functools.partial(spread_kernel, last, vectors)
    for_y, for_both, for_x = in_vmem(body, "spread_halves", (message(half),) * 3, held, *messages)
    came = [
        from_partner(for_y, "gy", 1 << last),
        from_diagonal(for_both, ("gx", "gy"), lambda x, y: (x ^ 1, y ^ (1 << last))),
        from_partner(for_x, "gx", 1),
    ]
    body = functools.partial(keep_kernel, vectors)
    (packed,) = in_vmem(body, "keep_half", message(half), held, *messages, *came)
    norm_factor = 1.0 / math.sqrt(3.0 * cells_x * shares * cells_y * groups * cells_z)
    step = 2
    while step < shares:
        arrived = from_partner(packed, "gx", step)
        step *= 2
        last_one = step >= shares
        body = functools.partial(both_kernel, vectors, norm_factor if last_one else None)
        shape = jax.ShapeDtypeStruct((half, vectors), bf16) if last_one else message(half)
        (packed,) = in_vmem(body, "finish_half" if last_one else "sum_both", shape, packed, arrived)
    finished = packed
    kept = [finished] + [from_step(finished, "ta", t) for t in range(1, times)]
    other = [from_partner(finished, "gx", 1)]
    for t in range(1, times):
        source = lambda row, x: ((row + t) % times, x ^ 1)
        other.append(from_diagonal(finished, ("ta", "gx"), source))
    split = own_ops % 2 == 0
    now_ops = own_ops // 2 if split else own_ops
    sums_shape = (2 * now_ops, 32, vectors)
    scratch = [
        pltpu.VMEM((2 * now_ops * vectors, 2 * vectors), bf16),
        pltpu.VMEM((2 * vectors, 2 * now_ops * vectors), bf16),
    ]
    live, sums = local_call(
        functools.partial(first_contract_kernel, times, split),
        "first_contraction",
        (jax.ShapeDtypeStruct((8, vectors), f32), jax.ShapeDtypeStruct(sums_shape, f32)),
        [smem_spec()] + [vmem_spec()] * (2 + times),
        (vmem_spec(),) * 2,
        scratch,
    )(slot_counts, weights, perams[0], *kept)
    margins = local_call(
        margins_kernel,
        "margins_out",
        jax.ShapeDtypeStruct((1, own_rows, vectors), f32),
        [vmem_spec()] * 2,
        vmem_spec(),
    )(*lax.optimization_barrier((kept[0], other[0], sums))[:2])
    correlators = local_call(
        functools.partial(second_contract_kernel, times, split),
        "second_contraction",
        jax.ShapeDtypeStruct((1, own_ops, 2), f32),
        [vmem_spec()] * (4 + 2 * times),
        vmem_spec(),
        [pltpu.VMEM(sums_shape, f32)] + scratch,
    )(weights, perams[0], *other, *kept, live, sums)
    return (margins.reshape(1, own_ops, 2, vectors, vectors), correlators)


def solution(mesh):
    placed = (
        P("ta", "gx", "gy", None, None, None, None),
        P("ta", "gx", "gy", None, None, None, None, None),
        P(),
        P(),
        P(("ta", "gx"), None, None, None),
        P(("ta", "gx"), None),
        P(("ta", "gx")),
    )
    return jax.shard_map(
        per_device,
        mesh=mesh,
        in_specs=placed,
        out_specs=(P("ta", "gy", None, None, None), P(("ta", "gx"), "gy", None)),
        check_vma=False,
    )
```

```python
import functools
import math

import jax
import jax.numpy as jnp
import numpy as np
from jax import lax
from jax.experimental import pallas as pl
from jax.experimental.pallas import tpu as pltpu
from jax.sharding import PartitionSpec as P

VMEM_LIMIT = 24 * 1024 * 1024
MOMENTA = 3
LINK_COLS = 54
TAIL = 16
FIXED_BITS = 14.0


def wave_constants(cells_z):
    z_row = np.arange(3 * cells_z) // 3
    columns = []
    for ahead in range(2):
        for momentum in range(MOMENTA):
            angle = 2.0 * math.pi * momentum * ((z_row + ahead) % cells_z) / cells_z
            columns.append(np.cos(angle))
            columns.append(np.sin(angle))
    left = np.stack(columns, axis=1).astype(np.float32)
    terms = []
    for _ in range(3):
        term = left.astype(jnp.bfloat16).astype(np.float32)
        terms.append(term)
        left = left - term
    return jnp.asarray(np.concatenate(terms, axis=1), jnp.bfloat16)


def iota(shape, axis):
    return lax.broadcasted_iota(jnp.int32, shape, axis)


def third(x):
    return (x * 21846) >> 16


def one_hot(condition):
    return condition.astype(jnp.float32).astype(jnp.bfloat16)


def planar_order(order):
    row, col = iota((order, order), 0), iota((order, order), 1)
    half = order // 2
    source = jnp.where(row < half, 2 * row, 2 * (row - half) + 1)
    return one_hot(col == source)


def side_by_side(planar):
    half = planar.shape[0] // 2
    return jnp.concatenate([planar[:half], planar[half:]], axis=1).astype(jnp.bfloat16)


def transport(matrix, pair, sign):
    half, vectors = matrix.shape[0] // 2, pair.shape[1] // 2
    parts = jnp.dot(matrix, pair, preferred_element_type=jnp.float32)
    real, imag = parts[:half], parts[half:]
    if sign > 0:
        return jnp.concatenate(
            [real[:, :vectors] - imag[:, vectors:], real[:, vectors:] + imag[:, :vectors]], axis=0
        )
    return jnp.concatenate(
        [real[:, :vectors] + imag[:, vectors:], real[:, vectors:] - imag[:, :vectors]], axis=0
    )


def natural_form(matrix, planar):
    half = matrix.shape[0] // 2
    turned = jnp.concatenate([-matrix[half:].astype(jnp.float32), matrix[:half].astype(jnp.float32)])
    whole = jnp.dot(matrix, planar[:half], preferred_element_type=jnp.float32) + jnp.dot(
        turned.astype(jnp.bfloat16), planar[half:], preferred_element_type=jnp.float32
    )
    return whole.astype(jnp.bfloat16)


def halo_fields(cells_x, cells_y):
    pairs = [(0, (cells_x - 1) * cells_y + y) for y in range(cells_y)]
    return pairs + [(1, x * cells_y + cells_y - 1) for x in range(cells_x)]


def local_fields(cells_x, cells_y):
    lines = cells_x * cells_y
    outside = halo_fields(cells_x, cells_y)
    every = [(code, line) for code in range(7) for line in range(lines)]
    return [pair for pair in every if pair not in outside]


def prepare_kernel(cells_x, cells_y, *refs):
    inputs, refs = refs[:6], refs[6:]
    matrix_ref, local_ref, left_ref, phase_ref, weight_ref, code_ref = refs[:6]
    held, link_rows_ref, sems = refs[6:12], refs[12], refs[13]
    copies = [
        pltpu.make_async_copy(src, dst, sems.at[k])
        for k, (src, dst) in enumerate(zip(inputs, held))
    ]
    for copy in copies:
        copy.start()
    v_ref, link_ref, dirs_ref, moms_ref, waves_ref, pair_ref = held
    f32, bf16 = jnp.float32, jnp.bfloat16
    order, vectors = v_ref.shape[2], v_ref.shape[3]
    half, cells_z = order // 2, order // 6
    lines = cells_x * cells_y
    times = weight_ref.shape[1]
    spread = one_hot(third(iota((half, cells_z), 0)) == iota((half, cells_z), 1))
    row, col = iota((half, LINK_COLS), 0), iota((half, LINK_COLS), 1)
    row_color = row - 3 * third(row)
    pair_at = third(col >> 1)
    col_in, col_out = (col >> 1) - 3 * pair_at, pair_at - 3 * third(pair_at)
    pick = [(row_color == col_out).astype(f32), (row_color == col_in).astype(f32)]
    wide = (LINK_COLS, 6 * 128)
    row, col = iota(wide, 0), iota(wide, 1)
    block, place = col >> 7, col & 127
    color = place - 3 * third(place)
    pair_at = third(row >> 1)
    row_in, row_out = (row >> 1) - 3 * pair_at, pair_at - 3 * third(pair_at)
    fits = 2 * third(pair_at) + (row & 1) == block
    expand = [one_hot(fits & (row_in == color)), one_hot(fits & (row_out == color))]
    row, col = iota((half, 128), 0), iota((half, 128), 1)
    near = ((third(row) == third(col)) & (col < half)).astype(f32)
    planar = planar_order(order)
    for copy in copies:
        copy.wait()
    for t in range(times):
        sink = pair_ref[0, 0] == t
        source = pair_ref[0, 1] == t
        weight_ref[0, t] = jnp.full(weight_ref.shape[2:], jnp.where(sink, 1.0, 0.0), f32)
        weight_ref[1, t] = jnp.full(weight_ref.shape[2:], jnp.where(source, 1.0, 0.0), f32)
    for line in range(lines):
        for k in range(LINK_COLS // 2):
            link_rows_ref[line, 2 * k : 2 * k + 2] = link_ref[line, k].astype(f32)
    outside = halo_fields(cells_x, cells_y)
    inside = local_fields(cells_x, cells_y)
    ordered = []
    for line in range(lines):
        here = jnp.dot(
            planar, v_ref[line // cells_y, line % cells_y], preferred_element_type=f32
        )
        ordered.append(here)
        local_ref[inside.index((6, line))] = here
    for line in range(lines):
        here = ordered[line]
        ahead_z = jnp.concatenate(
            [here[3:half], here[:3], here[half + 3 :], here[half : half + 3]], axis=0
        )
        columns = slice(line * order, (line + 1) * order)
        left_ref[0, :, columns] = here.T.astype(bf16)
        left_ref[1, :, columns] = ahead_z.T.astype(bf16)
        seen = lax.dot_general(
            spread,
            link_rows_ref[line].astype(bf16),
            (((1,), (1,)), ((), ())),
            preferred_element_type=f32,
        )
        pair = side_by_side(here)
        for way in range(2):
            blocks = jnp.dot(
                (seen * pick[way]).astype(bf16), expand[way], preferred_element_type=f32
            )
            for d in range(3):
                matrix = jnp.concatenate(
                    [
                        blocks[:, 256 * d : 256 * d + 128] * near,
                        blocks[:, 256 * d + 128 : 256 * d + 256] * near,
                    ],
                    axis=0,
                ).astype(bf16)
                if way == 1:
                    carried = transport(matrix[:, :half], pair, -1)
                    local_ref[inside.index((3 + d, line))] = carried.astype(bf16).astype(f32)
                elif (d, line) in outside:
                    matrix_ref[outside.index((d, line))] = natural_form(matrix[:, :half], planar)
                else:
                    ahead = ahead_z if d == 2 else ordered[line + (cells_y if d == 0 else 1)]
                    local_ref[inside.index((d, line))] = transport(
                        matrix[:, :half], side_by_side(ahead), 1
                    )
    wave_cols = waves_ref.shape[1]
    per_term = wave_cols // 3
    row, col = iota((wave_cols, 2 * vectors), 0), iota((wave_cols, 2 * vectors), 1)
    term = (row >= per_term).astype(jnp.int32) + (row >= 2 * per_term).astype(jnp.int32)
    wave_at = row - per_term * term - (col >= vectors).astype(jnp.int32)
    for o in range(phase_ref.shape[0]):
        code_ref[o] = jnp.full(code_ref.shape[1:], dirs_ref[o], jnp.int32).astype(f32)
        column = 2 * (jnp.where(dirs_ref[o] == 5, MOMENTA, 0) + moms_ref[o])
        phase_ref[o] = jnp.dot(
            waves_ref[...], one_hot(wave_at == column), preferred_element_type=f32
        )


def margin_kernel(cells_x, cells_y, groups, own_ops, *refs):
    matrix_ref, local_ref, left_ref, phase_ref, code_ref, halo_x_ref, halo_y_ref = refs[:7]
    swap_ref, hold_ref, field_ref, side_ref = refs[7:]
    f32, bf16 = jnp.float32, jnp.bfloat16
    me = lax.axis_index("gy")
    codes = {}
    for j in range(groups):
        for i in range(own_ops):
            codes[j, i] = jnp.max(code_ref[(me ^ j) * own_ops + i]).astype(jnp.int32)
    lines = cells_x * cells_y
    order, vectors = halo_x_ref.shape[2], halo_x_ref.shape[3]
    half = order // 2
    planar = planar_order(order)
    side_ref[0] = left_ref[0]
    side_ref[3] = left_ref[1]
    outside = halo_fields(cells_x, cells_y)
    for d in range(2):
        for line in range(lines):
            x, y = line // cells_y, line % cells_y
            columns = slice(line * order, (line + 1) * order)
            if (d, line) not in outside:
                ahead = line + (cells_y if d == 0 else 1)
                side_ref[1 + d, :, columns] = left_ref[0, :, ahead * order : (ahead + 1) * order]
                continue
            halo = halo_x_ref[0, y] if d == 0 else halo_y_ref[x, 0]
            ahead = jnp.dot(planar, halo, preferred_element_type=f32)
            side_ref[1 + d, :, columns] = ahead.T.astype(bf16)
            matrix = matrix_ref[outside.index((d, line))]
            field_ref[d, line] = jnp.dot(matrix, halo, preferred_element_type=f32)
    for k, (code, line) in enumerate(local_fields(cells_x, cells_y)):
        field_ref[code, line] = local_ref[k]
    for j in sorted(range(groups), key=lambda j: -(j & 1)):
        blocks = []
        for i in range(own_ops):
            o = (me ^ j) * own_ops + i
            code = codes[j, i]
            side = jnp.where((code >= 3) & (code < 6), code - 2, 0)
            cosine = phase_ref[o, :, 0:vectors]
            sine = phase_ref[o, :, vectors : 2 * vectors]
            pairs = []
            for line in range(lines):
                real, imag = field_ref[code, line, 0:half], field_ref[code, line, half:order]
                turned_r, turned_i = cosine * real - sine * imag, sine * real + cosine * imag
                pairs.append(jnp.concatenate([turned_r, turned_i], axis=1))
                pairs.append(jnp.concatenate([turned_i, -turned_r], axis=1))
            pair = jnp.concatenate(pairs, axis=0).astype(bf16)
            product = jnp.dot(side_ref[side], pair, preferred_element_type=f32)
            blocks += [product[:, :vectors], product[:, vectors:]]
        if j & 1:
            put_fixed(swap_ref.at[j >> 1], blocks)
            continue
        for k, block in enumerate(blocks):
            hold_ref[j >> 1, k * vectors : (k + 1) * vectors] = block


def scale_of(block):
    top = jnp.max(jnp.abs(block), axis=0, keepdims=True)
    return jnp.floor(jnp.log2(jnp.maximum(top, 1e-30))) + 1.0


def put_fixed(out_ref, blocks):
    rows, vectors = blocks[0].shape
    tail = iota((TAIL, vectors), 0)
    scales = jnp.zeros((TAIL, vectors), jnp.float32)
    for k, block in enumerate(blocks):
        scale = scale_of(block)
        scales = jnp.where(tail == k, scale, scales)
        fixed = jnp.floor(block * jnp.exp2(FIXED_BITS - scale) + 0.5)
        out_ref[k * rows : (k + 1) * rows] = fixed.astype(jnp.int32).astype(jnp.int16)
    out_ref[len(blocks) * rows :] = scales.astype(jnp.int32).astype(jnp.int16)


def from_fixed(ref, rows, k):
    scales = ref[ref.shape[0] - TAIL :].astype(jnp.int32).astype(jnp.float32)
    block = ref[k * rows : (k + 1) * rows].astype(jnp.int32).astype(jnp.float32)
    return block * jnp.exp2(scales[k : k + 1] - FIXED_BITS)


def group_block(held_ref, messages, j, start, rows):
    total = held_ref[j >> 1, pl.ds(start, rows)]
    for b, ref in enumerate(messages):
        total = total + fixed_at(ref.at[j >> (b + 1)], start, rows)
    return total


def fixed_at(ref, start, rows):
    tail = ref[ref.shape[0] - TAIL :].astype(jnp.int32).astype(jnp.float32)
    scale = jnp.max(
        jnp.where(iota(tail.shape, 0) == start // rows, tail, -1000.0), axis=0, keepdims=True
    )
    block = ref[pl.ds(start, rows)].astype(jnp.int32).astype(jnp.float32)
    return block * jnp.exp2(scale - FIXED_BITS)


def fold_kernel(level, vectors, held_ref, *refs):
    messages, out_ref = refs[:-1], refs[-1]
    for k in range(out_ref.shape[0]):
        blocks = [
            group_block(held_ref, messages, (2 * k + 1) << level, start, vectors)
            for start in range(0, held_ref.shape[1], vectors)
        ]
        put_fixed(out_ref.at[k], blocks)


def half_blocks(held_ref, messages, j, kept, vectors):
    me = lax.axis_index("gx") & 1
    half = held_ref.shape[1] // 2
    base = pl.multiple_of((me if kept else 1 - me) * half, half)
    steps = range(0, half, vectors)
    return [group_block(held_ref, messages, j, base + step, vectors) for step in steps]


def spread_kernel(level, vectors, held_ref, *refs):
    messages, (y_ref, diagonal_ref, x_ref) = refs[:-3], refs[-3:]
    put_fixed(y_ref, half_blocks(held_ref, messages, 1 << level, True, vectors))
    put_fixed(diagonal_ref, half_blocks(held_ref, messages, 1 << level, False, vectors))
    put_fixed(x_ref, half_blocks(held_ref, messages, 0, False, vectors))


def keep_kernel(vectors, held_ref, *refs):
    messages, came, out_ref = refs[:-4], refs[-4:-1], refs[-1]
    blocks = half_blocks(held_ref, messages, 0, True, vectors)
    for p in range(len(blocks)):
        for ref in came:
            blocks[p] = blocks[p] + from_fixed(ref, vectors, p)
    put_fixed(out_ref, blocks)


def both_kernel(vectors, norm_factor, own_ref, arrived_ref, out_ref):
    blocks = [
        from_fixed(own_ref, vectors, p) + from_fixed(arrived_ref, vectors, p)
        for p in range((own_ref.shape[0] - TAIL) // vectors)
    ]
    if norm_factor is None:
        put_fixed(out_ref, blocks)
        return
    for p, block in enumerate(blocks):
        out_ref[p * vectors : (p + 1) * vectors] = (block * norm_factor).astype(out_ref.dtype)


def contract(sums_ref, weight_ref, blocks, tau_ref, left_ref, right_ref):
    f32, bf16 = jnp.float32, jnp.bfloat16
    vectors = sums_ref.shape[2]
    count_ops = sums_ref.shape[0] // 2
    order = tau_ref.shape[2]
    spins = order // vectors
    me_t = lax.axis_index("ta")
    times = len(blocks)

    def chosen(end, k):
        total = jnp.zeros((vectors // 8, 8, vectors), f32)
        for t in range(times):
            weight = weight_ref[end, lax.rem(me_t + t, times)]
            total = total + blocks[t](k).astype(f32).reshape(total.shape) * weight
        return total.reshape(vectors, vectors)

    for o in range(count_ops):
        first = 2 * o * vectors
        a_r, a_i = chosen(0, 2 * o).astype(bf16), chosen(0, 2 * o + 1).astype(bf16)
        b_r, b_i = chosen(1, 2 * o).T.astype(bf16), chosen(1, 2 * o + 1).T.astype(bf16)
        real, imag = slice(first, first + vectors), slice(first + vectors, first + 2 * vectors)
        left_ref[real, 0:vectors] = a_r
        left_ref[real, vectors:] = -a_i
        left_ref[imag, 0:vectors] = a_i
        left_ref[imag, vectors:] = a_r
        right_ref[0:vectors, real] = b_r
        right_ref[0:vectors, imag] = -b_i
        right_ref[vectors:, real] = b_i
        right_ref[vectors:, imag] = b_r
    lanes = sums_ref.shape[1]
    fold = lambda t: jnp.sum(t.reshape(vectors // lanes, lanes, vectors), axis=0)
    sums = [jnp.zeros((lanes, vectors), f32) for _ in range(2 * count_ops)]
    for s in range(spins):
        rows = slice(s * vectors, (s + 1) * vectors)
        x = jnp.dot(
            left_ref[...],
            jnp.concatenate([tau_ref[0, rows], tau_ref[1, rows]], axis=0),
            preferred_element_type=f32,
        )
        for c in range(spins):
            cols = slice(c * vectors, (c + 1) * vectors)
            y = jnp.dot(
                jnp.concatenate([tau_ref[0, rows, cols], tau_ref[1, rows, cols]], axis=1),
                right_ref[...],
                preferred_element_type=f32,
            )
            for o in range(count_ops):
                first = 2 * o * vectors
                x_r = x[first : first + vectors, cols]
                x_i = x[first + vectors : first + 2 * vectors, cols]
                y_r = y[:, first : first + vectors]
                y_i = y[:, first + vectors : first + 2 * vectors]
                sums[2 * o] = sums[2 * o] + fold(x_r * y_r + x_i * y_i)
                sums[2 * o + 1] = sums[2 * o + 1] + fold(x_i * y_r - x_r * y_i)
    for k, total in enumerate(sums):
        sums_ref[k] = total


def part_of(ref, vectors):
    return lambda k: ref[k * vectors : (k + 1) * vectors]


def first_contract_kernel(times, split, live_ref, weight_ref, tau_ref, *refs):
    blocks, (live_out_ref, sums_ref, left_ref, right_ref) = refs[:times], refs[times:]
    live = jnp.where(live_ref[0] > 0, 1.0, 0.0)
    live_out_ref[...] = jnp.full(live_out_ref.shape, live, jnp.float32)
    if split:
        vectors = sums_ref.shape[2]
        blocks = [part_of(ref, vectors) for ref in blocks]
        contract(sums_ref, weight_ref, blocks, tau_ref, left_ref, right_ref)
    else:
        sums_ref[...] = jnp.zeros_like(sums_ref)


def margins_kernel(kept_ref, other_ref, margin_ref):
    half = kept_ref.shape[0]
    me = lax.axis_index("gx") & 1
    for place, ref in ((me, kept_ref), (1 - me, other_ref)):
        rows = pl.ds(pl.multiple_of(place * half, half), half)
        margin_ref[0, rows] = ref[...].astype(jnp.float32)


def second_contract_kernel(times, split, weight_ref, tau_ref, *refs):
    other, kept, refs = refs[:times], refs[times : 2 * times], refs[2 * times :]
    live_ref, first_sums_ref, corr_ref, sums_ref, left_ref, right_ref = refs
    vectors = sums_ref.shape[2]
    half = kept[0].shape[0]
    me = lax.axis_index("gx") & 1
    parts_per_half = half // vectors

    def either(kept_ref, other_ref):
        def part(k):
            row = (k % parts_per_half) * vectors
            own, far = kept_ref[row : row + vectors], other_ref[row : row + vectors]
            mine = (k // parts_per_half == me).astype(jnp.float32)
            return own.astype(jnp.float32) * mine + far.astype(jnp.float32) * (1.0 - mine)

        return part

    blocks = [part_of(ref, vectors) for ref in other]
    if not split:
        blocks = [either(a, b) for a, b in zip(kept, other)]
    contract(sums_ref, weight_ref, blocks, tau_ref, left_ref, right_ref)
    now_ops = sums_ref.shape[0] // 2
    known = [(sums_ref, (1 - me) * now_ops)] if split else [(sums_ref, 0)]
    if split:
        known.append((first_sums_ref, me * now_ops))
    shape = corr_ref.shape[1:]
    row, col = iota(shape, 0), iota(shape, 1)
    result = jnp.zeros(shape, jnp.float32)
    for ref, first in known:
        for k in range(2 * now_ops):
            total = jnp.sum(jnp.sum(ref[k], axis=0, keepdims=True), axis=1, keepdims=True)
            here = (row == first + k // 2) & (col == k % 2)
            result = jnp.where(here, total * (1.0 / vectors), result)
    corr_ref[0] = result * live_ref[0 : shape[0], 0 : shape[1]]


def vmem_spec():
    return pl.BlockSpec(memory_space=pltpu.VMEM)


def smem_spec():
    return pl.BlockSpec(memory_space=pltpu.SMEM)


def hbm_spec():
    return pl.BlockSpec(memory_space=pltpu.HBM)


def in_hbm(x):
    return pltpu.with_memory_space_constraint(x, pltpu.HBM)


def local_call(body, name, outs, in_specs, out_specs, scratch=(), cost=None):
    return pl.pallas_call(
        body,
        out_shape=outs,
        in_specs=in_specs,
        out_specs=out_specs,
        scratch_shapes=list(scratch),
        compiler_params=pltpu.CompilerParams(vmem_limit_bytes=VMEM_LIMIT),
        cost_estimate=cost,
        name=name,
    )


def from_step(block, axis, step):
    count = lax.axis_size(axis)
    return lax.ppermute(block, axis, [((i + step) % count, i) for i in range(count)])


def from_partner(block, axis, step):
    count = lax.axis_size(axis)
    return lax.ppermute(block, axis, [(i ^ step, i) for i in range(count)])


def from_diagonal(block, axes, sources):
    rows, columns = (lax.axis_size(axis) for axis in axes)
    perm = []
    for row in range(rows):
        for column in range(columns):
            from_row, from_column = sources(row, column)
            perm.append((from_row * columns + from_column, row * columns + column))
    return lax.ppermute(block, axes, perm)


def per_device(eigvecs, links, op_dirs, op_moms, perams, pair_times, slot_counts):
    f32, bf16 = jnp.float32, jnp.bfloat16
    _, cells_x, cells_y, cells_z, colors, _, vectors = eigvecs.shape
    order = cells_z * colors * 2
    lines = cells_x * cells_y
    count_ops = op_dirs.shape[0]
    times, shares, groups = lax.axis_size("ta"), lax.axis_size("gx"), lax.axis_size("gy")
    levels = groups.bit_length() - 1
    own_ops = count_ops // groups
    own_rows = own_ops * 2 * vectors
    field = eigvecs.reshape(cells_x, cells_y, order, vectors)
    halo_x = from_step(field[0:1], "gx", 1)
    halo_y = from_step(field, "gy", 1)
    link_field = links[0].transpose(0, 1, 3, 5, 6, 4, 2).reshape(lines, 27, 2, cells_z)
    outside, inside = halo_fields(cells_x, cells_y), local_fields(cells_x, cells_y)
    inputs = [field, link_field, op_dirs, op_moms, wave_constants(cells_z), pair_times]
    inputs = [in_hbm(x) for x in inputs]
    held = [
        pltpu.SMEM(x.shape, x.dtype) if x.dtype == jnp.int32 else pltpu.VMEM(x.shape, x.dtype)
        for x in inputs
    ]
    matrices, local, left, phases, weights, codes = local_call(
        functools.partial(prepare_kernel, cells_x, cells_y),
        "prepare_lines",
        (
            jax.ShapeDtypeStruct((len(outside), order, order), bf16),
            jax.ShapeDtypeStruct((len(inside), order, vectors), f32),
            jax.ShapeDtypeStruct((2, vectors, lines * order), bf16),
            jax.ShapeDtypeStruct((count_ops, order // 2, 2 * vectors), f32),
            jax.ShapeDtypeStruct((2, times, 8, vectors), f32),
            jax.ShapeDtypeStruct((count_ops, 8, vectors), f32),
        ),
        [hbm_spec()] * len(inputs),
        (vmem_spec(),) * 6,
        held
        + [
            pltpu.VMEM((lines, LINK_COLS, cells_z), f32),
            pltpu.SemaphoreType.DMA((len(inputs),)),
        ],
    )(*inputs)
    message = lambda rows, *lead: jax.ShapeDtypeStruct((*lead, rows + TAIL, vectors), jnp.int16)
    swap, held = local_call(
        functools.partial(margin_kernel, cells_x, cells_y, groups, own_ops),
        "partial_margins",
        (
            message(own_rows, groups // 2),
            jax.ShapeDtypeStruct((groups // 2, own_rows, vectors), f32),
        ),
        [vmem_spec()] * 7,
        (vmem_spec(),) * 2,
        [
            pltpu.VMEM((7, lines, order, vectors), f32),
            pltpu.VMEM((4, vectors, lines * order), bf16),
        ],
    )(matrices, local, left, phases, codes, halo_x, halo_y)

    def in_vmem(body, name, outs, *inputs):
        outs = outs if isinstance(outs, tuple) else (outs,)
        specs = (vmem_spec(),) * len(outs)
        return local_call(body, name, outs, [vmem_spec()] * len(inputs), specs)(*inputs)

    half = own_rows // 2
    messages = [from_partner(swap, "gy", 1)]
    last = levels - 1
    for b in range(1, last):
        body = functools.partial(fold_kernel, b, vectors)
        shape = message(own_rows, groups >> (b + 1))
        (sent,) = in_vmem(body, "fold_groups", shape, held, *messages)
        messages.append(from_partner(sent, "gy", 1 << b))
    body = functools.partial(spread_kernel, last, vectors)
    for_y, for_both, for_x = in_vmem(body, "spread_halves", (message(half),) * 3, held, *messages)
    came = [
        from_partner(for_y, "gy", 1 << last),
        from_diagonal(for_both, ("gx", "gy"), lambda x, y: (x ^ 1, y ^ (1 << last))),
        from_partner(for_x, "gx", 1),
    ]
    body = functools.partial(keep_kernel, vectors)
    (packed,) = in_vmem(body, "keep_half", message(half), held, *messages, *came)
    norm_factor = 1.0 / math.sqrt(3.0 * cells_x * shares * cells_y * groups * cells_z)
    step = 2
    while step < shares:
        arrived = from_partner(packed, "gx", step)
        step *= 2
        last_one = step >= shares
        body = functools.partial(both_kernel, vectors, norm_factor if last_one else None)
        shape = jax.ShapeDtypeStruct((half, vectors), bf16) if last_one else message(half)
        (packed,) = in_vmem(body, "finish_half" if last_one else "sum_both", shape, packed, arrived)
    finished = packed
    kept = [finished] + [from_step(finished, "ta", t) for t in range(1, times)]
    other = [from_partner(finished, "gx", 1)]
    for t in range(1, times):
        source = lambda row, x: ((row + t) % times, x ^ 1)
        other.append(from_diagonal(finished, ("ta", "gx"), source))
    split = own_ops % 2 == 0
    now_ops = own_ops // 2 if split else own_ops
    sums_shape = (2 * now_ops, 32, vectors)
    scratch = [
        pltpu.VMEM((2 * now_ops * vectors, 2 * vectors), bf16),
        pltpu.VMEM((2 * vectors, 2 * now_ops * vectors), bf16),
    ]
    live, sums = local_call(
        functools.partial(first_contract_kernel, times, split),
        "first_contraction",
        (jax.ShapeDtypeStruct((8, vectors), f32), jax.ShapeDtypeStruct(sums_shape, f32)),
        [smem_spec()] + [vmem_spec()] * (2 + times),
        (vmem_spec(),) * 2,
        scratch,
    )(slot_counts, weights, perams[0], *kept)
    margins = local_call(
        margins_kernel,
        "margins_out",
        jax.ShapeDtypeStruct((1, own_rows, vectors), f32),
        [vmem_spec()] * 2,
        vmem_spec(),
    )(*lax.optimization_barrier((kept[0], other[0], sums))[:2])
    correlators = local_call(
        functools.partial(second_contract_kernel, times, split),
        "second_contraction",
        jax.ShapeDtypeStruct((1, own_ops, 2), f32),
        [vmem_spec()] * (4 + 2 * times),
        vmem_spec(),
        [pltpu.VMEM(sums_shape, f32)] + scratch,
    )(weights, perams[0], *other, *kept, live, sums)
    return (margins.reshape(1, own_ops, 2, vectors, vectors), correlators)


def solution(mesh):
    placed = (
        P("ta", "gx", "gy", None, None, None, None),
        P("ta", "gx", "gy", None, None, None, None, None),
        P(),
        P(),
        P(("ta", "gx"), None, None, None),
        P(("ta", "gx"), None),
        P(("ta", "gx")),
    )
    return jax.shard_map(
        per_device,
        mesh=mesh,
        in_specs=placed,
        out_specs=(P("ta", "gy", None, None, None), P(("ta", "gx"), "gy", None)),
        check_vma=False,
    )
```

```python
import functools
import math

import jax
import jax.numpy as jnp
import numpy as np
from jax import lax
from jax.experimental import pallas as pl
from jax.experimental.pallas import tpu as pltpu
from jax.sharding import PartitionSpec as P

VMEM_LIMIT = 24 * 1024 * 1024
MOMENTA = 3
LINK_COLS = 54
TAIL = 16
FIXED_BITS = 14.0


def wave_constants(cells_z):
    z_row = np.arange(3 * cells_z) // 3
    columns = []
    for ahead in range(2):
        for momentum in range(MOMENTA):
            angle = 2.0 * math.pi * momentum * ((z_row + ahead) % cells_z) / cells_z
            columns.append(np.cos(angle))
            columns.append(np.sin(angle))
    left = np.stack(columns, axis=1).astype(np.float32)
    terms = []
    for _ in range(3):
        term = left.astype(jnp.bfloat16).astype(np.float32)
        terms.append(term)
        left = left - term
    return jnp.asarray(np.concatenate(terms, axis=1), jnp.bfloat16)


def iota(shape, axis):
    return lax.broadcasted_iota(jnp.int32, shape, axis)


def third(x):
    return (x * 21846) >> 16


def one_hot(condition):
    return condition.astype(jnp.float32).astype(jnp.bfloat16)


def planar_order(order):
    row, col = iota((order, order), 0), iota((order, order), 1)
    half = order // 2
    source = jnp.where(row < half, 2 * row, 2 * (row - half) + 1)
    return one_hot(col == source)


def side_by_side(planar):
    half = planar.shape[0] // 2
    return jnp.concatenate([planar[:half], planar[half:]], axis=1).astype(jnp.bfloat16)


def transport(matrix, pair, sign):
    half, vectors = matrix.shape[0] // 2, pair.shape[1] // 2
    parts = jnp.dot(matrix, pair, preferred_element_type=jnp.float32)
    real, imag = parts[:half], parts[half:]
    if sign > 0:
        return jnp.concatenate(
            [real[:, :vectors] - imag[:, vectors:], real[:, vectors:] + imag[:, :vectors]], axis=0
        )
    return jnp.concatenate(
        [real[:, :vectors] + imag[:, vectors:], real[:, vectors:] - imag[:, :vectors]], axis=0
    )


def natural_form(matrix, planar):
    half = matrix.shape[0] // 2
    turned = jnp.concatenate([-matrix[half:].astype(jnp.float32), matrix[:half].astype(jnp.float32)])
    whole = jnp.dot(matrix, planar[:half], preferred_element_type=jnp.float32) + jnp.dot(
        turned.astype(jnp.bfloat16), planar[half:], preferred_element_type=jnp.float32
    )
    return whole.astype(jnp.bfloat16)


def halo_fields(cells_x, cells_y):
    pairs = [(0, (cells_x - 1) * cells_y + y) for y in range(cells_y)]
    return pairs + [(1, x * cells_y + cells_y - 1) for x in range(cells_x)]


def local_fields(cells_x, cells_y):
    lines = cells_x * cells_y
    outside = halo_fields(cells_x, cells_y)
    every = [(code, line) for code in range(7) for line in range(lines)]
    return [pair for pair in every if pair not in outside]


def prepare_kernel(cells_x, cells_y, *refs):
    inputs, refs = refs[:6], refs[6:]
    matrix_ref, local_ref, left_ref, phase_ref, weight_ref, code_ref = refs[:6]
    held, link_rows_ref, sems = refs[6:12], refs[12], refs[13]
    copies = [
        pltpu.make_async_copy(src, dst, sems.at[k])
        for k, (src, dst) in enumerate(zip(inputs, held))
    ]
    for copy in copies:
        copy.start()
    v_ref, link_ref, dirs_ref, moms_ref, waves_ref, pair_ref = held
    f32, bf16 = jnp.float32, jnp.bfloat16
    order, vectors = v_ref.shape[2], v_ref.shape[3]
    half, cells_z = order // 2, order // 6
    lines = cells_x * cells_y
    times = weight_ref.shape[1]
    spread = one_hot(third(iota((half, cells_z), 0)) == iota((half, cells_z), 1))
    row, col = iota((half, LINK_COLS), 0), iota((half, LINK_COLS), 1)
    row_color = row - 3 * third(row)
    pair_at = third(col >> 1)
    col_in, col_out = (col >> 1) - 3 * pair_at, pair_at - 3 * third(pair_at)
    pick = [(row_color == col_out).astype(f32), (row_color == col_in).astype(f32)]
    wide = (LINK_COLS, 6 * 128)
    row, col = iota(wide, 0), iota(wide, 1)
    block, place = col >> 7, col & 127
    color = place - 3 * third(place)
    pair_at = third(row >> 1)
    row_in, row_out = (row >> 1) - 3 * pair_at, pair_at - 3 * third(pair_at)
    fits = 2 * third(pair_at) + (row & 1) == block
    expand = [one_hot(fits & (row_in == color)), one_hot(fits & (row_out == color))]
    row, col = iota((half, 128), 0), iota((half, 128), 1)
    near = ((third(row) == third(col)) & (col < half)).astype(f32)
    planar = planar_order(order)
    for copy in copies:
        copy.wait()
    for t in range(times):
        sink = pair_ref[0, 0] == t
        source = pair_ref[0, 1] == t
        weight_ref[0, t] = jnp.full(weight_ref.shape[2:], jnp.where(sink, 1.0, 0.0), f32)
        weight_ref[1, t] = jnp.full(weight_ref.shape[2:], jnp.where(source, 1.0, 0.0), f32)
    for line in range(lines):
        for k in range(LINK_COLS // 2):
            link_rows_ref[line, 2 * k : 2 * k + 2] = link_ref[line, k].astype(f32)
    outside = halo_fields(cells_x, cells_y)
    inside = local_fields(cells_x, cells_y)
    ordered = []
    for line in range(lines):
        here = jnp.dot(
            planar, v_ref[line // cells_y, line % cells_y], preferred_element_type=f32
        )
        ordered.append(here)
        local_ref[inside.index((6, line))] = here
    for line in range(lines):
        here = ordered[line]
        ahead_z = jnp.concatenate(
            [here[3:half], here[:3], here[half + 3 :], here[half : half + 3]], axis=0
        )
        columns = slice(line * order, (line + 1) * order)
        left_ref[0, :, columns] = here.T.astype(bf16)
        left_ref[1, :, columns] = ahead_z.T.astype(bf16)
        seen = lax.dot_general(
            spread,
            link_rows_ref[line].astype(bf16),
            (((1,), (1,)), ((), ())),
            preferred_element_type=f32,
        )
        pair = side_by_side(here)
        for way in range(2):
            blocks = jnp.dot(
                (seen * pick[way]).astype(bf16), expand[way], preferred_element_type=f32
            )
            for d in range(3):
                matrix = jnp.concatenate(
                    [
                        blocks[:, 256 * d : 256 * d + 128] * near,
                        blocks[:, 256 * d + 128 : 256 * d + 256] * near,
                    ],
                    axis=0,
                ).astype(bf16)
                if way == 1:
                    carried = transport(matrix[:, :half], pair, -1)
                    local_ref[inside.index((3 + d, line))] = carried.astype(bf16).astype(f32)
                elif (d, line) in outside:
                    matrix_ref[outside.index((d, line))] = natural_form(matrix[:, :half], planar)
                else:
                    ahead = ahead_z if d == 2 else ordered[line + (cells_y if d == 0 else 1)]
                    local_ref[inside.index((d, line))] = transport(
                        matrix[:, :half], side_by_side(ahead), 1
                    )
    wave_cols = waves_ref.shape[1]
    per_term = wave_cols // 3
    row, col = iota((wave_cols, 2 * vectors), 0), iota((wave_cols, 2 * vectors), 1)
    term = (row >= per_term).astype(jnp.int32) + (row >= 2 * per_term).astype(jnp.int32)
    wave_at = row - per_term * term - (col >= vectors).astype(jnp.int32)
    for o in range(phase_ref.shape[0]):
        code_ref[o] = jnp.full(code_ref.shape[1:], dirs_ref[o], jnp.int32).astype(f32)
        column = 2 * (jnp.where(dirs_ref[o] == 5, MOMENTA, 0) + moms_ref[o])
        phase_ref[o] = jnp.dot(
            waves_ref[...], one_hot(wave_at == column), preferred_element_type=f32
        )


def margin_kernel(cells_x, cells_y, groups, own_ops, *refs):
    matrix_ref, local_ref, left_ref, phase_ref, code_ref, halo_x_ref, halo_y_ref = refs[:7]
    swap_ref, hold_ref, field_ref, side_ref = refs[7:]
    f32, bf16 = jnp.float32, jnp.bfloat16
    me = lax.axis_index("gy")
    codes = {}
    for j in range(groups):
        for i in range(own_ops):
            codes[j, i] = jnp.max(code_ref[(me ^ j) * own_ops + i]).astype(jnp.int32)
    lines = cells_x * cells_y
    order, vectors = halo_x_ref.shape[2], halo_x_ref.shape[3]
    half = order // 2
    planar = planar_order(order)
    side_ref[0] = left_ref[0]
    side_ref[3] = left_ref[1]
    outside = halo_fields(cells_x, cells_y)
    for d in range(2):
        for line in range(lines):
            x, y = line // cells_y, line % cells_y
            columns = slice(line * order, (line + 1) * order)
            if (d, line) not in outside:
                ahead = line + (cells_y if d == 0 else 1)
                side_ref[1 + d, :, columns] = left_ref[0, :, ahead * order : (ahead + 1) * order]
                continue
            halo = halo_x_ref[0, y] if d == 0 else halo_y_ref[x, 0]
            side_ref[1 + d, :, columns] = lax.dot_general(
                halo, planar, (((0,), (1,)), ((), ())), preferred_element_type=f32
            ).astype(bf16)
            matrix = matrix_ref[outside.index((d, line))]
            field_ref[d, line] = jnp.dot(matrix, halo, preferred_element_type=f32)
    for k, (code, line) in enumerate(local_fields(cells_x, cells_y)):
        field_ref[code, line] = local_ref[k]
    for j in sorted(range(groups), key=lambda j: -(j & 1)):
        blocks = []
        for i in range(own_ops):
            o = (me ^ j) * own_ops + i
            code = codes[j, i]
            side = jnp.where((code >= 3) & (code < 6), code - 2, 0)
            cosine = phase_ref[o, :, 0:vectors]
            sine = phase_ref[o, :, vectors : 2 * vectors]
            pairs = []
            for line in range(lines):
                real, imag = field_ref[code, line, 0:half], field_ref[code, line, half:order]
                turned_r, turned_i = cosine * real - sine * imag, sine * real + cosine * imag
                pairs.append(jnp.concatenate([turned_r, turned_i], axis=1))
                pairs.append(jnp.concatenate([turned_i, -turned_r], axis=1))
            pair = jnp.concatenate(pairs, axis=0).astype(bf16)
            product = jnp.dot(side_ref[side], pair, preferred_element_type=f32)
            blocks += [product[:, :vectors], product[:, vectors:]]
        if j & 1:
            put_fixed(swap_ref.at[j >> 1], blocks)
            continue
        for k, block in enumerate(blocks):
            hold_ref[j >> 1, k * vectors : (k + 1) * vectors] = block


def scale_of(block):
    top = jnp.max(jnp.abs(block), axis=0, keepdims=True)
    return jnp.floor(jnp.log2(jnp.maximum(top, 1e-30))) + 1.0


def put_fixed(out_ref, blocks):
    rows, vectors = blocks[0].shape
    tail = iota((TAIL, vectors), 0)
    scales = jnp.zeros((TAIL, vectors), jnp.float32)
    for k, block in enumerate(blocks):
        scale = scale_of(block)
        scales = jnp.where(tail == k, scale, scales)
        fixed = jnp.floor(block * jnp.exp2(FIXED_BITS - scale) + 0.5)
        out_ref[k * rows : (k + 1) * rows] = fixed.astype(jnp.int32).astype(jnp.int16)
    out_ref[len(blocks) * rows :] = scales.astype(jnp.int32).astype(jnp.int16)


def from_fixed(ref, rows, k):
    scales = ref[ref.shape[0] - TAIL :].astype(jnp.int32).astype(jnp.float32)
    block = ref[k * rows : (k + 1) * rows].astype(jnp.int32).astype(jnp.float32)
    return block * jnp.exp2(scales[k : k + 1] - FIXED_BITS)


def group_block(held_ref, messages, j, start, rows):
    total = held_ref[j >> 1, pl.ds(start, rows)]
    for b, ref in enumerate(messages):
        total = total + fixed_at(ref.at[j >> (b + 1)], start, rows)
    return total


def fixed_at(ref, start, rows):
    tail = ref[ref.shape[0] - TAIL :].astype(jnp.int32).astype(jnp.float32)
    scale = jnp.max(
        jnp.where(iota(tail.shape, 0) == start // rows, tail, -1000.0), axis=0, keepdims=True
    )
    block = ref[pl.ds(start, rows)].astype(jnp.int32).astype(jnp.float32)
    return block * jnp.exp2(scale - FIXED_BITS)


def fold_kernel(level, vectors, held_ref, *refs):
    messages, out_ref = refs[:-1], refs[-1]
    for k in range(out_ref.shape[0]):
        blocks = [
            group_block(held_ref, messages, (2 * k + 1) << level, start, vectors)
            for start in range(0, held_ref.shape[1], vectors)
        ]
        put_fixed(out_ref.at[k], blocks)


def half_blocks(held_ref, messages, j, kept, vectors):
    me = lax.axis_index("gx") & 1
    half = held_ref.shape[1] // 2
    base = pl.multiple_of((me if kept else 1 - me) * half, half)
    steps = range(0, half, vectors)
    return [group_block(held_ref, messages, j, base + step, vectors) for step in steps]


def spread_kernel(level, vectors, held_ref, *refs):
    messages, (y_ref, diagonal_ref, x_ref) = refs[:-3], refs[-3:]
    put_fixed(y_ref, half_blocks(held_ref, messages, 1 << level, True, vectors))
    put_fixed(diagonal_ref, half_blocks(held_ref, messages, 1 << level, False, vectors))
    put_fixed(x_ref, half_blocks(held_ref, messages, 0, False, vectors))


def keep_kernel(vectors, held_ref, *refs):
    messages, came, out_ref = refs[:-4], refs[-4:-1], refs[-1]
    blocks = half_blocks(held_ref, messages, 0, True, vectors)
    for p in range(len(blocks)):
        for ref in came:
            blocks[p] = blocks[p] + from_fixed(ref, vectors, p)
    put_fixed(out_ref, blocks)


def both_kernel(vectors, norm_factor, own_ref, arrived_ref, out_ref):
    blocks = [
        from_fixed(own_ref, vectors, p) + from_fixed(arrived_ref, vectors, p)
        for p in range((own_ref.shape[0] - TAIL) // vectors)
    ]
    if norm_factor is None:
        put_fixed(out_ref, blocks)
        return
    for p, block in enumerate(blocks):
        out_ref[p * vectors : (p + 1) * vectors] = (block * norm_factor).astype(out_ref.dtype)


def contract(sums_ref, weight_ref, blocks, tau_ref, left_ref, right_ref):
    f32, bf16 = jnp.float32, jnp.bfloat16
    vectors = sums_ref.shape[2]
    count_ops = sums_ref.shape[0] // 2
    order = tau_ref.shape[2]
    spins = order // vectors
    me_t = lax.axis_index("ta")
    times = len(blocks)

    def chosen(end, k):
        total = jnp.zeros((vectors // 8, 8, vectors), f32)
        for t in range(times):
            weight = weight_ref[end, lax.rem(me_t + t, times)]
            total = total + blocks[t](k).astype(f32).reshape(total.shape) * weight
        return total.reshape(vectors, vectors)

    for o in range(count_ops):
        first = 2 * o * vectors
        a_r, a_i = chosen(0, 2 * o).astype(bf16), chosen(0, 2 * o + 1).astype(bf16)
        b_r, b_i = chosen(1, 2 * o).T.astype(bf16), chosen(1, 2 * o + 1).T.astype(bf16)
        real, imag = slice(first, first + vectors), slice(first + vectors, first + 2 * vectors)
        left_ref[real, 0:vectors] = a_r
        left_ref[real, vectors:] = -a_i
        left_ref[imag, 0:vectors] = a_i
        left_ref[imag, vectors:] = a_r
        right_ref[0:vectors, real] = b_r
        right_ref[0:vectors, imag] = -b_i
        right_ref[vectors:, real] = b_i
        right_ref[vectors:, imag] = b_r
    lanes = sums_ref.shape[1]
    fold = lambda t: jnp.sum(t.reshape(vectors // lanes, lanes, vectors), axis=0)
    sums = [jnp.zeros((lanes, vectors), f32) for _ in range(2 * count_ops)]
    for s in range(spins):
        rows = slice(s * vectors, (s + 1) * vectors)
        x = jnp.dot(
            left_ref[...],
            jnp.concatenate([tau_ref[0, rows], tau_ref[1, rows]], axis=0),
            preferred_element_type=f32,
        )
        for c in range(spins):
            cols = slice(c * vectors, (c + 1) * vectors)
            y = jnp.dot(
                jnp.concatenate([tau_ref[0, rows, cols], tau_ref[1, rows, cols]], axis=1),
                right_ref[...],
                preferred_element_type=f32,
            )
            for o in range(count_ops):
                first = 2 * o * vectors
                x_r = x[first : first + vectors, cols]
                x_i = x[first + vectors : first + 2 * vectors, cols]
                y_r = y[:, first : first + vectors]
                y_i = y[:, first + vectors : first + 2 * vectors]
                sums[2 * o] = sums[2 * o] + fold(x_r * y_r + x_i * y_i)
                sums[2 * o + 1] = sums[2 * o + 1] + fold(x_i * y_r - x_r * y_i)
    for k, total in enumerate(sums):
        sums_ref[k] = total


def part_of(ref, vectors):
    return lambda k: ref[k * vectors : (k + 1) * vectors]


def first_contract_kernel(times, split, live_ref, weight_ref, tau_ref, *refs):
    blocks, (live_out_ref, sums_ref, left_ref, right_ref) = refs[:times], refs[times:]
    live = jnp.where(live_ref[0] > 0, 1.0, 0.0)
    live_out_ref[...] = jnp.full(live_out_ref.shape, live, jnp.float32)
    if split:
        vectors = sums_ref.shape[2]
        blocks = [part_of(ref, vectors) for ref in blocks]
        contract(sums_ref, weight_ref, blocks, tau_ref, left_ref, right_ref)
    else:
        sums_ref[...] = jnp.zeros_like(sums_ref)


def margins_kernel(kept_ref, other_ref, margin_ref):
    half = kept_ref.shape[0]
    me = lax.axis_index("gx") & 1
    for place, ref in ((me, kept_ref), (1 - me, other_ref)):
        rows = pl.ds(pl.multiple_of(place * half, half), half)
        margin_ref[0, rows] = ref[...].astype(jnp.float32)


def second_contract_kernel(times, split, weight_ref, tau_ref, *refs):
    other, kept, refs = refs[:times], refs[times : 2 * times], refs[2 * times :]
    live_ref, first_sums_ref, corr_ref, sums_ref, left_ref, right_ref = refs
    vectors = sums_ref.shape[2]
    half = kept[0].shape[0]
    me = lax.axis_index("gx") & 1
    parts_per_half = half // vectors

    def either(kept_ref, other_ref):
        def part(k):
            row = (k % parts_per_half) * vectors
            own, far = kept_ref[row : row + vectors], other_ref[row : row + vectors]
            mine = (k // parts_per_half == me).astype(jnp.float32)
            return own.astype(jnp.float32) * mine + far.astype(jnp.float32) * (1.0 - mine)

        return part

    blocks = [part_of(ref, vectors) for ref in other]
    if not split:
        blocks = [either(a, b) for a, b in zip(kept, other)]
    contract(sums_ref, weight_ref, blocks, tau_ref, left_ref, right_ref)
    now_ops = sums_ref.shape[0] // 2
    known = [(sums_ref, (1 - me) * now_ops)] if split else [(sums_ref, 0)]
    if split:
        known.append((first_sums_ref, me * now_ops))
    shape = corr_ref.shape[1:]
    row, col = iota(shape, 0), iota(shape, 1)
    result = jnp.zeros(shape, jnp.float32)
    for ref, first in known:
        for k in range(2 * now_ops):
            total = jnp.sum(jnp.sum(ref[k], axis=0, keepdims=True), axis=1, keepdims=True)
            here = (row == first + k // 2) & (col == k % 2)
            result = jnp.where(here, total * (1.0 / vectors), result)
    corr_ref[0] = result * live_ref[0 : shape[0], 0 : shape[1]]


def vmem_spec():
    return pl.BlockSpec(memory_space=pltpu.VMEM)


def smem_spec():
    return pl.BlockSpec(memory_space=pltpu.SMEM)


def hbm_spec():
    return pl.BlockSpec(memory_space=pltpu.HBM)


def in_hbm(x):
    return pltpu.with_memory_space_constraint(x, pltpu.HBM)


def local_call(body, name, outs, in_specs, out_specs, scratch=(), cost=None):
    return pl.pallas_call(
        body,
        out_shape=outs,
        in_specs=in_specs,
        out_specs=out_specs,
        scratch_shapes=list(scratch),
        compiler_params=pltpu.CompilerParams(vmem_limit_bytes=VMEM_LIMIT),
        cost_estimate=cost,
        name=name,
    )


def from_step(block, axis, step):
    count = lax.axis_size(axis)
    return lax.ppermute(block, axis, [((i + step) % count, i) for i in range(count)])


def from_partner(block, axis, step):
    count = lax.axis_size(axis)
    return lax.ppermute(block, axis, [(i ^ step, i) for i in range(count)])


def from_diagonal(block, axes, sources):
    rows, columns = (lax.axis_size(axis) for axis in axes)
    perm = []
    for row in range(rows):
        for column in range(columns):
            from_row, from_column = sources(row, column)
            perm.append((from_row * columns + from_column, row * columns + column))
    return lax.ppermute(block, axes, perm)


def per_device(eigvecs, links, op_dirs, op_moms, perams, pair_times, slot_counts):
    f32, bf16 = jnp.float32, jnp.bfloat16
    _, cells_x, cells_y, cells_z, colors, _, vectors = eigvecs.shape
    order = cells_z * colors * 2
    lines = cells_x * cells_y
    count_ops = op_dirs.shape[0]
    times, shares, groups = lax.axis_size("ta"), lax.axis_size("gx"), lax.axis_size("gy")
    levels = groups.bit_length() - 1
    own_ops = count_ops // groups
    own_rows = own_ops * 2 * vectors
    field = eigvecs.reshape(cells_x, cells_y, order, vectors)
    halo_x = from_step(field[0:1], "gx", 1)
    halo_y = from_step(field, "gy", 1)
    link_field = links[0].transpose(0, 1, 3, 5, 6, 4, 2).reshape(lines, 27, 2, cells_z)
    outside, inside = halo_fields(cells_x, cells_y), local_fields(cells_x, cells_y)
    inputs = [field, link_field, op_dirs, op_moms, wave_constants(cells_z), pair_times]
    inputs = [in_hbm(x) for x in inputs]
    held = [
        pltpu.SMEM(x.shape, x.dtype) if x.dtype == jnp.int32 else pltpu.VMEM(x.shape, x.dtype)
        for x in inputs
    ]
    matrices, local, left, phases, weights, codes = local_call(
        functools.partial(prepare_kernel, cells_x, cells_y),
        "prepare_lines",
        (
            jax.ShapeDtypeStruct((len(outside), order, order), bf16),
            jax.ShapeDtypeStruct((len(inside), order, vectors), f32),
            jax.ShapeDtypeStruct((2, vectors, lines * order), bf16),
            jax.ShapeDtypeStruct((count_ops, order // 2, 2 * vectors), f32),
            jax.ShapeDtypeStruct((2, times, 8, vectors), f32),
            jax.ShapeDtypeStruct((count_ops, 8, vectors), f32),
        ),
        [hbm_spec()] * len(inputs),
        (vmem_spec(),) * 6,
        held
        + [
            pltpu.VMEM((lines, LINK_COLS, cells_z), f32),
            pltpu.SemaphoreType.DMA((len(inputs),)),
        ],
    )(*inputs)
    message = lambda rows, *lead: jax.ShapeDtypeStruct((*lead, rows + TAIL, vectors), jnp.int16)
    swap, held = local_call(
        functools.partial(margin_kernel, cells_x, cells_y, groups, own_ops),
        "partial_margins",
        (
            message(own_rows, groups // 2),
            jax.ShapeDtypeStruct((groups // 2, own_rows, vectors), f32),
        ),
        [vmem_spec()] * 7,
        (vmem_spec(),) * 2,
        [
            pltpu.VMEM((7, lines, order, vectors), f32),
            pltpu.VMEM((4, vectors, lines * order), bf16),
        ],
    )(matrices, local, left, phases, codes, halo_x, halo_y)

    def in_vmem(body, name, outs, *inputs):
        outs = outs if isinstance(outs, tuple) else (outs,)
        specs = (vmem_spec(),) * len(outs)
        return local_call(body, name, outs, [vmem_spec()] * len(inputs), specs)(*inputs)

    half = own_rows // 2
    messages = [from_partner(swap, "gy", 1)]
    last = levels - 1
    for b in range(1, last):
        body = functools.partial(fold_kernel, b, vectors)
        shape = message(own_rows, groups >> (b + 1))
        (sent,) = in_vmem(body, "fold_groups", shape, held, *messages)
        messages.append(from_partner(sent, "gy", 1 << b))
    body = functools.partial(spread_kernel, last, vectors)
    for_y, for_both, for_x = in_vmem(body, "spread_halves", (message(half),) * 3, held, *messages)
    came = [
        from_partner(for_y, "gy", 1 << last),
        from_diagonal(for_both, ("gx", "gy"), lambda x, y: (x ^ 1, y ^ (1 << last))),
        from_partner(for_x, "gx", 1),
    ]
    body = functools.partial(keep_kernel, vectors)
    (packed,) = in_vmem(body, "keep_half", message(half), held, *messages, *came)
    norm_factor = 1.0 / math.sqrt(3.0 * cells_x * shares * cells_y * groups * cells_z)
    step = 2
    while step < shares:
        arrived = from_partner(packed, "gx", step)
        step *= 2
        last_one = step >= shares
        body = functools.partial(both_kernel, vectors, norm_factor if last_one else None)
        shape = jax.ShapeDtypeStruct((half, vectors), bf16) if last_one else message(half)
        (packed,) = in_vmem(body, "finish_half" if last_one else "sum_both", shape, packed, arrived)
    finished = packed
    kept = [finished] + [from_step(finished, "ta", t) for t in range(1, times)]
    other = [from_partner(finished, "gx", 1)]
    for t in range(1, times):
        source = lambda row, x: ((row + t) % times, x ^ 1)
        other.append(from_diagonal(finished, ("ta", "gx"), source))
    split = own_ops % 2 == 0
    now_ops = own_ops // 2 if split else own_ops
    sums_shape = (2 * now_ops, 32, vectors)
    scratch = [
        pltpu.VMEM((2 * now_ops * vectors, 2 * vectors), bf16),
        pltpu.VMEM((2 * vectors, 2 * now_ops * vectors), bf16),
    ]
    live, sums = local_call(
        functools.partial(first_contract_kernel, times, split),
        "first_contraction",
        (jax.ShapeDtypeStruct((8, vectors), f32), jax.ShapeDtypeStruct(sums_shape, f32)),
        [smem_spec()] + [vmem_spec()] * (2 + times),
        (vmem_spec(),) * 2,
        scratch,
    )(slot_counts, weights, perams[0], *kept)
    margins = local_call(
        margins_kernel,
        "margins_out",
        jax.ShapeDtypeStruct((1, own_rows, vectors), f32),
        [vmem_spec()] * 2,
        vmem_spec(),
    )(*lax.optimization_barrier((kept[0], other[0], sums))[:2])
    correlators = local_call(
        functools.partial(second_contract_kernel, times, split),
        "second_contraction",
        jax.ShapeDtypeStruct((1, own_ops, 2), f32),
        [vmem_spec()] * (4 + 2 * times),
        vmem_spec(),
        [pltpu.VMEM(sums_shape, f32)] + scratch,
    )(weights, perams[0], *other, *kept, live, sums)
    return (margins.reshape(1, own_ops, 2, vectors, vectors), correlators)


def solution(mesh):
    placed = (
        P("ta", "gx", "gy", None, None, None, None),
        P("ta", "gx", "gy", None, None, None, None, None),
        P(),
        P(),
        P(("ta", "gx"), None, None, None),
        P(("ta", "gx"), None),
        P(("ta", "gx")),
    )
    return jax.shard_map(
        per_device,
        mesh=mesh,
        in_specs=placed,
        out_specs=(P("ta", "gy", None, None, None), P(("ta", "gx"), "gy", None)),
        check_vma=False,
    )
```

```python
import functools
import math

import jax
import jax.numpy as jnp
import numpy as np
from jax import lax
from jax.experimental import pallas as pl
from jax.experimental.pallas import tpu as pltpu
from jax.sharding import PartitionSpec as P

VMEM_LIMIT = 24 * 1024 * 1024
MOMENTA = 3
LINK_COLS = 54
TAIL = 16
FIXED_BITS = 14.0


def wave_constants(cells_z):
    z_row = np.arange(3 * cells_z) // 3
    columns = []
    for ahead in range(2):
        for momentum in range(MOMENTA):
            angle = 2.0 * math.pi * momentum * ((z_row + ahead) % cells_z) / cells_z
            columns.append(np.cos(angle))
            columns.append(np.sin(angle))
    left = np.stack(columns, axis=1).astype(np.float32)
    terms = []
    for _ in range(3):
        term = left.astype(jnp.bfloat16).astype(np.float32)
        terms.append(term)
        left = left - term
    return jnp.asarray(np.concatenate(terms, axis=1), jnp.bfloat16)


def iota(shape, axis):
    return lax.broadcasted_iota(jnp.int32, shape, axis)


def third(x):
    return (x * 21846) >> 16


def one_hot(condition):
    return condition.astype(jnp.float32).astype(jnp.bfloat16)


def planar_order(order, ahead=0):
    row, col = iota((order, order), 0), iota((order, order), 1)
    half = order // 2
    part = (row >= half).astype(jnp.int32)
    site = row - part * half + ahead
    source = 2 * jnp.where(site >= half, site - half, site) + part
    return one_hot(col == source)


def side_by_side(planar):
    half = planar.shape[0] // 2
    return jnp.concatenate([planar[:half], planar[half:]], axis=1).astype(jnp.bfloat16)


def transport(matrix, pair, sign):
    half, vectors = matrix.shape[0] // 2, pair.shape[1] // 2
    parts = jnp.dot(matrix, pair, preferred_element_type=jnp.float32)
    real, imag = parts[:half], parts[half:]
    if sign > 0:
        return jnp.concatenate(
            [real[:, :vectors] - imag[:, vectors:], real[:, vectors:] + imag[:, :vectors]], axis=0
        )
    return jnp.concatenate(
        [real[:, :vectors] + imag[:, vectors:], real[:, vectors:] - imag[:, :vectors]], axis=0
    )


def natural_form(matrix, planar):
    half = matrix.shape[0] // 2
    turned = jnp.concatenate([-matrix[half:].astype(jnp.float32), matrix[:half].astype(jnp.float32)])
    whole = jnp.dot(matrix, planar[:half], preferred_element_type=jnp.float32) + jnp.dot(
        turned.astype(jnp.bfloat16), planar[half:], preferred_element_type=jnp.float32
    )
    return whole.astype(jnp.bfloat16)


def halo_fields(cells_x, cells_y):
    pairs = [(0, (cells_x - 1) * cells_y + y) for y in range(cells_y)]
    return pairs + [(1, x * cells_y + cells_y - 1) for x in range(cells_x)]


def local_fields(cells_x, cells_y):
    lines = cells_x * cells_y
    outside = halo_fields(cells_x, cells_y)
    every = [(code, line) for code in range(7) for line in range(lines)]
    return [pair for pair in every if pair not in outside]


def prepare_kernel(cells_x, cells_y, *refs):
    inputs, refs = refs[:6], refs[6:]
    matrix_ref, local_ref, left_ref, phase_ref, weight_ref, code_ref = refs[:6]
    held, link_rows_ref, sems = refs[6:12], refs[12], refs[13]
    copies = [
        pltpu.make_async_copy(src, dst, sems.at[k])
        for k, (src, dst) in enumerate(zip(inputs, held))
    ]
    for copy in copies:
        copy.start()
    v_ref, link_ref, dirs_ref, moms_ref, waves_ref, pair_ref = held
    f32, bf16 = jnp.float32, jnp.bfloat16
    order, vectors = v_ref.shape[2], v_ref.shape[3]
    half, cells_z = order // 2, order // 6
    lines = cells_x * cells_y
    times = weight_ref.shape[1]
    spread = one_hot(third(iota((half, cells_z), 0)) == iota((half, cells_z), 1))
    row, col = iota((half, LINK_COLS), 0), iota((half, LINK_COLS), 1)
    row_color = row - 3 * third(row)
    pair_at = third(col >> 1)
    col_in, col_out = (col >> 1) - 3 * pair_at, pair_at - 3 * third(pair_at)
    pick = [(row_color == col_out).astype(f32), (row_color == col_in).astype(f32)]
    wide = (LINK_COLS, 6 * 128)
    row, col = iota(wide, 0), iota(wide, 1)
    block, place = col >> 7, col & 127
    color = place - 3 * third(place)
    pair_at = third(row >> 1)
    row_in, row_out = (row >> 1) - 3 * pair_at, pair_at - 3 * third(pair_at)
    fits = 2 * third(pair_at) + (row & 1) == block
    expand = [one_hot(fits & (row_in == color)), one_hot(fits & (row_out == color))]
    row, col = iota((half, 128), 0), iota((half, 128), 1)
    near = ((third(row) == third(col)) & (col < half)).astype(f32)
    planar = planar_order(order)
    planar_ahead = planar_order(order, 3)
    for copy in copies:
        copy.wait()
    for t in range(times):
        sink = pair_ref[0, 0] == t
        source = pair_ref[0, 1] == t
        weight_ref[0, t] = jnp.full(weight_ref.shape[2:], jnp.where(sink, 1.0, 0.0), f32)
        weight_ref[1, t] = jnp.full(weight_ref.shape[2:], jnp.where(source, 1.0, 0.0), f32)
    for line in range(lines):
        for k in range(LINK_COLS // 2):
            link_rows_ref[line, 2 * k : 2 * k + 2] = link_ref[line, k].astype(f32)
    outside = halo_fields(cells_x, cells_y)
    inside = local_fields(cells_x, cells_y)
    ordered = []
    for line in range(lines):
        here = jnp.dot(
            planar, v_ref[line // cells_y, line % cells_y], preferred_element_type=f32
        )
        ordered.append(here)
        local_ref[inside.index((6, line))] = here
    for line in range(lines):
        here = ordered[line]
        ahead_z = jnp.concatenate(
            [here[3:half], here[:3], here[half + 3 :], here[half : half + 3]], axis=0
        )
        columns = slice(line * order, (line + 1) * order)
        for k, reordering in enumerate((planar, planar_ahead)):
            left_ref[k, :, columns] = lax.dot_general(
                v_ref[line // cells_y, line % cells_y],
                reordering,
                (((0,), (1,)), ((), ())),
                preferred_element_type=f32,
            ).astype(bf16)
        seen = lax.dot_general(
            spread,
            link_rows_ref[line].astype(bf16),
            (((1,), (1,)), ((), ())),
            preferred_element_type=f32,
        )
        pair = side_by_side(here)
        for way in range(2):
            blocks = jnp.dot(
                (seen * pick[way]).astype(bf16), expand[way], preferred_element_type=f32
            )
            for d in range(3):
                matrix = jnp.concatenate(
                    [
                        blocks[:, 256 * d : 256 * d + 128] * near,
                        blocks[:, 256 * d + 128 : 256 * d + 256] * near,
                    ],
                    axis=0,
                ).astype(bf16)
                if way == 1:
                    carried = transport(matrix[:, :half], pair, -1)
                    local_ref[inside.index((3 + d, line))] = carried.astype(bf16).astype(f32)
                elif (d, line) in outside:
                    matrix_ref[outside.index((d, line))] = natural_form(matrix[:, :half], planar)
                else:
                    ahead = ahead_z if d == 2 else ordered[line + (cells_y if d == 0 else 1)]
                    local_ref[inside.index((d, line))] = transport(
                        matrix[:, :half], side_by_side(ahead), 1
                    )
    wave_cols = waves_ref.shape[1]
    per_term = wave_cols // 3
    row, col = iota((wave_cols, 2 * vectors), 0), iota((wave_cols, 2 * vectors), 1)
    term = (row >= per_term).astype(jnp.int32) + (row >= 2 * per_term).astype(jnp.int32)
    wave_at = row - per_term * term - (col >= vectors).astype(jnp.int32)
    for o in range(phase_ref.shape[0]):
        code_ref[o] = jnp.full(code_ref.shape[1:], dirs_ref[o], jnp.int32).astype(f32)
        column = 2 * (jnp.where(dirs_ref[o] == 5, MOMENTA, 0) + moms_ref[o])
        phase_ref[o] = jnp.dot(
            waves_ref[...], one_hot(wave_at == column), preferred_element_type=f32
        )


def margin_kernel(cells_x, cells_y, groups, own_ops, *refs):
    matrix_ref, local_ref, left_ref, phase_ref, code_ref, halo_x_ref, halo_y_ref = refs[:7]
    swap_ref, hold_ref, field_ref, side_ref = refs[7:]
    f32, bf16 = jnp.float32, jnp.bfloat16
    me = lax.axis_index("gy")
    codes = {}
    for j in range(groups):
        for i in range(own_ops):
            codes[j, i] = jnp.max(code_ref[(me ^ j) * own_ops + i]).astype(jnp.int32)
    lines = cells_x * cells_y
    order, vectors = halo_x_ref.shape[2], halo_x_ref.shape[3]
    half = order // 2
    planar = planar_order(order)
    side_ref[0] = left_ref[0]
    side_ref[3] = left_ref[1]
    outside = halo_fields(cells_x, cells_y)
    for d in range(2):
        for line in range(lines):
            x, y = line // cells_y, line % cells_y
            columns = slice(line * order, (line + 1) * order)
            if (d, line) not in outside:
                ahead = line + (cells_y if d == 0 else 1)
                side_ref[1 + d, :, columns] = left_ref[0, :, ahead * order : (ahead + 1) * order]
                continue
            halo = halo_x_ref[0, y] if d == 0 else halo_y_ref[x, 0]
            side_ref[1 + d, :, columns] = lax.dot_general(
                halo, planar, (((0,), (1,)), ((), ())), preferred_element_type=f32
            ).astype(bf16)
            matrix = matrix_ref[outside.index((d, line))]
            field_ref[d, line] = jnp.dot(matrix, halo, preferred_element_type=f32)
    for k, (code, line) in enumerate(local_fields(cells_x, cells_y)):
        field_ref[code, line] = local_ref[k]
    for j in sorted(range(groups), key=lambda j: -(j & 1)):
        blocks = []
        for i in range(own_ops):
            o = (me ^ j) * own_ops + i
            code = codes[j, i]
            side = jnp.where((code >= 3) & (code < 6), code - 2, 0)
            cosine = phase_ref[o, :, 0:vectors]
            sine = phase_ref[o, :, vectors : 2 * vectors]
            pairs = []
            for line in range(lines):
                real, imag = field_ref[code, line, 0:half], field_ref[code, line, half:order]
                turned_r, turned_i = cosine * real - sine * imag, sine * real + cosine * imag
                pairs.append(jnp.concatenate([turned_r, turned_i], axis=1))
                pairs.append(jnp.concatenate([turned_i, -turned_r], axis=1))
            pair = jnp.concatenate(pairs, axis=0).astype(bf16)
            product = jnp.dot(side_ref[side], pair, preferred_element_type=f32)
            blocks += [product[:, :vectors], product[:, vectors:]]
        if j & 1:
            put_fixed(swap_ref.at[j >> 1], blocks)
            continue
        for k, block in enumerate(blocks):
            hold_ref[j >> 1, k * vectors : (k + 1) * vectors] = block


def scale_of(block):
    top = jnp.max(jnp.abs(block), axis=0, keepdims=True)
    return jnp.floor(jnp.log2(jnp.maximum(top, 1e-30))) + 1.0


def put_fixed(out_ref, blocks):
    rows, vectors = blocks[0].shape
    tail = iota((TAIL, vectors), 0)
    scales = jnp.zeros((TAIL, vectors), jnp.float32)
    for k, block in enumerate(blocks):
        scale = scale_of(block)
        scales = jnp.where(tail == k, scale, scales)
        fixed = jnp.floor(block * jnp.exp2(FIXED_BITS - scale) + 0.5)
        out_ref[k * rows : (k + 1) * rows] = fixed.astype(jnp.int32).astype(jnp.int16)
    out_ref[len(blocks) * rows :] = scales.astype(jnp.int32).astype(jnp.int16)


def from_fixed(ref, rows, k):
    scales = ref[ref.shape[0] - TAIL :].astype(jnp.int32).astype(jnp.float32)
    block = ref[k * rows : (k + 1) * rows].astype(jnp.int32).astype(jnp.float32)
    return block * jnp.exp2(scales[k : k + 1] - FIXED_BITS)


def group_block(held_ref, messages, j, start, rows):
    total = held_ref[j >> 1, pl.ds(start, rows)]
    for b, ref in enumerate(messages):
        total = total + fixed_at(ref.at[j >> (b + 1)], start, rows)
    return total


def fixed_at(ref, start, rows):
    tail = ref[ref.shape[0] - TAIL :].astype(jnp.int32).astype(jnp.float32)
    scale = jnp.max(
        jnp.where(iota(tail.shape, 0) == start // rows, tail, -1000.0), axis=0, keepdims=True
    )
    block = ref[pl.ds(start, rows)].astype(jnp.int32).astype(jnp.float32)
    return block * jnp.exp2(scale - FIXED_BITS)


def fold_kernel(level, vectors, held_ref, *refs):
    messages, out_ref = refs[:-1], refs[-1]
    for k in range(out_ref.shape[0]):
        blocks = [
            group_block(held_ref, messages, (2 * k + 1) << level, start, vectors)
            for start in range(0, held_ref.shape[1], vectors)
        ]
        put_fixed(out_ref.at[k], blocks)


def half_blocks(held_ref, messages, j, kept, vectors):
    me = lax.axis_index("gx") & 1
    half = held_ref.shape[1] // 2
    base = pl.multiple_of((me if kept else 1 - me) * half, half)
    steps = range(0, half, vectors)
    return [group_block(held_ref, messages, j, base + step, vectors) for step in steps]


def spread_kernel(level, vectors, held_ref, *refs):
    messages, (y_ref, diagonal_ref, x_ref) = refs[:-3], refs[-3:]
    put_fixed(y_ref, half_blocks(held_ref, messages, 1 << level, True, vectors))
    put_fixed(diagonal_ref, half_blocks(held_ref, messages, 1 << level, False, vectors))
    put_fixed(x_ref, half_blocks(held_ref, messages, 0, False, vectors))


def keep_kernel(vectors, held_ref, *refs):
    messages, came, out_ref = refs[:-4], refs[-4:-1], refs[-1]
    blocks = half_blocks(held_ref, messages, 0, True, vectors)
    for p in range(len(blocks)):
        for ref in came:
            blocks[p] = blocks[p] + from_fixed(ref, vectors, p)
    put_fixed(out_ref, blocks)


def both_kernel(vectors, norm_factor, own_ref, arrived_ref, out_ref):
    blocks = [
        from_fixed(own_ref, vectors, p) + from_fixed(arrived_ref, vectors, p)
        for p in range((own_ref.shape[0] - TAIL) // vectors)
    ]
    if norm_factor is None:
        put_fixed(out_ref, blocks)
        return
    for p, block in enumerate(blocks):
        out_ref[p * vectors : (p + 1) * vectors] = (block * norm_factor).astype(out_ref.dtype)


def contract(sums_ref, weight_ref, blocks, tau_ref, left_ref, right_ref):
    f32, bf16 = jnp.float32, jnp.bfloat16
    vectors = sums_ref.shape[2]
    count_ops = sums_ref.shape[0] // 2
    order = tau_ref.shape[2]
    spins = order // vectors
    me_t = lax.axis_index("ta")
    times = len(blocks)

    def chosen(end, k):
        total = jnp.zeros((vectors // 8, 8, vectors), f32)
        for t in range(times):
            weight = weight_ref[end, lax.rem(me_t + t, times)]
            total = total + blocks[t](k).astype(f32).reshape(total.shape) * weight
        return total.reshape(vectors, vectors)

    for o in range(count_ops):
        first = 2 * o * vectors
        a_r, a_i = chosen(0, 2 * o).astype(bf16), chosen(0, 2 * o + 1).astype(bf16)
        b_r, b_i = chosen(1, 2 * o).T.astype(bf16), chosen(1, 2 * o + 1).T.astype(bf16)
        real, imag = slice(first, first + vectors), slice(first + vectors, first + 2 * vectors)
        left_ref[real, 0:vectors] = a_r
        left_ref[real, vectors:] = -a_i
        left_ref[imag, 0:vectors] = a_i
        left_ref[imag, vectors:] = a_r
        right_ref[0:vectors, real] = b_r
        right_ref[0:vectors, imag] = -b_i
        right_ref[vectors:, real] = b_i
        right_ref[vectors:, imag] = b_r
    lanes = sums_ref.shape[1]
    fold = lambda t: jnp.sum(t.reshape(vectors // lanes, lanes, vectors), axis=0)
    sums = [jnp.zeros((lanes, vectors), f32) for _ in range(2 * count_ops)]
    for s in range(spins):
        rows = slice(s * vectors, (s + 1) * vectors)
        x = jnp.dot(
            left_ref[...],
            jnp.concatenate([tau_ref[0, rows], tau_ref[1, rows]], axis=0),
            preferred_element_type=f32,
        )
        for c in range(spins):
            cols = slice(c * vectors, (c + 1) * vectors)
            y = jnp.dot(
                jnp.concatenate([tau_ref[0, rows, cols], tau_ref[1, rows, cols]], axis=1),
                right_ref[...],
                preferred_element_type=f32,
            )
            for o in range(count_ops):
                first = 2 * o * vectors
                x_r = x[first : first + vectors, cols]
                x_i = x[first + vectors : first + 2 * vectors, cols]
                y_r = y[:, first : first + vectors]
                y_i = y[:, first + vectors : first + 2 * vectors]
                sums[2 * o] = sums[2 * o] + fold(x_r * y_r + x_i * y_i)
                sums[2 * o + 1] = sums[2 * o + 1] + fold(x_i * y_r - x_r * y_i)
    for k, total in enumerate(sums):
        sums_ref[k] = total


def part_of(ref, vectors):
    return lambda k: ref[k * vectors : (k + 1) * vectors]


def first_contract_kernel(times, split, live_ref, weight_ref, tau_ref, *refs):
    blocks, (live_out_ref, sums_ref, left_ref, right_ref) = refs[:times], refs[times:]
    live = jnp.where(live_ref[0] > 0, 1.0, 0.0)
    live_out_ref[...] = jnp.full(live_out_ref.shape, live, jnp.float32)
    if split:
        vectors = sums_ref.shape[2]
        blocks = [part_of(ref, vectors) for ref in blocks]
        contract(sums_ref, weight_ref, blocks, tau_ref, left_ref, right_ref)
    else:
        sums_ref[...] = jnp.zeros_like(sums_ref)


def margins_kernel(kept_ref, other_ref, margin_ref):
    half = kept_ref.shape[0]
    me = lax.axis_index("gx") & 1
    for place, ref in ((me, kept_ref), (1 - me, other_ref)):
        rows = pl.ds(pl.multiple_of(place * half, half), half)
        margin_ref[0, rows] = ref[...].astype(jnp.float32)


def second_contract_kernel(times, split, weight_ref, tau_ref, *refs):
    other, kept, refs = refs[:times], refs[times : 2 * times], refs[2 * times :]
    live_ref, first_sums_ref, corr_ref, sums_ref, left_ref, right_ref = refs
    vectors = sums_ref.shape[2]
    half = kept[0].shape[0]
    me = lax.axis_index("gx") & 1
    parts_per_half = half // vectors

    def either(kept_ref, other_ref):
        def part(k):
            row = (k % parts_per_half) * vectors
            own, far = kept_ref[row : row + vectors], other_ref[row : row + vectors]
            mine = (k // parts_per_half == me).astype(jnp.float32)
            return own.astype(jnp.float32) * mine + far.astype(jnp.float32) * (1.0 - mine)

        return part

    blocks = [part_of(ref, vectors) for ref in other]
    if not split:
        blocks = [either(a, b) for a, b in zip(kept, other)]
    contract(sums_ref, weight_ref, blocks, tau_ref, left_ref, right_ref)
    now_ops = sums_ref.shape[0] // 2
    known = [(sums_ref, (1 - me) * now_ops)] if split else [(sums_ref, 0)]
    if split:
        known.append((first_sums_ref, me * now_ops))
    shape = corr_ref.shape[1:]
    row, col = iota(shape, 0), iota(shape, 1)
    result = jnp.zeros(shape, jnp.float32)
    for ref, first in known:
        for k in range(2 * now_ops):
            total = jnp.sum(jnp.sum(ref[k], axis=0, keepdims=True), axis=1, keepdims=True)
            here = (row == first + k // 2) & (col == k % 2)
            result = jnp.where(here, total * (1.0 / vectors), result)
    corr_ref[0] = result * live_ref[0 : shape[0], 0 : shape[1]]


def vmem_spec():
    return pl.BlockSpec(memory_space=pltpu.VMEM)


def smem_spec():
    return pl.BlockSpec(memory_space=pltpu.SMEM)


def hbm_spec():
    return pl.BlockSpec(memory_space=pltpu.HBM)


def in_hbm(x):
    return pltpu.with_memory_space_constraint(x, pltpu.HBM)


def local_call(body, name, outs, in_specs, out_specs, scratch=(), cost=None):
    return pl.pallas_call(
        body,
        out_shape=outs,
        in_specs=in_specs,
        out_specs=out_specs,
        scratch_shapes=list(scratch),
        compiler_params=pltpu.CompilerParams(vmem_limit_bytes=VMEM_LIMIT),
        cost_estimate=cost,
        name=name,
    )


def from_step(block, axis, step):
    count = lax.axis_size(axis)
    return lax.ppermute(block, axis, [((i + step) % count, i) for i in range(count)])


def from_partner(block, axis, step):
    count = lax.axis_size(axis)
    return lax.ppermute(block, axis, [(i ^ step, i) for i in range(count)])


def from_diagonal(block, axes, sources):
    rows, columns = (lax.axis_size(axis) for axis in axes)
    perm = []
    for row in range(rows):
        for column in range(columns):
            from_row, from_column = sources(row, column)
            perm.append((from_row * columns + from_column, row * columns + column))
    return lax.ppermute(block, axes, perm)


def per_device(eigvecs, links, op_dirs, op_moms, perams, pair_times, slot_counts):
    f32, bf16 = jnp.float32, jnp.bfloat16
    _, cells_x, cells_y, cells_z, colors, _, vectors = eigvecs.shape
    order = cells_z * colors * 2
    lines = cells_x * cells_y
    count_ops = op_dirs.shape[0]
    times, shares, groups = lax.axis_size("ta"), lax.axis_size("gx"), lax.axis_size("gy")
    levels = groups.bit_length() - 1
    own_ops = count_ops // groups
    own_rows = own_ops * 2 * vectors
    field = eigvecs.reshape(cells_x, cells_y, order, vectors)
    halo_x = from_step(field[0:1], "gx", 1)
    halo_y = from_step(field, "gy", 1)
    link_field = links[0].transpose(0, 1, 3, 5, 6, 4, 2).reshape(lines, 27, 2, cells_z)
    outside, inside = halo_fields(cells_x, cells_y), local_fields(cells_x, cells_y)
    inputs = [field, link_field, op_dirs, op_moms, wave_constants(cells_z), pair_times]
    inputs = [in_hbm(x) for x in inputs]
    held = [
        pltpu.SMEM(x.shape, x.dtype) if x.dtype == jnp.int32 else pltpu.VMEM(x.shape, x.dtype)
        for x in inputs
    ]
    matrices, local, left, phases, weights, codes = local_call(
        functools.partial(prepare_kernel, cells_x, cells_y),
        "prepare_lines",
        (
            jax.ShapeDtypeStruct((len(outside), order, order), bf16),
            jax.ShapeDtypeStruct((len(inside), order, vectors), f32),
            jax.ShapeDtypeStruct((2, vectors, lines * order), bf16),
            jax.ShapeDtypeStruct((count_ops, order // 2, 2 * vectors), f32),
            jax.ShapeDtypeStruct((2, times, 8, vectors), f32),
            jax.ShapeDtypeStruct((count_ops, 8, vectors), f32),
        ),
        [hbm_spec()] * len(inputs),
        (vmem_spec(),) * 6,
        held
        + [
            pltpu.VMEM((lines, LINK_COLS, cells_z), f32),
            pltpu.SemaphoreType.DMA((len(inputs),)),
        ],
    )(*inputs)
    message = lambda rows, *lead: jax.ShapeDtypeStruct((*lead, rows + TAIL, vectors), jnp.int16)
    swap, held = local_call(
        functools.partial(margin_kernel, cells_x, cells_y, groups, own_ops),
        "partial_margins",
        (
            message(own_rows, groups // 2),
            jax.ShapeDtypeStruct((groups // 2, own_rows, vectors), f32),
        ),
        [vmem_spec()] * 7,
        (vmem_spec(),) * 2,
        [
            pltpu.VMEM((7, lines, order, vectors), f32),
            pltpu.VMEM((4, vectors, lines * order), bf16),
        ],
    )(matrices, local, left, phases, codes, halo_x, halo_y)

    def in_vmem(body, name, outs, *inputs):
        outs = outs if isinstance(outs, tuple) else (outs,)
        specs = (vmem_spec(),) * len(outs)
        return local_call(body, name, outs, [vmem_spec()] * len(inputs), specs)(*inputs)

    half = own_rows // 2
    messages = [from_partner(swap, "gy", 1)]
    last = levels - 1
    for b in range(1, last):
        body = functools.partial(fold_kernel, b, vectors)
        shape = message(own_rows, groups >> (b + 1))
        (sent,) = in_vmem(body, "fold_groups", shape, held, *messages)
        messages.append(from_partner(sent, "gy", 1 << b))
    body = functools.partial(spread_kernel, last, vectors)
    for_y, for_both, for_x = in_vmem(body, "spread_halves", (message(half),) * 3, held, *messages)
    came = [
        from_partner(for_y, "gy", 1 << last),
        from_diagonal(for_both, ("gx", "gy"), lambda x, y: (x ^ 1, y ^ (1 << last))),
        from_partner(for_x, "gx", 1),
    ]
    body = functools.partial(keep_kernel, vectors)
    (packed,) = in_vmem(body, "keep_half", message(half), held, *messages, *came)
    norm_factor = 1.0 / math.sqrt(3.0 * cells_x * shares * cells_y * groups * cells_z)
    step = 2
    while step < shares:
        arrived = from_partner(packed, "gx", step)
        step *= 2
        last_one = step >= shares
        body = functools.partial(both_kernel, vectors, norm_factor if last_one else None)
        shape = jax.ShapeDtypeStruct((half, vectors), bf16) if last_one else message(half)
        (packed,) = in_vmem(body, "finish_half" if last_one else "sum_both", shape, packed, arrived)
    finished = packed
    kept = [finished] + [from_step(finished, "ta", t) for t in range(1, times)]
    other = [from_partner(finished, "gx", 1)]
    for t in range(1, times):
        source = lambda row, x: ((row + t) % times, x ^ 1)
        other.append(from_diagonal(finished, ("ta", "gx"), source))
    split = own_ops % 2 == 0
    now_ops = own_ops // 2 if split else own_ops
    sums_shape = (2 * now_ops, 32, vectors)
    scratch = [
        pltpu.VMEM((2 * now_ops * vectors, 2 * vectors), bf16),
        pltpu.VMEM((2 * vectors, 2 * now_ops * vectors), bf16),
    ]
    live, sums = local_call(
        functools.partial(first_contract_kernel, times, split),
        "first_contraction",
        (jax.ShapeDtypeStruct((8, vectors), f32), jax.ShapeDtypeStruct(sums_shape, f32)),
        [smem_spec()] + [vmem_spec()] * (2 + times),
        (vmem_spec(),) * 2,
        scratch,
    )(slot_counts, weights, perams[0], *kept)
    margins = local_call(
        margins_kernel,
        "margins_out",
        jax.ShapeDtypeStruct((1, own_rows, vectors), f32),
        [vmem_spec()] * 2,
        vmem_spec(),
    )(*lax.optimization_barrier((kept[0], other[0], sums))[:2])
    correlators = local_call(
        functools.partial(second_contract_kernel, times, split),
        "second_contraction",
        jax.ShapeDtypeStruct((1, own_ops, 2), f32),
        [vmem_spec()] * (4 + 2 * times),
        vmem_spec(),
        [pltpu.VMEM(sums_shape, f32)] + scratch,
    )(weights, perams[0], *other, *kept, live, sums)
    return (margins.reshape(1, own_ops, 2, vectors, vectors), correlators)


def solution(mesh):
    placed = (
        P("ta", "gx", "gy", None, None, None, None),
        P("ta", "gx", "gy", None, None, None, None, None),
        P(),
        P(),
        P(("ta", "gx"), None, None, None),
        P(("ta", "gx"), None),
        P(("ta", "gx")),
    )
    return jax.shard_map(
        per_device,
        mesh=mesh,
        in_specs=placed,
        out_specs=(P("ta", "gy", None, None, None), P(("ta", "gx"), "gy", None)),
        check_vma=False,
    )
```

```python
import functools
import math

import jax
import jax.numpy as jnp
import numpy as np
from jax import lax
from jax.experimental import pallas as pl
from jax.experimental.pallas import tpu as pltpu
from jax.sharding import PartitionSpec as P

VMEM_LIMIT = 24 * 1024 * 1024
MOMENTA = 3
LINK_COLS = 54
TAIL = 16
FIXED_BITS = 14.0


def wave_constants(cells_z):
    z_row = np.arange(3 * cells_z) // 3
    columns = []
    for ahead in range(2):
        for momentum in range(MOMENTA):
            angle = 2.0 * math.pi * momentum * ((z_row + ahead) % cells_z) / cells_z
            columns.append(np.cos(angle))
            columns.append(np.sin(angle))
    left = np.stack(columns, axis=1).astype(np.float32)
    terms = []
    for _ in range(3):
        term = left.astype(jnp.bfloat16).astype(np.float32)
        terms.append(term)
        left = left - term
    return jnp.asarray(np.concatenate(terms, axis=1), jnp.bfloat16)


def iota(shape, axis):
    return lax.broadcasted_iota(jnp.int32, shape, axis)


def third(x):
    return (x * 21846) >> 16


def one_hot(condition):
    return condition.astype(jnp.float32).astype(jnp.bfloat16)


def planar_order(order, ahead=0):
    row, col = iota((order, order), 0), iota((order, order), 1)
    half = order // 2
    part = (row >= half).astype(jnp.int32)
    site = row - part * half + ahead
    source = 2 * jnp.where(site >= half, site - half, site) + part
    return one_hot(col == source)


def side_by_side(planar):
    half = planar.shape[0] // 2
    return jnp.concatenate([planar[:half], planar[half:]], axis=1).astype(jnp.bfloat16)


def transport(matrix, pair, sign):
    half, vectors = matrix.shape[0] // 2, pair.shape[1] // 2
    parts = jnp.dot(matrix, pair, preferred_element_type=jnp.float32)
    real, imag = parts[:half], parts[half:]
    if sign > 0:
        return jnp.concatenate(
            [real[:, :vectors] - imag[:, vectors:], real[:, vectors:] + imag[:, :vectors]], axis=0
        )
    return jnp.concatenate(
        [real[:, :vectors] + imag[:, vectors:], real[:, vectors:] - imag[:, :vectors]], axis=0
    )


def natural_form(matrix, planar):
    half = matrix.shape[0] // 2
    turned = jnp.concatenate([-matrix[half:].astype(jnp.float32), matrix[:half].astype(jnp.float32)])
    whole = jnp.dot(matrix, planar[:half], preferred_element_type=jnp.float32) + jnp.dot(
        turned.astype(jnp.bfloat16), planar[half:], preferred_element_type=jnp.float32
    )
    return whole.astype(jnp.bfloat16)


def halo_fields(cells_x, cells_y):
    pairs = [(0, (cells_x - 1) * cells_y + y) for y in range(cells_y)]
    return pairs + [(1, x * cells_y + cells_y - 1) for x in range(cells_x)]


def local_fields(cells_x, cells_y):
    lines = cells_x * cells_y
    outside = halo_fields(cells_x, cells_y)
    every = [(code, line) for code in range(7) for line in range(lines)]
    return [pair for pair in every if pair not in outside]


def prepare_kernel(cells_x, cells_y, *refs):
    inputs, refs = refs[:6], refs[6:]
    matrix_ref, local_ref, left_ref, phase_ref, weight_ref, code_ref = refs[:6]
    held, link_rows_ref, sems = refs[6:12], refs[12], refs[13]
    copies = [
        pltpu.make_async_copy(src, dst, sems.at[k])
        for k, (src, dst) in enumerate(zip(inputs, held))
    ]
    for copy in copies:
        copy.start()
    v_ref, link_ref, dirs_ref, moms_ref, waves_ref, pair_ref = held
    f32, bf16 = jnp.float32, jnp.bfloat16
    order, vectors = v_ref.shape[2], v_ref.shape[3]
    half, cells_z = order // 2, order // 6
    lines = cells_x * cells_y
    times = weight_ref.shape[1]
    spread = one_hot(third(iota((half, cells_z), 0)) == iota((half, cells_z), 1))
    row, col = iota((half, LINK_COLS), 0), iota((half, LINK_COLS), 1)
    row_color = row - 3 * third(row)
    pair_at = third(col >> 1)
    col_in, col_out = (col >> 1) - 3 * pair_at, pair_at - 3 * third(pair_at)
    pick = [(row_color == col_out).astype(f32), (row_color == col_in).astype(f32)]
    wide = (LINK_COLS, 6 * 128)
    row, col = iota(wide, 0), iota(wide, 1)
    block, place = col >> 7, col & 127
    color = place - 3 * third(place)
    pair_at = third(row >> 1)
    row_in, row_out = (row >> 1) - 3 * pair_at, pair_at - 3 * third(pair_at)
    fits = 2 * third(pair_at) + (row & 1) == block
    expand = [one_hot(fits & (row_in == color)), one_hot(fits & (row_out == color))]
    row, col = iota((half, 128), 0), iota((half, 128), 1)
    near = ((third(row) == third(col)) & (col < half)).astype(f32)
    planar = planar_order(order)
    planar_ahead = planar_order(order, 3)
    copies[0].wait()
    copies[1].wait()
    for line in range(lines):
        for k in range(LINK_COLS // 2):
            link_rows_ref[line, 2 * k : 2 * k + 2] = link_ref[line, k].astype(f32)
    outside = halo_fields(cells_x, cells_y)
    inside = local_fields(cells_x, cells_y)
    ordered = []
    for line in range(lines):
        here = jnp.dot(
            planar, v_ref[line // cells_y, line % cells_y], preferred_element_type=f32
        )
        ordered.append(here)
        local_ref[inside.index((6, line))] = here
    for line in range(lines):
        here = ordered[line]
        ahead_z = jnp.concatenate(
            [here[3:half], here[:3], here[half + 3 :], here[half : half + 3]], axis=0
        )
        columns = slice(line * order, (line + 1) * order)
        for k, reordering in enumerate((planar, planar_ahead)):
            left_ref[k, :, columns] = lax.dot_general(
                v_ref[line // cells_y, line % cells_y],
                reordering,
                (((0,), (1,)), ((), ())),
                preferred_element_type=f32,
            ).astype(bf16)
        seen = lax.dot_general(
            spread,
            link_rows_ref[line].astype(bf16),
            (((1,), (1,)), ((), ())),
            preferred_element_type=f32,
        )
        pair = side_by_side(here)
        for way in range(2):
            blocks = jnp.dot(
                (seen * pick[way]).astype(bf16), expand[way], preferred_element_type=f32
            )
            for d in range(3):
                matrix = jnp.concatenate(
                    [
                        blocks[:, 256 * d : 256 * d + 128] * near,
                        blocks[:, 256 * d + 128 : 256 * d + 256] * near,
                    ],
                    axis=0,
                ).astype(bf16)
                if way == 1:
                    carried = transport(matrix[:, :half], pair, -1)
                    local_ref[inside.index((3 + d, line))] = carried.astype(bf16).astype(f32)
                elif (d, line) in outside:
                    matrix_ref[outside.index((d, line))] = natural_form(matrix[:, :half], planar)
                else:
                    ahead = ahead_z if d == 2 else ordered[line + (cells_y if d == 0 else 1)]
                    local_ref[inside.index((d, line))] = transport(
                        matrix[:, :half], side_by_side(ahead), 1
                    )
    for copy in copies[2:]:
        copy.wait()
    for t in range(times):
        sink = pair_ref[0, 0] == t
        source = pair_ref[0, 1] == t
        weight_ref[0, t] = jnp.full(weight_ref.shape[2:], jnp.where(sink, 1.0, 0.0), f32)
        weight_ref[1, t] = jnp.full(weight_ref.shape[2:], jnp.where(source, 1.0, 0.0), f32)
    wave_cols = waves_ref.shape[1]
    per_term = wave_cols // 3
    row, col = iota((wave_cols, 2 * vectors), 0), iota((wave_cols, 2 * vectors), 1)
    term = (row >= per_term).astype(jnp.int32) + (row >= 2 * per_term).astype(jnp.int32)
    wave_at = row - per_term * term - (col >= vectors).astype(jnp.int32)
    for o in range(phase_ref.shape[0]):
        code_ref[o] = jnp.full(code_ref.shape[1:], dirs_ref[o], jnp.int32).astype(f32)
        column = 2 * (jnp.where(dirs_ref[o] == 5, MOMENTA, 0) + moms_ref[o])
        phase_ref[o] = jnp.dot(
            waves_ref[...], one_hot(wave_at == column), preferred_element_type=f32
        )


def margin_kernel(cells_x, cells_y, groups, own_ops, *refs):
    matrix_ref, local_ref, left_ref, phase_ref, code_ref, halo_x_ref, halo_y_ref = refs[:7]
    swap_ref, hold_ref, field_ref, side_ref = refs[7:]
    f32, bf16 = jnp.float32, jnp.bfloat16
    me = lax.axis_index("gy")
    codes = {}
    for j in range(groups):
        for i in range(own_ops):
            codes[j, i] = jnp.max(code_ref[(me ^ j) * own_ops + i]).astype(jnp.int32)
    lines = cells_x * cells_y
    order, vectors = halo_x_ref.shape[2], halo_x_ref.shape[3]
    half = order // 2
    planar = planar_order(order)
    side_ref[0] = left_ref[0]
    side_ref[3] = left_ref[1]
    outside = halo_fields(cells_x, cells_y)
    for d in range(2):
        for line in range(lines):
            x, y = line // cells_y, line % cells_y
            columns = slice(line * order, (line + 1) * order)
            if (d, line) not in outside:
                ahead = line + (cells_y if d == 0 else 1)
                side_ref[1 + d, :, columns] = left_ref[0, :, ahead * order : (ahead + 1) * order]
                continue
            halo = halo_x_ref[0, y] if d == 0 else halo_y_ref[x, 0]
            side_ref[1 + d, :, columns] = lax.dot_general(
                halo, planar, (((0,), (1,)), ((), ())), preferred_element_type=f32
            ).astype(bf16)
            matrix = matrix_ref[outside.index((d, line))]
            field_ref[d, line] = jnp.dot(matrix, halo, preferred_element_type=f32)
    for k, (code, line) in enumerate(local_fields(cells_x, cells_y)):
        field_ref[code, line] = local_ref[k]
    for j in sorted(range(groups), key=lambda j: -(j & 1)):
        blocks = []
        for i in range(own_ops):
            o = (me ^ j) * own_ops + i
            code = codes[j, i]
            side = jnp.where((code >= 3) & (code < 6), code - 2, 0)
            cosine = phase_ref[o, :, 0:vectors]
            sine = phase_ref[o, :, vectors : 2 * vectors]
            pairs = []
            for line in range(lines):
                real, imag = field_ref[code, line, 0:half], field_ref[code, line, half:order]
                turned_r, turned_i = cosine * real - sine * imag, sine * real + cosine * imag
                pairs.append(jnp.concatenate([turned_r, turned_i], axis=1))
                pairs.append(jnp.concatenate([turned_i, -turned_r], axis=1))
            pair = jnp.concatenate(pairs, axis=0).astype(bf16)
            product = jnp.dot(side_ref[side], pair, preferred_element_type=f32)
            blocks += [product[:, :vectors], product[:, vectors:]]
        if j & 1:
            put_fixed(swap_ref.at[j >> 1], blocks)
            continue
        for k, block in enumerate(blocks):
            hold_ref[j >> 1, k * vectors : (k + 1) * vectors] = block


def scale_of(block):
    top = jnp.max(jnp.abs(block), axis=0, keepdims=True)
    return jnp.floor(jnp.log2(jnp.maximum(top, 1e-30))) + 1.0


def put_fixed(out_ref, blocks):
    rows, vectors = blocks[0].shape
    tail = iota((TAIL, vectors), 0)
    scales = jnp.zeros((TAIL, vectors), jnp.float32)
    for k, block in enumerate(blocks):
        scale = scale_of(block)
        scales = jnp.where(tail == k, scale, scales)
        fixed = jnp.floor(block * jnp.exp2(FIXED_BITS - scale) + 0.5)
        out_ref[k * rows : (k + 1) * rows] = fixed.astype(jnp.int32).astype(jnp.int16)
    out_ref[len(blocks) * rows :] = scales.astype(jnp.int32).astype(jnp.int16)


def from_fixed(ref, rows, k):
    scales = ref[ref.shape[0] - TAIL :].astype(jnp.int32).astype(jnp.float32)
    block = ref[k * rows : (k + 1) * rows].astype(jnp.int32).astype(jnp.float32)
    return block * jnp.exp2(scales[k : k + 1] - FIXED_BITS)


def group_block(held_ref, messages, j, start, rows):
    total = held_ref[j >> 1, pl.ds(start, rows)]
    for b, ref in enumerate(messages):
        total = total + fixed_at(ref.at[j >> (b + 1)], start, rows)
    return total


def fixed_at(ref, start, rows):
    tail = ref[ref.shape[0] - TAIL :].astype(jnp.int32).astype(jnp.float32)
    scale = jnp.max(
        jnp.where(iota(tail.shape, 0) == start // rows, tail, -1000.0), axis=0, keepdims=True
    )
    block = ref[pl.ds(start, rows)].astype(jnp.int32).astype(jnp.float32)
    return block * jnp.exp2(scale - FIXED_BITS)


def fold_kernel(level, vectors, held_ref, *refs):
    messages, out_ref = refs[:-1], refs[-1]
    for k in range(out_ref.shape[0]):
        blocks = [
            group_block(held_ref, messages, (2 * k + 1) << level, start, vectors)
            for start in range(0, held_ref.shape[1], vectors)
        ]
        put_fixed(out_ref.at[k], blocks)


def half_blocks(held_ref, messages, j, kept, vectors):
    me = lax.axis_index("gx") & 1
    half = held_ref.shape[1] // 2
    base = pl.multiple_of((me if kept else 1 - me) * half, half)
    steps = range(0, half, vectors)
    return [group_block(held_ref, messages, j, base + step, vectors) for step in steps]


def spread_kernel(level, vectors, held_ref, *refs):
    messages, (y_ref, diagonal_ref, x_ref) = refs[:-3], refs[-3:]
    put_fixed(y_ref, half_blocks(held_ref, messages, 1 << level, True, vectors))
    put_fixed(diagonal_ref, half_blocks(held_ref, messages, 1 << level, False, vectors))
    put_fixed(x_ref, half_blocks(held_ref, messages, 0, False, vectors))


def keep_kernel(vectors, held_ref, *refs):
    messages, came, out_ref = refs[:-4], refs[-4:-1], refs[-1]
    blocks = half_blocks(held_ref, messages, 0, True, vectors)
    for p in range(len(blocks)):
        for ref in came:
            blocks[p] = blocks[p] + from_fixed(ref, vectors, p)
    put_fixed(out_ref, blocks)


def both_kernel(vectors, norm_factor, own_ref, arrived_ref, out_ref):
    blocks = [
        from_fixed(own_ref, vectors, p) + from_fixed(arrived_ref, vectors, p)
        for p in range((own_ref.shape[0] - TAIL) // vectors)
    ]
    if norm_factor is None:
        put_fixed(out_ref, blocks)
        return
    for p, block in enumerate(blocks):
        out_ref[p * vectors : (p + 1) * vectors] = (block * norm_factor).astype(out_ref.dtype)


def contract(sums_ref, weight_ref, blocks, tau_ref, left_ref, right_ref):
    f32, bf16 = jnp.float32, jnp.bfloat16
    vectors = sums_ref.shape[2]
    count_ops = sums_ref.shape[0] // 2
    order = tau_ref.shape[2]
    spins = order // vectors
    me_t = lax.axis_index("ta")
    times = len(blocks)

    def chosen(end, k):
        total = jnp.zeros((vectors // 8, 8, vectors), f32)
        for t in range(times):
            weight = weight_ref[end, lax.rem(me_t + t, times)]
            total = total + blocks[t](k).astype(f32).reshape(total.shape) * weight
        return total.reshape(vectors, vectors)

    for o in range(count_ops):
        first = 2 * o * vectors
        a_r, a_i = chosen(0, 2 * o).astype(bf16), chosen(0, 2 * o + 1).astype(bf16)
        b_r, b_i = chosen(1, 2 * o).T.astype(bf16), chosen(1, 2 * o + 1).T.astype(bf16)
        real, imag = slice(first, first + vectors), slice(first + vectors, first + 2 * vectors)
        left_ref[real, 0:vectors] = a_r
        left_ref[real, vectors:] = -a_i
        left_ref[imag, 0:vectors] = a_i
        left_ref[imag, vectors:] = a_r
        right_ref[0:vectors, real] = b_r
        right_ref[0:vectors, imag] = -b_i
        right_ref[vectors:, real] = b_i
        right_ref[vectors:, imag] = b_r
    lanes = sums_ref.shape[1]
    fold = lambda t: jnp.sum(t.reshape(vectors // lanes, lanes, vectors), axis=0)
    sums = [jnp.zeros((lanes, vectors), f32) for _ in range(2 * count_ops)]
    for s in range(spins):
        rows = slice(s * vectors, (s + 1) * vectors)
        x = jnp.dot(
            left_ref[...],
            jnp.concatenate([tau_ref[0, rows], tau_ref[1, rows]], axis=0),
            preferred_element_type=f32,
        )
        for c in range(spins):
            cols = slice(c * vectors, (c + 1) * vectors)
            y = jnp.dot(
                jnp.concatenate([tau_ref[0, rows, cols], tau_ref[1, rows, cols]], axis=1),
                right_ref[...],
                preferred_element_type=f32,
            )
            for o in range(count_ops):
                first = 2 * o * vectors
                x_r = x[first : first + vectors, cols]
                x_i = x[first + vectors : first + 2 * vectors, cols]
                y_r = y[:, first : first + vectors]
                y_i = y[:, first + vectors : first + 2 * vectors]
                sums[2 * o] = sums[2 * o] + fold(x_r * y_r + x_i * y_i)
                sums[2 * o + 1] = sums[2 * o + 1] + fold(x_i * y_r - x_r * y_i)
    for k, total in enumerate(sums):
        sums_ref[k] = total


def part_of(ref, vectors):
    return lambda k: ref[k * vectors : (k + 1) * vectors]


def first_contract_kernel(times, split, live_ref, weight_ref, tau_ref, *refs):
    blocks, (live_out_ref, sums_ref, left_ref, right_ref) = refs[:times], refs[times:]
    live = jnp.where(live_ref[0] > 0, 1.0, 0.0)
    live_out_ref[...] = jnp.full(live_out_ref.shape, live, jnp.float32)
    if split:
        vectors = sums_ref.shape[2]
        blocks = [part_of(ref, vectors) for ref in blocks]
        contract(sums_ref, weight_ref, blocks, tau_ref, left_ref, right_ref)
    else:
        sums_ref[...] = jnp.zeros_like(sums_ref)


def margins_kernel(kept_ref, other_ref, margin_ref):
    half = kept_ref.shape[0]
    me = lax.axis_index("gx") & 1
    for place, ref in ((me, kept_ref), (1 - me, other_ref)):
        rows = pl.ds(pl.multiple_of(place * half, half), half)
        margin_ref[0, rows] = ref[...].astype(jnp.float32)


def second_contract_kernel(times, split, weight_ref, tau_ref, *refs):
    other, kept, refs = refs[:times], refs[times : 2 * times], refs[2 * times :]
    live_ref, first_sums_ref, corr_ref, sums_ref, left_ref, right_ref = refs
    vectors = sums_ref.shape[2]
    half = kept[0].shape[0]
    me = lax.axis_index("gx") & 1
    parts_per_half = half // vectors

    def either(kept_ref, other_ref):
        def part(k):
            row = (k % parts_per_half) * vectors
            own, far = kept_ref[row : row + vectors], other_ref[row : row + vectors]
            mine = (k // parts_per_half == me).astype(jnp.float32)
            return own.astype(jnp.float32) * mine + far.astype(jnp.float32) * (1.0 - mine)

        return part

    blocks = [part_of(ref, vectors) for ref in other]
    if not split:
        blocks = [either(a, b) for a, b in zip(kept, other)]
    contract(sums_ref, weight_ref, blocks, tau_ref, left_ref, right_ref)
    now_ops = sums_ref.shape[0] // 2
    known = [(sums_ref, (1 - me) * now_ops)] if split else [(sums_ref, 0)]
    if split:
        known.append((first_sums_ref, me * now_ops))
    shape = corr_ref.shape[1:]
    row, col = iota(shape, 0), iota(shape, 1)
    result = jnp.zeros(shape, jnp.float32)
    for ref, first in known:
        for k in range(2 * now_ops):
            total = jnp.sum(jnp.sum(ref[k], axis=0, keepdims=True), axis=1, keepdims=True)
            here = (row == first + k // 2) & (col == k % 2)
            result = jnp.where(here, total * (1.0 / vectors), result)
    corr_ref[0] = result * live_ref[0 : shape[0], 0 : shape[1]]


def vmem_spec():
    return pl.BlockSpec(memory_space=pltpu.VMEM)


def smem_spec():
    return pl.BlockSpec(memory_space=pltpu.SMEM)


def hbm_spec():
    return pl.BlockSpec(memory_space=pltpu.HBM)


def in_hbm(x):
    return pltpu.with_memory_space_constraint(x, pltpu.HBM)


def local_call(body, name, outs, in_specs, out_specs, scratch=(), cost=None):
    return pl.pallas_call(
        body,
        out_shape=outs,
        in_specs=in_specs,
        out_specs=out_specs,
        scratch_shapes=list(scratch),
        compiler_params=pltpu.CompilerParams(vmem_limit_bytes=VMEM_LIMIT),
        cost_estimate=cost,
        name=name,
    )


def from_step(block, axis, step):
    count = lax.axis_size(axis)
    return lax.ppermute(block, axis, [((i + step) % count, i) for i in range(count)])


def from_partner(block, axis, step):
    count = lax.axis_size(axis)
    return lax.ppermute(block, axis, [(i ^ step, i) for i in range(count)])


def from_diagonal(block, axes, sources):
    rows, columns = (lax.axis_size(axis) for axis in axes)
    perm = []
    for row in range(rows):
        for column in range(columns):
            from_row, from_column = sources(row, column)
            perm.append((from_row * columns + from_column, row * columns + column))
    return lax.ppermute(block, axes, perm)


def per_device(eigvecs, links, op_dirs, op_moms, perams, pair_times, slot_counts):
    f32, bf16 = jnp.float32, jnp.bfloat16
    _, cells_x, cells_y, cells_z, colors, _, vectors = eigvecs.shape
    order = cells_z * colors * 2
    lines = cells_x * cells_y
    count_ops = op_dirs.shape[0]
    times, shares, groups = lax.axis_size("ta"), lax.axis_size("gx"), lax.axis_size("gy")
    levels = groups.bit_length() - 1
    own_ops = count_ops // groups
    own_rows = own_ops * 2 * vectors
    field = eigvecs.reshape(cells_x, cells_y, order, vectors)
    halo_x = from_step(field[0:1], "gx", 1)
    halo_y = from_step(field, "gy", 1)
    link_field = links[0].transpose(0, 1, 3, 5, 6, 4, 2).reshape(lines, 27, 2, cells_z)
    outside, inside = halo_fields(cells_x, cells_y), local_fields(cells_x, cells_y)
    inputs = [field, link_field, op_dirs, op_moms, wave_constants(cells_z), pair_times]
    inputs = [in_hbm(x) for x in inputs]
    held = [
        pltpu.SMEM(x.shape, x.dtype) if x.dtype == jnp.int32 else pltpu.VMEM(x.shape, x.dtype)
        for x in inputs
    ]
    matrices, local, left, phases, weights, codes = local_call(
        functools.partial(prepare_kernel, cells_x, cells_y),
        "prepare_lines",
        (
            jax.ShapeDtypeStruct((len(outside), order, order), bf16),
            jax.ShapeDtypeStruct((len(inside), order, vectors), f32),
            jax.ShapeDtypeStruct((2, vectors, lines * order), bf16),
            jax.ShapeDtypeStruct((count_ops, order // 2, 2 * vectors), f32),
            jax.ShapeDtypeStruct((2, times, 8, vectors), f32),
            jax.ShapeDtypeStruct((count_ops, 8, vectors), f32),
        ),
        [hbm_spec()] * len(inputs),
        (vmem_spec(),) * 6,
        held
        + [
            pltpu.VMEM((lines, LINK_COLS, cells_z), f32),
            pltpu.SemaphoreType.DMA((len(inputs),)),
        ],
    )(*inputs)
    message = lambda rows, *lead: jax.ShapeDtypeStruct((*lead, rows + TAIL, vectors), jnp.int16)
    swap, held = local_call(
        functools.partial(margin_kernel, cells_x, cells_y, groups, own_ops),
        "partial_margins",
        (
            message(own_rows, groups // 2),
            jax.ShapeDtypeStruct((groups // 2, own_rows, vectors), f32),
        ),
        [vmem_spec()] * 7,
        (vmem_spec(),) * 2,
        [
            pltpu.VMEM((7, lines, order, vectors), f32),
            pltpu.VMEM((4, vectors, lines * order), bf16),
        ],
    )(matrices, local, left, phases, codes, halo_x, halo_y)

    def in_vmem(body, name, outs, *inputs):
        outs = outs if isinstance(outs, tuple) else (outs,)
        specs = (vmem_spec(),) * len(outs)
        return local_call(body, name, outs, [vmem_spec()] * len(inputs), specs)(*inputs)

    half = own_rows // 2
    messages = [from_partner(swap, "gy", 1)]
    last = levels - 1
    for b in range(1, last):
        body = functools.partial(fold_kernel, b, vectors)
        shape = message(own_rows, groups >> (b + 1))
        (sent,) = in_vmem(body, "fold_groups", shape, held, *messages)
        messages.append(from_partner(sent, "gy", 1 << b))
    body = functools.partial(spread_kernel, last, vectors)
    for_y, for_both, for_x = in_vmem(body, "spread_halves", (message(half),) * 3, held, *messages)
    came = [
        from_partner(for_y, "gy", 1 << last),
        from_diagonal(for_both, ("gx", "gy"), lambda x, y: (x ^ 1, y ^ (1 << last))),
        from_partner(for_x, "gx", 1),
    ]
    body = functools.partial(keep_kernel, vectors)
    (packed,) = in_vmem(body, "keep_half", message(half), held, *messages, *came)
    norm_factor = 1.0 / math.sqrt(3.0 * cells_x * shares * cells_y * groups * cells_z)
    step = 2
    while step < shares:
        arrived = from_partner(packed, "gx", step)
        step *= 2
        last_one = step >= shares
        body = functools.partial(both_kernel, vectors, norm_factor if last_one else None)
        shape = jax.ShapeDtypeStruct((half, vectors), bf16) if last_one else message(half)
        (packed,) = in_vmem(body, "finish_half" if last_one else "sum_both", shape, packed, arrived)
    finished = packed
    kept = [finished] + [from_step(finished, "ta", t) for t in range(1, times)]
    other = [from_partner(finished, "gx", 1)]
    for t in range(1, times):
        source = lambda row, x: ((row + t) % times, x ^ 1)
        other.append(from_diagonal(finished, ("ta", "gx"), source))
    split = own_ops % 2 == 0
    now_ops = own_ops // 2 if split else own_ops
    sums_shape = (2 * now_ops, 32, vectors)
    scratch = [
        pltpu.VMEM((2 * now_ops * vectors, 2 * vectors), bf16),
        pltpu.VMEM((2 * vectors, 2 * now_ops * vectors), bf16),
    ]
    live, sums = local_call(
        functools.partial(first_contract_kernel, times, split),
        "first_contraction",
        (jax.ShapeDtypeStruct((8, vectors), f32), jax.ShapeDtypeStruct(sums_shape, f32)),
        [smem_spec()] + [vmem_spec()] * (2 + times),
        (vmem_spec(),) * 2,
        scratch,
    )(slot_counts, weights, perams[0], *kept)
    margins = local_call(
        margins_kernel,
        "margins_out",
        jax.ShapeDtypeStruct((1, own_rows, vectors), f32),
        [vmem_spec()] * 2,
        vmem_spec(),
    )(*lax.optimization_barrier((kept[0], other[0], sums))[:2])
    correlators = local_call(
        functools.partial(second_contract_kernel, times, split),
        "second_contraction",
        jax.ShapeDtypeStruct((1, own_ops, 2), f32),
        [vmem_spec()] * (4 + 2 * times),
        vmem_spec(),
        [pltpu.VMEM(sums_shape, f32)] + scratch,
    )(weights, perams[0], *other, *kept, live, sums)
    return (margins.reshape(1, own_ops, 2, vectors, vectors), correlators)


def solution(mesh):
    placed = (
        P("ta", "gx", "gy", None, None, None, None),
        P("ta", "gx", "gy", None, None, None, None, None),
        P(),
        P(),
        P(("ta", "gx"), None, None, None),
        P(("ta", "gx"), None),
        P(("ta", "gx")),
    )
    return jax.shard_map(
        per_device,
        mesh=mesh,
        in_specs=placed,
        out_specs=(P("ta", "gy", None, None, None), P(("ta", "gx"), "gy", None)),
        check_vma=False,
    )
```
